32 devices in a mesh: dp: 8 (over z, y), seq: 4 (over x, core).
Axes of the slice: x: 2, y: 2, z: 4, core: 2. Of those that a mesh axis runs over, the one named last changes fastest.
Arguments:
- block_in: bfloat16 [32, 1024, 1024], P('dp', 'seq'), may hold values from -6 to 6
- text_states: bfloat16 [32, 128, 1024], P('dp'), may hold values from -6 to 6
- caption_len: int32 [32], P('dp'), may hold values from 1 to 128, as said below
- out_grad: bfloat16 [32, 1024, 1024], P('dp', 'seq'), may hold values from -6 to 6
- first_gain: bfloat16 [1024], P(('dp', 'seq')), may hold values from 0.5 to 1.5
- first_bias: bfloat16 [1024], P(('dp', 'seq')), may hold values from -1 to 1
- query_weight: bfloat16 [1024, 1024], P(('dp', 'seq')), may hold values from -0.1875 to 0.1875
- key_weight: bfloat16 [1024, 1024], P(('dp', 'seq')), may hold values from -0.1875 to 0.1875
- value_weight: bfloat16 [1024, 1024], P(('dp', 'seq')), may hold values from -0.1875 to 0.1875
- output_weight: bfloat16 [1024, 1024], P(('dp', 'seq')), may hold values from -0.75 to 0.75
- second_gain: bfloat16 [1024], P(('dp', 'seq')), may hold values from 0.5 to 1.5
- second_bias: bfloat16 [1024], P(('dp', 'seq')), may hold values from -1 to 1
- cross_query: bfloat16 [1024, 1024], P(('dp', 'seq')), may hold values from -0.1875 to 0.1875
- cross_key: bfloat16 [1024, 1024], P(('dp', 'seq')), may hold values from -0.1875 to 0.1875
- cross_value: bfloat16 [1024, 1024], P(('dp', 'seq')), may hold values from -0.1875 to 0.1875
- cross_output: bfloat16 [1024, 1024], P(('dp', 'seq')), may hold values from -0.5 to 0.5
- third_gain: bfloat16 [1024], P(('dp', 'seq')), may hold values from 0.5 to 1.5
- third_bias: bfloat16 [1024], P(('dp', 'seq')), may hold values from -1 to 1
- up_weight: bfloat16 [1024, 4096], P(('dp', 'seq')), may hold values from -0.1875 to 0.1875
- down_weight: bfloat16 [4096, 1024], P(('dp', 'seq')), may hold values from -0.125 to 0.125
Outputs:
- block_out: bfloat16 [32, 1024, 1024], P('dp', 'seq')
- input_grad: float32 [32, 1024, 1024], P('dp', 'seq')
- text_grad: float32 [32, 128, 1024], P('dp', 'seq')
- first_gain_grad: float32 [1024], P(('dp', 'seq'))
- first_bias_grad: float32 [1024], P(('dp', 'seq'))
- query_grad: float32 [1024, 1024], P(('dp', 'seq'))
- key_grad: float32 [1024, 1024], P(('dp', 'seq'))
- value_grad: float32 [1024, 1024], P(('dp', 'seq'))
- output_grad: float32 [1024, 1024], P(('dp', 'seq'))
- second_gain_grad: float32 [1024], P(('dp', 'seq'))
- second_bias_grad: float32 [1024], P(('dp', 'seq'))
- cross_query_grad: float32 [1024, 1024], P(('dp', 'seq'))
- cross_key_grad: float32 [1024, 1024], P(('dp', 'seq'))
- cross_value_grad: float32 [1024, 1024], P(('dp', 'seq'))
- cross_output_grad: float32 [1024, 1024], P(('dp', 'seq'))
- third_gain_grad: float32 [1024], P(('dp', 'seq'))
- third_bias_grad: float32 [1024], P(('dp', 'seq'))
- up_grad: float32 [1024, 4096], P(('dp', 'seq'))
- down_grad: float32 [4096, 1024], P(('dp', 'seq'))
The draws below stay inside these ranges and needn't reach their ends.
Inputs may be any that keep to these rules, and one draw needn't show every extreme that they name: `caption_len`: caption lengths have a long tail toward short captions; in every draw some item has all 128 positions.
All inputs are finite; a program needn't handle non-finite values.
Results may differ from the reference program's by a relative error of at most 0.018.
Values may be sent and summed in bfloat16 or wider, within the bound.
A program may use at most 320 MiB of HBM per device.

```python
import jax
import jax.numpy as jnp
from jax import lax

D = 1024
HEAD_DIM = 64
FF = 4096
TEXT_W = 1024
TEXT_LEN = 128
SEQ_LEN = 1024
ITEMS = 32


def draw_caption_len(key, part):
    key = jax.random.fold_in(key, 7)
    first_key, second_key, third_key = jax.random.split(key, 3)
    left = jax.random.randint(first_key, (ITEMS,), 1, TEXT_LEN + 1)
    right = jax.random.randint(second_key, (ITEMS,), 1, TEXT_LEN + 1)
    tail = jnp.maximum(1, left * right // TEXT_LEN)
    chosen = jax.random.randint(third_key, (), 0, ITEMS)
    return jnp.where(jnp.arange(ITEMS) == chosen, TEXT_LEN, tail).astype(jnp.int32)


def block_levels(rng, extent, pieces, low, top_value):
    level, own = 1.0, jax.random.fold_in(rng, 6)
    for position, shards_of in pieces:
        steps = jnp.exp(jax.random.uniform(jax.random.fold_in(own, position), (shards_of,), jnp.float32, low / len(pieces), top_value / len(pieces)))
        level = level * jnp.repeat(steps, extent[position] // shards_of).reshape([-1 if axis == position else 1 for axis in range(len(extent))])
    return level


def normal_values(rng, shape, deviation, bound, shards=(), kind=jnp.bfloat16):
    values = deviation * jax.random.normal(rng, shape, jnp.float32)
    if shards:
        values = values * block_levels(rng, shape, shards, -0.22, 0.18)
    return jnp.clip(values, -bound, bound).astype(kind)


def setup_inputs(seed: int = 0) -> dict:
    key_of = jax.random.split(jax.random.key(seed), 21)
    return {
        "block_in": normal_values(key_of[0], (ITEMS, SEQ_LEN, D), 1.0, 6.0, ((0, 8), (1, 4))),
        "text_states": normal_values(key_of[1], (ITEMS, TEXT_LEN, TEXT_W), 1.0, 6.0, ((0, 8),)),
        "caption_len": draw_caption_len(jax.random.fold_in(key_of[20], 71), 0),
        "out_grad": normal_values(key_of[3], (ITEMS, SEQ_LEN, D), 1.0, 6.0, ((0, 8), (1, 4))),
        "first_gain": jnp.clip(1.0 + 0.1 * jax.random.normal(key_of[4], (D,), jnp.float32), 0.5, 1.5).astype(jnp.bfloat16),
        "first_bias": normal_values(key_of[5], (D,), 0.2, 1.0, ((0, 32),)),
        "query_weight": normal_values(key_of[6], (D, D), D ** -0.5, 0.1875, ((0, 32),)),
        "key_weight": normal_values(key_of[7], (D, D), D ** -0.5, 0.1875, ((0, 32),)),
        "value_weight": normal_values(key_of[8], (D, D), D ** -0.5, 0.1875, ((0, 32),)),
        "output_weight": normal_values(key_of[9], (D, D), (D // 16) ** -0.5, 0.75, ((0, 32),)),
        "second_gain": jnp.clip(1.0 + 0.1 * jax.random.normal(key_of[10], (D,), jnp.float32), 0.5, 1.5).astype(jnp.bfloat16),
        "second_bias": normal_values(key_of[11], (D,), 0.2, 1.0, ((0, 32),)),
        "cross_query": normal_values(key_of[12], (D, D), D ** -0.5, 0.1875, ((0, 32),)),
        "cross_key": normal_values(key_of[13], (TEXT_W, D), TEXT_W ** -0.5, 0.1875, ((0, 32),)),
        "cross_value": normal_values(key_of[14], (TEXT_W, D), TEXT_W ** -0.5, 0.1875, ((0, 32),)),
        "cross_output": normal_values(key_of[15], (D, D), (D // 8) ** -0.5, 0.5, ((0, 32),)),
        "third_gain": jnp.clip(1.0 + 0.1 * jax.random.normal(key_of[16], (D,), jnp.float32), 0.5, 1.5).astype(jnp.bfloat16),
        "third_bias": normal_values(key_of[17], (D,), 0.2, 1.0, ((0, 32),)),
        "up_weight": normal_values(key_of[18], (D, FF), D ** -0.5, 0.1875, ((0, 32),)),
        "down_weight": normal_values(key_of[19], (FF, D), (FF // 2) ** -0.5, 0.125, ((0, 32),)),
    }


EPS = 1e-05
HIGH = lax.Precision.HIGHEST

@jax.custom_vjp
def low(v):
    return lax.optimization_barrier(v.astype(jnp.bfloat16)).astype(jnp.float32)

@jax.custom_vjp
def low_back(v):
    return v

def low_keep(v):
    return (low(v), None)

def low_pass(kept, grad):
    return (grad,)

def back_keep(v):
    return (v, None)

def back_low(kept, grad):
    return (low(grad),)
low.defvjp(low_keep, low_pass)
low_back.defvjp(back_keep, back_low)

def layer_norm(values_in, gain, bias):
    center = values_in - lax.optimization_barrier(jnp.mean(values_in, axis=-1, keepdims=True))
    spread = lax.optimization_barrier(jnp.mean(center * center, axis=-1, keepdims=True))
    return center * lax.rsqrt(spread + EPS) * gain + bias

def matmul(left, right):
    return jnp.dot(left, right, precision=HIGH)

def attend(query_rows, key_rows, value_rows, visible):
    head_count = query_rows.shape[-1] // HEAD_DIM
    query_heads = query_rows.reshape(query_rows.shape[0], head_count, HEAD_DIM)
    key_heads = key_rows.reshape(key_rows.shape[0], head_count, HEAD_DIM)
    value_heads = value_rows.reshape(value_rows.shape[0], head_count, HEAD_DIM)
    scores = jnp.einsum('qhd,khd->hqk', query_heads, key_heads, precision=HIGH) * HEAD_DIM ** (-0.5)
    scores = low_back(scores)
    scores = jnp.where(visible[None, :, :], scores, -1e+30)
    weights = low(jax.nn.softmax(scores, axis=-1))
    mixed = jnp.einsum('hqk,khd->qhd', weights, value_heads, precision=HIGH)
    return mixed.reshape(query_rows.shape[0], head_count * HEAD_DIM)

def item_forward(params, item_in, text_in, caption):
    first_gain, first_bias, query_weight, key_weight, value_weight, output_weight, second_gain, second_bias, cross_query, cross_key, cross_value, cross_output, third_gain, third_bias, up_weight, down_weight = params
    positions = jnp.arange(SEQ_LEN, dtype=jnp.int32)
    causal = positions[None, :] <= positions[:, None]
    text_pos = jnp.arange(TEXT_LEN, dtype=jnp.int32)
    visible = jnp.broadcast_to(text_pos[None, :] < caption, (SEQ_LEN, TEXT_LEN))
    normed_one = low(layer_norm(item_in, first_gain, first_bias))
    query_rows = low(low_back(matmul(normed_one, query_weight)))
    key_rows = low(low_back(matmul(normed_one, key_weight)))
    value_rows = low(low_back(matmul(normed_one, value_weight)))
    attended = low(low_back(attend(query_rows, key_rows, value_rows, causal)))
    after_self = item_in + low_back(matmul(attended, output_weight))
    normed_two = low(layer_norm(after_self, second_gain, second_bias))
    cross_rows = low(low_back(matmul(normed_two, cross_query)))
    text_keys = low(low_back(matmul(text_in, cross_key)))
    text_values = low(low_back(matmul(text_in, cross_value)))
    crossed = low(low_back(attend(cross_rows, text_keys, text_values, visible)))
    after_cross = after_self + low_back(matmul(crossed, cross_output))
    normed_three = low(layer_norm(after_cross, third_gain, third_bias))
    hidden = low_back(matmul(normed_three, up_weight))
    activated = low(jax.nn.gelu(hidden, approximate=False))
    return after_cross + low_back(matmul(activated, down_weight))

def reference(block_in, text_states, caption_len, out_grad, first_gain, first_bias, query_weight, key_weight, value_weight, output_weight, second_gain, second_bias, cross_query, cross_key, cross_value, cross_output, third_gain, third_bias, up_weight, down_weight):
    params = (first_gain.astype(jnp.float32), first_bias.astype(jnp.float32), query_weight.astype(jnp.float32), key_weight.astype(jnp.float32), value_weight.astype(jnp.float32), output_weight.astype(jnp.float32), second_gain.astype(jnp.float32), second_bias.astype(jnp.float32), cross_query.astype(jnp.float32), cross_key.astype(jnp.float32), cross_value.astype(jnp.float32), cross_output.astype(jnp.float32), third_gain.astype(jnp.float32), third_bias.astype(jnp.float32), up_weight.astype(jnp.float32), down_weight.astype(jnp.float32))

    def one_item(totals, inputs):
        item_in, text_in, caption, cotangent = inputs

        def forward(params_in, item_values, text_values):
            return item_forward(params_in, item_values, text_values, caption)
        result, pull = jax.vjp(forward, params, item_in.astype(jnp.float32), text_in.astype(jnp.float32))
        param_grads, item_grad, text_item_grad = pull(cotangent.astype(jnp.float32))
        totals = tuple((left + right for left, right in zip(totals, param_grads)))
        return (totals, (result.astype(jnp.bfloat16), item_grad, text_item_grad))
    start = tuple((jnp.zeros_like(param) for param in params))
    totals, (block_out, input_grad, text_grad) = lax.scan(one_item, start, (block_in, text_states, caption_len, out_grad))
    return (block_out, input_grad, text_grad, totals[0], totals[1], totals[2], totals[3], totals[4], totals[5], totals[6], totals[7], totals[8], totals[9], totals[10], totals[11], totals[12], totals[13], totals[14], totals[15])
```

```python
import functools

import jax
import jax.numpy as jnp
from jax import lax
from jax.experimental import pallas as pl
from jax.experimental.pallas import tpu as pltpu
from jax.sharding import PartitionSpec as P

MESH = pl.DeviceIdType.MESH
ANY = pl.ANY


class Place:
    def __init__(self, dims):
        self.nz, self.ny, self.nx, self.nc = dims
        dp, seq = lax.axis_index("dp"), lax.axis_index("seq")
        self.z, self.y = lax.div(dp, self.ny), lax.rem(dp, self.ny)
        self.x, self.c = lax.div(seq, self.nc), lax.rem(seq, self.nc)
        self.dp, self.seq = dp, seq

    def dev(self, z=None, y=None, x=None, c=None):
        z = self.z if z is None else z
        y = self.y if y is None else y
        x = self.x if x is None else x
        c = self.c if c is None else c
        return (z * self.ny + y, x * self.nc + c)

    def z_others(self):
        return [lax.rem(self.z + k, self.nz) for k in range(1, self.nz)]


def hello(peers):
    barrier = pltpu.get_barrier_semaphore()
    for peer in peers:
        pl.semaphore_signal(barrier, inc=1, device_id=peer, device_id_type=MESH)
    pl.semaphore_wait(barrier, len(peers))


def push(src, dst, send, recv, device):
    pltpu.make_async_remote_copy(
        src_ref=src, dst_ref=dst, send_sem=send, recv_sem=recv, device_id=device, device_id_type=MESH
    ).start()


def drain(ref, sem):
    pltpu.make_async_copy(ref, ref, sem).wait()


def gather_kernel(dims, units, chunks, n, exch, *refs):
    ni = n + (1 if exch else 0)
    ins, outs = refs[:ni], refs[ni : 2 * ni]
    local_sem, send, recv = refs[2 * ni : 2 * ni + 3]
    at = Place(dims)
    nz = dims[0]
    z, y, x, c = at.z, at.y, at.x, at.c
    oy, ox, oc = 1 - y, 1 - x, 1 - c
    peers = [at.dev(z=k) for k in at.z_others()] + [at.dev(y=oy), at.dev(x=ox), at.dev(c=oc)]
    if exch:
        peers = peers + [at.dev(x=ox, c=oc)]
    hello(peers)

    def part(u, *where):
        a, r0, nr, c0, ncol, _ = units[u]
        return outs[a].at[(*where, pl.ds(r0, nr), pl.ds(c0, ncol))]

    every = slice(None)

    def first_of(u, there):
        if units[u][5] == 0:
            return part(u, every, y, ox if there else x, c)
        return part(u, every, oy if there else y, x, c)

    def second_of(u, there):
        if units[u][5] == 0:
            return part(u, every, oy if there else y, every, c)
        return part(u, every, every, ox if there else x, c)

    def z_go(u):
        a, r0, nr, c0, ncol, _ = units[u]
        for k in at.z_others():
            push(ins[a].at[pl.ds(r0, nr), pl.ds(c0, ncol)], part(u, z, y, x, c), send.at[u], recv.at[u, 0], at.dev(z=k))

    def core_go(u, block):
        push(block, block, send.at[u], recv.at[u, 3], at.dev(c=oc))

    def first_go(u):
        drain(part(u, slice(0, nz - 1), y, x, c), recv.at[u, 0])
        block = first_of(u, False)
        push(block, block, send.at[u], recv.at[u, 1], at.dev(x=ox) if units[u][5] == 0 else at.dev(y=oy))
        core_go(u, block)

    def second_go(u):
        drain(first_of(u, True), recv.at[u, 1])
        core_go(u, first_of(u, True))
        block = second_of(u, False)
        push(block, block, send.at[u], recv.at[u, 2], at.dev(y=oy) if units[u][5] == 0 else at.dev(x=ox))

    def third_go(u):
        drain(second_of(u, True), recv.at[u, 2])
        core_go(u, second_of(u, True))

    def finish(u):
        drain(part(u, every, every, every, oc), recv.at[u, 3])
        drain(part(u, slice(0, nz - 1), y, x, c), send.at[u])
        drain(first_of(u, False), send.at[u])
        drain(second_of(u, False), send.at[u])
        drain(part(u, every, every, every, c), send.at[u])

    for a in range(n):
        pltpu.make_async_copy(ins[a], outs[a].at[z, y, x, c], local_sem).start()
    if exch:
        src, dst = ins[n], outs[n]
        me = at.seq
        pltpu.make_async_copy(src.at[me], dst.at[me], local_sem).start()
        last = len(units)
        for px, pc in ((ox, c), (ox, oc), (x, oc)):
            push(src.at[px * 2 + pc], dst.at[me], send.at[last], recv.at[last, 0], at.dev(x=px, c=pc))
    for u in chunks[0]:
        z_go(u)
    for a in range(n):
        pltpu.make_async_copy(ins[a], outs[a].at[z, y, x, c], local_sem).wait()
    if exch:
        pltpu.make_async_copy(src.at[me], dst.at[me], local_sem).wait()
    count = len(chunks)
    for t in range(count + 2):
        if t + 1 < count:
            for u in chunks[t + 1]:
                z_go(u)
        if t < count:
            for u in chunks[t]:
                first_go(u)
        if 0 <= t - 1 < count:
            for u in chunks[t - 1]:
                second_go(u)
        if 0 <= t - 2 < count:
            for u in chunks[t - 2]:
                third_go(u)
    for u in range(len(units)):
        finish(u)
    if exch:
        drain(dst.at[0:3], recv.at[last, 0])
        drain(dst.at[0:3], send.at[last])


AG_UNITS = [(0, 0, 16, 0, 128, 0), (1, 0, 32, 0, 1024, 0), (2, 0, 32, 0, 1024, 1), (3, 0, 32, 0, 1024, 0), (4, 0, 32, 0, 1024, 1)]
AG_UNITS += [(5, 0, 32, 0, 1024, 0), (6, 0, 32, 0, 1024, 1), (7, 0, 32, 0, 1024, 0), (8, 0, 32, 0, 1024, 1)]
AG_UNITS += [(9, 0, 32, 1024 * j, 1024, j % 2) for j in range(4)]
AG_UNITS += [(10, 32 * j, 32, 0, 1024, j % 2) for j in range(4)]
AG_CHUNKS = [(0, 1, 2), (3, 4), (5, 6), (7, 8), (9, 10), (11, 12), (13, 14), (15, 16)]


def gather(dims, shards, units, chunks, exch=None, cid=1):
    n = len(shards)
    ins = list(shards) + ([exch] if exch is not None else [])
    out_shape = [jax.ShapeDtypeStruct(tuple(dims) + s.shape, s.dtype) for s in shards]
    if exch is not None:
        out_shape.append(jax.ShapeDtypeStruct(exch.shape, exch.dtype))
    m, nu = len(ins), len(units) + 1
    outs = pl.pallas_call(
        functools.partial(gather_kernel, dims, units, chunks, n, exch is not None),
        out_shape=out_shape,
        in_specs=[pl.BlockSpec(memory_space=ANY)] * m,
        out_specs=[pl.BlockSpec(memory_space=ANY)] * m,
        scratch_shapes=[pltpu.SemaphoreType.DMA, pltpu.SemaphoreType.DMA((nu,)), pltpu.SemaphoreType.DMA((nu, 4))],
        compiler_params=pltpu.CompilerParams(collective_id=cid, has_side_effects=True),
        name="gather",
    )(*ins)
    return [o.reshape((-1,) + o.shape[5:]) for o in outs[:n]], (outs[n] if exch is not None else None)


def add_to(dst, src):
    dst[...] = dst[...] + src[...]


def scatter_kernel(dims, units, n, *refs):
    ins, outs = refs[:n], refs[n : 2 * n]
    m = len(units)
    rest = refs[2 * n :]
    own, rc, r2, r3, r4 = (rest[k * m : (k + 1) * m] for k in range(5))
    local_sem, send, recv = rest[5 * m : 5 * m + 3]
    at = Place(dims)
    nz, ny, nx, nc = dims
    z, y, x, c = at.z, at.y, at.x, at.c
    oy, ox, oc = 1 - y, 1 - x, 1 - c
    hello([at.dev(z=k) for k in at.z_others()] + [at.dev(y=oy), at.dev(x=ox), at.dev(c=oc)])
    every = slice(None)

    def source(i, core):
        a, r0, nr, c0, ncol, _ = units[i]
        return ins[a].at[(every, every, every, core, pl.ds(r0, nr), pl.ds(c0, ncol))]

    def core_go(i):
        pltpu.make_async_copy(source(i, c), own[i], local_sem.at[i]).start()
        push(source(i, oc), rc[i], send.at[i], recv.at[i, 0], at.dev(c=oc))

    def first_go(i):
        drain(own[i], local_sem.at[i])
        drain(rc[i], recv.at[i, 0])

        @pl.loop(0, nz)
        def _(a):
            for b in range(ny):
                for d in range(nx):
                    add_to(own[i].at[a, b, d], rc[i].at[a, b, d])

        if units[i][5] == 0:
            push(own[i].at[:, oy], r2[i], send.at[i], recv.at[i, 1], at.dev(y=oy))
        else:
            push(own[i].at[:, :, ox], r2[i], send.at[i], recv.at[i, 1], at.dev(x=ox))

    def second_go(i):
        drain(r2[i], recv.at[i, 1])

        @pl.loop(0, nz)
        def _(a):
            for b in range(2):
                add_to(own[i].at[a, y, b] if units[i][5] == 0 else own[i].at[a, b, x], r2[i].at[a, b])

        if units[i][5] == 0:
            push(own[i].at[:, y, ox], r3[i], send.at[i], recv.at[i, 2], at.dev(x=ox))
        else:
            push(own[i].at[:, oy, x], r3[i], send.at[i], recv.at[i, 2], at.dev(y=oy))

    def third_go(i):
        drain(r3[i], recv.at[i, 2])

        @pl.loop(0, nz)
        def _(a):
            add_to(own[i].at[a, y, x], r3[i].at[a])

        for k in range(1, nz):
            far = lax.rem(z + k, nz)
            push(own[i].at[far, y, x], r4[i].at[k - 1], send.at[i], recv.at[i, 3], at.dev(z=far))

    def finish(i):
        a, r0, nr, c0, ncol, _ = units[i]
        drain(r4[i], recv.at[i, 3])
        total = own[i][z, y, x].astype(jnp.float32)
        for k in range(nz - 1):
            total = total + r4[i][k].astype(jnp.float32)
        outs[a][pl.ds(r0, nr), pl.ds(c0, ncol)] = total
        for block in (rc[i], r2[i], r3[i], r4[i]):
            drain(block, send.at[i])

    for t in range(m + 4):
        if t < m:
            core_go(t)
        if 0 <= t - 1 < m:
            first_go(t - 1)
        if 0 <= t - 2 < m:
            second_go(t - 2)
        if 0 <= t - 3 < m:
            third_go(t - 3)
        if 0 <= t - 4 < m:
            finish(t - 4)


def scatter(dims, grads, split, cid):
    nz, ny, nx, nc = dims
    n = len(grads)
    views, outs, units = [], [], []
    own, r2, r3, r4 = [], [], [], []
    for a, g in enumerate(grads):
        rows, cols = g.shape[0] // (nz * ny * nx * nc), g.shape[1]
        views.append(g.reshape(nz, ny, nx, nc, rows, cols))
        outs.append(jax.ShapeDtypeStruct((rows, cols), jnp.float32))
        for j in range(split):
            if rows > cols // 8:
                nr, ncol = rows // split, cols
                units.append((a, j * nr, nr, 0, ncol, len(units) % 2))
            else:
                nr, ncol = rows, cols // split
                units.append((a, 0, nr, j * ncol, ncol, len(units) % 2))
            own.append(pltpu.VMEM((nz, ny, nx, nr, ncol), g.dtype))
            r2.append(pltpu.VMEM((nz, 2, nr, ncol), g.dtype))
            r3.append(pltpu.VMEM((nz, nr, ncol), g.dtype))
            r4.append(pltpu.VMEM((nz - 1, nr, ncol), g.dtype))
    m = len(units)
    return pl.pallas_call(
        functools.partial(scatter_kernel, dims, units, n),
        out_shape=outs,
        in_specs=[pl.BlockSpec(memory_space=ANY)] * n,
        out_specs=[pl.BlockSpec(memory_space=pltpu.VMEM)] * n,
        scratch_shapes=own + own + r2 + r3 + r4
        + [pltpu.SemaphoreType.DMA((m,)), pltpu.SemaphoreType.DMA((m,)), pltpu.SemaphoreType.DMA((m, 4))],
        compiler_params=pltpu.CompilerParams(collective_id=cid, has_side_effects=True, vmem_limit_bytes=60 * 2**20),
        name="scatter",
    )(*views)
LOG2E = 1.4426950408889634
NT = (((1,), (1,)), ((), ()))
NN = (((1,), (0,)), ((), ()))
def dot(a, b, dims=NN):
    return lax.dot_general(a, b, dims, preferred_element_type=jnp.float32)

def half_mask(x, h):
    lane = lax.broadcasted_iota(jnp.int32, x.shape, 1)
    keep = lane < 64 if h == 0 else lane >= 64
    return jnp.where(keep, x, jnp.zeros_like(x))

def hide(scores, limit, causal, start):
    rows, cols = scores.shape
    if causal:
        key = lax.broadcasted_iota(jnp.int32, (cols, cols), 0)
        query = lax.broadcasted_iota(jnp.int32, (cols, cols), 1)
        tail = jnp.where(key <= query, scores[rows - cols:], -1e30)
        return tail if rows == cols else jnp.concatenate([scores[:rows - cols], tail], axis=0)
    key = lax.broadcasted_iota(jnp.int32, (rows, cols), 0)
    return jnp.where(key < limit, scores, -1e30)

def attend_kernel(causal, block, limit_ref, q_ref, k_ref, v_ref, o_ref, lse_ref):
    limit = None if causal else limit_ref[0]
    rows, keys = q_ref.shape[0], k_ref.shape[0]
    v_t = v_ref[...].T
    ones = jnp.ones((16, keys), v_t.dtype)
    for i in range(rows // block):
        n = (i + 1) * block if causal else keys
        span = pl.ds(i * block, block)
        halves = []
        for h in range(2):
            q = half_mask(q_ref[span, :], h)
            s = hide(dot(k_ref[0:n, :], q, NT), limit, causal, i * block)
            peak = jnp.max(s, axis=0, keepdims=True)
            e = jnp.exp2(s - peak).astype(jnp.bfloat16)
            v_aug = jnp.concatenate([v_t[h * 64:(h + 1) * 64, :n], ones[:, :n]], axis=0)
            mixed = dot(v_aug, e)
            total = mixed[64:65]
            halves.append(mixed[:64] / total)
            lse_ref[0, h:h + 1, span] = peak + jnp.log2(total)
        o_ref[span, :] = jnp.concatenate(halves, axis=0).T.astype(o_ref.dtype)

def attend(q, k, v, limit=None, block=256, vmem=48):
    causal = limit is None
    rows, width = q.shape
    keys = k.shape[0]
    pairs = width // 128
    if limit is None:
        limit = jnp.zeros((1,), jnp.int32)
    col = lambda j: (0, j)
    return pl.pallas_call(
        functools.partial(attend_kernel, causal, block),
        grid=(pairs,),
        out_shape=[jax.ShapeDtypeStruct(q.shape, jnp.bfloat16), jax.ShapeDtypeStruct((pairs, 8, rows), jnp.float32)],
        in_specs=[pl.BlockSpec(memory_space=pltpu.SMEM), pl.BlockSpec((rows, 128), col), pl.BlockSpec((keys, 128), col), pl.BlockSpec((keys, 128), col)],
        out_specs=[pl.BlockSpec((rows, 128), col), pl.BlockSpec((1, 8, rows), lambda j: (j, 0, 0))],
        compiler_params=pltpu.CompilerParams(vmem_limit_bytes=vmem * 2**20),
    )(limit, q, k, v)

def attend_back_kernel(causal, block, limit_ref, q_ref, k_ref, v_ref, g_ref, o_ref, lse_ref, dq_ref, dk_ref, dv_ref, dk_acc, dv_acc):
    limit = None if causal else limit_ref[0]
    rows, keys = q_ref.shape[0], k_ref.shape[0]
    k_t = k_ref[...].T
    sel_row = lax.broadcasted_iota(jnp.int32, (16, 128), 0)
    sel_lane = lax.broadcasted_iota(jnp.int32, (16, 128), 1)
    pick = jnp.where(sel_row == lax.div(sel_lane, 64), 1.0, 0.0).astype(jnp.bfloat16)
    dk_acc[...] = jnp.zeros_like(dk_acc)
    dv_acc[...] = jnp.zeros_like(dv_acc)
    for i in range(rows // block):
        n = (i + 1) * block if causal else keys
        span = pl.ds(i * block, block)
        prod = g_ref[span, :].astype(jnp.float32) * o_ref[span, :].astype(jnp.float32)
        high = prod.astype(jnp.bfloat16)
        low = (prod - high.astype(jnp.float32)).astype(jnp.bfloat16)
        delta = dot(pick, high, NT) + dot(pick, low, NT)
        halves = []
        for h in range(2):
            q = half_mask(q_ref[span, :], h)
            g = half_mask(g_ref[span, :], h)
            s = hide(dot(k_ref[0:n, :], q, NT), limit, causal, i * block)
            p = jnp.exp2(s - lse_ref[0, h:h + 1, span])
            dp = dot(v_ref[0:n, :], g, NT)
            ds = (p * (dp - delta[h:h + 1])).astype(jnp.bfloat16)
            dv_acc[0:n, :] += dot(p.astype(jnp.bfloat16), g)
            dk_acc[0:n, :] += dot(ds, q)
            halves.append(dot(k_t[h * 64:(h + 1) * 64, :n], ds))
        dq_ref[span, :] = (jnp.concatenate(halves, axis=0).T * 0.125).astype(dq_ref.dtype)
    dk_ref[...] = (dk_acc[...] * (1.0 / LOG2E)).astype(dk_ref.dtype)
    dv_ref[...] = dv_acc[...].astype(dv_ref.dtype)

def attend_back(q, k, v, g, o, lse, limit=None, block=256, vmem=48):
    causal = limit is None
    rows, width = q.shape
    keys = k.shape[0]
    pairs = width // 128
    if limit is None:
        limit = jnp.zeros((1,), jnp.int32)
    col = lambda j: (0, j)
    rspec, kspec = pl.BlockSpec((rows, 128), col), pl.BlockSpec((keys, 128), col)
    return pl.pallas_call(
        functools.partial(attend_back_kernel, causal, block),
        grid=(pairs,),
        out_shape=[jax.ShapeDtypeStruct(q.shape, jnp.bfloat16)] + [jax.ShapeDtypeStruct(k.shape, jnp.bfloat16)] * 2,
        in_specs=[pl.BlockSpec(memory_space=pltpu.SMEM), rspec, kspec, kspec, rspec, rspec, pl.BlockSpec((1, 8, rows), lambda j: (j, 0, 0))],
        out_specs=[rspec, kspec, kspec],
        scratch_shapes=[pltpu.VMEM((keys, 128), jnp.float32)] * 2,
        compiler_params=pltpu.CompilerParams(vmem_limit_bytes=vmem * 2**20),
    )(limit, q, k, v, g, o, lse)
def gelu_parts(u):
    t = 1.0 / (1.0 + (0.3275911 * 0.7071067811865476) * jnp.abs(u))
    e = jnp.exp(-0.5 * (u * u))
    poly = t * (0.254829592 + t * (-0.284496736 + t * (1.421413741 + t * (-1.453152027 + t * 1.061405429))))
    tail = 0.5 * poly * e
    return jnp.where(u < 0, tail, 1.0 - tail), e * 0.3989422804014327


def ffn_kernel(dims, sent, h_ref, g_ref, x_ref, up_ref, down_ref, out_ref, dh_ref, ddown_ref, grad_ref, rest_ref,
               h_t, acc, act, du, made, own, rc, r2a, r2b, r3, r4, local_sem, send, recv):
    j = pl.program_id(0)
    steps = pl.num_programs(0)
    at = Place(dims)
    nz, ny, nx, nc = dims
    z, y, x, c = at.z, at.y, at.x, at.c
    oy, ox, oc = 1 - y, 1 - x, 1 - c
    rows, width = h_ref.shape
    chunk = up_ref.shape[1]
    half = chunk // 2
    block = rows // 2
    left, right = pl.ds(0, half), pl.ds(half, half)
    every = slice(None)

    def made_at(slot, core):
        return made.at[(slot, every, every, every, core)]

    def core_go(i):
        slot = lax.rem(i, 2)
        pltpu.make_async_copy(made_at(slot, c), own.at[i], local_sem.at[i]).start()
        push(made_at(slot, oc), rc.at[i], send.at[i, 0], recv.at[i, 0], at.dev(c=oc))

    def first_go(i):
        drain(own.at[i], local_sem.at[i])
        drain(rc.at[i], recv.at[i, 0])
        drain(rc.at[i], send.at[i, 0])

        @pl.loop(0, nz)
        def _(a):
            for b in range(ny):
                for d in range(nx):
                    add_to(own.at[i, a, b, d], rc.at[i, a, b, d])

        push(own.at[i, :, oy, :, :, left], r2a.at[i], send.at[i, 1], recv.at[i, 1], at.dev(y=oy))
        push(own.at[i, :, :, ox, :, right], r2b.at[i], send.at[i, 1], recv.at[i, 2], at.dev(x=ox))

    def second_go(i):
        drain(r2a.at[i], recv.at[i, 1])
        drain(r2b.at[i], recv.at[i, 2])

        @pl.loop(0, nz)
        def _(a):
            for b in range(2):
                add_to(own.at[i, a, y, b, :, left], r2a.at[i, a, b])
                add_to(own.at[i, a, b, x, :, right], r2b.at[i, a, b])

        push(own.at[i, :, y, ox, :, left], r3.at[i, :, :, left], send.at[i, 1], recv.at[i, 3], at.dev(x=ox))
        push(own.at[i, :, oy, x, :, right], r3.at[i, :, :, right], send.at[i, 1], recv.at[i, 4], at.dev(y=oy))

    def third_go(i):
        drain(r3.at[i, :, :, left], recv.at[i, 3])
        drain(r3.at[i, :, :, right], recv.at[i, 4])

        @pl.loop(0, nz)
        def _(a):
            add_to(own.at[i, a, y, x], r3.at[i, a])

        for k in range(1, nz):
            far = lax.rem(z + k, nz)
            push(own.at[i, far, y, x], r4.at[i, k - 1], send.at[i, 1], recv.at[i, 5], at.dev(z=far))

    def finish(i):
        drain(r4.at[i], recv.at[i, 5])
        total = own[i, z, y, x].astype(jnp.float32)
        for k in range(nz - 1):
            total = total + r4[i, k].astype(jnp.float32)
        grad_ref[i] = total
        for part in (r2a.at[i], r2b.at[i], r3.at[i], r4.at[i]):
            drain(part, send.at[i, 1])

    @pl.when(j == 0)
    def _():
        hello([at.dev(z=k) for k in at.z_others()] + [at.dev(y=oy), at.dev(x=ox), at.dev(c=oc)])
        acc[...] = x_ref[...]
        dh_ref[...] = jnp.zeros_like(dh_ref)

        @pl.loop(0, rows // block)
        def _(r):
            span = pl.ds(pl.multiple_of(r * block, block), block)
            h_t[:, span] = h_ref[span, :].T

    def after(late, then):
        pl.when((j >= late) & (j - late < sent))(lambda: then(j - late))

    after(1, first_go)
    for r in range(rows // block):
        span = pl.ds(r * block, block)
        u = dot(h_ref[span, :], up_ref[...])
        g = dot(g_ref[span, :], down_ref[...], NT)
        big, small = gelu_parts(u)
        a = (u * big).astype(jnp.bfloat16)
        d = (g * (big + u * small)).astype(jnp.bfloat16)
        act[span, :] = a
        du[span, :] = d
        acc[span, :] += dot(a, down_ref[...])
        dh_ref[span, :] += dot(d, up_ref[...], NT)

    after(1, second_go)
    slot = lax.rem(j, 2)
    each = rows // (nz * ny * nx * nc)

    @pl.loop(0, nz)
    def _(a):
        n = ny * nx * nc * each
        part = dot(h_t[pl.ds(pl.multiple_of(a * n, n), n), :], du[...]).astype(made.dtype)
        made[slot, a] = part.reshape(ny, nx, nc, each, chunk)

    after(0, core_go)
    after(1, third_go)
    ddown_ref[...] = lax.dot_general(act[...], g_ref[...], (((0,), (0,)), ((), ())), preferred_element_type=jnp.float32).astype(ddown_ref.dtype)
    after(1, finish)

    @pl.when(j >= sent)
    def _():
        pltpu.make_async_copy(made.at[slot], rest_ref.at[j - sent], local_sem.at[j]).start()

    @pl.when(j == steps - 1)
    def _():
        out_ref[...] = acc[...].astype(out_ref.dtype)
        for i in range(sent, 4):
            drain(rest_ref.at[i - sent], local_sem.at[i])


def ffn(dims, h, g, x, w_up, w_down, cid, sent=3, steps=4):
    nz, ny, nx, nc = dims
    rows, width = h.shape
    inner = w_up.shape[1]
    chunk = inner // steps
    each = width // (nz * ny * nx * nc)
    bf, f32 = jnp.bfloat16, jnp.float32
    fixed = lambda j: (0, 0)
    whole = pl.BlockSpec((rows, width), fixed)
    once = pl.BlockSpec((rows, width), fixed, pipeline_mode=pl.Buffered(1))
    tile = (each, chunk)
    out, dh, ddown, grad, rest = pl.pallas_call(
        functools.partial(ffn_kernel, dims, sent),
        grid=(steps,),
        out_shape=[
            jax.ShapeDtypeStruct((rows, width), bf),
            jax.ShapeDtypeStruct((rows, width), f32),
            jax.ShapeDtypeStruct((inner, width), bf),
            jax.ShapeDtypeStruct((sent, each, chunk), f32),
            jax.ShapeDtypeStruct((steps - sent, nz, ny, nx, nc, each, chunk), bf),
        ],
        in_specs=[once, once, once, pl.BlockSpec((width, chunk), lambda j: (0, j)), pl.BlockSpec((chunk, width), lambda j: (j, 0))],
        out_specs=[once, once, pl.BlockSpec((chunk, width), lambda j: (j, 0)),
                   pl.BlockSpec((sent, each, chunk), lambda j: (0, 0, 0)), pl.BlockSpec(memory_space=ANY)],
        scratch_shapes=[
            pltpu.VMEM((width, rows), bf), pltpu.VMEM((rows, width), f32), pltpu.VMEM((rows, chunk), bf), pltpu.VMEM((rows, chunk), bf),
            pltpu.VMEM((2, nz, ny, nx, nc) + tile, bf),
            pltpu.VMEM((sent, nz, ny, nx) + tile, bf), pltpu.VMEM((sent, nz, ny, nx) + tile, bf),
            pltpu.VMEM((sent, nz, nx, each, chunk // 2), bf), pltpu.VMEM((sent, nz, ny, each, chunk // 2), bf),
            pltpu.VMEM((sent, nz) + tile, bf), pltpu.VMEM((sent, nz - 1) + tile, bf),
            pltpu.SemaphoreType.DMA((steps,)), pltpu.SemaphoreType.DMA((sent, 2)), pltpu.SemaphoreType.DMA((sent, 6)),
        ],
        compiler_params=pltpu.CompilerParams(collective_id=cid, has_side_effects=True, vmem_limit_bytes=62 * 2**20, dimension_semantics=("arbitrary",)),
        name="feed_forward",
    )(h, g, x, w_up, w_down)
    grad = jnp.moveaxis(grad, 0, 1).reshape(each, sent * chunk)
    rest = jnp.moveaxis(rest, 0, 5).reshape(width, (steps - sent) * chunk)
    return out, dh, ddown, grad, rest

HEAD_DIM = 64


EPS = 1e-05


def norm_rows(values_in, gain, bias):
    center = values_in - jnp.mean(values_in, axis=-1, keepdims=True)
    spread = jnp.mean(center * center, axis=-1, keepdims=True)
    return center * lax.rsqrt(spread + EPS) * gain + bias


def contract_rows(left, right):
    return lax.dot_general(
        left, right, (((0,), (0,)), ((), ())), preferred_element_type=jnp.float32
    )


def times_transposed(left, right):
    return lax.dot_general(
        left, right, (((1,), (1,)), ((), ())), preferred_element_type=jnp.float32
    )


def product(left, right):
    return jnp.dot(left, right, preferred_element_type=jnp.float32)


def local_plain(
    block_in,
    text_states,
    caption_len,
    out_grad,
    first_gain,
    first_bias,
    query_weight,
    key_weight,
    value_weight,
    output_weight,
    second_gain,
    second_bias,
    cross_query,
    cross_key,
    cross_value,
    cross_output,
    third_gain,
    third_bias,
    up_weight,
    down_weight,
):
    gathered = (
        lax.all_gather(first_gain, ("dp", "seq"), axis=0, tiled=True),
        lax.all_gather(first_bias, ("dp", "seq"), axis=0, tiled=True),
        lax.all_gather(query_weight, ("dp", "seq"), axis=0, tiled=True),
        lax.all_gather(key_weight, ("dp", "seq"), axis=0, tiled=True),
        lax.all_gather(value_weight, ("dp", "seq"), axis=0, tiled=True),
        lax.all_gather(output_weight, ("dp", "seq"), axis=0, tiled=True),
        lax.all_gather(second_gain, ("dp", "seq"), axis=0, tiled=True),
        lax.all_gather(second_bias, ("dp", "seq"), axis=0, tiled=True),
        lax.all_gather(cross_query, ("dp", "seq"), axis=0, tiled=True),
        lax.all_gather(cross_key, ("dp", "seq"), axis=0, tiled=True),
        lax.all_gather(cross_value, ("dp", "seq"), axis=0, tiled=True),
        lax.all_gather(cross_output, ("dp", "seq"), axis=0, tiled=True),
        lax.all_gather(third_gain, ("dp", "seq"), axis=0, tiled=True),
        lax.all_gather(third_bias, ("dp", "seq"), axis=0, tiled=True),
        lax.all_gather(up_weight, ("dp", "seq"), axis=0, tiled=True),
        lax.all_gather(down_weight, ("dp", "seq"), axis=0, tiled=True),
    )
    (
        gain_one,
        bias_one,
        w_query,
        w_key,
        w_value,
        w_output,
        gain_two,
        bias_two,
        w_cquery,
        w_ckey,
        w_cvalue,
        w_coutput,
        gain_three,
        bias_three,
        w_up,
        w_down,
    ) = gathered
    item_count, seg_len, model_width = block_in.shape
    row_count = item_count * seg_len
    head_count = model_width // HEAD_DIM
    score_scale = HEAD_DIM ** (-0.5)
    text_count = text_states.shape[1]
    inputs_f = block_in.astype(jnp.float32).reshape(row_count, model_width)
    normed_one, pull_one = jax.vjp(
        norm_rows, inputs_f, gain_one.astype(jnp.float32), bias_one.astype(jnp.float32)
    )
    normed_one = normed_one.astype(jnp.bfloat16)
    query_rows = product(normed_one, w_query).astype(jnp.bfloat16)
    key_rows = product(normed_one, w_key).astype(jnp.bfloat16)
    value_rows = product(normed_one, w_value).astype(jnp.bfloat16)
    key_all, value_all = (
        lax.all_gather(
            key_rows.reshape(item_count, seg_len, model_width), "seq", axis=1, tiled=True
        ),
        lax.all_gather(
            value_rows.reshape(item_count, seg_len, model_width), "seq", axis=1, tiled=True
        ),
    )
    key_count = key_all.shape[1]
    first_pos = lax.axis_index("seq") * seg_len
    query_pos = first_pos + jnp.arange(seg_len, dtype=jnp.int32)
    causal = jnp.arange(key_count, dtype=jnp.int32)[None, :] <= query_pos[:, None]

    def self_scores(query_item, key_item):
        query_heads = query_item.reshape(seg_len, head_count, HEAD_DIM)
        key_heads = key_item.reshape(key_count, head_count, HEAD_DIM)
        scores = jnp.einsum(
            "qhd,khd->hqk", query_heads, key_heads, preferred_element_type=jnp.float32
        )
        return jnp.where(causal[None, :, :], scores * score_scale, -1e30)

    def self_forward(operands):
        query_item, key_item, value_item = operands
        scores = self_scores(query_item, key_item)
        row_peak = jnp.max(scores, axis=-1, keepdims=True)
        row_total = jnp.sum(jnp.exp(scores - row_peak), axis=-1, keepdims=True)
        log_total = row_peak + jnp.log(row_total)
        prob_bf = jnp.exp(scores - log_total).astype(jnp.bfloat16)
        value_heads = value_item.reshape(key_count, head_count, HEAD_DIM)
        mixed = jnp.einsum("hqk,khd->qhd", prob_bf, value_heads, preferred_element_type=jnp.float32)
        return (mixed.reshape(seg_len, model_width).astype(jnp.bfloat16), log_total)

    attended, log_totals = lax.map(
        self_forward, (query_rows.reshape(item_count, seg_len, model_width), key_all, value_all)
    )
    attended_rows = attended.reshape(row_count, model_width)
    after_self = inputs_f + product(attended_rows, w_output)
    normed_two, pull_two = jax.vjp(
        norm_rows, after_self, gain_two.astype(jnp.float32), bias_two.astype(jnp.float32)
    )
    normed_two = normed_two.astype(jnp.bfloat16)
    cross_rows = product(normed_two, w_cquery).astype(jnp.bfloat16)
    cross_heads = cross_rows.reshape(item_count, seg_len, head_count, HEAD_DIM)
    text_keys = jnp.einsum(
        "itc,cd->itd", text_states, w_ckey, preferred_element_type=jnp.float32
    ).astype(jnp.bfloat16)
    text_values = jnp.einsum(
        "itc,cd->itd", text_states, w_cvalue, preferred_element_type=jnp.float32
    ).astype(jnp.bfloat16)
    text_kheads = text_keys.reshape(item_count, text_count, head_count, HEAD_DIM)
    text_vheads = text_values.reshape(item_count, text_count, head_count, HEAD_DIM)
    text_mask = jnp.arange(text_count, dtype=jnp.int32)[None, :] < caption_len[:, None]
    cross_scores = jnp.einsum(
        "iqhd,ithd->ihqt", cross_heads, text_kheads, preferred_element_type=jnp.float32
    )
    cross_scores = jnp.where(text_mask[:, None, None, :], cross_scores * score_scale, -1e30)
    cross_peak = jnp.max(cross_scores, axis=-1, keepdims=True)
    cross_exp = jnp.exp(cross_scores - cross_peak)
    cross_prob = cross_exp / jnp.sum(cross_exp, axis=-1, keepdims=True)
    cross_prob_bf = cross_prob.astype(jnp.bfloat16)
    crossed = jnp.einsum(
        "ihqt,ithd->iqhd", cross_prob_bf, text_vheads, preferred_element_type=jnp.float32
    )
    crossed_rows = crossed.reshape(row_count, model_width).astype(jnp.bfloat16)
    after_cross = after_self + product(crossed_rows, w_coutput)
    normed_three, pull_three = jax.vjp(
        norm_rows, after_cross, gain_three.astype(jnp.float32), bias_three.astype(jnp.float32)
    )
    normed_three = normed_three.astype(jnp.bfloat16)
    hidden = product(normed_three, w_up)
    activated, pull_gelu = jax.vjp(lambda inner: jax.nn.gelu(inner, approximate=False), hidden)
    activated = activated.astype(jnp.bfloat16)
    layer_out = after_cross + product(activated, w_down)
    block_out = layer_out.astype(jnp.bfloat16).reshape(item_count, seg_len, model_width)
    back_weights = (
        lax.all_gather(first_gain, ("dp", "seq"), axis=0, tiled=True),
        lax.all_gather(first_bias, ("dp", "seq"), axis=0, tiled=True),
        lax.all_gather(query_weight, ("dp", "seq"), axis=0, tiled=True),
        lax.all_gather(key_weight, ("dp", "seq"), axis=0, tiled=True),
        lax.all_gather(value_weight, ("dp", "seq"), axis=0, tiled=True),
        lax.all_gather(output_weight, ("dp", "seq"), axis=0, tiled=True),
        lax.all_gather(second_gain, ("dp", "seq"), axis=0, tiled=True),
        lax.all_gather(second_bias, ("dp", "seq"), axis=0, tiled=True),
        lax.all_gather(cross_query, ("dp", "seq"), axis=0, tiled=True),
        lax.all_gather(cross_key, ("dp", "seq"), axis=0, tiled=True),
        lax.all_gather(cross_value, ("dp", "seq"), axis=0, tiled=True),
        lax.all_gather(cross_output, ("dp", "seq"), axis=0, tiled=True),
        lax.all_gather(third_gain, ("dp", "seq"), axis=0, tiled=True),
        lax.all_gather(third_bias, ("dp", "seq"), axis=0, tiled=True),
        lax.all_gather(up_weight, ("dp", "seq"), axis=0, tiled=True),
        lax.all_gather(down_weight, ("dp", "seq"), axis=0, tiled=True),
    )
    (
        unused_gain,
        unused_bias,
        w_query,
        w_key,
        w_value,
        w_output,
        unused_gtwo,
        unused_btwo,
        w_cquery,
        w_ckey,
        w_cvalue,
        w_coutput,
        unused_gthree,
        unused_bthree,
        w_up,
        w_down,
    ) = back_weights
    grad_rows = out_grad.reshape(row_count, model_width)
    down_part = contract_rows(activated, grad_rows)
    act_grad = times_transposed(grad_rows, w_down)
    hidden_grad = pull_gelu(act_grad)[0].astype(jnp.bfloat16)
    up_part = contract_rows(normed_three, hidden_grad)
    normed_three_grad = times_transposed(hidden_grad, w_up)
    resid_three, gain_three_part, bias_three_part = pull_three(normed_three_grad)
    cross_grad = grad_rows.astype(jnp.float32) + resid_three
    cross_out_bf = cross_grad.astype(jnp.bfloat16)
    coutput_part = contract_rows(crossed_rows, cross_out_bf)
    crossed_grad = times_transposed(cross_out_bf, w_coutput).astype(jnp.bfloat16)
    crossed_heads = crossed_grad.reshape(item_count, seg_len, head_count, HEAD_DIM)
    cross_dprob = jnp.einsum(
        "iqhd,ithd->ihqt", crossed_heads, text_vheads, preferred_element_type=jnp.float32
    )
    cross_dscore = cross_prob * (
        cross_dprob - jnp.sum(cross_dprob * cross_prob, axis=-1, keepdims=True)
    )
    cross_dscore = cross_dscore.astype(jnp.bfloat16)
    cquery_grad = (
        (
            jnp.einsum(
                "ihqt,ithd->iqhd", cross_dscore, text_kheads, preferred_element_type=jnp.float32
            )
            * score_scale
        )
        .astype(jnp.bfloat16)
        .reshape(row_count, model_width)
    )
    tkey_part = (
        jnp.einsum("ihqt,iqhd->ithd", cross_dscore, cross_heads, preferred_element_type=jnp.float32)
        * score_scale
    ).reshape(item_count, text_count, model_width)
    tvalue_part = jnp.einsum(
        "ihqt,iqhd->ithd", cross_prob_bf, crossed_heads, preferred_element_type=jnp.float32
    ).reshape(item_count, text_count, model_width)
    cquery_part = contract_rows(normed_two, cquery_grad)
    normed_two_grad = times_transposed(cquery_grad, w_cquery)
    resid_two, gain_two_part, bias_two_part = pull_two(normed_two_grad)
    self_grad = cross_grad + resid_two
    self_out_bf = self_grad.astype(jnp.bfloat16)
    output_part = contract_rows(attended_rows, self_out_bf)
    attended_grad = times_transposed(self_out_bf, w_output).astype(jnp.bfloat16)
    query_items = query_rows.reshape(item_count, seg_len, model_width)
    dout_items = attended_grad.reshape(item_count, seg_len, model_width)

    def self_backward(operands):
        query_item, key_item, value_item, dout_item, log_total = operands
        scores = self_scores(query_item, key_item)
        probs = jnp.exp(scores - log_total)
        prob_bf = probs.astype(jnp.bfloat16)
        query_heads = query_item.reshape(seg_len, head_count, HEAD_DIM)
        key_heads = key_item.reshape(key_count, head_count, HEAD_DIM)
        value_heads = value_item.reshape(key_count, head_count, HEAD_DIM)
        dout_heads = dout_item.reshape(seg_len, head_count, HEAD_DIM)
        dprob = jnp.einsum(
            "qhd,khd->hqk", dout_heads, value_heads, preferred_element_type=jnp.float32
        )
        dscore = (probs * (dprob - jnp.sum(dprob * probs, axis=-1, keepdims=True))).astype(
            jnp.bfloat16
        )
        dquery = (
            (
                jnp.einsum("hqk,khd->qhd", dscore, key_heads, preferred_element_type=jnp.float32)
                * score_scale
            )
            .astype(jnp.bfloat16)
            .reshape(seg_len, model_width)
        )
        dkey = (
            jnp.einsum("hqk,qhd->khd", dscore, query_heads, preferred_element_type=jnp.float32)
            * score_scale
        ).reshape(key_count, model_width)
        dvalue = jnp.einsum(
            "hqk,qhd->khd", prob_bf, dout_heads, preferred_element_type=jnp.float32
        ).reshape(key_count, model_width)
        return (dquery, dkey, dvalue)

    query_grad_items, key_part, value_part = lax.map(
        self_backward, (query_items, key_all, value_all, dout_items, log_totals)
    )
    key_own, value_own, tkey_own, tvalue_own = (
        lax.psum_scatter(
            key_part.astype(jnp.bfloat16), "seq", scatter_dimension=1, tiled=True
        ).astype(jnp.float32),
        lax.psum_scatter(
            value_part.astype(jnp.bfloat16), "seq", scatter_dimension=1, tiled=True
        ).astype(jnp.float32),
        lax.psum_scatter(
            tkey_part.astype(jnp.bfloat16), "seq", scatter_dimension=1, tiled=True
        ).astype(jnp.float32),
        lax.psum_scatter(
            tvalue_part.astype(jnp.bfloat16), "seq", scatter_dimension=1, tiled=True
        ).astype(jnp.float32),
    )
    key_grad_rows = key_own.astype(jnp.bfloat16).reshape(row_count, model_width)
    value_grad_rows = value_own.astype(jnp.bfloat16).reshape(row_count, model_width)
    query_grad_rows = query_grad_items.reshape(row_count, model_width)
    tkey_bf = tkey_own.astype(jnp.bfloat16)
    tvalue_bf = tvalue_own.astype(jnp.bfloat16)
    query_part = contract_rows(normed_one, query_grad_rows)
    key_wpart = contract_rows(normed_one, key_grad_rows)
    value_wpart = contract_rows(normed_one, value_grad_rows)
    normed_one_grad = (
        times_transposed(query_grad_rows, w_query)
        + times_transposed(key_grad_rows, w_key)
        + times_transposed(value_grad_rows, w_value)
    )
    resid_one, gain_one_part, bias_one_part = pull_one(normed_one_grad)
    input_grad = (self_grad + resid_one).reshape(item_count, seg_len, model_width)
    text_rows = tkey_own.shape[1]
    text_start = lax.axis_index("seq") * text_rows
    text_slice = lax.dynamic_slice_in_dim(text_states, text_start, text_rows, 1)
    ckey_part = jnp.einsum("itc,itd->cd", text_slice, tkey_bf, preferred_element_type=jnp.float32)
    cvalue_part = jnp.einsum(
        "itc,itd->cd", text_slice, tvalue_bf, preferred_element_type=jnp.float32
    )
    text_grad = jnp.einsum(
        "itd,cd->itc", tkey_bf, w_ckey, preferred_element_type=jnp.float32
    ) + jnp.einsum("itd,cd->itc", tvalue_bf, w_cvalue, preferred_element_type=jnp.float32)
    (
        first_gain_grad,
        first_bias_grad,
        query_grad,
        key_grad,
        value_grad,
        output_grad,
        second_gain_grad,
        second_bias_grad,
        cross_query_grad,
        cross_key_grad,
        cross_value_grad,
        cross_output_grad,
        third_gain_grad,
        third_bias_grad,
        up_grad,
        down_grad,
    ) = (
        lax.psum_scatter(gain_one_part, ("dp", "seq"), scatter_dimension=0, tiled=True),
        lax.psum_scatter(bias_one_part, ("dp", "seq"), scatter_dimension=0, tiled=True),
        lax.psum_scatter(query_part, ("dp", "seq"), scatter_dimension=0, tiled=True),
        lax.psum_scatter(key_wpart, ("dp", "seq"), scatter_dimension=0, tiled=True),
        lax.psum_scatter(value_wpart, ("dp", "seq"), scatter_dimension=0, tiled=True),
        lax.psum_scatter(output_part, ("dp", "seq"), scatter_dimension=0, tiled=True),
        lax.psum_scatter(gain_two_part, ("dp", "seq"), scatter_dimension=0, tiled=True),
        lax.psum_scatter(bias_two_part, ("dp", "seq"), scatter_dimension=0, tiled=True),
        lax.psum_scatter(cquery_part, ("dp", "seq"), scatter_dimension=0, tiled=True),
        lax.psum_scatter(ckey_part, ("dp", "seq"), scatter_dimension=0, tiled=True),
        lax.psum_scatter(cvalue_part, ("dp", "seq"), scatter_dimension=0, tiled=True),
        lax.psum_scatter(coutput_part, ("dp", "seq"), scatter_dimension=0, tiled=True),
        lax.psum_scatter(gain_three_part, ("dp", "seq"), scatter_dimension=0, tiled=True),
        lax.psum_scatter(bias_three_part, ("dp", "seq"), scatter_dimension=0, tiled=True),
        lax.psum_scatter(up_part, ("dp", "seq"), scatter_dimension=0, tiled=True),
        lax.psum_scatter(down_part, ("dp", "seq"), scatter_dimension=0, tiled=True),
    )
    return (
        block_out,
        input_grad,
        text_grad,
        first_gain_grad,
        first_bias_grad,
        query_grad,
        key_grad,
        value_grad,
        output_grad,
        second_gain_grad,
        second_bias_grad,
        cross_query_grad,
        cross_key_grad,
        cross_value_grad,
        cross_output_grad,
        third_gain_grad,
        third_bias_grad,
        up_grad,
        down_grad,
    )


def small_rows(vectors):
    packed = jnp.stack(vectors)
    return jnp.pad(packed, ((0, 16 - packed.shape[0]), (0, 128 - packed.shape[1])))


def local(seq_size, *args):
    block_in = args[0]
    if block_in.shape[0] != seq_size or seq_size != 4 or block_in.shape[1] * seq_size != 1024:
        return local_plain(*args)
    return local_items(seq_size, *args)


def local_items(
    seq_size,
    block_in,
    text_states,
    caption_len,
    out_grad,
    first_gain,
    first_bias,
    query_weight,
    key_weight,
    value_weight,
    output_weight,
    second_gain,
    second_bias,
    cross_query,
    cross_key,
    cross_value,
    cross_output,
    third_gain,
    third_bias,
    up_weight,
    down_weight,
):
    ny, nx, nc = 2, seq_size // 2, 2
    dp_size = 1024 // first_gain.shape[0] // seq_size
    dims = (dp_size // ny, ny, nx, nc)
    bf, f32 = jnp.bfloat16, jnp.float32
    seg, width = block_in.shape[1], block_in.shape[2]
    rows = seq_size * seg
    me = lax.axis_index("seq")
    small = small_rows([first_gain, first_bias, second_gain, second_bias, third_gain, third_bias])
    shards = [small, query_weight, key_weight, value_weight, output_weight, cross_query, cross_key, cross_value, cross_output, up_weight, down_weight]
    full, mine = gather(dims, shards, AG_UNITS, AG_CHUNKS, block_in)
    small, w_query, w_key, w_value, w_output, w_cquery, w_ckey, w_cvalue, w_coutput, w_up, w_down = full
    vectors = small.reshape(-1, 16, 128)[:, :6, : first_gain.shape[0]]
    vectors = jnp.moveaxis(vectors, 1, 0).reshape(6, width).astype(f32)
    gain_one, bias_one, gain_two, bias_two, gain_three, bias_three = [vectors[i] for i in range(6)]
    inputs_f = mine.reshape(rows, width).astype(f32)
    grad_rows = lax.all_to_all(out_grad, "seq", 0, 0, tiled=True).reshape(rows, width)
    text = lax.dynamic_slice_in_dim(text_states, me, 1, 0)[0]
    limit = lax.dynamic_slice_in_dim(caption_len, me, 1, 0)
    unit = LOG2E / 8

    normed_one, pull_one = jax.vjp(norm_rows, inputs_f, gain_one, bias_one)
    normed_one = normed_one.astype(bf)
    q = (product(normed_one, w_query) * unit).astype(bf)
    k = product(normed_one, w_key).astype(bf)
    v = product(normed_one, w_value).astype(bf)
    o, lse = attend(q, k, v, block=512)
    after_self = inputs_f + product(o, w_output)
    normed_two, pull_two = jax.vjp(norm_rows, after_self, gain_two, bias_two)
    normed_two = normed_two.astype(bf)
    cq = (product(normed_two, w_cquery) * unit).astype(bf)
    ck = product(text, w_ckey).astype(bf)
    cv = product(text, w_cvalue).astype(bf)
    o2, lse2 = attend(cq, ck, cv, limit=limit, block=512)
    after_cross = after_self + product(o2, w_coutput)
    normed_three, pull_three = jax.vjp(norm_rows, after_cross, gain_three, bias_three)
    normed_three = normed_three.astype(bf)
    block_out, dh3, down_part, up_grad_done, up_part = ffn(dims, normed_three, grad_rows, after_cross, w_up, w_down, 4)
    block_out = lax.all_to_all(block_out.reshape(seq_size, seg, width), "seq", 0, 0, tiled=True)

    resid_three, gain_three_part, bias_three_part = pull_three(dh3)
    cross_grad = grad_rows.astype(f32) + resid_three
    dy2 = cross_grad.astype(bf)
    coutput_part = contract_rows(o2, dy2).astype(bf)
    do2 = times_transposed(dy2, w_coutput).astype(bf)
    dcq, dck, dcv = attend_back(cq, ck, cv, do2, o2, lse2, limit=limit, block=512)
    cquery_part = contract_rows(normed_two, dcq).astype(bf)
    ckey_part = contract_rows(text, dck).astype(bf)
    cvalue_part = contract_rows(text, dcv).astype(bf)
    text_grad = times_transposed(dck, w_ckey) + times_transposed(dcv, w_cvalue)
    text_grad = lax.all_to_all(text_grad.reshape(seq_size, -1, width), "seq", 0, 0, tiled=True)
    resid_two, gain_two_part, bias_two_part = pull_two(times_transposed(dcq, w_cquery))
    self_grad = cross_grad + resid_two
    dy1 = self_grad.astype(bf)
    output_part = contract_rows(o, dy1).astype(bf)
    do = times_transposed(dy1, w_output).astype(bf)
    dq, dk, dv = attend_back(q, k, v, do, o, lse)
    query_part = contract_rows(normed_one, dq).astype(bf)
    key_part = contract_rows(normed_one, dk).astype(bf)
    value_part = contract_rows(normed_one, dv).astype(bf)
    normed_one_grad = times_transposed(dq, w_query) + times_transposed(dk, w_key) + times_transposed(dv, w_value)
    resid_one, gain_one_part, bias_one_part = pull_one(normed_one_grad)
    input_grad = (self_grad + resid_one).astype(bf).reshape(seq_size, seg, width)
    input_grad = lax.all_to_all(input_grad, "seq", 0, 0, tiled=True).astype(f32)

    up_grad, down_grad = scatter(dims, [up_part, down_part], 4, 2)
    up_grad = jnp.concatenate([up_grad_done, up_grad], axis=1)
    parts = jnp.stack([gain_one_part, bias_one_part, gain_two_part, bias_two_part, gain_three_part, bias_three_part])
    parts = jnp.moveaxis(parts.reshape(6, -1, first_gain.shape[0]), 0, 1)
    parts = jnp.pad(parts, ((0, 0), (0, 2), (0, 128 - parts.shape[2]))).reshape(-1, 128)
    query_grad, key_grad, value_grad, output_grad, cquery_grad, ckey_grad, cvalue_grad, coutput_grad, small_grad = scatter(
        dims, [query_part, key_part, value_part, output_part, cquery_part, ckey_part, cvalue_part, coutput_part, parts], 1, 3
    )
    vec = [small_grad[i, : first_gain.shape[0]] for i in range(6)]
    return (
        block_out, input_grad, text_grad,
        vec[0], vec[1], query_grad, key_grad, value_grad, output_grad,
        vec[2], vec[3], cquery_grad, ckey_grad, cvalue_grad, coutput_grad,
        vec[4], vec[5], up_grad, down_grad,
    )


def solution(mesh):
    return jax.shard_map(
        functools.partial(local, mesh.shape['seq']),
        mesh=mesh,
        in_specs=(
            P("dp", "seq", None),
            P("dp", None, None),
            P("dp"),
            P("dp", "seq", None),
            P(("dp", "seq")),
            P(("dp", "seq")),
            P(("dp", "seq"), None),
            P(("dp", "seq"), None),
            P(("dp", "seq"), None),
            P(("dp", "seq"), None),
            P(("dp", "seq")),
            P(("dp", "seq")),
            P(("dp", "seq"), None),
            P(("dp", "seq"), None),
            P(("dp", "seq"), None),
            P(("dp", "seq"), None),
            P(("dp", "seq")),
            P(("dp", "seq")),
            P(("dp", "seq"), None),
            P(("dp", "seq"), None),
        ),
        out_specs=(
            P("dp", "seq", None),
            P("dp", "seq", None),
            P("dp", "seq", None),
            P(("dp", "seq")),
            P(("dp", "seq")),
            P(("dp", "seq"), None),
            P(("dp", "seq"), None),
            P(("dp", "seq"), None),
            P(("dp", "seq"), None),
            P(("dp", "seq")),
            P(("dp", "seq")),
            P(("dp", "seq"), None),
            P(("dp", "seq"), None),
            P(("dp", "seq"), None),
            P(("dp", "seq"), None),
            P(("dp", "seq")),
            P(("dp", "seq")),
            P(("dp", "seq"), None),
            P(("dp", "seq"), None),
        ),
        check_vma=False,
    )
```

```python
import functools

import jax
import jax.numpy as jnp
from jax import lax
from jax.experimental import pallas as pl
from jax.experimental.pallas import tpu as pltpu
from jax.sharding import PartitionSpec as P

MESH = pl.DeviceIdType.MESH
ANY = pl.ANY


class Place:
    def __init__(self, dims):
        self.nz, self.ny, self.nx, self.nc = dims
        dp, seq = lax.axis_index("dp"), lax.axis_index("seq")
        self.z, self.y = lax.div(dp, self.ny), lax.rem(dp, self.ny)
        self.x, self.c = lax.div(seq, self.nc), lax.rem(seq, self.nc)
        self.dp, self.seq = dp, seq

    def dev(self, z=None, y=None, x=None, c=None):
        z = self.z if z is None else z
        y = self.y if y is None else y
        x = self.x if x is None else x
        c = self.c if c is None else c
        return (z * self.ny + y, x * self.nc + c)

    def z_others(self):
        return [lax.rem(self.z + k, self.nz) for k in range(1, self.nz)]


def hello(peers):
    barrier = pltpu.get_barrier_semaphore()
    for peer in peers:
        pl.semaphore_signal(barrier, inc=1, device_id=peer, device_id_type=MESH)
    pl.semaphore_wait(barrier, len(peers))


def push(src, dst, send, recv, device):
    pltpu.make_async_remote_copy(
        src_ref=src, dst_ref=dst, send_sem=send, recv_sem=recv, device_id=device, device_id_type=MESH
    ).start()


def drain(ref, sem):
    pltpu.make_async_copy(ref, ref, sem).wait()


def add_to(dst, src):
    dst[...] = dst[...] + src[...]


LOG2E = 1.4426950408889634
NT = (((1,), (1,)), ((), ()))
NN = (((1,), (0,)), ((), ()))
def dot(a, b, dims=NN):
    return lax.dot_general(a, b, dims, preferred_element_type=jnp.float32)

def half_mask(x, h):
    lane = lax.broadcasted_iota(jnp.int32, x.shape, 1)
    keep = lane < 64 if h == 0 else lane >= 64
    return jnp.where(keep, x, jnp.zeros_like(x))

def hide(scores, limit, causal, start):
    rows, cols = scores.shape
    if causal:
        key = lax.broadcasted_iota(jnp.int32, (cols, cols), 0)
        query = lax.broadcasted_iota(jnp.int32, (cols, cols), 1)
        tail = jnp.where(key <= query, scores[rows - cols:], -1e30)
        return tail if rows == cols else jnp.concatenate([scores[:rows - cols], tail], axis=0)
    key = lax.broadcasted_iota(jnp.int32, (rows, cols), 0)
    return jnp.where(key < limit, scores, -1e30)

def attend_kernel(causal, block, limit_ref, q_ref, k_ref, v_ref, o_ref, lse_ref):
    limit = None if causal else limit_ref[0]
    rows, keys = q_ref.shape[0], k_ref.shape[0]
    v_t = v_ref[...].T
    ones = jnp.ones((16, keys), v_t.dtype)
    for i in range(rows // block):
        n = (i + 1) * block if causal else keys
        span = pl.ds(i * block, block)
        halves = []
        for h in range(2):
            q = half_mask(q_ref[span, :], h)
            s = hide(dot(k_ref[0:n, :], q, NT), limit, causal, i * block)
            peak = jnp.max(s, axis=0, keepdims=True)
            e = jnp.exp2(s - peak).astype(jnp.bfloat16)
            v_aug = jnp.concatenate([v_t[h * 64:(h + 1) * 64, :n], ones[:, :n]], axis=0)
            mixed = dot(v_aug, e)
            total = mixed[64:65]
            halves.append(mixed[:64] / total)
            lse_ref[0, h:h + 1, span] = peak + jnp.log2(total)
        o_ref[span, :] = jnp.concatenate(halves, axis=0).T.astype(o_ref.dtype)

def attend_back_kernel(causal, block, limit_ref, q_ref, k_ref, v_ref, g_ref, o_ref, lse_ref, dq_ref, dk_ref, dv_ref, dk_acc, dv_acc):
    limit = None if causal else limit_ref[0]
    rows, keys = q_ref.shape[0], k_ref.shape[0]
    k_t = k_ref[...].T
    sel_row = lax.broadcasted_iota(jnp.int32, (16, 128), 0)
    sel_lane = lax.broadcasted_iota(jnp.int32, (16, 128), 1)
    pick = jnp.where(sel_row == lax.div(sel_lane, 64), 1.0, 0.0).astype(jnp.bfloat16)
    dk_acc[...] = jnp.zeros_like(dk_acc)
    dv_acc[...] = jnp.zeros_like(dv_acc)
    for i in range(rows // block):
        n = (i + 1) * block if causal else keys
        span = pl.ds(i * block, block)
        prod = g_ref[span, :].astype(jnp.float32) * o_ref[span, :].astype(jnp.float32)
        high = prod.astype(jnp.bfloat16)
        low = (prod - high.astype(jnp.float32)).astype(jnp.bfloat16)
        delta = dot(pick, high, NT) + dot(pick, low, NT)
        halves = []
        for h in range(2):
            q = half_mask(q_ref[span, :], h)
            g = half_mask(g_ref[span, :], h)
            s = hide(dot(k_ref[0:n, :], q, NT), limit, causal, i * block)
            p = jnp.exp2(s - lse_ref[0, h:h + 1, span])
            dp = dot(v_ref[0:n, :], g, NT)
            ds = (p * (dp - delta[h:h + 1])).astype(jnp.bfloat16)
            dv_acc[0:n, :] += dot(p.astype(jnp.bfloat16), g)
            dk_acc[0:n, :] += dot(ds, q)
            halves.append(dot(k_t[h * 64:(h + 1) * 64, :n], ds))
        dq_ref[span, :] = (jnp.concatenate(halves, axis=0).T * 0.125).astype(dq_ref.dtype)
    dk_ref[...] = (dk_acc[...] * (1.0 / LOG2E)).astype(dk_ref.dtype)
    dv_ref[...] = dv_acc[...].astype(dv_ref.dtype)

def gelu_parts(u):
    t = 1.0 / (1.0 + (0.3275911 * 0.7071067811865476) * jnp.abs(u))
    e = jnp.exp(-0.5 * (u * u))
    poly = t * (0.254829592 + t * (-0.284496736 + t * (1.421413741 + t * (-1.453152027 + t * 1.061405429))))
    tail = 0.5 * poly * e
    return jnp.where(u < 0, tail, 1.0 - tail), e * 0.3989422804014327


def ffn_kernel(dims, sent, h_ref, g_ref, x_ref, up_ref, down_ref, out_ref, dh_ref, ddown_ref, grad_ref, rest_ref,
               h_t, acc, act, du, made, own, rc, r2a, r2b, r3, r4, local_sem, send, recv):
    j = pl.program_id(0)
    steps = pl.num_programs(0)
    at = Place(dims)
    nz, ny, nx, nc = dims
    z, y, x, c = at.z, at.y, at.x, at.c
    oy, ox, oc = 1 - y, 1 - x, 1 - c
    rows, width = h_ref.shape
    chunk = up_ref.shape[1]
    half = chunk // 2
    block = rows // 2
    left, right = pl.ds(0, half), pl.ds(half, half)
    every = slice(None)

    def made_at(slot, core):
        return made.at[(slot, every, every, every, core)]

    def core_go(i):
        slot = lax.rem(i, 2)
        pltpu.make_async_copy(made_at(slot, c), own.at[i], local_sem.at[i]).start()
        push(made_at(slot, oc), rc.at[i], send.at[i, 0], recv.at[i, 0], at.dev(c=oc))

    def first_go(i):
        drain(own.at[i], local_sem.at[i])
        drain(rc.at[i], recv.at[i, 0])
        drain(rc.at[i], send.at[i, 0])

        @pl.loop(0, nz)
        def _(a):
            for b in range(ny):
                for d in range(nx):
                    add_to(own.at[i, a, b, d], rc.at[i, a, b, d])

        push(own.at[i, :, oy, :, :, left], r2a.at[i], send.at[i, 1], recv.at[i, 1], at.dev(y=oy))
        push(own.at[i, :, :, ox, :, right], r2b.at[i], send.at[i, 1], recv.at[i, 2], at.dev(x=ox))

    def second_go(i):
        drain(r2a.at[i], recv.at[i, 1])
        drain(r2b.at[i], recv.at[i, 2])

        @pl.loop(0, nz)
        def _(a):
            for b in range(2):
                add_to(own.at[i, a, y, b, :, left], r2a.at[i, a, b])
                add_to(own.at[i, a, b, x, :, right], r2b.at[i, a, b])

        push(own.at[i, :, y, ox, :, left], r3.at[i, :, :, left], send.at[i, 1], recv.at[i, 3], at.dev(x=ox))
        push(own.at[i, :, oy, x, :, right], r3.at[i, :, :, right], send.at[i, 1], recv.at[i, 4], at.dev(y=oy))

    def third_go(i):
        drain(r3.at[i, :, :, left], recv.at[i, 3])
        drain(r3.at[i, :, :, right], recv.at[i, 4])

        @pl.loop(0, nz)
        def _(a):
            add_to(own.at[i, a, y, x], r3.at[i, a])

        for k in range(1, nz):
            far = lax.rem(z + k, nz)
            push(own.at[i, far, y, x], r4.at[i, k - 1], send.at[i, 1], recv.at[i, 5], at.dev(z=far))

    def finish(i):
        drain(r4.at[i], recv.at[i, 5])
        total = own[i, z, y, x].astype(jnp.float32)
        for k in range(nz - 1):
            total = total + r4[i, k].astype(jnp.float32)
        grad_ref[i] = total
        for part in (r2a.at[i], r2b.at[i], r3.at[i], r4.at[i]):
            drain(part, send.at[i, 1])

    @pl.when(j == 0)
    def _():
        hello([at.dev(z=k) for k in at.z_others()] + [at.dev(y=oy), at.dev(x=ox), at.dev(c=oc)])
        acc[...] = x_ref[...]
        dh_ref[...] = jnp.zeros_like(dh_ref)

        @pl.loop(0, rows // block)
        def _(r):
            span = pl.ds(pl.multiple_of(r * block, block), block)
            h_t[:, span] = h_ref[span, :].T

    def after(late, then):
        pl.when((j >= late) & (j - late < sent))(lambda: then(j - late))

    after(1, first_go)
    for r in range(rows // block):
        span = pl.ds(r * block, block)
        u = dot(h_ref[span, :], up_ref[...])
        g = dot(g_ref[span, :], down_ref[...], NT)
        big, small = gelu_parts(u)
        a = (u * big).astype(jnp.bfloat16)
        d = (g * (big + u * small)).astype(jnp.bfloat16)
        act[span, :] = a
        du[span, :] = d
        acc[span, :] += dot(a, down_ref[...])
        dh_ref[span, :] += dot(d, up_ref[...], NT)

    after(1, second_go)
    slot = lax.rem(j, 2)
    each = rows // (nz * ny * nx * nc)

    @pl.loop(0, nz)
    def _(a):
        n = ny * nx * nc * each
        part = dot(h_t[pl.ds(pl.multiple_of(a * n, n), n), :], du[...]).astype(made.dtype)
        made[slot, a] = part.reshape(ny, nx, nc, each, chunk)

    after(0, core_go)
    after(1, third_go)
    ddown_ref[...] = lax.dot_general(act[...], g_ref[...], (((0,), (0,)), ((), ())), preferred_element_type=jnp.float32).astype(ddown_ref.dtype)
    after(1, finish)

    @pl.when(j >= sent)
    def _():
        pltpu.make_async_copy(made.at[slot], rest_ref.at[j - sent], local_sem.at[j]).start()

    @pl.when(j == steps - 1)
    def _():
        out_ref[...] = acc[...].astype(out_ref.dtype)
        for i in range(sent, 4):
            drain(rest_ref.at[i - sent], local_sem.at[i])


def ffn(dims, h, g, x, w_up, w_down, cid, sent=3, steps=4):
    nz, ny, nx, nc = dims
    rows, width = h.shape
    inner = w_up.shape[1]
    chunk = inner // steps
    each = width // (nz * ny * nx * nc)
    bf, f32 = jnp.bfloat16, jnp.float32
    fixed = lambda j: (0, 0)
    whole = pl.BlockSpec((rows, width), fixed)
    once = pl.BlockSpec((rows, width), fixed, pipeline_mode=pl.Buffered(1))
    tile = (each, chunk)
    out, dh, ddown, grad, rest = pl.pallas_call(
        functools.partial(ffn_kernel, dims, sent),
        grid=(steps,),
        out_shape=[
            jax.ShapeDtypeStruct((rows, width), bf),
            jax.ShapeDtypeStruct((rows, width), f32),
            jax.ShapeDtypeStruct((inner, width), bf),
            jax.ShapeDtypeStruct((sent, each, chunk), f32),
            jax.ShapeDtypeStruct((steps - sent, nz, ny, nx, nc, each, chunk), bf),
        ],
        in_specs=[once, once, once, pl.BlockSpec((width, chunk), lambda j: (0, j)), pl.BlockSpec((chunk, width), lambda j: (j, 0))],
        out_specs=[once, once, pl.BlockSpec((chunk, width), lambda j: (j, 0)),
                   pl.BlockSpec((sent, each, chunk), lambda j: (0, 0, 0)), pl.BlockSpec(memory_space=ANY)],
        scratch_shapes=[
            pltpu.VMEM((width, rows), bf), pltpu.VMEM((rows, width), f32), pltpu.VMEM((rows, chunk), bf), pltpu.VMEM((rows, chunk), bf),
            pltpu.VMEM((2, nz, ny, nx, nc) + tile, bf),
            pltpu.VMEM((sent, nz, ny, nx) + tile, bf), pltpu.VMEM((sent, nz, ny, nx) + tile, bf),
            pltpu.VMEM((sent, nz, nx, each, chunk // 2), bf), pltpu.VMEM((sent, nz, ny, each, chunk // 2), bf),
            pltpu.VMEM((sent, nz) + tile, bf), pltpu.VMEM((sent, nz - 1) + tile, bf),
            pltpu.SemaphoreType.DMA((steps,)), pltpu.SemaphoreType.DMA((sent, 2)), pltpu.SemaphoreType.DMA((sent, 6)),
        ],
        compiler_params=pltpu.CompilerParams(collective_id=cid, has_side_effects=True, vmem_limit_bytes=62 * 2**20, dimension_semantics=("arbitrary",)),
        name="feed_forward",
    )(h, g, x, w_up, w_down)
    grad = jnp.moveaxis(grad, 0, 1).reshape(each, sent * chunk)
    rest = jnp.moveaxis(rest, 0, 5).reshape(width, (steps - sent) * chunk)
    return out, dh, ddown, grad, rest
class Gather:
    def __init__(self, dims, units, chunks, ins, outs, send, recv):
        self.at, self.nz = Place(dims), dims[0]
        self.units, self.chunks, self.ins, self.outs, self.send, self.recv = units, chunks, ins, outs, send, recv

    def part(self, u, *where):
        a, r0, nr, c0, ncol, _ = self.units[u]
        return self.outs[a].at[(*where, pl.ds(r0, nr), pl.ds(c0, ncol))]

    def first_of(self, u, there):
        at, every = self.at, slice(None)
        if self.units[u][5] == 0:
            return self.part(u, every, at.y, 1 - at.x if there else at.x, at.c)
        return self.part(u, every, 1 - at.y if there else at.y, at.x, at.c)

    def second_of(self, u, there):
        at, every = self.at, slice(None)
        if self.units[u][5] == 0:
            return self.part(u, every, 1 - at.y if there else at.y, every, at.c)
        return self.part(u, every, every, 1 - at.x if there else at.x, at.c)

    def z_go(self, u):
        at = self.at
        a, r0, nr, c0, ncol, _ = self.units[u]
        src = self.ins[a].at[pl.ds(r0, nr), pl.ds(c0, ncol)]
        for k in at.z_others():
            push(src, self.part(u, at.z, at.y, at.x, at.c), self.send.at[u], self.recv.at[u, 0], at.dev(z=k))

    def core_go(self, u, block):
        push(block, block, self.send.at[u], self.recv.at[u, 3], self.at.dev(c=1 - self.at.c))

    def along(self, first):
        return self.at.dev(x=1 - self.at.x) if first else self.at.dev(y=1 - self.at.y)

    def first_go(self, u):
        at = self.at
        drain(self.part(u, slice(0, self.nz - 1), at.y, at.x, at.c), self.recv.at[u, 0])
        block = self.first_of(u, False)
        push(block, block, self.send.at[u], self.recv.at[u, 1], self.along(self.units[u][5] == 0))
        self.core_go(u, block)

    def second_go(self, u):
        drain(self.first_of(u, True), self.recv.at[u, 1])
        self.core_go(u, self.first_of(u, True))
        block = self.second_of(u, False)
        push(block, block, self.send.at[u], self.recv.at[u, 2], self.along(self.units[u][5] == 1))

    def third_go(self, u):
        drain(self.second_of(u, True), self.recv.at[u, 2])
        self.core_go(u, self.second_of(u, True))

    def arrived(self, u):
        drain(self.part(u, slice(None), slice(None), slice(None), 1 - self.at.c), self.recv.at[u, 3])

    def sent(self, u):
        at, every = self.at, slice(None)
        drain(self.part(u, slice(0, self.nz - 1), at.y, at.x, at.c), self.send.at[u])
        drain(self.first_of(u, False), self.send.at[u])
        drain(self.second_of(u, False), self.send.at[u])
        drain(self.part(u, every, every, every, at.c), self.send.at[u])

    def round(self, t):
        count = len(self.chunks)
        steps = ((t + 1, self.z_go), (t, self.first_go), (t - 1, self.second_go), (t - 2, self.third_go))
        for k, go in steps:
            if 0 <= k < count:
                for u in self.chunks[k]:
                    go(u)


def norm_parts(values_in):
    center = values_in - jnp.mean(values_in, axis=-1, keepdims=True)
    return center * lax.rsqrt(jnp.mean(center * center, axis=-1, keepdims=True) + EPS)


FW_UNITS = [(0, 0, 16, 0, 128, 0)] + [(a, 0, 32, 0, 1024, 1 if a in (4, 8) else 0) for a in range(1, 9)]
FW_UNITS += [(9, 0, 32, 1024 * j, 1024, 1 if j == 3 else 0) for j in range(4)]
FW_UNITS += [(10, 32 * j, 32, 0, 1024, 1 if j == 3 else 0) for j in range(4)]
FW_CHUNKS = [(0, 1, 2), (3, 4), (5, 6), (7, 8), (9, 10), (11, 12), (13, 14), (15, 16)]


def forward_kernel(dims, n, *refs):
    shards, refs = refs[:n], refs[n:]
    block_in, out_grad, text_states, limits = refs[:4]
    full, refs = refs[4 : 4 + n], refs[4 + n :]
    g_out, x_out, q_out, k_out, v_out, cq_out, ck_out, cv_out, o_out, o2_out, h1_out, h2_out, h3_out, x1_out, x2_out, lse_out, lse2_out, vec = refs[:18]
    x_in, q, k, v, cq, ck, cv, o, o2, h1, h2, h3, x1, x2, lse, lse2, text, small = refs[18:36]
    w = refs[36:44]
    limit, local_sem, out_sem, send, recv, ex_send, ex_recv = refs[44:]
    at = Place(dims)
    oy, ox, oc, me = 1 - at.y, 1 - at.x, 1 - at.c, at.seq
    hello([at.dev(z=p) for p in at.z_others()] + [at.dev(y=oy), at.dev(x=ox), at.dev(c=oc), at.dev(x=ox, c=oc)])
    net = Gather(dims, FW_UNITS, FW_CHUNKS, shards, full, send, recv)
    rows, width = q.shape
    block = 256
    f32, bf = jnp.float32, jnp.bfloat16
    others = ((ox, at.c), (ox, oc), (at.x, oc))

    def exchange(src, dst, i):
        for px, pc in others:
            push(src.at[px * 2 + pc], dst.at[me], ex_send.at[i], ex_recv.at[i], at.dev(x=px, c=pc))
        pltpu.make_async_copy(src.at[me], dst.at[me], local_sem.at[n + i]).start()

    def exchanged(dst, i):
        drain(dst.at[0:3], ex_recv.at[i])
        drain(dst.at[0], local_sem.at[n + i])

    keep = []

    def put(src, dst):
        pltpu.make_async_copy(src, dst, out_sem.at[len(keep)]).start()
        keep.append(src)

    loads = 4 + n

    def load(a):
        net.arrived(a)
        pltpu.make_async_copy(full[a], w[a - 1], local_sem.at[loads + a]).start()

    def loaded(a):
        drain(w[a - 1], local_sem.at[loads + a])
        return lambda: w[a - 1][...].reshape(width, width)

    for a in range(n):
        pltpu.make_async_copy(shards[a], full[a].at[at.z, at.y, at.x, at.c], local_sem.at[a]).start()
    for u in FW_CHUNKS[0]:
        net.z_go(u)
    exchange(block_in, x_in, 0)
    pltpu.make_async_copy(text_states.at[me], text, local_sem.at[n + 2]).start()
    for a in range(n):
        drain(shards[a], local_sem.at[a])
    drain(text, local_sem.at[n + 2])
    limit[0] = limits[me]
    net.round(0)
    net.round(1)
    net.round(2)
    net.arrived(0)
    pltpu.make_async_copy(full[0], small, local_sem.at[n + 3]).start()
    drain(small, local_sem.at[n + 3])
    packed = small[...].reshape(-1, 16, 128).astype(f32)
    devices = packed.shape[0]
    piece = width // devices
    spread = jnp.where(
        lax.rem(lax.broadcasted_iota(jnp.int32, (128, width), 1), piece) == lax.broadcasted_iota(jnp.int32, (128, width), 0), 1.0, 0.0
    ).astype(bf)
    mine = lax.div(lax.broadcasted_iota(jnp.int32, (devices, width), 1), piece) == lax.broadcasted_iota(jnp.int32, (devices, width), 0)
    vec[...] = jnp.zeros_like(vec)
    for i in range(6):
        vec[i : i + 1, :] = jnp.sum(jnp.where(mine, dot(packed[:, i, :].astype(bf), spread), 0.0), axis=0, keepdims=True)
    exchanged(x_in, 0)
    exchange(out_grad, g_out, 1)
    put(x_in, x_out)

    @pl.loop(0, 4)
    def _(r):
        span = pl.ds(pl.multiple_of(r * block, block), block)
        x = x_in[r].astype(f32)
        x1[span, :] = x
        h1[span, :] = (norm_parts(x) * vec[0:1, :] + vec[1:2, :]).astype(bf)

    put(h1, h1_out)
    load(1)
    load(2)
    net.round(3)
    load(3)

    def project(src, a, dst, scale):
        weight = loaded(a)

        @pl.loop(0, rows // block)
        def _(r):
            span = pl.ds(pl.multiple_of(r * block, block), block)
            made = dot(src[span, :], weight())
            dst[span, :] = (made if scale is None else made * scale).astype(bf)

    project(h1, 1, q, LOG2E / 8)
    project(h1, 2, k, None)
    project(h1, 3, v, None)
    put(q, q_out)
    put(k, k_out)
    put(v, v_out)

    def pairs(first, last, causal, qs, ks, vs, os, ls):
        @pl.loop(first, last)
        def _(j):
            cols = pl.ds(pl.multiple_of(j * 128, 128), 128)
            attend_kernel(
                causal, 512, limit, qs.at[:, cols], ks.at[:, cols], vs.at[:, cols], os.at[:, cols], ls.at[pl.ds(j, 1)]
            )

    count = width // 128
    net.round(4)
    load(4)
    load(5)
    load(6)
    pairs(0, count // 2, True, q, k, v, o, lse)
    net.round(5)
    load(7)
    load(8)
    pairs(count // 2, count, True, q, k, v, o, lse)
    put(o, o_out)
    put(lse, lse_out)
    net.round(6)
    w_out, w_cq = loaded(4), loaded(5)

    @pl.loop(0, rows // block)
    def _(r):
        span = pl.ds(pl.multiple_of(r * block, block), block)
        x = x1[span, :] + dot(o[span, :], w_out())
        x1[span, :] = x
        h = (norm_parts(x) * vec[2:3, :] + vec[3:4, :]).astype(bf)
        h2[span, :] = h
        cq[span, :] = (dot(h, w_cq()) * (LOG2E / 8)).astype(bf)

    put(x1, x1_out)
    put(h2, h2_out)
    put(cq, cq_out)
    ck[...] = dot(text[...], loaded(6)()).astype(bf)
    cv[...] = dot(text[...], loaded(7)()).astype(bf)
    put(ck, ck_out)
    put(cv, cv_out)
    net.round(7)
    pairs(0, count, False, cq, ck, cv, o2, lse2)
    put(o2, o2_out)
    put(lse2, lse2_out)
    net.round(8)
    w_co = loaded(8)

    @pl.loop(0, rows // block)
    def _(r):
        span = pl.ds(pl.multiple_of(r * block, block), block)
        x = x1[span, :] + dot(o2[span, :], w_co())
        x2[span, :] = x
        h3[span, :] = (norm_parts(x) * vec[4:5, :] + vec[5:6, :]).astype(bf)

    put(x2, x2_out)
    put(h3, h3_out)
    net.round(9)
    exchanged(g_out, 1)
    for u in range(9, len(FW_UNITS)):
        net.arrived(u)
    for u in range(len(FW_UNITS)):
        net.sent(u)
    drain(x_in.at[0:3], ex_send.at[0])
    drain(g_out.at[0:3], ex_send.at[1])
    for i, src in enumerate(keep):
        drain(src, out_sem.at[i])


def forward(dims, shards, block_in, out_grad, text_states, limits, cid):
    n = len(shards)
    bf, f32 = jnp.bfloat16, jnp.float32
    items, seg, width = block_in.shape
    rows, texts = items * seg, text_states.shape[1]
    wide, pairs = jax.ShapeDtypeStruct((rows, width), bf), width // 128
    short = jax.ShapeDtypeStruct((texts, width), bf)
    long = jax.ShapeDtypeStruct((rows, width), f32)
    sums = jax.ShapeDtypeStruct((pairs, 8, rows), f32)
    seg4 = jax.ShapeDtypeStruct(block_in.shape, bf)
    whole = [jax.ShapeDtypeStruct(tuple(dims) + s.shape, s.dtype) for s in shards]
    saved = [wide, wide, wide, wide, short, short, wide, wide, wide, wide, wide, long, long, sums, sums]
    out_shape = whole + [seg4, seg4] + saved + [jax.ShapeDtypeStruct((8, width), f32)]
    held = [pltpu.VMEM(s.shape, s.dtype) for s in [seg4] + saved + [short]] + [pltpu.VMEM(tuple(dims) + (16, 128), bf)]
    held += [pltpu.VMEM(s.shape, s.dtype) for s in whole[1:9]]
    units = len(FW_UNITS)
    any_spec = pl.BlockSpec(memory_space=ANY)
    outs = pl.pallas_call(
        functools.partial(forward_kernel, dims, n),
        out_shape=out_shape,
        in_specs=[any_spec] * (n + 3) + [pl.BlockSpec(memory_space=pltpu.SMEM)],
        out_specs=[any_spec] * (len(out_shape) - 1) + [pl.BlockSpec(memory_space=pltpu.VMEM)],
        scratch_shapes=held
        + [
            pltpu.SMEM((1,), jnp.int32),
            pltpu.SemaphoreType.DMA((2 * n + 8,)), pltpu.SemaphoreType.DMA((20,)),
            pltpu.SemaphoreType.DMA((units,)), pltpu.SemaphoreType.DMA((units, 4)),
            pltpu.SemaphoreType.DMA((2,)), pltpu.SemaphoreType.DMA((2,)),
        ],
        compiler_params=pltpu.CompilerParams(collective_id=cid, has_side_effects=True, vmem_limit_bytes=62 * 2**20),
        name="forward",
    )(*shards, block_in, out_grad, text_states, limits)
    full = [o.reshape((-1,) + o.shape[5:]) for o in outs[:n]]
    return full, outs[n:]
class Scatter:
    def __init__(self, dims, send, recv, local):
        self.at, self.dims, self.send, self.recv, self.local, self.units = Place(dims), dims, send, recv, local, []

    def add(self, source, own, rc, r2, r3, r4, out, path, whole):
        self.units.append((source, own, rc, r2, r3, r4, out, path, whole))
        return len(self.units) - 1

    def own(self, u, *where):
        own, whole = self.units[u][1], self.units[u][8]
        return own.at[(*where, self.at.c)] if whole else own.at[where]

    def core_go(self, u):
        source, own, rc, whole = (self.units[u][k] for k in (0, 1, 2, 8))
        every, at = slice(None), self.at
        if not whole:
            pltpu.make_async_copy(source(every, every, every, at.c), own, self.local.at[u]).start()
        push(source(every, every, every, 1 - at.c), rc, self.send.at[u], self.recv.at[u, 0], at.dev(c=1 - at.c))

    def toward(self, u, leg):
        at = self.at
        return at.dev(y=1 - at.y) if (self.units[u][7] == 0) == (leg == 0) else at.dev(x=1 - at.x)

    def first_go(self, u):
        _, own, rc, r2, _, _, _, path, whole = self.units[u]
        nz, ny, nx, _ = self.dims
        at, every = self.at, slice(None)
        if not whole:
            drain(own, self.local.at[u])
        drain(rc, self.recv.at[u, 0])

        @pl.loop(0, nz)
        def _(a):
            for b in range(ny):
                for d in range(nx):
                    add_to(self.own(u, a, b, d), rc.at[a, b, d])

        block = self.own(u, every, 1 - at.y, every) if path == 0 else self.own(u, every, every, 1 - at.x)
        push(block, r2, self.send.at[u], self.recv.at[u, 1], self.toward(u, 0))

    def second_go(self, u):
        _, _, _, r2, r3, _, _, path, _ = self.units[u]
        nz, at, every = self.dims[0], self.at, slice(None)
        drain(r2, self.recv.at[u, 1])

        @pl.loop(0, nz)
        def _(a):
            for b in range(2):
                add_to(self.own(u, a, at.y, b) if path == 0 else self.own(u, a, b, at.x), r2.at[a, b])

        block = self.own(u, every, at.y, 1 - at.x) if path == 0 else self.own(u, every, 1 - at.y, at.x)
        push(block, r3, self.send.at[u], self.recv.at[u, 2], self.toward(u, 1))

    def third_go(self, u):
        _, _, _, _, r3, r4, _, _, _ = self.units[u]
        nz, at = self.dims[0], self.at
        drain(r3, self.recv.at[u, 2])

        @pl.loop(0, nz)
        def _(a):
            add_to(self.own(u, a, at.y, at.x), r3.at[a])

        for k in range(1, nz):
            far = lax.rem(at.z + k, nz)
            push(self.own(u, far, at.y, at.x), r4.at[k - 1], self.send.at[u], self.recv.at[u, 3], at.dev(z=far))

    def finish(self, u):
        _, _, rc, r2, r3, r4, out, _, _ = self.units[u]
        nz, at = self.dims[0], self.at
        drain(r4, self.recv.at[u, 3])
        total = self.own(u, at.z, at.y, at.x)[...].astype(jnp.float32)
        for k in range(nz - 1):
            total = total + r4[k].astype(jnp.float32)
        out[...] = total
        for block in (rc, r2, r3, r4):
            drain(block, self.send.at[u])


def scatter_room(dims, tile, dtype, whole):
    nz, ny, nx, nc = dims
    lead = (nz, ny, nx, nc) if whole else (nz, ny, nx)
    return [
        pltpu.VMEM(lead + tile, dtype), pltpu.VMEM((nz, ny, nx) + tile, dtype), pltpu.VMEM((nz, 2) + tile, dtype),
        pltpu.VMEM((nz,) + tile, dtype), pltpu.VMEM((nz - 1,) + tile, dtype),
    ]


def norm_back(x, dh, gain):
    center = x - jnp.mean(x, axis=-1, keepdims=True)
    r = lax.rsqrt(jnp.mean(center * center, axis=-1, keepdims=True) + EPS)
    n = center * r
    dn = dh * gain
    dx = r * (dn - jnp.mean(dn, axis=-1, keepdims=True) - n * jnp.mean(dn * n, axis=-1, keepdims=True))
    return dx, dh * n


def row_sum(rows):
    return jnp.sum(rows, axis=0, keepdims=True)


TN = (((0,), (0,)), ((), ()))


def middle_kernel(dims, *refs):
    (g_in, dh_in, x2_in, x1_in, vec, o2_in, cq_in, ck_in, cv_in, lse_in, h2_in, o_in, wco_in, wcq_in, wck_in, wcv_in, wo_in,
     text_in, limits, block_in, down_in, up_in) = refs[:22]
    block_out, text_out, dx_out, do_out, gco_out, gcq_out, gck_out, gcv_out, go_out, sums, down_out, up_out = refs[22:34]
    (x2, dh3, dx, g, dy, do, o2, wco, cq, dcq, wcq, wck, wcv, ck, cv, dck, dcv, lse, text, tg, stage, dk_acc, dv_acc, limit,
     load_sem, out_sem, ex_send, ex_recv, send, recv, local) = refs[34:65]
    rooms = refs[65:]
    at = Place(dims)
    nz = dims[0]
    oy, ox, oc, me = 1 - at.y, 1 - at.x, 1 - at.c, at.seq
    hello([at.dev(z=p) for p in at.z_others()] + [at.dev(y=oy), at.dev(x=ox), at.dev(c=oc), at.dev(x=ox, c=oc)])
    others = ((ox, at.c), (ox, oc), (at.x, oc))
    rows, width = g.shape
    block = 256
    f32, bf = jnp.float32, jnp.bfloat16
    every = slice(None)
    net = Scatter(dims, send, recv, local)
    quarter = width // 4
    for j in range(4):
        cols = pl.ds(j * quarter, quarter)
        net.add(lambda *w, cols=cols: down_in.at[(*w, every, cols)], *rooms[5 * j : 5 * j + 5], down_out.at[:, cols], 1 if j == 1 else 0, False)
    net.add(lambda *w: up_in.at[w], *rooms[20:25], up_out, 0, False)
    for u in (0, 1, 4, 2, 3):
        net.core_go(u)

    def exchange(src, dst, i):
        for px, pc in others:
            push(src.at[px * 2 + pc], dst.at[me], ex_send.at[i], ex_recv.at[i], at.dev(x=px, c=pc))
        pltpu.make_async_copy(src.at[me], dst.at[me], local.at[5 + i]).start()

    started = []

    def load(src, dst):
        pltpu.make_async_copy(src, dst, load_sem.at[len(started)]).start()
        started.append(dst)
        return len(started) - 1

    def loaded(i):
        drain(started[i], load_sem.at[i])

    kept = []

    def put(src, dst):
        pltpu.make_async_copy(src, dst, out_sem.at[len(kept)]).start()
        kept.append(src)
        return len(kept) - 1

    def kept_done(i):
        drain(kept[i], out_sem.at[i])

    def span_of(r):
        return pl.ds(pl.multiple_of(r * block, block), block)

    def weight_grad(src, grad, slot, dst):
        @pl.loop(0, nz)
        def _(a):
            part = dot(src[:, pl.ds(pl.multiple_of(a * block, block), block)], grad[...], TN).astype(bf)
            stage[slot, a] = part.reshape(stage.shape[2:])

        return put(stage.at[slot], dst)

    first = [load(dh_in, dh3), load(x2_in, x2), load(g_in, g), load(wco_in, wco), load(o2_in, o2)]
    second = [load(cq_in, cq), load(ck_in, ck), load(cv_in, cv), load(lse_in, lse)]
    third = [load(text_in.at[me], text), load(wcq_in, wcq), load(wck_in, wck), load(wcv_in, wcv)]
    limit[0] = limits[me]
    exchange(block_in, block_out, 0)
    for i in first:
        loaded(i)
    sums[...] = jnp.zeros_like(sums)

    def last_norm(r):
        span = span_of(r)
        d = dh3[span, :]
        grad, gain_terms = norm_back(x2[span, :], d, vec[4:5, :])
        sums[4:5, :] += row_sum(gain_terms)
        sums[5:6, :] += row_sum(d)
        total = g[span, :].astype(f32) + grad
        dx[span, :] = total
        low = total.astype(bf)
        dy[span, :] = low
        do[span, :] = dot(low, wco[...], NT).astype(bf)

    pl.loop(0, 2)(last_norm)
    net.first_go(0)
    net.first_go(1)
    pl.loop(2, 4)(last_norm)
    x1_load = load(x1_in, x2)
    o_load = load(o_in, g)
    h2_load = load(h2_in, wco)
    co_put = weight_grad(o2, dy, 0, gco_out)
    net.first_go(4)
    for i in second:
        loaded(i)
    dck_pairs = width // 128

    def cross(j):
        cols = pl.ds(pl.multiple_of(j * 128, 128), 128)
        attend_back_kernel(
            False, 512, limit, cq.at[:, cols], ck.at[:, cols], cv.at[:, cols], do.at[:, cols], o2.at[:, cols], lse.at[pl.ds(j, 1)],
            dcq.at[:, cols], dck.at[:, cols], dcv.at[:, cols], dk_acc, dv_acc,
        )

    pl.loop(0, dck_pairs // 2)(cross)
    net.second_go(0)
    net.second_go(1)
    net.first_go(2)
    pl.loop(dck_pairs // 2, dck_pairs)(cross)
    wo_load = load(wo_in, cq)
    net.third_go(0)
    net.second_go(4)
    net.first_go(3)
    for i in third:
        loaded(i)
    loaded(h2_load)
    cq_put = weight_grad(wco, dcq, 1, gcq_out)
    loaded(x1_load)
    loaded(wo_load)

    def middle_norm(r):
        span = span_of(r)
        d = dot(dcq[span, :], wcq[...], NT)
        grad, gain_terms = norm_back(x2[span, :], d, vec[2:3, :])
        sums[2:3, :] += row_sum(gain_terms)
        sums[3:4, :] += row_sum(d)
        total = dx[span, :] + grad
        dx[span, :] = total
        low = total.astype(bf)
        dy[span, :] = low
        do[span, :] = dot(low, cq[...], NT).astype(bf)

    pl.loop(0, 2)(middle_norm)
    net.third_go(1)
    net.second_go(2)
    net.third_go(4)
    net.finish(0)
    pl.loop(2, 4)(middle_norm)
    put(dx, dx_out)
    put(do, do_out)
    kept_done(co_put)
    net.second_go(3)
    net.third_go(2)
    net.finish(1)
    net.finish(4)
    loaded(o_load)
    o_put = weight_grad(g, dy, 0, go_out)
    kept_done(cq_put)
    ck_put = weight_grad(text, dck, 1, gck_out)
    tg[...] = (dot(dck[...], wck[...], NT) + dot(dcv[...], wcv[...], NT)).reshape(tg.shape)
    exchange(tg, text_out, 1)
    net.third_go(3)
    net.finish(2)
    kept_done(o_put)
    cv_put = weight_grad(text, dcv, 0, gcv_out)
    net.finish(3)
    for i, dst in ((0, block_out), (1, text_out)):
        drain(dst.at[0:3], ex_recv.at[i])
        drain(dst.at[0:3], ex_send.at[i])
        drain(dst.at[0], local.at[5 + i])
    for i in range(len(kept)):
        if i not in (co_put, cq_put, o_put):
            kept_done(i)


def middle(dims, args, cid):
    nz, ny, nx, nc = dims
    g, dh, x2, x1, vec, o2, cq, ck, cv, lse, h2, o, wco, wcq, wck, wcv, wo, text, limits, block_out, down, up = args
    rows, width = g.shape
    texts = text.shape[1]
    devices = nz * ny * nx * nc
    bf, f32 = jnp.bfloat16, jnp.float32
    each = width // devices
    long = down.shape[0] // devices
    down = down.reshape(nz, ny, nx, nc, long, width)
    up = up.reshape(nz, ny, nx, nc, each, up.shape[1])
    seg = block_out.shape
    held = jax.ShapeDtypeStruct((nz, ny, nx, nc, each, width), bf)
    wide, deep = jax.ShapeDtypeStruct((rows, width), bf), jax.ShapeDtypeStruct((rows, width), f32)
    out_shape = [
        jax.ShapeDtypeStruct(seg, bf), jax.ShapeDtypeStruct((seg[0], texts // seg[0], width), f32), deep, wide, held, held, held, held, held,
        jax.ShapeDtypeStruct((8, width), f32), jax.ShapeDtypeStruct((long, width), f32), jax.ShapeDtypeStruct((each, up.shape[5]), f32),
    ]
    any_spec, vm = pl.BlockSpec(memory_space=ANY), pl.BlockSpec(memory_space=pltpu.VMEM)
    big, square, short = pltpu.VMEM((rows, width), f32), pltpu.VMEM((rows, width), bf), pltpu.VMEM((texts, width), bf)
    dma = pltpu.SemaphoreType.DMA
    scratch = [big, big, big] + [square] * 10 + [short] * 4 + [pltpu.VMEM(lse.shape, f32), short]
    scratch += [pltpu.VMEM((seg[0], texts // seg[0], width), f32), pltpu.VMEM((2,) + held.shape, bf)]
    scratch += [pltpu.VMEM((texts, 128), f32)] * 2 + [pltpu.SMEM((1,), jnp.int32)]
    scratch += [dma((20,)), dma((12,)), dma((2,)), dma((2,)), dma((5,)), dma((5, 4)), dma((8,))]
    for _ in range(4):
        scratch += scatter_room(dims, (long, width // 4), bf, False)
    scratch += scatter_room(dims, (each, up.shape[5]), bf, False)
    specs = [any_spec] * 4 + [vm] + [any_spec] * 13 + [pl.BlockSpec(memory_space=pltpu.SMEM)] + [any_spec] * 3
    return pl.pallas_call(
        functools.partial(middle_kernel, dims),
        out_shape=out_shape,
        in_specs=specs,
        out_specs=[any_spec] * 9 + [vm] * 3,
        scratch_shapes=scratch,
        compiler_params=pltpu.CompilerParams(collective_id=cid, has_side_effects=True, vmem_limit_bytes=63 * 2**20),
        name="middle",
    )(g, dh, x2, x1, vec, o2, cq, ck, cv, lse, h2, o, wco, wcq, wck, wcv, wo, text, limits, block_out, down, up)


def last_kernel(dims, *refs):
    q_in, k_in, v_in, do_in, o_in, lse_in, h1_in, wq_in, wk_in, wv_in, x_in, dx_in, vec, gco, gcq, gck, gcv, go, sums_in = refs[:19]
    grad_out, co_out, cq_out, ck_out, cv_out, o_out, q_out, k_out, v_out, small_out = refs[19:29]
    (q, k, v, do, o, lse, h_t, dq, dk, dv, dx, send_rows, small, dk_acc, dv_acc, sums,
     load_sem, ex_send, ex_recv, send, recv, local) = refs[29:51]
    rooms = refs[51:]
    at = Place(dims)
    nz, ny, nx, nc = dims
    oy, ox, oc, me = 1 - at.y, 1 - at.x, 1 - at.c, at.seq
    hello([at.dev(z=p) for p in at.z_others()] + [at.dev(y=oy), at.dev(x=ox), at.dev(c=oc), at.dev(x=ox, c=oc)])
    rows, width = q.shape
    block = 256
    f32, bf = jnp.float32, jnp.bfloat16
    every = slice(None)
    net = Scatter(dims, send, recv, local)
    for j, (src, out, path) in enumerate(((gco, co_out, 0), (gcq, cq_out, 1), (gck, ck_out, 0), (gcv, cv_out, 1), (go, o_out, 0))):
        net.add(lambda *w, src=src: src.at[w], *rooms[5 * j : 5 * j + 5], out, path, False)
    half = width // 2
    for j in range(6):
        room = rooms[25 + 5 * j : 30 + 5 * j]
        out = (q_out, k_out, v_out)[j % 3].at[:, pl.ds((j // 3) * half, half)]
        net.add(lambda *w, held=room[0]: held.at[w], *room, out, 0 if j in (0, 1, 3, 4, 5) else 1, True)
    net.add(lambda *w: small.at[w], small, *rooms[55:59], small_out, 0, True)
    for u in range(5):
        net.core_go(u)
    started = []

    def load(src, dst):
        pltpu.make_async_copy(src, dst, load_sem.at[len(started)]).start()
        started.append(dst)
        return len(started) - 1

    def loaded(i):
        drain(started[i], load_sem.at[i])

    first = [load(a, b) for a, b in ((q_in, q), (k_in, k), (v_in, v), (do_in, do), (o_in, o), (lse_in, lse), (h1_in, dq), (dx_in, dx))]
    for i in first:
        loaded(i)

    @pl.loop(0, rows // block)
    def _(r):
        span = pl.ds(pl.multiple_of(r * block, block), block)
        h_t[:, span] = dq[span, :].T

    def pairs(a, b):
        @pl.loop(a, b)
        def _(j):
            cols = pl.ds(pl.multiple_of(j * 128, 128), 128)
            attend_back_kernel(
                True, 256, None, q.at[:, cols], k.at[:, cols], v.at[:, cols], do.at[:, cols], o.at[:, cols], lse.at[pl.ds(j, 1)],
                dq.at[:, cols], dk.at[:, cols], dv.at[:, cols], dk_acc, dv_acc,
            )

    def weight_grads(part):
        for j, grad in enumerate((dq, dk, dv)):
            u = 5 + 3 * part + j
            room = net.units[u][1]

            @pl.loop(0, nz)
            def _(a, room=room, grad=grad):
                span = pl.ds(pl.multiple_of(a * block, block), block)
                made = dot(h_t[span, :], grad[:, pl.ds(part * half, half)]).astype(bf)
                room[a] = made.reshape(room.shape[1:])

            net.core_go(u)

    count = width // 128
    net.first_go(0)
    net.first_go(1)
    pairs(0, 2)
    net.first_go(2)
    net.second_go(0)
    net.second_go(1)
    pairs(2, 4)
    net.first_go(3)
    net.second_go(2)
    net.third_go(0)
    net.third_go(1)
    weight_grads(0)
    net.first_go(4)
    net.second_go(3)
    net.third_go(2)
    net.finish(0)
    pairs(4, 6)
    net.finish(1)
    net.first_go(5)
    net.first_go(6)
    net.first_go(7)
    net.second_go(4)
    net.third_go(3)
    net.finish(2)
    pairs(6, count)
    net.second_go(5)
    net.second_go(6)
    net.second_go(7)
    net.third_go(4)
    net.finish(3)
    weights = [load(a, b) for a, b in ((wq_in, q), (wk_in, k), (wv_in, v), (x_in, do))]
    weight_grads(1)
    net.third_go(5)
    net.third_go(6)
    net.third_go(7)
    net.first_go(8)
    net.first_go(9)
    net.first_go(10)
    net.finish(4)
    for i in weights:
        loaded(i)
    sums[...] = sums_in[...]

    def last_norm(r):
        span = pl.ds(pl.multiple_of(r * block, block), block)
        d = dot(dq[span, :], q[...], NT) + dot(dk[span, :], k[...], NT) + dot(dv[span, :], v[...], NT)
        grad, gain_terms = norm_back(do[span, :].astype(f32), d, vec[0:1, :])
        sums[0:1, :] += row_sum(gain_terms)
        sums[1:2, :] += row_sum(d)
        send_rows[r] = (dx[span, :] + grad).astype(bf)

    for px, pc in ((ox, at.c), (ox, oc), (at.x, oc)):
        last_norm(px * 2 + pc)
        push(send_rows.at[px * 2 + pc], grad_out.at[me], ex_send, ex_recv, at.dev(x=px, c=pc))
    last_norm(me)
    pltpu.make_async_copy(send_rows.at[me], grad_out.at[me], local.at[12]).start()
    devices = nz * ny * nx * nc
    piece = width // devices
    lanes = lax.broadcasted_iota(jnp.int32, (width, 128), 0)
    fold = jnp.where(lax.rem(lanes, piece) == lax.broadcasted_iota(jnp.int32, (width, 128), 1), 1.0, 0.0).astype(bf)
    mine = lax.div(lax.broadcasted_iota(jnp.int32, (devices, width), 1), piece) == lax.broadcasted_iota(jnp.int32, (devices, width), 0)
    shares = []
    for i in range(6):
        spread = jnp.where(mine, sums[i : i + 1, :], 0.0)
        total = jnp.zeros((devices, 128), f32)
        for _ in range(3):
            low = spread.astype(bf)
            spread = spread - low.astype(f32)
            total = total + dot(low, fold)
        shares.append(total[:, None, :])
    shares.append(jnp.zeros((devices, 2, 128), f32))
    small[...] = jnp.concatenate(shares, axis=1).reshape(small.shape)
    net.core_go(11)
    net.second_go(8)
    net.second_go(9)
    net.second_go(10)
    net.finish(5)
    net.finish(6)
    net.finish(7)
    net.first_go(11)
    net.third_go(8)
    net.third_go(9)
    net.third_go(10)
    net.second_go(11)
    net.third_go(11)
    net.finish(8)
    net.finish(9)
    net.finish(10)
    net.finish(11)
    drain(grad_out.at[0:3], ex_recv)
    drain(grad_out.at[0:3], ex_send)
    drain(grad_out.at[0], local.at[12])


def last(dims, args, cid):
    nz, ny, nx, nc = dims
    q, k, v, do, o, lse, h1, wq, wk, wv, x, dx, vec, gco, gcq, gck, gcv, go, sums = args
    rows, width = q.shape
    bf, f32 = jnp.bfloat16, jnp.float32
    each = width // (nz * ny * nx * nc)
    shard = jax.ShapeDtypeStruct((each, width), f32)
    out_shape = [jax.ShapeDtypeStruct((4, rows // 4, width), bf)] + [shard] * 8 + [jax.ShapeDtypeStruct((8, 128), f32)]
    any_spec, vm = pl.BlockSpec(memory_space=ANY), pl.BlockSpec(memory_space=pltpu.VMEM)
    square = pltpu.VMEM((rows, width), bf)
    dma = pltpu.SemaphoreType.DMA
    scratch = [square] * 5 + [pltpu.VMEM(lse.shape, f32)] + [square] * 4 + [pltpu.VMEM((rows, width), f32), pltpu.VMEM((4, rows // 4, width), bf)]
    scratch += [pltpu.VMEM((nz, ny, nx, nc, 8, 128), f32)] + [pltpu.VMEM((rows, 128), f32)] * 2 + [pltpu.VMEM((8, width), f32)]
    scratch += [dma((16,)), dma, dma, dma((12,)), dma((12, 4)), dma((13,))]
    for _ in range(5):
        scratch += scatter_room(dims, (each, width), bf, False)
    for _ in range(6):
        scratch += scatter_room(dims, (each, width // 2), bf, True)
    scratch += scatter_room(dims, (8, 128), f32, True)[1:]
    return pl.pallas_call(
        functools.partial(last_kernel, dims),
        out_shape=out_shape,
        in_specs=[any_spec] * 12 + [vm] + [any_spec] * 5 + [vm],
        out_specs=[any_spec] + [vm] * 9,
        scratch_shapes=scratch,
        compiler_params=pltpu.CompilerParams(collective_id=cid, has_side_effects=True, vmem_limit_bytes=63 * 2**20),
        name="last",
    )(q, k, v, do, o, lse, h1, wq, wk, wv, x, dx, vec, gco, gcq, gck, gcv, go, sums)

HEAD_DIM = 64


EPS = 1e-05


def norm_rows(values_in, gain, bias):
    center = values_in - jnp.mean(values_in, axis=-1, keepdims=True)
    spread = jnp.mean(center * center, axis=-1, keepdims=True)
    return center * lax.rsqrt(spread + EPS) * gain + bias


def contract_rows(left, right):
    return lax.dot_general(
        left, right, (((0,), (0,)), ((), ())), preferred_element_type=jnp.float32
    )


def times_transposed(left, right):
    return lax.dot_general(
        left, right, (((1,), (1,)), ((), ())), preferred_element_type=jnp.float32
    )


def product(left, right):
    return jnp.dot(left, right, preferred_element_type=jnp.float32)


def local_plain(
    block_in,
    text_states,
    caption_len,
    out_grad,
    first_gain,
    first_bias,
    query_weight,
    key_weight,
    value_weight,
    output_weight,
    second_gain,
    second_bias,
    cross_query,
    cross_key,
    cross_value,
    cross_output,
    third_gain,
    third_bias,
    up_weight,
    down_weight,
):
    gathered = (
        lax.all_gather(first_gain, ("dp", "seq"), axis=0, tiled=True),
        lax.all_gather(first_bias, ("dp", "seq"), axis=0, tiled=True),
        lax.all_gather(query_weight, ("dp", "seq"), axis=0, tiled=True),
        lax.all_gather(key_weight, ("dp", "seq"), axis=0, tiled=True),
        lax.all_gather(value_weight, ("dp", "seq"), axis=0, tiled=True),
        lax.all_gather(output_weight, ("dp", "seq"), axis=0, tiled=True),
        lax.all_gather(second_gain, ("dp", "seq"), axis=0, tiled=True),
        lax.all_gather(second_bias, ("dp", "seq"), axis=0, tiled=True),
        lax.all_gather(cross_query, ("dp", "seq"), axis=0, tiled=True),
        lax.all_gather(cross_key, ("dp", "seq"), axis=0, tiled=True),
        lax.all_gather(cross_value, ("dp", "seq"), axis=0, tiled=True),
        lax.all_gather(cross_output, ("dp", "seq"), axis=0, tiled=True),
        lax.all_gather(third_gain, ("dp", "seq"), axis=0, tiled=True),
        lax.all_gather(third_bias, ("dp", "seq"), axis=0, tiled=True),
        lax.all_gather(up_weight, ("dp", "seq"), axis=0, tiled=True),
        lax.all_gather(down_weight, ("dp", "seq"), axis=0, tiled=True),
    )
    (
        gain_one,
        bias_one,
        w_query,
        w_key,
        w_value,
        w_output,
        gain_two,
        bias_two,
        w_cquery,
        w_ckey,
        w_cvalue,
        w_coutput,
        gain_three,
        bias_three,
        w_up,
        w_down,
    ) = gathered
    item_count, seg_len, model_width = block_in.shape
    row_count = item_count * seg_len
    head_count = model_width // HEAD_DIM
    score_scale = HEAD_DIM ** (-0.5)
    text_count = text_states.shape[1]
    inputs_f = block_in.astype(jnp.float32).reshape(row_count, model_width)
    normed_one, pull_one = jax.vjp(
        norm_rows, inputs_f, gain_one.astype(jnp.float32), bias_one.astype(jnp.float32)
    )
    normed_one = normed_one.astype(jnp.bfloat16)
    query_rows = product(normed_one, w_query).astype(jnp.bfloat16)
    key_rows = product(normed_one, w_key).astype(jnp.bfloat16)
    value_rows = product(normed_one, w_value).astype(jnp.bfloat16)
    key_all, value_all = (
        lax.all_gather(
            key_rows.reshape(item_count, seg_len, model_width), "seq", axis=1, tiled=True
        ),
        lax.all_gather(
            value_rows.reshape(item_count, seg_len, model_width), "seq", axis=1, tiled=True
        ),
    )
    key_count = key_all.shape[1]
    first_pos = lax.axis_index("seq") * seg_len
    query_pos = first_pos + jnp.arange(seg_len, dtype=jnp.int32)
    causal = jnp.arange(key_count, dtype=jnp.int32)[None, :] <= query_pos[:, None]

    def self_scores(query_item, key_item):
        query_heads = query_item.reshape(seg_len, head_count, HEAD_DIM)
        key_heads = key_item.reshape(key_count, head_count, HEAD_DIM)
        scores = jnp.einsum(
            "qhd,khd->hqk", query_heads, key_heads, preferred_element_type=jnp.float32
        )
        return jnp.where(causal[None, :, :], scores * score_scale, -1e30)

    def self_forward(operands):
        query_item, key_item, value_item = operands
        scores = self_scores(query_item, key_item)
        row_peak = jnp.max(scores, axis=-1, keepdims=True)
        row_total = jnp.sum(jnp.exp(scores - row_peak), axis=-1, keepdims=True)
        log_total = row_peak + jnp.log(row_total)
        prob_bf = jnp.exp(scores - log_total).astype(jnp.bfloat16)
        value_heads = value_item.reshape(key_count, head_count, HEAD_DIM)
        mixed = jnp.einsum("hqk,khd->qhd", prob_bf, value_heads, preferred_element_type=jnp.float32)
        return (mixed.reshape(seg_len, model_width).astype(jnp.bfloat16), log_total)

    attended, log_totals = lax.map(
        self_forward, (query_rows.reshape(item_count, seg_len, model_width), key_all, value_all)
    )
    attended_rows = attended.reshape(row_count, model_width)
    after_self = inputs_f + product(attended_rows, w_output)
    normed_two, pull_two = jax.vjp(
        norm_rows, after_self, gain_two.astype(jnp.float32), bias_two.astype(jnp.float32)
    )
    normed_two = normed_two.astype(jnp.bfloat16)
    cross_rows = product(normed_two, w_cquery).astype(jnp.bfloat16)
    cross_heads = cross_rows.reshape(item_count, seg_len, head_count, HEAD_DIM)
    text_keys = jnp.einsum(
        "itc,cd->itd", text_states, w_ckey, preferred_element_type=jnp.float32
    ).astype(jnp.bfloat16)
    text_values = jnp.einsum(
        "itc,cd->itd", text_states, w_cvalue, preferred_element_type=jnp.float32
    ).astype(jnp.bfloat16)
    text_kheads = text_keys.reshape(item_count, text_count, head_count, HEAD_DIM)
    text_vheads = text_values.reshape(item_count, text_count, head_count, HEAD_DIM)
    text_mask = jnp.arange(text_count, dtype=jnp.int32)[None, :] < caption_len[:, None]
    cross_scores = jnp.einsum(
        "iqhd,ithd->ihqt", cross_heads, text_kheads, preferred_element_type=jnp.float32
    )
    cross_scores = jnp.where(text_mask[:, None, None, :], cross_scores * score_scale, -1e30)
    cross_peak = jnp.max(cross_scores, axis=-1, keepdims=True)
    cross_exp = jnp.exp(cross_scores - cross_peak)
    cross_prob = cross_exp / jnp.sum(cross_exp, axis=-1, keepdims=True)
    cross_prob_bf = cross_prob.astype(jnp.bfloat16)
    crossed = jnp.einsum(
        "ihqt,ithd->iqhd", cross_prob_bf, text_vheads, preferred_element_type=jnp.float32
    )
    crossed_rows = crossed.reshape(row_count, model_width).astype(jnp.bfloat16)
    after_cross = after_self + product(crossed_rows, w_coutput)
    normed_three, pull_three = jax.vjp(
        norm_rows, after_cross, gain_three.astype(jnp.float32), bias_three.astype(jnp.float32)
    )
    normed_three = normed_three.astype(jnp.bfloat16)
    hidden = product(normed_three, w_up)
    activated, pull_gelu = jax.vjp(lambda inner: jax.nn.gelu(inner, approximate=False), hidden)
    activated = activated.astype(jnp.bfloat16)
    layer_out = after_cross + product(activated, w_down)
    block_out = layer_out.astype(jnp.bfloat16).reshape(item_count, seg_len, model_width)
    back_weights = (
        lax.all_gather(first_gain, ("dp", "seq"), axis=0, tiled=True),
        lax.all_gather(first_bias, ("dp", "seq"), axis=0, tiled=True),
        lax.all_gather(query_weight, ("dp", "seq"), axis=0, tiled=True),
        lax.all_gather(key_weight, ("dp", "seq"), axis=0, tiled=True),
        lax.all_gather(value_weight, ("dp", "seq"), axis=0, tiled=True),
        lax.all_gather(output_weight, ("dp", "seq"), axis=0, tiled=True),
        lax.all_gather(second_gain, ("dp", "seq"), axis=0, tiled=True),
        lax.all_gather(second_bias, ("dp", "seq"), axis=0, tiled=True),
        lax.all_gather(cross_query, ("dp", "seq"), axis=0, tiled=True),
        lax.all_gather(cross_key, ("dp", "seq"), axis=0, tiled=True),
        lax.all_gather(cross_value, ("dp", "seq"), axis=0, tiled=True),
        lax.all_gather(cross_output, ("dp", "seq"), axis=0, tiled=True),
        lax.all_gather(third_gain, ("dp", "seq"), axis=0, tiled=True),
        lax.all_gather(third_bias, ("dp", "seq"), axis=0, tiled=True),
        lax.all_gather(up_weight, ("dp", "seq"), axis=0, tiled=True),
        lax.all_gather(down_weight, ("dp", "seq"), axis=0, tiled=True),
    )
    (
        unused_gain,
        unused_bias,
        w_query,
        w_key,
        w_value,
        w_output,
        unused_gtwo,
        unused_btwo,
        w_cquery,
        w_ckey,
        w_cvalue,
        w_coutput,
        unused_gthree,
        unused_bthree,
        w_up,
        w_down,
    ) = back_weights
    grad_rows = out_grad.reshape(row_count, model_width)
    down_part = contract_rows(activated, grad_rows)
    act_grad = times_transposed(grad_rows, w_down)
    hidden_grad = pull_gelu(act_grad)[0].astype(jnp.bfloat16)
    up_part = contract_rows(normed_three, hidden_grad)
    normed_three_grad = times_transposed(hidden_grad, w_up)
    resid_three, gain_three_part, bias_three_part = pull_three(normed_three_grad)
    cross_grad = grad_rows.astype(jnp.float32) + resid_three
    cross_out_bf = cross_grad.astype(jnp.bfloat16)
    coutput_part = contract_rows(crossed_rows, cross_out_bf)
    crossed_grad = times_transposed(cross_out_bf, w_coutput).astype(jnp.bfloat16)
    crossed_heads = crossed_grad.reshape(item_count, seg_len, head_count, HEAD_DIM)
    cross_dprob = jnp.einsum(
        "iqhd,ithd->ihqt", crossed_heads, text_vheads, preferred_element_type=jnp.float32
    )
    cross_dscore = cross_prob * (
        cross_dprob - jnp.sum(cross_dprob * cross_prob, axis=-1, keepdims=True)
    )
    cross_dscore = cross_dscore.astype(jnp.bfloat16)
    cquery_grad = (
        (
            jnp.einsum(
                "ihqt,ithd->iqhd", cross_dscore, text_kheads, preferred_element_type=jnp.float32
            )
            * score_scale
        )
        .astype(jnp.bfloat16)
        .reshape(row_count, model_width)
    )
    tkey_part = (
        jnp.einsum("ihqt,iqhd->ithd", cross_dscore, cross_heads, preferred_element_type=jnp.float32)
        * score_scale
    ).reshape(item_count, text_count, model_width)
    tvalue_part = jnp.einsum(
        "ihqt,iqhd->ithd", cross_prob_bf, crossed_heads, preferred_element_type=jnp.float32
    ).reshape(item_count, text_count, model_width)
    cquery_part = contract_rows(normed_two, cquery_grad)
    normed_two_grad = times_transposed(cquery_grad, w_cquery)
    resid_two, gain_two_part, bias_two_part = pull_two(normed_two_grad)
    self_grad = cross_grad + resid_two
    self_out_bf = self_grad.astype(jnp.bfloat16)
    output_part = contract_rows(attended_rows, self_out_bf)
    attended_grad = times_transposed(self_out_bf, w_output).astype(jnp.bfloat16)
    query_items = query_rows.reshape(item_count, seg_len, model_width)
    dout_items = attended_grad.reshape(item_count, seg_len, model_width)

    def self_backward(operands):
        query_item, key_item, value_item, dout_item, log_total = operands
        scores = self_scores(query_item, key_item)
        probs = jnp.exp(scores - log_total)
        prob_bf = probs.astype(jnp.bfloat16)
        query_heads = query_item.reshape(seg_len, head_count, HEAD_DIM)
        key_heads = key_item.reshape(key_count, head_count, HEAD_DIM)
        value_heads = value_item.reshape(key_count, head_count, HEAD_DIM)
        dout_heads = dout_item.reshape(seg_len, head_count, HEAD_DIM)
        dprob = jnp.einsum(
            "qhd,khd->hqk", dout_heads, value_heads, preferred_element_type=jnp.float32
        )
        dscore = (probs * (dprob - jnp.sum(dprob * probs, axis=-1, keepdims=True))).astype(
            jnp.bfloat16
        )
        dquery = (
            (
                jnp.einsum("hqk,khd->qhd", dscore, key_heads, preferred_element_type=jnp.float32)
                * score_scale
            )
            .astype(jnp.bfloat16)
            .reshape(seg_len, model_width)
        )
        dkey = (
            jnp.einsum("hqk,qhd->khd", dscore, query_heads, preferred_element_type=jnp.float32)
            * score_scale
        ).reshape(key_count, model_width)
        dvalue = jnp.einsum(
            "hqk,qhd->khd", prob_bf, dout_heads, preferred_element_type=jnp.float32
        ).reshape(key_count, model_width)
        return (dquery, dkey, dvalue)

    query_grad_items, key_part, value_part = lax.map(
        self_backward, (query_items, key_all, value_all, dout_items, log_totals)
    )
    key_own, value_own, tkey_own, tvalue_own = (
        lax.psum_scatter(
            key_part.astype(jnp.bfloat16), "seq", scatter_dimension=1, tiled=True
        ).astype(jnp.float32),
        lax.psum_scatter(
            value_part.astype(jnp.bfloat16), "seq", scatter_dimension=1, tiled=True
        ).astype(jnp.float32),
        lax.psum_scatter(
            tkey_part.astype(jnp.bfloat16), "seq", scatter_dimension=1, tiled=True
        ).astype(jnp.float32),
        lax.psum_scatter(
            tvalue_part.astype(jnp.bfloat16), "seq", scatter_dimension=1, tiled=True
        ).astype(jnp.float32),
    )
    key_grad_rows = key_own.astype(jnp.bfloat16).reshape(row_count, model_width)
    value_grad_rows = value_own.astype(jnp.bfloat16).reshape(row_count, model_width)
    query_grad_rows = query_grad_items.reshape(row_count, model_width)
    tkey_bf = tkey_own.astype(jnp.bfloat16)
    tvalue_bf = tvalue_own.astype(jnp.bfloat16)
    query_part = contract_rows(normed_one, query_grad_rows)
    key_wpart = contract_rows(normed_one, key_grad_rows)
    value_wpart = contract_rows(normed_one, value_grad_rows)
    normed_one_grad = (
        times_transposed(query_grad_rows, w_query)
        + times_transposed(key_grad_rows, w_key)
        + times_transposed(value_grad_rows, w_value)
    )
    resid_one, gain_one_part, bias_one_part = pull_one(normed_one_grad)
    input_grad = (self_grad + resid_one).reshape(item_count, seg_len, model_width)
    text_rows = tkey_own.shape[1]
    text_start = lax.axis_index("seq") * text_rows
    text_slice = lax.dynamic_slice_in_dim(text_states, text_start, text_rows, 1)
    ckey_part = jnp.einsum("itc,itd->cd", text_slice, tkey_bf, preferred_element_type=jnp.float32)
    cvalue_part = jnp.einsum(
        "itc,itd->cd", text_slice, tvalue_bf, preferred_element_type=jnp.float32
    )
    text_grad = jnp.einsum(
        "itd,cd->itc", tkey_bf, w_ckey, preferred_element_type=jnp.float32
    ) + jnp.einsum("itd,cd->itc", tvalue_bf, w_cvalue, preferred_element_type=jnp.float32)
    (
        first_gain_grad,
        first_bias_grad,
        query_grad,
        key_grad,
        value_grad,
        output_grad,
        second_gain_grad,
        second_bias_grad,
        cross_query_grad,
        cross_key_grad,
        cross_value_grad,
        cross_output_grad,
        third_gain_grad,
        third_bias_grad,
        up_grad,
        down_grad,
    ) = (
        lax.psum_scatter(gain_one_part, ("dp", "seq"), scatter_dimension=0, tiled=True),
        lax.psum_scatter(bias_one_part, ("dp", "seq"), scatter_dimension=0, tiled=True),
        lax.psum_scatter(query_part, ("dp", "seq"), scatter_dimension=0, tiled=True),
        lax.psum_scatter(key_wpart, ("dp", "seq"), scatter_dimension=0, tiled=True),
        lax.psum_scatter(value_wpart, ("dp", "seq"), scatter_dimension=0, tiled=True),
        lax.psum_scatter(output_part, ("dp", "seq"), scatter_dimension=0, tiled=True),
        lax.psum_scatter(gain_two_part, ("dp", "seq"), scatter_dimension=0, tiled=True),
        lax.psum_scatter(bias_two_part, ("dp", "seq"), scatter_dimension=0, tiled=True),
        lax.psum_scatter(cquery_part, ("dp", "seq"), scatter_dimension=0, tiled=True),
        lax.psum_scatter(ckey_part, ("dp", "seq"), scatter_dimension=0, tiled=True),
        lax.psum_scatter(cvalue_part, ("dp", "seq"), scatter_dimension=0, tiled=True),
        lax.psum_scatter(coutput_part, ("dp", "seq"), scatter_dimension=0, tiled=True),
        lax.psum_scatter(gain_three_part, ("dp", "seq"), scatter_dimension=0, tiled=True),
        lax.psum_scatter(bias_three_part, ("dp", "seq"), scatter_dimension=0, tiled=True),
        lax.psum_scatter(up_part, ("dp", "seq"), scatter_dimension=0, tiled=True),
        lax.psum_scatter(down_part, ("dp", "seq"), scatter_dimension=0, tiled=True),
    )
    return (
        block_out,
        input_grad,
        text_grad,
        first_gain_grad,
        first_bias_grad,
        query_grad,
        key_grad,
        value_grad,
        output_grad,
        second_gain_grad,
        second_bias_grad,
        cross_query_grad,
        cross_key_grad,
        cross_value_grad,
        cross_output_grad,
        third_gain_grad,
        third_bias_grad,
        up_grad,
        down_grad,
    )


def small_rows(vectors):
    packed = jnp.stack(vectors)
    return jnp.pad(packed, ((0, 16 - packed.shape[0]), (0, 128 - packed.shape[1])))


def local(seq_size, *args):
    block_in = args[0]
    if block_in.shape[0] != seq_size or seq_size != 4 or block_in.shape[1] * seq_size != 1024:
        return local_plain(*args)
    return local_items(seq_size, *args)


def local_items(
    seq_size,
    block_in,
    text_states,
    caption_len,
    out_grad,
    first_gain,
    first_bias,
    query_weight,
    key_weight,
    value_weight,
    output_weight,
    second_gain,
    second_bias,
    cross_query,
    cross_key,
    cross_value,
    cross_output,
    third_gain,
    third_bias,
    up_weight,
    down_weight,
):
    ny, nx, nc = 2, seq_size // 2, 2
    dp_size = 1024 // first_gain.shape[0] // seq_size
    dims = (dp_size // ny, ny, nx, nc)
    bf, f32 = jnp.bfloat16, jnp.float32
    seg, width = block_in.shape[1], block_in.shape[2]
    rows = seq_size * seg
    me = lax.axis_index("seq")
    small = small_rows([first_gain, first_bias, second_gain, second_bias, third_gain, third_bias])
    shards = [small, query_weight, key_weight, value_weight, output_weight, cross_query, cross_key, cross_value, cross_output, up_weight, down_weight]
    full, kept = forward(dims, shards, block_in, out_grad, text_states, caption_len, 1)
    small, w_query, w_key, w_value, w_output, w_cquery, w_ckey, w_cvalue, w_coutput, w_up, w_down = full
    grad_rows, inputs, q, k, v, cq, ck, cv, o, o2, normed_one, normed_two, normed_three, after_self, after_cross, lse, lse2, vectors = kept
    grad_rows = grad_rows.reshape(rows, width)
    block_out, dh3, down_part, up_grad_done, up_part = ffn(dims, normed_three, grad_rows, after_cross, w_up, w_down, 4)
    (
        block_out, text_grad, self_grad, do, g_co, g_cq, g_ck, g_cv, g_o, sums, down_grad, up_grad,
    ) = middle(dims, (
        grad_rows, dh3, after_cross, after_self, vectors, o2, cq, ck, cv, lse2, normed_two, o, w_coutput, w_cquery, w_ckey, w_cvalue,
        w_output, text_states, caption_len, block_out.reshape(seq_size, seg, width), down_part, up_part,
    ), 2)
    up_grad = jnp.concatenate([up_grad_done, up_grad], axis=1)
    (
        input_grad, coutput_grad, cquery_grad, ckey_grad, cvalue_grad, output_grad, query_grad, key_grad, value_grad, small_grad,
    ) = last(dims, (
        q, k, v, do, o, lse, normed_one, w_query, w_key, w_value, inputs.reshape(rows, width), self_grad, vectors,
        g_co, g_cq, g_ck, g_cv, g_o, sums,
    ), 3)
    input_grad = input_grad.astype(f32)
    vec = [small_grad[i, : first_gain.shape[0]] for i in range(6)]
    return (
        block_out, input_grad, text_grad,
        vec[0], vec[1], query_grad, key_grad, value_grad, output_grad,
        vec[2], vec[3], cquery_grad, ckey_grad, cvalue_grad, coutput_grad,
        vec[4], vec[5], up_grad, down_grad,
    )


def solution(mesh):
    return jax.shard_map(
        functools.partial(local, mesh.shape['seq']),
        mesh=mesh,
        in_specs=(
            P("dp", "seq", None),
            P("dp", None, None),
            P("dp"),
            P("dp", "seq", None),
            P(("dp", "seq")),
            P(("dp", "seq")),
            P(("dp", "seq"), None),
            P(("dp", "seq"), None),
            P(("dp", "seq"), None),
            P(("dp", "seq"), None),
            P(("dp", "seq")),
            P(("dp", "seq")),
            P(("dp", "seq"), None),
            P(("dp", "seq"), None),
            P(("dp", "seq"), None),
            P(("dp", "seq"), None),
            P(("dp", "seq")),
            P(("dp", "seq")),
            P(("dp", "seq"), None),
            P(("dp", "seq"), None),
        ),
        out_specs=(
            P("dp", "seq", None),
            P("dp", "seq", None),
            P("dp", "seq", None),
            P(("dp", "seq")),
            P(("dp", "seq")),
            P(("dp", "seq"), None),
            P(("dp", "seq"), None),
            P(("dp", "seq"), None),
            P(("dp", "seq"), None),
            P(("dp", "seq")),
            P(("dp", "seq")),
            P(("dp", "seq"), None),
            P(("dp", "seq"), None),
            P(("dp", "seq"), None),
            P(("dp", "seq"), None),
            P(("dp", "seq")),
            P(("dp", "seq")),
            P(("dp", "seq"), None),
            P(("dp", "seq"), None),
        ),
        check_vma=False,
    )
```

```python
import functools
import itertools

import jax
import jax.numpy as jnp
from jax import lax
from jax.experimental import pallas as pl
from jax.experimental.pallas import tpu as pltpu
from jax.sharding import PartitionSpec as P

MESH = pl.DeviceIdType.MESH
ANY = pl.ANY


class Place:
    def __init__(self, dims):
        self.nz, self.ny, self.nx, self.nc = dims
        dp, seq = lax.axis_index("dp"), lax.axis_index("seq")
        self.z, self.y = lax.div(dp, self.ny), lax.rem(dp, self.ny)
        self.x, self.c = lax.div(seq, self.nc), lax.rem(seq, self.nc)
        self.dp, self.seq = dp, seq

    def dev(self, z=None, y=None, x=None, c=None):
        z = self.z if z is None else z
        y = self.y if y is None else y
        x = self.x if x is None else x
        c = self.c if c is None else c
        return (z * self.ny + y, x * self.nc + c)

    def z_others(self):
        return [lax.rem(self.z + k, self.nz) for k in range(1, self.nz)]


def hello(peers):
    barrier = pltpu.get_barrier_semaphore()
    for peer in peers:
        pl.semaphore_signal(barrier, inc=1, device_id=peer, device_id_type=MESH)
    pl.semaphore_wait(barrier, len(peers))


def push(src, dst, send, recv, device):
    pltpu.make_async_remote_copy(
        src_ref=src, dst_ref=dst, send_sem=send, recv_sem=recv, device_id=device, device_id_type=MESH
    ).start()


def drain(ref, sem):
    pltpu.make_async_copy(ref, ref, sem).wait()


def add_to(dst, src):
    dst[...] = dst[...] + src[...]


LOG2E = 1.4426950408889634
NT = (((1,), (1,)), ((), ()))
NN = (((1,), (0,)), ((), ()))
def dot(a, b, dims=NN):
    return lax.dot_general(a, b, dims, preferred_element_type=jnp.float32)

def half_mask(x, h):
    lane = lax.broadcasted_iota(jnp.int32, x.shape, 1)
    keep = lane < 64 if h == 0 else lane >= 64
    return jnp.where(keep, x, jnp.zeros_like(x))

def hide(scores, limit, causal, start):
    rows, cols = scores.shape
    if causal:
        key = lax.broadcasted_iota(jnp.int32, (cols, cols), 0)
        query = lax.broadcasted_iota(jnp.int32, (cols, cols), 1)
        tail = jnp.where(key <= query, scores[rows - cols:], -1e30)
        return tail if rows == cols else jnp.concatenate([scores[:rows - cols], tail], axis=0)
    key = lax.broadcasted_iota(jnp.int32, (rows, cols), 0)
    return jnp.where(key < limit, scores, -1e30)

def attend_kernel(causal, block, limit_ref, q_ref, k_ref, v_ref, o_ref, lse_ref):
    limit = None if causal else limit_ref[0]
    rows, keys = q_ref.shape[0], k_ref.shape[0]
    v_t = v_ref[...].T
    ones = jnp.ones((16, keys), v_t.dtype)
    for i in range(rows // block):
        n = (i + 1) * block if causal else keys
        span = pl.ds(i * block, block)
        halves = []
        for h in range(2):
            q = half_mask(q_ref[span, :], h)
            s = hide(dot(k_ref[0:n, :], q, NT), limit, causal, i * block)
            peak = jnp.max(s, axis=0, keepdims=True)
            e = jnp.exp2(s - peak).astype(jnp.bfloat16)
            v_aug = jnp.concatenate([v_t[h * 64:(h + 1) * 64, :n], ones[:, :n]], axis=0)
            mixed = dot(v_aug, e)
            total = mixed[64:65]
            halves.append(mixed[:64] / total)
            lse_ref[0, h:h + 1, span] = peak + jnp.log2(total)
        o_ref[span, :] = jnp.concatenate(halves, axis=0).T.astype(o_ref.dtype)

def attend_back_kernel(causal, block, limit_ref, q_ref, k_ref, v_ref, g_ref, o_ref, lse_ref, dq_ref, dk_ref, dv_ref, dk_acc, dv_acc):
    limit = None if causal else limit_ref[0]
    rows, keys = q_ref.shape[0], k_ref.shape[0]
    k_t = k_ref[...].T
    sel_row = lax.broadcasted_iota(jnp.int32, (16, 128), 0)
    sel_lane = lax.broadcasted_iota(jnp.int32, (16, 128), 1)
    pick = jnp.where(sel_row == lax.div(sel_lane, 64), 1.0, 0.0).astype(jnp.bfloat16)
    dk_acc[...] = jnp.zeros_like(dk_acc)
    dv_acc[...] = jnp.zeros_like(dv_acc)
    for i in range(rows // block):
        n = (i + 1) * block if causal else keys
        span = pl.ds(i * block, block)
        prod = g_ref[span, :].astype(jnp.float32) * o_ref[span, :].astype(jnp.float32)
        high = prod.astype(jnp.bfloat16)
        low = (prod - high.astype(jnp.float32)).astype(jnp.bfloat16)
        delta = dot(pick, high, NT) + dot(pick, low, NT)
        halves = []
        for h in range(2):
            q = half_mask(q_ref[span, :], h)
            g = half_mask(g_ref[span, :], h)
            s = hide(dot(k_ref[0:n, :], q, NT), limit, causal, i * block)
            p = jnp.exp2(s - lse_ref[0, h:h + 1, span])
            dp = dot(v_ref[0:n, :], g, NT)
            ds = (p * (dp - delta[h:h + 1])).astype(jnp.bfloat16)
            dv_acc[0:n, :] += dot(p.astype(jnp.bfloat16), g)
            dk_acc[0:n, :] += dot(ds, q)
            halves.append(dot(k_t[h * 64:(h + 1) * 64, :n], ds))
        dq_ref[span, :] = (jnp.concatenate(halves, axis=0).T * 0.125).astype(dq_ref.dtype)
    dk_ref[...] = (dk_acc[...] * (1.0 / LOG2E)).astype(dk_ref.dtype)
    dv_ref[...] = dv_acc[...].astype(dv_ref.dtype)

def gelu_parts(u):
    t = 1.0 / (1.0 + (0.3275911 * 0.7071067811865476) * jnp.abs(u))
    e = jnp.exp(-0.5 * (u * u))
    poly = t * (0.254829592 + t * (-0.284496736 + t * (1.421413741 + t * (-1.453152027 + t * 1.061405429))))
    tail = 0.5 * poly * e
    return jnp.where(u < 0, tail, 1.0 - tail), e * 0.3989422804014327


def ffn_kernel(dims, sent, h_ref, g_ref, x_ref, up_ref, down_ref, out_ref, dh_ref, ddown_ref, grad_ref, rest_ref,
               h_t, acc, act, du, made, own, rc, r2a, r2b, r3, r4, local_sem, send, recv):
    j = pl.program_id(0)
    steps = pl.num_programs(0)
    at = Place(dims)
    nz, ny, nx, nc = dims
    z, y, x, c = at.z, at.y, at.x, at.c
    oy, ox, oc = 1 - y, 1 - x, 1 - c
    rows, width = h_ref.shape
    chunk = up_ref.shape[1]
    half = chunk // 2
    block = rows // 2
    left, right = pl.ds(0, half), pl.ds(half, half)
    every = slice(None)

    def made_at(slot, core):
        return made.at[(slot, every, every, every, core)]

    def core_go(i):
        slot = lax.rem(i, 2)
        pltpu.make_async_copy(made_at(slot, c), own.at[i], local_sem.at[i]).start()
        push(made_at(slot, oc), rc.at[i], send.at[i, 0], recv.at[i, 0], at.dev(c=oc))

    def first_go(i):
        drain(own.at[i], local_sem.at[i])
        drain(rc.at[i], recv.at[i, 0])
        drain(rc.at[i], send.at[i, 0])

        @pl.loop(0, nz)
        def _(a):
            for b in range(ny):
                for d in range(nx):
                    add_to(own.at[i, a, b, d], rc.at[i, a, b, d])

        push(own.at[i, :, oy, :, :, left], r2a.at[i], send.at[i, 1], recv.at[i, 1], at.dev(y=oy))
        push(own.at[i, :, :, ox, :, right], r2b.at[i], send.at[i, 1], recv.at[i, 2], at.dev(x=ox))

    def second_go(i):
        drain(r2a.at[i], recv.at[i, 1])
        drain(r2b.at[i], recv.at[i, 2])

        @pl.loop(0, nz)
        def _(a):
            for b in range(2):
                add_to(own.at[i, a, y, b, :, left], r2a.at[i, a, b])
                add_to(own.at[i, a, b, x, :, right], r2b.at[i, a, b])

        push(own.at[i, :, y, ox, :, left], r3.at[i, :, :, left], send.at[i, 1], recv.at[i, 3], at.dev(x=ox))
        push(own.at[i, :, oy, x, :, right], r3.at[i, :, :, right], send.at[i, 1], recv.at[i, 4], at.dev(y=oy))

    def third_go(i):
        drain(r3.at[i, :, :, left], recv.at[i, 3])
        drain(r3.at[i, :, :, right], recv.at[i, 4])

        @pl.loop(0, nz)
        def _(a):
            add_to(own.at[i, a, y, x], r3.at[i, a])

        for k in range(1, nz):
            far = lax.rem(z + k, nz)
            push(own.at[i, far, y, x], r4.at[i, k - 1], send.at[i, 1], recv.at[i, 5], at.dev(z=far))

    def finish(i):
        drain(r4.at[i], recv.at[i, 5])
        total = own[i, z, y, x].astype(jnp.float32)
        for k in range(nz - 1):
            total = total + r4[i, k].astype(jnp.float32)
        grad_ref[i] = total
        for part in (r2a.at[i], r2b.at[i], r3.at[i], r4.at[i]):
            drain(part, send.at[i, 1])

    @pl.when(j == 0)
    def _():
        hello([at.dev(z=k) for k in at.z_others()] + [at.dev(y=oy), at.dev(x=ox), at.dev(c=oc)])
        acc[...] = x_ref[...]
        dh_ref[...] = jnp.zeros_like(dh_ref)

        @pl.loop(0, rows // block)
        def _(r):
            span = pl.ds(pl.multiple_of(r * block, block), block)
            h_t[:, span] = h_ref[span, :].T

    def after(late, then):
        pl.when((j >= late) & (j - late < sent))(lambda: then(j - late))

    after(1, first_go)
    for r in range(rows // block):
        span = pl.ds(r * block, block)
        u = dot(h_ref[span, :], up_ref[...])
        g = dot(g_ref[span, :], down_ref[...], NT)
        big, small = gelu_parts(u)
        a = (u * big).astype(jnp.bfloat16)
        d = (g * (big + u * small)).astype(jnp.bfloat16)
        act[span, :] = a
        du[span, :] = d
        acc[span, :] += dot(a, down_ref[...])
        dh_ref[span, :] += dot(d, up_ref[...], NT)

    after(1, second_go)
    slot = lax.rem(j, 2)
    each = rows // (nz * ny * nx * nc)

    @pl.loop(0, nz)
    def _(a):
        n = ny * nx * nc * each
        part = dot(h_t[pl.ds(pl.multiple_of(a * n, n), n), :], du[...]).astype(made.dtype)
        made[slot, a] = part.reshape(ny, nx, nc, each, chunk)

    after(0, core_go)
    after(1, third_go)
    ddown_ref[...] = lax.dot_general(act[...], g_ref[...], (((0,), (0,)), ((), ())), preferred_element_type=jnp.float32).astype(ddown_ref.dtype)
    after(1, finish)

    @pl.when(j >= sent)
    def _():
        pltpu.make_async_copy(made.at[slot], rest_ref.at[j - sent], local_sem.at[j]).start()

    @pl.when(j == steps - 1)
    def _():
        out_ref[...] = acc[...].astype(out_ref.dtype)
        for i in range(sent, 4):
            drain(rest_ref.at[i - sent], local_sem.at[i])


def ffn(dims, h, g, x, w_up, w_down, cid, sent=3, steps=4):
    nz, ny, nx, nc = dims
    rows, width = h.shape
    inner = w_up.shape[1]
    chunk = inner // steps
    each = width // (nz * ny * nx * nc)
    bf, f32 = jnp.bfloat16, jnp.float32
    fixed = lambda j: (0, 0)
    whole = pl.BlockSpec((rows, width), fixed)
    once = pl.BlockSpec((rows, width), fixed, pipeline_mode=pl.Buffered(1))
    tile = (each, chunk)
    out, dh, ddown, grad, rest = pl.pallas_call(
        functools.partial(ffn_kernel, dims, sent),
        grid=(steps,),
        out_shape=[
            jax.ShapeDtypeStruct((rows, width), bf),
            jax.ShapeDtypeStruct((rows, width), f32),
            jax.ShapeDtypeStruct((inner, width), bf),
            jax.ShapeDtypeStruct((sent, each, chunk), f32),
            jax.ShapeDtypeStruct((steps - sent, nz, ny, nx, nc, each, chunk), bf),
        ],
        in_specs=[once, once, once, pl.BlockSpec((width, chunk), lambda j: (0, j)), pl.BlockSpec((chunk, width), lambda j: (j, 0))],
        out_specs=[once, once, pl.BlockSpec((chunk, width), lambda j: (j, 0)),
                   pl.BlockSpec((sent, each, chunk), lambda j: (0, 0, 0)), pl.BlockSpec(memory_space=ANY)],
        scratch_shapes=[
            pltpu.VMEM((width, rows), bf), pltpu.VMEM((rows, width), f32), pltpu.VMEM((rows, chunk), bf), pltpu.VMEM((rows, chunk), bf),
            pltpu.VMEM((2, nz, ny, nx, nc) + tile, bf),
            pltpu.VMEM((sent, nz, ny, nx) + tile, bf), pltpu.VMEM((sent, nz, ny, nx) + tile, bf),
            pltpu.VMEM((sent, nz, nx, each, chunk // 2), bf), pltpu.VMEM((sent, nz, ny, each, chunk // 2), bf),
            pltpu.VMEM((sent, nz) + tile, bf), pltpu.VMEM((sent, nz - 1) + tile, bf),
            pltpu.SemaphoreType.DMA((steps,)), pltpu.SemaphoreType.DMA((sent, 2)), pltpu.SemaphoreType.DMA((sent, 6)),
        ],
        compiler_params=pltpu.CompilerParams(collective_id=cid, has_side_effects=True, vmem_limit_bytes=62 * 2**20, dimension_semantics=("arbitrary",)),
        name="feed_forward",
    )(h, g, x, w_up, w_down)
    grad = jnp.moveaxis(grad, 0, 1).reshape(each, sent * chunk)
    rest = jnp.moveaxis(rest, 0, 5).reshape(width, (steps - sent) * chunk)
    return out, dh, ddown, grad, rest
class Gather:
    def __init__(self, dims, units, ins, outs, send, recv):
        self.at, self.nz = Place(dims), dims[0]
        self.units, self.ins, self.outs, self.send, self.recv = units, ins, outs, send, recv

    def part(self, u, where, core=None):
        a, r0, nr, c0, ncol, _ = self.units[u]
        return self.outs[a].at[(*where, self.at.c if core is None else core, pl.ds(r0, nr), pl.ds(c0, ncol))]

    def held(self, u, k):
        where = [self.at.z, self.at.y, self.at.x]
        for axis in self.units[u][5][:k]:
            where[axis] = slice(None)
        return where

    def coming(self, u, k):
        where = self.held(u, k)
        axis = self.units[u][5][k]
        where[axis] = (slice(0, self.nz - 1), 1 - self.at.y, 1 - self.at.x)[axis]
        return where

    def to_core(self, u, where):
        block = self.part(u, where)
        push(block, block, self.send.at[u], self.recv.at[u, 3], self.at.dev(c=1 - self.at.c))

    def pass_on(self, u, k):
        axis = self.units[u][5][k]
        if axis == 0 and k == 0:
            self.to_core(u, self.held(u, 1))
        elif axis == 0:
            for z in self.at.z_others():
                where = self.held(u, k)
                where[0] = z
                self.to_core(u, where)
        else:
            self.to_core(u, self.coming(u, k))
            if k == 0:
                self.to_core(u, self.held(u, 0))

    def go(self, u, k):
        at = self.at
        if k > 0:
            drain(self.part(u, self.coming(u, k - 1)), self.recv.at[u, k - 1])
        if k < 3:
            a, r0, nr, c0, ncol, order = self.units[u]
            dst = self.part(u, self.held(u, k))
            src = self.ins[a].at[pl.ds(r0, nr), pl.ds(c0, ncol)] if k == 0 else dst
            targets = ([at.dev(z=z) for z in at.z_others()], [at.dev(y=1 - at.y)], [at.dev(x=1 - at.x)])[order[k]]
            for device in targets:
                push(src, dst, self.send.at[u], self.recv.at[u, k], device)
        if k > 0:
            self.pass_on(u, k - 1)

    def arrived(self, u):
        drain(self.part(u, [slice(None)] * 3, 1 - self.at.c), self.recv.at[u, 3])

    def sent(self, u):
        for k in range(3):
            where = self.held(u, k)
            if self.units[u][5][k] == 0:
                where[0] = slice(0, self.nz - 1)
            drain(self.part(u, where), self.send.at[u])
        drain(self.part(u, [slice(None)] * 3), self.send.at[u])


def norm_parts(values_in):
    center = values_in - jnp.mean(values_in, axis=-1, keepdims=True)
    return center * lax.rsqrt(jnp.mean(center * center, axis=-1, keepdims=True) + EPS)


FW_PATHS = ((0, 2, 1), (2, 0, 1), (0, 1, 2), (2, 0, 1), (0, 1, 2), (2, 0, 1), (0, 1, 2), (0, 1, 2), (0, 1, 2), (2, 0, 1), (0, 1, 2), (0, 2, 1), (0, 1, 2), (2, 0, 1), (2, 1, 0), (0, 1, 2))
FW_UNITS = [(0, 0, 16, 0, 128, (0, 2, 1))] + [(a, 0, 32, 0, 1024, FW_PATHS[a - 1]) for a in range(1, 9)]
FW_UNITS += [(9, 0, 32, 1024 * j, 1024, FW_PATHS[8 + j]) for j in range(4)]
FW_UNITS += [(10, 32 * j, 32, 0, 1024, FW_PATHS[12 + j]) for j in range(4)]
FW_ORDER = (
    (0, 0), (2, 0), (4, 0), (5, 0), (11, 0), (6, 0), (1, 0), (5, 1), (3, 0), (11, 1), (0, 1), (16, 0), (5, 2),
    (1, 1), (0, 2), (8, 0), (11, 2), (3, 1), (7, 0), (2, 1), (0, 3), (10, 0), (4, 1), (14, 0), (6, 1), (15, 0),
    (16, 1), (-2, 0), (9, 0), (3, 2), (8, 1), (12, 0), (16, 2), (5, 3), (7, 1), (13, 0), (5, 4), (8, 2), (1, 2),
    (7, 2), (2, 2), (11, 3), (10, 1), (14, 1), (15, 1), (1, 3), (4, 2), (1, 4), (-2, 1), (3, 3), (2, 3), (6, 2),
    (3, 4), (15, 2), (2, 4), (-2, 2), (9, 1), (-2, 3), (16, 3), (-2, 4), (12, 1), (4, 3), (13, 1), (-2, 5), (4, 4),
    (8, 3), (-2, 6), (6, 3), (8, 4), (10, 2), (9, 2), (6, 4), (-2, 7), (7, 3), (13, 2), (-2, 8), (7, 4), (12, 2),
    (-1, 0), (14, 2), (-2, 9), (10, 3), (-2, 10), (9, 3), (-2, 11), (-2, 12), (12, 3), (13, 3), (-2, 13), (15, 3),
    (-2, 14), (14, 3),
)


def forward_kernel(dims, n, *refs):
    shards, refs = refs[:n], refs[n:]
    block_in, out_grad, text_states, limits = refs[:4]
    full, refs = refs[4 : 4 + n], refs[4 + n :]
    g_out, x_out, q_out, k_out, v_out, cq_out, ck_out, cv_out, o_out, o2_out, h1_out, h2_out, h3_out, x1_out, x2_out, lse_out, lse2_out, vec = refs[:18]
    x_in, q, k, v, cq, ck, cv, o, o2, h1, h2, h3, x1, x2, lse, lse2, text, small = refs[18:36]
    w = refs[36:44]
    limit, local_sem, out_sem, send, recv, ex_send, ex_recv = refs[44:]
    at = Place(dims)
    oy, ox, oc, me = 1 - at.y, 1 - at.x, 1 - at.c, at.seq
    hello([at.dev(z=p) for p in at.z_others()] + [at.dev(y=oy), at.dev(x=ox), at.dev(c=oc), at.dev(x=ox, c=oc)])
    net = Gather(dims, FW_UNITS, shards, full, send, recv)
    rows, width = q.shape
    block = 256
    f32, bf = jnp.float32, jnp.bfloat16
    others = ((ox, at.c), (ox, oc), (at.x, oc))

    def exchange(src, dst, i):
        for px, pc in others:
            push(src.at[px * 2 + pc], dst.at[me], ex_send.at[i], ex_recv.at[i], at.dev(x=px, c=pc))
        pltpu.make_async_copy(src.at[me], dst.at[me], local_sem.at[n + i]).start()

    def exchanged(dst, i):
        drain(dst.at[0:3], ex_recv.at[i])
        drain(dst.at[0], local_sem.at[n + i])

    keep = []

    def put(src, dst):
        pltpu.make_async_copy(src, dst, out_sem.at[len(keep)]).start()
        keep.append(src)

    loads = 4 + n

    def load(a):
        net.arrived(a)
        pltpu.make_async_copy(full[a], w[a - 1], local_sem.at[loads + a]).start()

    def loaded(a):
        drain(w[a - 1], local_sem.at[loads + a])

    def weight(a):
        return w[a - 1][...].reshape(width, width)

    def span_of(r):
        return pl.ds(pl.multiple_of(r * block, block), block)

    def first_norm():
        net.arrived(0)
        pltpu.make_async_copy(full[0], small, local_sem.at[n + 3]).start()
        drain(small, local_sem.at[n + 3])
        packed = small[...].reshape(-1, 16, 128).astype(f32)
        devices = packed.shape[0]
        piece = width // devices
        lane = lax.rem(lax.broadcasted_iota(jnp.int32, (128, width), 1), piece)
        spread = jnp.where(lane == lax.broadcasted_iota(jnp.int32, (128, width), 0), 1.0, 0.0).astype(bf)
        owner = lax.div(lax.broadcasted_iota(jnp.int32, (devices, width), 1), piece)
        mine = owner == lax.broadcasted_iota(jnp.int32, (devices, width), 0)
        vec[...] = jnp.zeros_like(vec)
        for i in range(6):
            vec[i : i + 1, :] = row_sum(jnp.where(mine, dot(packed[:, i, :].astype(bf), spread), 0.0))
        exchanged(x_in, 0)
        put(x_in, x_out)

        @pl.loop(0, 4)
        def _(r):
            x = x_in[r].astype(f32)
            x1[span_of(r), :] = x
            h1[span_of(r), :] = (norm_parts(x) * vec[0:1, :] + vec[1:2, :]).astype(bf)

        put(h1, h1_out)

    def project(a, dst, scale, kept):
        loaded(a)

        @pl.loop(0, rows // block)
        def _(r):
            made = dot(h1[span_of(r), :], weight(a))
            dst[span_of(r), :] = (made if scale is None else made * scale).astype(bf)

        put(dst, kept)

    def pairs(first, last, causal, qs, ks, vs, os, ls):
        @pl.loop(first, last)
        def _(j):
            cols = pl.ds(pl.multiple_of(j * 128, 128), 128)
            attend_kernel(causal, 512, limit, qs.at[:, cols], ks.at[:, cols], vs.at[:, cols], os.at[:, cols], ls.at[pl.ds(j, 1)])

    count = width // 128

    def self_attention(i):
        pairs(i * count // 4, (i + 1) * count // 4, True, q, k, v, o, lse)
        if i == 3:
            put(o, o_out)
            put(lse, lse_out)

    def second_norm(i):
        if i == 0:
            loaded(4)
            loaded(5)

        @pl.loop(2 * i, 2 * i + 2)
        def _(r):
            x = x1[span_of(r), :] + dot(o[span_of(r), :], weight(4))
            x1[span_of(r), :] = x
            h = (norm_parts(x) * vec[2:3, :] + vec[3:4, :]).astype(bf)
            h2[span_of(r), :] = h
            cq[span_of(r), :] = (dot(h, weight(5)) * (LOG2E / 8)).astype(bf)

        if i == 1:
            put(x1, x1_out)
            put(h2, h2_out)
            put(cq, cq_out)

    def text_rows():
        loaded(6)
        loaded(7)
        ck[...] = dot(text[...], weight(6)).astype(bf)
        cv[...] = dot(text[...], weight(7)).astype(bf)
        put(ck, ck_out)
        put(cv, cv_out)

    def cross_attention(i):
        pairs(i * count // 2, (i + 1) * count // 2, False, cq, ck, cv, o2, lse2)
        if i == 1:
            put(o2, o2_out)
            put(lse2, lse2_out)

    def third_norm(i):
        if i == 0:
            loaded(8)

        @pl.loop(2 * i, 2 * i + 2)
        def _(r):
            x = x1[span_of(r), :] + dot(o2[span_of(r), :], weight(8))
            x2[span_of(r), :] = x
            h3[span_of(r), :] = (norm_parts(x) * vec[4:5, :] + vec[5:6, :]).astype(bf)

        if i == 1:
            put(x2, x2_out)
            put(h3, h3_out)

    pieces = [first_norm, lambda: project(1, q, LOG2E / 8, q_out), lambda: project(2, k, None, k_out), lambda: project(3, v, None, v_out)]
    pieces += [functools.partial(self_attention, i) for i in range(4)] + [functools.partial(second_norm, i) for i in range(2)] + [text_rows]
    pieces += [functools.partial(cross_attention, i) for i in range(2)] + [functools.partial(third_norm, i) for i in range(2)]

    for a in range(n):
        pltpu.make_async_copy(shards[a], full[a].at[at.z, at.y, at.x, at.c], local_sem.at[a]).start()
    exchange(block_in, x_in, 0)
    pltpu.make_async_copy(text_states.at[me], text, local_sem.at[n + 2]).start()
    limit[0] = limits[me]
    placed = False
    for u, step in FW_ORDER:
        if step > 0 and not placed:
            placed = True
            for a in range(n):
                drain(shards[a], local_sem.at[a])
            drain(text, local_sem.at[n + 2])
        if u == -1:
            exchange(out_grad, g_out, 1)
        elif u == -2:
            pieces[step]()
        elif step == 4:
            load(u)
        else:
            net.go(u, step)
    exchanged(g_out, 1)
    for u in range(9, len(FW_UNITS)):
        net.arrived(u)
    for u in range(len(FW_UNITS)):
        net.sent(u)
    drain(x_in.at[0:3], ex_send.at[0])
    drain(g_out.at[0:3], ex_send.at[1])
    for i, src in enumerate(keep):
        drain(src, out_sem.at[i])


def forward(dims, shards, block_in, out_grad, text_states, limits, cid):
    n = len(shards)
    bf, f32 = jnp.bfloat16, jnp.float32
    items, seg, width = block_in.shape
    rows, texts = items * seg, text_states.shape[1]
    wide, pairs = jax.ShapeDtypeStruct((rows, width), bf), width // 128
    short = jax.ShapeDtypeStruct((texts, width), bf)
    long = jax.ShapeDtypeStruct((rows, width), f32)
    sums = jax.ShapeDtypeStruct((pairs, 8, rows), f32)
    seg4 = jax.ShapeDtypeStruct(block_in.shape, bf)
    whole = [jax.ShapeDtypeStruct(tuple(dims) + s.shape, s.dtype) for s in shards]
    saved = [wide, wide, wide, wide, short, short, wide, wide, wide, wide, wide, long, long, sums, sums]
    out_shape = whole + [seg4, seg4] + saved + [jax.ShapeDtypeStruct((8, width), f32)]
    held = [pltpu.VMEM(s.shape, s.dtype) for s in [seg4] + saved + [short]] + [pltpu.VMEM(tuple(dims) + (16, 128), bf)]
    held += [pltpu.VMEM(s.shape, s.dtype) for s in whole[1:9]]
    units = len(FW_UNITS)
    any_spec = pl.BlockSpec(memory_space=ANY)
    outs = pl.pallas_call(
        functools.partial(forward_kernel, dims, n),
        out_shape=out_shape,
        in_specs=[any_spec] * (n + 3) + [pl.BlockSpec(memory_space=pltpu.SMEM)],
        out_specs=[any_spec] * (len(out_shape) - 1) + [pl.BlockSpec(memory_space=pltpu.VMEM)],
        scratch_shapes=held
        + [
            pltpu.SMEM((1,), jnp.int32),
            pltpu.SemaphoreType.DMA((2 * n + 8,)), pltpu.SemaphoreType.DMA((20,)),
            pltpu.SemaphoreType.DMA((units,)), pltpu.SemaphoreType.DMA((units, 4)),
            pltpu.SemaphoreType.DMA((2,)), pltpu.SemaphoreType.DMA((2,)),
        ],
        compiler_params=pltpu.CompilerParams(collective_id=cid, has_side_effects=True, vmem_limit_bytes=62 * 2**20),
        name="forward",
    )(*shards, block_in, out_grad, text_states, limits)
    full = [o.reshape((-1,) + o.shape[5:]) for o in outs[:n]]
    return full, outs[n:]
def run_order(order, event, pieces):
    i = 0
    while i < len(order):
        unit, step = order[i]
        i += 1
        if unit != -2:
            event(unit, step)
            continue
        piece = pieces[step]
        if callable(piece):
            piece()
            continue
        body, first = piece
        last, between = first, {first: []}
        while i < len(order):
            unit, step = order[i]
            if unit != -2:
                between[last].append((unit, step))
            else:
                piece = pieces[step]
                if callable(piece) or piece[0] is not body:
                    break
                last = piece[1]
                between[last] = []
            i += 1

        def one(j, body=body, between=between):
            body(j)
            for k, events in between.items():
                if events:
                    pl.when(j == k)(functools.partial(run_order, events, event, pieces))

        pl.loop(first, last + 1)(one)


class Scatter:
    def __init__(self, dims, send, recv, local):
        self.at, self.dims, self.send, self.recv, self.local, self.units = Place(dims), dims, send, recv, local, []

    def add(self, source, room, out, order, whole):
        self.units.append((source, room[0], room[1:], out, order, whole))

    def own(self, u, where):
        own, whole = self.units[u][1], self.units[u][5]
        return own.at[(*where, self.at.c)] if whole else own.at[tuple(where)]

    def left(self, u, k):
        where = [slice(None)] * 3
        for axis in self.units[u][4][:k]:
            where[axis] = (self.at.z, self.at.y, self.at.x)[axis]
        return where

    def add_in(self, u, k, bufs):
        where = self.left(u, k)
        open_axes = [axis for axis in range(3) if axis not in self.units[u][4][:k]]

        def one(index):
            spot = list(where)
            for axis, i in zip(open_axes, index):
                spot[axis] = i
            dst = self.own(u, spot)
            if len(bufs) == 1:
                dst[...] = dst[...] + bufs[0][tuple(index)]
            else:
                total = dst[...].astype(jnp.float32)
                for buf in bufs:
                    total = total + buf[tuple(index)].astype(jnp.float32)
                dst[...] = total.astype(dst.dtype)

        sizes = [self.dims[axis] for axis in open_axes]
        inner = list(itertools.product(*[range(n) for n in sizes[1:]]))

        @pl.loop(0, sizes[0])
        def _(i):
            for rest in inner:
                one((i, *rest))

    def bufs(self, u, k):
        buf = self.units[u][2][k]
        return [buf.at[i] for i in range(self.dims[0] - 1)] if self.units[u][4][k - 1] == 0 else [buf]

    def go(self, u, k):
        source, own, room, out, order, whole = self.units[u]
        at, every = self.at, slice(None)
        if k == 0:
            if not whole:
                pltpu.make_async_copy(source(every, every, every, at.c), own, self.local.at[u]).start()
            push(source(every, every, every, 1 - at.c), room[0], self.send.at[u], self.recv.at[u, 0], at.dev(c=1 - at.c))
            return
        drain(room[k - 1], self.recv.at[u, k - 1])
        if k == 4:
            total = self.own(u, (at.z, at.y, at.x))[...].astype(jnp.float32)
            for buf in self.bufs(u, 3):
                total = total + buf[...].astype(jnp.float32)
            out[...] = total
            for block in room:
                drain(block, self.send.at[u])
            return
        if k == 1:
            if not whole:
                drain(own, self.local.at[u])
            self.add_in(u, 0, [room[0]])
        else:
            self.add_in(u, k - 1, self.bufs(u, k - 1))
        where = self.left(u, k - 1)
        axis = order[k - 1]
        if axis == 0:
            for i in range(1, self.dims[0]):
                where[0] = lax.rem(at.z + i, self.dims[0])
                push(self.own(u, where), room[k].at[i - 1], self.send.at[u], self.recv.at[u, k], at.dev(z=where[0]))
        else:
            where[axis] = (None, 1 - at.y, 1 - at.x)[axis]
            device = at.dev(y=1 - at.y) if axis == 1 else at.dev(x=1 - at.x)
            push(self.own(u, where), room[k], self.send.at[u], self.recv.at[u, k], device)


def scatter_room(dims, tile, dtype, order, whole):
    nz, ny, nx, nc = dims
    rooms = [((nz, ny, nx, nc) if whole else (nz, ny, nx)) + tile, (nz, ny, nx) + tile]
    for k in range(3):
        lead = tuple(dims[axis] for axis in range(3) if axis not in order[: k + 1])
        rooms.append(((nz - 1,) if order[k] == 0 else ()) + lead + tile)
    return [pltpu.VMEM(shape, dtype) for shape in rooms]


def norm_back(x, dh, gain):
    center = x - jnp.mean(x, axis=-1, keepdims=True)
    r = lax.rsqrt(jnp.mean(center * center, axis=-1, keepdims=True) + EPS)
    n = center * r
    dn = dh * gain
    dx = r * (dn - jnp.mean(dn, axis=-1, keepdims=True) - n * jnp.mean(dn * n, axis=-1, keepdims=True))
    return dx, dh * n


def row_sum(rows):
    return jnp.sum(rows, axis=0, keepdims=True)


TN = (((0,), (0,)), ((), ()))


MIDDLE_PATHS = (
    (0, 2, 1), (1, 0, 2), (1, 0, 2), (1, 2, 0), (2, 1, 0), (2, 1, 0),
)
MIDDLE_ORDER = (
    (0, 0), (1, 0), (2, 0), (3, 0), (4, 0), (-2, 0), (0, 1), (1, 1), (-2, 1), (2, 1), (3, 1), (4, 1), (-2, 2),
    (5, 0), (-2, 3), (-2, 4), (5, 1), (-2, 5), (1, 2), (-2, 6), (-2, 7), (-2, 8), (-2, 9), (-2, 10), (-2, 11),
    (0, 2), (2, 2), (4, 2), (-2, 12), (-2, 13), (1, 3), (3, 2), (5, 2), (-2, 14), (4, 3), (0, 3), (1, 4), (-2, 15),
    (2, 3), (5, 3), (3, 3), (0, 4), (4, 4), (5, 4), (2, 4), (3, 4),
)
LAST_SPLIT = 640
LAST_PATHS = (
    (0, 2, 1), (1, 0, 2), (2, 0, 1), (2, 1, 0), (1, 2, 0), (2, 1, 0), (2, 1, 0), (0, 1, 2), (1, 0, 2), (1, 0, 2),
    (0, 1, 2),
)
LAST_ORDER = (
    (0, 0), (1, 0), (2, 0), (3, 0), (-2, 0), (0, 1), (-2, 1), (1, 1), (2, 1), (3, 1), (-2, 2), (-2, 3), (-2, 4),
    (-2, 5), (1, 2), (2, 2), (-2, 6), (4, 0), (5, 0), (6, 0), (0, 2), (-2, 7), (3, 2), (4, 1), (5, 1), (6, 1),
    (0, 3), (-2, 8), (1, 3), (-2, 9), (3, 3), (-2, 10), (7, 0), (8, 0), (9, 0), (5, 2), (2, 3), (-2, 11), (4, 2),
    (7, 1), (8, 1), (0, 4), (9, 1), (6, 2), (1, 4), (-2, 12), (3, 4), (5, 3), (2, 4), (-2, 13), (-2, 14), (8, 2),
    (-2, 15), (10, 0), (7, 2), (9, 2), (10, 1), (5, 4), (6, 3), (4, 3), (7, 3), (8, 3), (9, 3), (10, 2), (10, 3),
    (6, 4), (7, 4), (8, 4), (9, 4), (10, 4), (4, 4),
)


def middle_kernel(dims, *refs):
    (g_in, dh_in, x2_in, x1_in, vec, o2_in, cq_in, ck_in, cv_in, lse_in, h2_in, o_in, wco_in, wcq_in, wck_in, wcv_in, wo_in,
     text_in, limits, block_in, down_in, up_in) = refs[:22]
    block_out, text_out, dx_out, do_out, gcq_out, gck_out, gcv_out, go_out, sums, down_out, up_out, co_out = refs[22:34]
    (x2, dh3, dx, g, dy, do, o2, wco, cq, dcq, wcq, wck, wcv, ck, cv, dck, dcv, lse, text, tg, stage, dk_acc, dv_acc, limit,
     load_sem, out_sem, ex_send, ex_recv, send, recv, local) = refs[34:65]
    rooms = refs[65:]
    at = Place(dims)
    nz = dims[0]
    oy, ox, oc, me = 1 - at.y, 1 - at.x, 1 - at.c, at.seq
    hello([at.dev(z=p) for p in at.z_others()] + [at.dev(y=oy), at.dev(x=ox), at.dev(c=oc), at.dev(x=ox, c=oc)])
    others = ((ox, at.c), (ox, oc), (at.x, oc))
    rows, width = g.shape
    block = 256
    f32, bf = jnp.float32, jnp.bfloat16
    every = slice(None)
    net = Scatter(dims, send, recv, local)
    quarter = width // 4
    room = [rooms[5 * j : 5 * j + 5] for j in range(6)]
    for j in range(4):
        cols = pl.ds(j * quarter, quarter)
        net.add(lambda *w, cols=cols: down_in.at[(*w, every, cols)], room[j], down_out.at[:, cols], MIDDLE_PATHS[j], False)
    net.add(lambda *w: up_in.at[w], room[4], up_out, MIDDLE_PATHS[4], False)
    net.add(lambda *w: room[5][0].at[w], room[5], co_out, MIDDLE_PATHS[5], True)

    def exchange(src, dst, i):
        for px, pc in others:
            push(src.at[px * 2 + pc], dst.at[me], ex_send.at[i], ex_recv.at[i], at.dev(x=px, c=pc))
        pltpu.make_async_copy(src.at[me], dst.at[me], local.at[6 + i]).start()

    started = []

    def load(src, dst):
        pltpu.make_async_copy(src, dst, load_sem.at[len(started)]).start()
        started.append(dst)
        return len(started) - 1

    def loaded(i):
        drain(started[i], load_sem.at[i])

    kept = []

    def put(src, dst):
        pltpu.make_async_copy(src, dst, out_sem.at[len(kept)]).start()
        kept.append(src)
        return len(kept) - 1

    def kept_done(i):
        drain(kept[i], out_sem.at[i])

    def span_of(r):
        return pl.ds(pl.multiple_of(r * block, block), block)

    def weight_grad(src, grad, made):
        @pl.loop(0, nz)
        def _(a):
            part = dot(src[:, pl.ds(pl.multiple_of(a * block, block), block)], grad[...], TN).astype(bf)
            made[a] = part.reshape(made.shape[1:])

    first = [load(dh_in, dh3), load(x2_in, x2), load(g_in, g), load(wco_in, wco), load(o2_in, o2)]
    second = [load(cq_in, cq), load(ck_in, ck), load(cv_in, cv), load(lse_in, lse)]
    third = [load(text_in.at[me], text), load(wcq_in, wcq), load(wck_in, wck), load(wcv_in, wcv)]
    limit[0] = limits[me]
    run_order(MIDDLE_ORDER[:5], net.go, [])
    exchange(block_in, block_out, 0)
    for i in first:
        loaded(i)
    sums[...] = jnp.zeros_like(sums)

    def last_norm(r):
        span = span_of(r)
        d = dh3[span, :]
        grad, gain_terms = norm_back(x2[span, :], d, vec[4:5, :])
        sums[4:5, :] += row_sum(gain_terms)
        sums[5:6, :] += row_sum(d)
        total = g[span, :].astype(f32) + grad
        dx[span, :] = total
        low = total.astype(bf)
        dy[span, :] = low
        do[span, :] = dot(low, wco[...], NT).astype(bf)

    def middle_norm(r):
        span = span_of(r)
        d = dot(dcq[span, :], wcq[...], NT)
        grad, gain_terms = norm_back(x2[span, :], d, vec[2:3, :])
        sums[2:3, :] += row_sum(gain_terms)
        sums[3:4, :] += row_sum(d)
        total = dx[span, :] + grad
        dx[span, :] = total
        low = total.astype(bf)
        dy[span, :] = low
        do[span, :] = dot(low, cq[...], NT).astype(bf)

    later = {}

    def after_last_norm():
        pl.loop(2, 4)(last_norm)
        later["x1"], later["o"], later["h2"] = load(x1_in, x2), load(o_in, g), load(h2_in, wco)

    def output_weight_grad():
        weight_grad(o2, dy, room[5][0])
        for i in second:
            loaded(i)

    def cross(j):
        cols = pl.ds(pl.multiple_of(j * 128, 128), 128)
        attend_back_kernel(
            False, 512, limit, cq.at[:, cols], ck.at[:, cols], cv.at[:, cols], do.at[:, cols], o2.at[:, cols], lse.at[pl.ds(j, 1)],
            dcq.at[:, cols], dck.at[:, cols], dcv.at[:, cols], dk_acc, dv_acc,
        )

    def query_weight_grad():
        later["wo"] = load(wo_in, cq)
        for i in third:
            loaded(i)
        loaded(later["h2"])
        weight_grad(wco, dcq, stage.at[0])
        later["cq"] = put(stage.at[0], gcq_out)
        loaded(later["x1"])
        loaded(later["wo"])

    def after_middle_norm():
        pl.loop(2, 4)(middle_norm)
        put(dx, dx_out)
        put(do, do_out)

    def self_weight_grad():
        loaded(later["o"])
        weight_grad(g, dy, stage.at[1])
        later["o"] = put(stage.at[1], go_out)

    def text_weight_grads():
        tg[...] = (dot(dck[...], wck[...], NT) + dot(dcv[...], wcv[...], NT)).reshape(tg.shape)
        exchange(tg, text_out, 1)
        kept_done(later["cq"])
        weight_grad(text, dck, stage.at[0])
        put(stage.at[0], gck_out)
        kept_done(later["o"])
        weight_grad(text, dcv, stage.at[1])
        put(stage.at[1], gcv_out)

    pieces = [lambda: pl.loop(0, 2)(last_norm), after_last_norm, output_weight_grad]
    pieces += [(cross, j) for j in range(width // 128)]
    pieces += [query_weight_grad, lambda: pl.loop(0, 2)(middle_norm), after_middle_norm, self_weight_grad, text_weight_grads]
    run_order(MIDDLE_ORDER[5:], net.go, pieces)
    for i, dst in ((0, block_out), (1, text_out)):
        drain(dst.at[0:3], ex_recv.at[i])
        drain(dst.at[0:3], ex_send.at[i])
        drain(dst.at[0], local.at[6 + i])
    for i in range(len(kept)):
        if i not in (later["cq"], later["o"]):
            kept_done(i)


def middle(dims, args, cid):
    nz, ny, nx, nc = dims
    g, dh, x2, x1, vec, o2, cq, ck, cv, lse, h2, o, wco, wcq, wck, wcv, wo, text, limits, block_out, down, up = args
    rows, width = g.shape
    texts = text.shape[1]
    devices = nz * ny * nx * nc
    bf, f32 = jnp.bfloat16, jnp.float32
    each = width // devices
    long = down.shape[0] // devices
    down = down.reshape(nz, ny, nx, nc, long, width)
    up = up.reshape(nz, ny, nx, nc, each, up.shape[1])
    seg = block_out.shape
    held = jax.ShapeDtypeStruct((nz, ny, nx, nc, each, width), bf)
    wide, deep = jax.ShapeDtypeStruct((rows, width), bf), jax.ShapeDtypeStruct((rows, width), f32)
    out_shape = [
        jax.ShapeDtypeStruct(seg, bf), jax.ShapeDtypeStruct((seg[0], texts // seg[0], width), f32), deep, wide, held, held, held, held,
        jax.ShapeDtypeStruct((8, width), f32), jax.ShapeDtypeStruct((long, width), f32), jax.ShapeDtypeStruct((each, up.shape[5]), f32),
        jax.ShapeDtypeStruct((each, width), f32),
    ]
    any_spec, vm = pl.BlockSpec(memory_space=ANY), pl.BlockSpec(memory_space=pltpu.VMEM)
    big, square, short = pltpu.VMEM((rows, width), f32), pltpu.VMEM((rows, width), bf), pltpu.VMEM((texts, width), bf)
    dma = pltpu.SemaphoreType.DMA
    scratch = [big, big, big] + [square] * 10 + [short] * 4 + [pltpu.VMEM(lse.shape, f32), short]
    scratch += [pltpu.VMEM((seg[0], texts // seg[0], width), f32), pltpu.VMEM((2,) + held.shape, bf)]
    scratch += [pltpu.VMEM((texts, 128), f32)] * 2 + [pltpu.SMEM((1,), jnp.int32)]
    scratch += [dma((20,)), dma((12,)), dma((2,)), dma((2,)), dma((6,)), dma((6, 4)), dma((8,))]
    for j in range(4):
        scratch += scatter_room(dims, (long, width // 4), bf, MIDDLE_PATHS[j], False)
    scratch += scatter_room(dims, (each, up.shape[5]), bf, MIDDLE_PATHS[4], False)
    scratch += scatter_room(dims, (each, width), bf, MIDDLE_PATHS[5], True)
    specs = [any_spec] * 4 + [vm] + [any_spec] * 13 + [pl.BlockSpec(memory_space=pltpu.SMEM)] + [any_spec] * 3
    return pl.pallas_call(
        functools.partial(middle_kernel, dims),
        out_shape=out_shape,
        in_specs=specs,
        out_specs=[any_spec] * 8 + [vm] * 4,
        scratch_shapes=scratch,
        compiler_params=pltpu.CompilerParams(collective_id=cid, has_side_effects=True, vmem_limit_bytes=63 * 2**20),
        name="middle",
    )(g, dh, x2, x1, vec, o2, cq, ck, cv, lse, h2, o, wco, wcq, wck, wcv, wo, text, limits, block_out, down, up)


def last_kernel(dims, *refs):
    q_in, k_in, v_in, do_in, o_in, lse_in, h1_in, wq_in, wk_in, wv_in, x_in, dx_in, vec, gcq, gck, gcv, go, sums_in = refs[:18]
    grad_out, cq_out, ck_out, cv_out, o_out, q_out, k_out, v_out, small_out = refs[18:27]
    (q, k, v, do, o, lse, h_t, dq, dk, dv, dx, send_rows, small, dk_acc, dv_acc, sums,
     load_sem, ex_send, ex_recv, send, recv, local) = refs[27:49]
    rooms = refs[49:]
    at = Place(dims)
    nz, ny, nx, nc = dims
    oy, ox, oc, me = 1 - at.y, 1 - at.x, 1 - at.c, at.seq
    hello([at.dev(z=p) for p in at.z_others()] + [at.dev(y=oy), at.dev(x=ox), at.dev(c=oc), at.dev(x=ox, c=oc)])
    rows, width = q.shape
    block = 256
    f32, bf = jnp.float32, jnp.bfloat16
    every = slice(None)
    net = Scatter(dims, send, recv, local)
    room = [rooms[5 * j : 5 * j + 5] for j in range(10)] + [[small, *rooms[50:54]]]
    for j, (src, out) in enumerate(((gcq, cq_out), (gck, ck_out), (gcv, cv_out), (go, o_out))):
        net.add(lambda *w, src=src: src.at[w], room[j], out, LAST_PATHS[j], False)
    parts = ((0, LAST_SPLIT), (LAST_SPLIT, width - LAST_SPLIT))
    for j in range(6):
        out = (q_out, k_out, v_out)[j % 3].at[:, pl.ds(*parts[j // 3])]
        net.add(lambda *w, held=room[4 + j][0]: held.at[w], room[4 + j], out, LAST_PATHS[4 + j], True)
    net.add(lambda *w: small.at[w], room[10], small_out, LAST_PATHS[10], True)
    run_order(LAST_ORDER[:4], net.go, [])
    started = []

    def load(src, dst):
        pltpu.make_async_copy(src, dst, load_sem.at[len(started)]).start()
        started.append(dst)
        return len(started) - 1

    def loaded(i):
        drain(started[i], load_sem.at[i])

    first = [load(a, b) for a, b in ((q_in, q), (k_in, k), (v_in, v), (do_in, do), (o_in, o), (lse_in, lse), (h1_in, dq), (dx_in, dx))]

    def transpose():
        for i in first:
            loaded(i)

        @pl.loop(0, rows // block)
        def _(r):
            span = pl.ds(pl.multiple_of(r * block, block), block)
            h_t[:, span] = dq[span, :].T

    def pair(j):
        cols = pl.ds(pl.multiple_of(j * 128, 128), 128)
        attend_back_kernel(
            True, 256, None, q.at[:, cols], k.at[:, cols], v.at[:, cols], do.at[:, cols], o.at[:, cols], lse.at[pl.ds(j, 1)],
            dq.at[:, cols], dk.at[:, cols], dv.at[:, cols], dk_acc, dv_acc,
        )

    weights = []

    def weight_grads(part):
        if part == 1:
            weights.extend(load(a, b) for a, b in ((wq_in, q), (wk_in, k), (wv_in, v), (x_in, do)))
        for j, grad in enumerate((dq, dk, dv)):
            made = room[4 + 3 * part + j][0]

            @pl.loop(0, nz)
            def _(a, made=made, grad=grad):
                span = pl.ds(pl.multiple_of(a * block, block), block)
                product = dot(h_t[span, :], grad[:, pl.ds(*parts[part])]).astype(bf)
                made[a] = product.reshape(made.shape[1:])

        if part == 1:
            for i in weights:
                loaded(i)
            sums[...] = sums_in[...]

    def last_norm(r):
        span = pl.ds(pl.multiple_of(r * block, block), block)
        d = dot(dq[span, :], q[...], NT) + dot(dk[span, :], k[...], NT) + dot(dv[span, :], v[...], NT)
        grad, gain_terms = norm_back(do[span, :].astype(f32), d, vec[0:1, :])
        sums[0:1, :] += row_sum(gain_terms)
        sums[1:2, :] += row_sum(d)
        send_rows[r] = (dx[span, :] + grad).astype(bf)

    targets = ((ox, at.c), (ox, oc), (at.x, oc), (at.x, at.c))

    def send_norm(i):
        px, pc = targets[i]
        last_norm(px * 2 + pc)
        if i < 3:
            push(send_rows.at[px * 2 + pc], grad_out.at[me], ex_send, ex_recv, at.dev(x=px, c=pc))
        else:
            pltpu.make_async_copy(send_rows.at[me], grad_out.at[me], local.at[11]).start()

    def share_sums():
        devices = nz * ny * nx * nc
        piece = width // devices
        lanes = lax.broadcasted_iota(jnp.int32, (width, 128), 0)
        fold = jnp.where(lax.rem(lanes, piece) == lax.broadcasted_iota(jnp.int32, (width, 128), 1), 1.0, 0.0).astype(bf)
        mine = lax.div(lax.broadcasted_iota(jnp.int32, (devices, width), 1), piece) == lax.broadcasted_iota(jnp.int32, (devices, width), 0)
        shares = []
        for i in range(6):
            spread = jnp.where(mine, sums[i : i + 1, :], 0.0)
            total = jnp.zeros((devices, 128), f32)
            for _ in range(3):
                low = spread.astype(bf)
                spread = spread - low.astype(f32)
                total = total + dot(low, fold)
            shares.append(total[:, None, :])
        shares.append(jnp.zeros((devices, 2, 128), f32))
        small[...] = jnp.concatenate(shares, axis=1).reshape(small.shape)

    split = LAST_SPLIT // 128
    pieces = [transpose] + [(pair, j) for j in range(split)] + [lambda: weight_grads(0)]
    pieces += [(pair, j) for j in range(split, width // 128)] + [lambda: weight_grads(1)]
    pieces += [functools.partial(send_norm, i) for i in range(4)] + [share_sums]
    run_order(LAST_ORDER[4:], net.go, pieces)
    drain(grad_out.at[0:3], ex_recv)
    drain(grad_out.at[0:3], ex_send)
    drain(grad_out.at[0], local.at[11])


def last(dims, args, cid):
    nz, ny, nx, nc = dims
    q, k, v, do, o, lse, h1, wq, wk, wv, x, dx, vec, gcq, gck, gcv, go, sums = args
    rows, width = q.shape
    bf, f32 = jnp.bfloat16, jnp.float32
    each = width // (nz * ny * nx * nc)
    shard = jax.ShapeDtypeStruct((each, width), f32)
    out_shape = [jax.ShapeDtypeStruct((4, rows // 4, width), bf)] + [shard] * 7 + [jax.ShapeDtypeStruct((8, 128), f32)]
    any_spec, vm = pl.BlockSpec(memory_space=ANY), pl.BlockSpec(memory_space=pltpu.VMEM)
    square = pltpu.VMEM((rows, width), bf)
    dma = pltpu.SemaphoreType.DMA
    scratch = [square] * 5 + [pltpu.VMEM(lse.shape, f32)] + [square] * 4 + [pltpu.VMEM((rows, width), f32), pltpu.VMEM((4, rows // 4, width), bf)]
    scratch += [pltpu.VMEM((nz, ny, nx, nc, 8, 128), f32)] + [pltpu.VMEM((rows, 128), f32)] * 2 + [pltpu.VMEM((8, width), f32)]
    scratch += [dma((16,)), dma, dma, dma((11,)), dma((11, 4)), dma((12,))]
    for j in range(4):
        scratch += scatter_room(dims, (each, width), bf, LAST_PATHS[j], False)
    for j in range(6):
        scratch += scatter_room(dims, (each, LAST_SPLIT if j < 3 else width - LAST_SPLIT), bf, LAST_PATHS[4 + j], True)
    scratch += scatter_room(dims, (8, 128), f32, LAST_PATHS[10], True)[1:]
    return pl.pallas_call(
        functools.partial(last_kernel, dims),
        out_shape=out_shape,
        in_specs=[any_spec] * 12 + [vm] + [any_spec] * 4 + [vm],
        out_specs=[any_spec] + [vm] * 8,
        scratch_shapes=scratch,
        compiler_params=pltpu.CompilerParams(collective_id=cid, has_side_effects=True, vmem_limit_bytes=63 * 2**20),
        name="last",
    )(q, k, v, do, o, lse, h1, wq, wk, wv, x, dx, vec, gcq, gck, gcv, go, sums)

HEAD_DIM = 64


EPS = 1e-05


def norm_rows(values_in, gain, bias):
    center = values_in - jnp.mean(values_in, axis=-1, keepdims=True)
    spread = jnp.mean(center * center, axis=-1, keepdims=True)
    return center * lax.rsqrt(spread + EPS) * gain + bias


def contract_rows(left, right):
    return lax.dot_general(
        left, right, (((0,), (0,)), ((), ())), preferred_element_type=jnp.float32
    )


def times_transposed(left, right):
    return lax.dot_general(
        left, right, (((1,), (1,)), ((), ())), preferred_element_type=jnp.float32
    )


def product(left, right):
    return jnp.dot(left, right, preferred_element_type=jnp.float32)


def local_plain(
    block_in,
    text_states,
    caption_len,
    out_grad,
    first_gain,
    first_bias,
    query_weight,
    key_weight,
    value_weight,
    output_weight,
    second_gain,
    second_bias,
    cross_query,
    cross_key,
    cross_value,
    cross_output,
    third_gain,
    third_bias,
    up_weight,
    down_weight,
):
    gathered = (
        lax.all_gather(first_gain, ("dp", "seq"), axis=0, tiled=True),
        lax.all_gather(first_bias, ("dp", "seq"), axis=0, tiled=True),
        lax.all_gather(query_weight, ("dp", "seq"), axis=0, tiled=True),
        lax.all_gather(key_weight, ("dp", "seq"), axis=0, tiled=True),
        lax.all_gather(value_weight, ("dp", "seq"), axis=0, tiled=True),
        lax.all_gather(output_weight, ("dp", "seq"), axis=0, tiled=True),
        lax.all_gather(second_gain, ("dp", "seq"), axis=0, tiled=True),
        lax.all_gather(second_bias, ("dp", "seq"), axis=0, tiled=True),
        lax.all_gather(cross_query, ("dp", "seq"), axis=0, tiled=True),
        lax.all_gather(cross_key, ("dp", "seq"), axis=0, tiled=True),
        lax.all_gather(cross_value, ("dp", "seq"), axis=0, tiled=True),
        lax.all_gather(cross_output, ("dp", "seq"), axis=0, tiled=True),
        lax.all_gather(third_gain, ("dp", "seq"), axis=0, tiled=True),
        lax.all_gather(third_bias, ("dp", "seq"), axis=0, tiled=True),
        lax.all_gather(up_weight, ("dp", "seq"), axis=0, tiled=True),
        lax.all_gather(down_weight, ("dp", "seq"), axis=0, tiled=True),
    )
    (
        gain_one,
        bias_one,
        w_query,
        w_key,
        w_value,
        w_output,
        gain_two,
        bias_two,
        w_cquery,
        w_ckey,
        w_cvalue,
        w_coutput,
        gain_three,
        bias_three,
        w_up,
        w_down,
    ) = gathered
    item_count, seg_len, model_width = block_in.shape
    row_count = item_count * seg_len
    head_count = model_width // HEAD_DIM
    score_scale = HEAD_DIM ** (-0.5)
    text_count = text_states.shape[1]
    inputs_f = block_in.astype(jnp.float32).reshape(row_count, model_width)
    normed_one, pull_one = jax.vjp(
        norm_rows, inputs_f, gain_one.astype(jnp.float32), bias_one.astype(jnp.float32)
    )
    normed_one = normed_one.astype(jnp.bfloat16)
    query_rows = product(normed_one, w_query).astype(jnp.bfloat16)
    key_rows = product(normed_one, w_key).astype(jnp.bfloat16)
    value_rows = product(normed_one, w_value).astype(jnp.bfloat16)
    key_all, value_all = (
        lax.all_gather(
            key_rows.reshape(item_count, seg_len, model_width), "seq", axis=1, tiled=True
        ),
        lax.all_gather(
            value_rows.reshape(item_count, seg_len, model_width), "seq", axis=1, tiled=True
        ),
    )
    key_count = key_all.shape[1]
    first_pos = lax.axis_index("seq") * seg_len
    query_pos = first_pos + jnp.arange(seg_len, dtype=jnp.int32)
    causal = jnp.arange(key_count, dtype=jnp.int32)[None, :] <= query_pos[:, None]

    def self_scores(query_item, key_item):
        query_heads = query_item.reshape(seg_len, head_count, HEAD_DIM)
        key_heads = key_item.reshape(key_count, head_count, HEAD_DIM)
        scores = jnp.einsum(
            "qhd,khd->hqk", query_heads, key_heads, preferred_element_type=jnp.float32
        )
        return jnp.where(causal[None, :, :], scores * score_scale, -1e30)

    def self_forward(operands):
        query_item, key_item, value_item = operands
        scores = self_scores(query_item, key_item)
        row_peak = jnp.max(scores, axis=-1, keepdims=True)
        row_total = jnp.sum(jnp.exp(scores - row_peak), axis=-1, keepdims=True)
        log_total = row_peak + jnp.log(row_total)
        prob_bf = jnp.exp(scores - log_total).astype(jnp.bfloat16)
        value_heads = value_item.reshape(key_count, head_count, HEAD_DIM)
        mixed = jnp.einsum("hqk,khd->qhd", prob_bf, value_heads, preferred_element_type=jnp.float32)
        return (mixed.reshape(seg_len, model_width).astype(jnp.bfloat16), log_total)

    attended, log_totals = lax.map(
        self_forward, (query_rows.reshape(item_count, seg_len, model_width), key_all, value_all)
    )
    attended_rows = attended.reshape(row_count, model_width)
    after_self = inputs_f + product(attended_rows, w_output)
    normed_two, pull_two = jax.vjp(
        norm_rows, after_self, gain_two.astype(jnp.float32), bias_two.astype(jnp.float32)
    )
    normed_two = normed_two.astype(jnp.bfloat16)
    cross_rows = product(normed_two, w_cquery).astype(jnp.bfloat16)
    cross_heads = cross_rows.reshape(item_count, seg_len, head_count, HEAD_DIM)
    text_keys = jnp.einsum(
        "itc,cd->itd", text_states, w_ckey, preferred_element_type=jnp.float32
    ).astype(jnp.bfloat16)
    text_values = jnp.einsum(
        "itc,cd->itd", text_states, w_cvalue, preferred_element_type=jnp.float32
    ).astype(jnp.bfloat16)
    text_kheads = text_keys.reshape(item_count, text_count, head_count, HEAD_DIM)
    text_vheads = text_values.reshape(item_count, text_count, head_count, HEAD_DIM)
    text_mask = jnp.arange(text_count, dtype=jnp.int32)[None, :] < caption_len[:, None]
    cross_scores = jnp.einsum(
        "iqhd,ithd->ihqt", cross_heads, text_kheads, preferred_element_type=jnp.float32
    )
    cross_scores = jnp.where(text_mask[:, None, None, :], cross_scores * score_scale, -1e30)
    cross_peak = jnp.max(cross_scores, axis=-1, keepdims=True)
    cross_exp = jnp.exp(cross_scores - cross_peak)
    cross_prob = cross_exp / jnp.sum(cross_exp, axis=-1, keepdims=True)
    cross_prob_bf = cross_prob.astype(jnp.bfloat16)
    crossed = jnp.einsum(
        "ihqt,ithd->iqhd", cross_prob_bf, text_vheads, preferred_element_type=jnp.float32
    )
    crossed_rows = crossed.reshape(row_count, model_width).astype(jnp.bfloat16)
    after_cross = after_self + product(crossed_rows, w_coutput)
    normed_three, pull_three = jax.vjp(
        norm_rows, after_cross, gain_three.astype(jnp.float32), bias_three.astype(jnp.float32)
    )
    normed_three = normed_three.astype(jnp.bfloat16)
    hidden = product(normed_three, w_up)
    activated, pull_gelu = jax.vjp(lambda inner: jax.nn.gelu(inner, approximate=False), hidden)
    activated = activated.astype(jnp.bfloat16)
    layer_out = after_cross + product(activated, w_down)
    block_out = layer_out.astype(jnp.bfloat16).reshape(item_count, seg_len, model_width)
    back_weights = (
        lax.all_gather(first_gain, ("dp", "seq"), axis=0, tiled=True),
        lax.all_gather(first_bias, ("dp", "seq"), axis=0, tiled=True),
        lax.all_gather(query_weight, ("dp", "seq"), axis=0, tiled=True),
        lax.all_gather(key_weight, ("dp", "seq"), axis=0, tiled=True),
        lax.all_gather(value_weight, ("dp", "seq"), axis=0, tiled=True),
        lax.all_gather(output_weight, ("dp", "seq"), axis=0, tiled=True),
        lax.all_gather(second_gain, ("dp", "seq"), axis=0, tiled=True),
        lax.all_gather(second_bias, ("dp", "seq"), axis=0, tiled=True),
        lax.all_gather(cross_query, ("dp", "seq"), axis=0, tiled=True),
        lax.all_gather(cross_key, ("dp", "seq"), axis=0, tiled=True),
        lax.all_gather(cross_value, ("dp", "seq"), axis=0, tiled=True),
        lax.all_gather(cross_output, ("dp", "seq"), axis=0, tiled=True),
        lax.all_gather(third_gain, ("dp", "seq"), axis=0, tiled=True),
        lax.all_gather(third_bias, ("dp", "seq"), axis=0, tiled=True),
        lax.all_gather(up_weight, ("dp", "seq"), axis=0, tiled=True),
        lax.all_gather(down_weight, ("dp", "seq"), axis=0, tiled=True),
    )
    (
        unused_gain,
        unused_bias,
        w_query,
        w_key,
        w_value,
        w_output,
        unused_gtwo,
        unused_btwo,
        w_cquery,
        w_ckey,
        w_cvalue,
        w_coutput,
        unused_gthree,
        unused_bthree,
        w_up,
        w_down,
    ) = back_weights
    grad_rows = out_grad.reshape(row_count, model_width)
    down_part = contract_rows(activated, grad_rows)
    act_grad = times_transposed(grad_rows, w_down)
    hidden_grad = pull_gelu(act_grad)[0].astype(jnp.bfloat16)
    up_part = contract_rows(normed_three, hidden_grad)
    normed_three_grad = times_transposed(hidden_grad, w_up)
    resid_three, gain_three_part, bias_three_part = pull_three(normed_three_grad)
    cross_grad = grad_rows.astype(jnp.float32) + resid_three
    cross_out_bf = cross_grad.astype(jnp.bfloat16)
    coutput_part = contract_rows(crossed_rows, cross_out_bf)
    crossed_grad = times_transposed(cross_out_bf, w_coutput).astype(jnp.bfloat16)
    crossed_heads = crossed_grad.reshape(item_count, seg_len, head_count, HEAD_DIM)
    cross_dprob = jnp.einsum(
        "iqhd,ithd->ihqt", crossed_heads, text_vheads, preferred_element_type=jnp.float32
    )
    cross_dscore = cross_prob * (
        cross_dprob - jnp.sum(cross_dprob * cross_prob, axis=-1, keepdims=True)
    )
    cross_dscore = cross_dscore.astype(jnp.bfloat16)
    cquery_grad = (
        (
            jnp.einsum(
                "ihqt,ithd->iqhd", cross_dscore, text_kheads, preferred_element_type=jnp.float32
            )
            * score_scale
        )
        .astype(jnp.bfloat16)
        .reshape(row_count, model_width)
    )
    tkey_part = (
        jnp.einsum("ihqt,iqhd->ithd", cross_dscore, cross_heads, preferred_element_type=jnp.float32)
        * score_scale
    ).reshape(item_count, text_count, model_width)
    tvalue_part = jnp.einsum(
        "ihqt,iqhd->ithd", cross_prob_bf, crossed_heads, preferred_element_type=jnp.float32
    ).reshape(item_count, text_count, model_width)
    cquery_part = contract_rows(normed_two, cquery_grad)
    normed_two_grad = times_transposed(cquery_grad, w_cquery)
    resid_two, gain_two_part, bias_two_part = pull_two(normed_two_grad)
    self_grad = cross_grad + resid_two
    self_out_bf = self_grad.astype(jnp.bfloat16)
    output_part = contract_rows(attended_rows, self_out_bf)
    attended_grad = times_transposed(self_out_bf, w_output).astype(jnp.bfloat16)
    query_items = query_rows.reshape(item_count, seg_len, model_width)
    dout_items = attended_grad.reshape(item_count, seg_len, model_width)

    def self_backward(operands):
        query_item, key_item, value_item, dout_item, log_total = operands
        scores = self_scores(query_item, key_item)
        probs = jnp.exp(scores - log_total)
        prob_bf = probs.astype(jnp.bfloat16)
        query_heads = query_item.reshape(seg_len, head_count, HEAD_DIM)
        key_heads = key_item.reshape(key_count, head_count, HEAD_DIM)
        value_heads = value_item.reshape(key_count, head_count, HEAD_DIM)
        dout_heads = dout_item.reshape(seg_len, head_count, HEAD_DIM)
        dprob = jnp.einsum(
            "qhd,khd->hqk", dout_heads, value_heads, preferred_element_type=jnp.float32
        )
        dscore = (probs * (dprob - jnp.sum(dprob * probs, axis=-1, keepdims=True))).astype(
            jnp.bfloat16
        )
        dquery = (
            (
                jnp.einsum("hqk,khd->qhd", dscore, key_heads, preferred_element_type=jnp.float32)
                * score_scale
            )
            .astype(jnp.bfloat16)
            .reshape(seg_len, model_width)
        )
        dkey = (
            jnp.einsum("hqk,qhd->khd", dscore, query_heads, preferred_element_type=jnp.float32)
            * score_scale
        ).reshape(key_count, model_width)
        dvalue = jnp.einsum(
            "hqk,qhd->khd", prob_bf, dout_heads, preferred_element_type=jnp.float32
        ).reshape(key_count, model_width)
        return (dquery, dkey, dvalue)

    query_grad_items, key_part, value_part = lax.map(
        self_backward, (query_items, key_all, value_all, dout_items, log_totals)
    )
    key_own, value_own, tkey_own, tvalue_own = (
        lax.psum_scatter(
            key_part.astype(jnp.bfloat16), "seq", scatter_dimension=1, tiled=True
        ).astype(jnp.float32),
        lax.psum_scatter(
            value_part.astype(jnp.bfloat16), "seq", scatter_dimension=1, tiled=True
        ).astype(jnp.float32),
        lax.psum_scatter(
            tkey_part.astype(jnp.bfloat16), "seq", scatter_dimension=1, tiled=True
        ).astype(jnp.float32),
        lax.psum_scatter(
            tvalue_part.astype(jnp.bfloat16), "seq", scatter_dimension=1, tiled=True
        ).astype(jnp.float32),
    )
    key_grad_rows = key_own.astype(jnp.bfloat16).reshape(row_count, model_width)
    value_grad_rows = value_own.astype(jnp.bfloat16).reshape(row_count, model_width)
    query_grad_rows = query_grad_items.reshape(row_count, model_width)
    tkey_bf = tkey_own.astype(jnp.bfloat16)
    tvalue_bf = tvalue_own.astype(jnp.bfloat16)
    query_part = contract_rows(normed_one, query_grad_rows)
    key_wpart = contract_rows(normed_one, key_grad_rows)
    value_wpart = contract_rows(normed_one, value_grad_rows)
    normed_one_grad = (
        times_transposed(query_grad_rows, w_query)
        + times_transposed(key_grad_rows, w_key)
        + times_transposed(value_grad_rows, w_value)
    )
    resid_one, gain_one_part, bias_one_part = pull_one(normed_one_grad)
    input_grad = (self_grad + resid_one).reshape(item_count, seg_len, model_width)
    text_rows = tkey_own.shape[1]
    text_start = lax.axis_index("seq") * text_rows
    text_slice = lax.dynamic_slice_in_dim(text_states, text_start, text_rows, 1)
    ckey_part = jnp.einsum("itc,itd->cd", text_slice, tkey_bf, preferred_element_type=jnp.float32)
    cvalue_part = jnp.einsum(
        "itc,itd->cd", text_slice, tvalue_bf, preferred_element_type=jnp.float32
    )
    text_grad = jnp.einsum(
        "itd,cd->itc", tkey_bf, w_ckey, preferred_element_type=jnp.float32
    ) + jnp.einsum("itd,cd->itc", tvalue_bf, w_cvalue, preferred_element_type=jnp.float32)
    (
        first_gain_grad,
        first_bias_grad,
        query_grad,
        key_grad,
        value_grad,
        output_grad,
        second_gain_grad,
        second_bias_grad,
        cross_query_grad,
        cross_key_grad,
        cross_value_grad,
        cross_output_grad,
        third_gain_grad,
        third_bias_grad,
        up_grad,
        down_grad,
    ) = (
        lax.psum_scatter(gain_one_part, ("dp", "seq"), scatter_dimension=0, tiled=True),
        lax.psum_scatter(bias_one_part, ("dp", "seq"), scatter_dimension=0, tiled=True),
        lax.psum_scatter(query_part, ("dp", "seq"), scatter_dimension=0, tiled=True),
        lax.psum_scatter(key_wpart, ("dp", "seq"), scatter_dimension=0, tiled=True),
        lax.psum_scatter(value_wpart, ("dp", "seq"), scatter_dimension=0, tiled=True),
        lax.psum_scatter(output_part, ("dp", "seq"), scatter_dimension=0, tiled=True),
        lax.psum_scatter(gain_two_part, ("dp", "seq"), scatter_dimension=0, tiled=True),
        lax.psum_scatter(bias_two_part, ("dp", "seq"), scatter_dimension=0, tiled=True),
        lax.psum_scatter(cquery_part, ("dp", "seq"), scatter_dimension=0, tiled=True),
        lax.psum_scatter(ckey_part, ("dp", "seq"), scatter_dimension=0, tiled=True),
        lax.psum_scatter(cvalue_part, ("dp", "seq"), scatter_dimension=0, tiled=True),
        lax.psum_scatter(coutput_part, ("dp", "seq"), scatter_dimension=0, tiled=True),
        lax.psum_scatter(gain_three_part, ("dp", "seq"), scatter_dimension=0, tiled=True),
        lax.psum_scatter(bias_three_part, ("dp", "seq"), scatter_dimension=0, tiled=True),
        lax.psum_scatter(up_part, ("dp", "seq"), scatter_dimension=0, tiled=True),
        lax.psum_scatter(down_part, ("dp", "seq"), scatter_dimension=0, tiled=True),
    )
    return (
        block_out,
        input_grad,
        text_grad,
        first_gain_grad,
        first_bias_grad,
        query_grad,
        key_grad,
        value_grad,
        output_grad,
        second_gain_grad,
        second_bias_grad,
        cross_query_grad,
        cross_key_grad,
        cross_value_grad,
        cross_output_grad,
        third_gain_grad,
        third_bias_grad,
        up_grad,
        down_grad,
    )


def small_rows(vectors):
    packed = jnp.stack(vectors)
    return jnp.pad(packed, ((0, 16 - packed.shape[0]), (0, 128 - packed.shape[1])))


def local(seq_size, *args):
    block_in = args[0]
    if block_in.shape[0] != seq_size or seq_size != 4 or block_in.shape[1] * seq_size != 1024:
        return local_plain(*args)
    return local_items(seq_size, *args)


def local_items(
    seq_size,
    block_in,
    text_states,
    caption_len,
    out_grad,
    first_gain,
    first_bias,
    query_weight,
    key_weight,
    value_weight,
    output_weight,
    second_gain,
    second_bias,
    cross_query,
    cross_key,
    cross_value,
    cross_output,
    third_gain,
    third_bias,
    up_weight,
    down_weight,
):
    ny, nx, nc = 2, seq_size // 2, 2
    dp_size = 1024 // first_gain.shape[0] // seq_size
    dims = (dp_size // ny, ny, nx, nc)
    bf, f32 = jnp.bfloat16, jnp.float32
    seg, width = block_in.shape[1], block_in.shape[2]
    rows = seq_size * seg
    me = lax.axis_index("seq")
    small = small_rows([first_gain, first_bias, second_gain, second_bias, third_gain, third_bias])
    shards = [small, query_weight, key_weight, value_weight, output_weight, cross_query, cross_key, cross_value, cross_output, up_weight, down_weight]
    full, kept = forward(dims, shards, block_in, out_grad, text_states, caption_len, 1)
    small, w_query, w_key, w_value, w_output, w_cquery, w_ckey, w_cvalue, w_coutput, w_up, w_down = full
    grad_rows, inputs, q, k, v, cq, ck, cv, o, o2, normed_one, normed_two, normed_three, after_self, after_cross, lse, lse2, vectors = kept
    grad_rows = grad_rows.reshape(rows, width)
    block_out, dh3, down_part, up_grad_done, up_part = ffn(dims, normed_three, grad_rows, after_cross, w_up, w_down, 4)
    (
        block_out, text_grad, self_grad, do, g_cq, g_ck, g_cv, g_o, sums, down_grad, up_grad, coutput_grad,
    ) = middle(dims, (
        grad_rows, dh3, after_cross, after_self, vectors, o2, cq, ck, cv, lse2, normed_two, o, w_coutput, w_cquery, w_ckey, w_cvalue,
        w_output, text_states, caption_len, block_out.reshape(seq_size, seg, width), down_part, up_part,
    ), 2)
    up_grad = jnp.concatenate([up_grad_done, up_grad], axis=1)
    (
        input_grad, cquery_grad, ckey_grad, cvalue_grad, output_grad, query_grad, key_grad, value_grad, small_grad,
    ) = last(dims, (
        q, k, v, do, o, lse, normed_one, w_query, w_key, w_value, inputs.reshape(rows, width), self_grad, vectors,
        g_cq, g_ck, g_cv, g_o, sums,
    ), 3)
    input_grad = input_grad.astype(f32)
    vec = [small_grad[i, : first_gain.shape[0]] for i in range(6)]
    return (
        block_out, input_grad, text_grad,
        vec[0], vec[1], query_grad, key_grad, value_grad, output_grad,
        vec[2], vec[3], cquery_grad, ckey_grad, cvalue_grad, coutput_grad,
        vec[4], vec[5], up_grad, down_grad,
    )


def solution(mesh):
    return jax.shard_map(
        functools.partial(local, mesh.shape['seq']),
        mesh=mesh,
        in_specs=(
            P("dp", "seq", None),
            P("dp", None, None),
            P("dp"),
            P("dp", "seq", None),
            P(("dp", "seq")),
            P(("dp", "seq")),
            P(("dp", "seq"), None),
            P(("dp", "seq"), None),
            P(("dp", "seq"), None),
            P(("dp", "seq"), None),
            P(("dp", "seq")),
            P(("dp", "seq")),
            P(("dp", "seq"), None),
            P(("dp", "seq"), None),
            P(("dp", "seq"), None),
            P(("dp", "seq"), None),
            P(("dp", "seq")),
            P(("dp", "seq")),
            P(("dp", "seq"), None),
            P(("dp", "seq"), None),
        ),
        out_specs=(
            P("dp", "seq", None),
            P("dp", "seq", None),
            P("dp", "seq", None),
            P(("dp", "seq")),
            P(("dp", "seq")),
            P(("dp", "seq"), None),
            P(("dp", "seq"), None),
            P(("dp", "seq"), None),
            P(("dp", "seq"), None),
            P(("dp", "seq")),
            P(("dp", "seq")),
            P(("dp", "seq"), None),
            P(("dp", "seq"), None),
            P(("dp", "seq"), None),
            P(("dp", "seq"), None),
            P(("dp", "seq")),
            P(("dp", "seq")),
            P(("dp", "seq"), None),
            P(("dp", "seq"), None),
        ),
        check_vma=False,
    )
```

```python
import functools
import itertools

import jax
import jax.numpy as jnp
from jax import lax
from jax.experimental import pallas as pl
from jax.experimental.pallas import tpu as pltpu
from jax.sharding import PartitionSpec as P

MESH = pl.DeviceIdType.MESH
ANY = pl.ANY


class Place:
    def __init__(self, dims):
        self.nz, self.ny, self.nx, self.nc = dims
        dp, seq = lax.axis_index("dp"), lax.axis_index("seq")
        self.z, self.y = lax.div(dp, self.ny), lax.rem(dp, self.ny)
        self.x, self.c = lax.div(seq, self.nc), lax.rem(seq, self.nc)
        self.dp, self.seq = dp, seq

    def dev(self, z=None, y=None, x=None, c=None):
        z = self.z if z is None else z
        y = self.y if y is None else y
        x = self.x if x is None else x
        c = self.c if c is None else c
        return (z * self.ny + y, x * self.nc + c)

    def z_others(self):
        if self.nz != 4:
            return [lax.rem(self.z + k, self.nz) for k in range(1, self.nz)]
        near, far = 1 + lax.rem(self.z, 2), 3 - 3 * lax.div(self.z, 2)
        return [near, 6 - self.z - near - far, far]


def hello(peers):
    barrier = pltpu.get_barrier_semaphore()
    for peer in peers:
        pl.semaphore_signal(barrier, inc=1, device_id=peer, device_id_type=MESH)
    pl.semaphore_wait(barrier, len(peers))


def push(src, dst, send, recv, device):
    pltpu.make_async_remote_copy(
        src_ref=src, dst_ref=dst, send_sem=send, recv_sem=recv, device_id=device, device_id_type=MESH
    ).start()


def drain(ref, sem):
    pltpu.make_async_copy(ref, ref, sem).wait()


def add_to(dst, src):
    dst[...] = dst[...] + src[...]


LOG2E = 1.4426950408889634
NT = (((1,), (1,)), ((), ()))
NN = (((1,), (0,)), ((), ()))
def dot(a, b, dims=NN):
    return lax.dot_general(a, b, dims, preferred_element_type=jnp.float32)

def half_mask(x, h):
    lane = lax.broadcasted_iota(jnp.int32, x.shape, 1)
    keep = lane < 64 if h == 0 else lane >= 64
    return jnp.where(keep, x, jnp.zeros_like(x))

def hide(scores, limit, causal, start):
    rows, cols = scores.shape
    if causal:
        key = lax.broadcasted_iota(jnp.int32, (cols, cols), 0)
        query = lax.broadcasted_iota(jnp.int32, (cols, cols), 1)
        tail = jnp.where(key <= query, scores[rows - cols:], -1e30)
        return tail if rows == cols else jnp.concatenate([scores[:rows - cols], tail], axis=0)
    key = lax.broadcasted_iota(jnp.int32, (rows, cols), 0)
    return jnp.where(key < limit, scores, -1e30)

def attend_kernel(causal, block, limit_ref, q_ref, k_ref, v_ref, o_ref, lse_ref):
    limit = None if causal else limit_ref[0]
    rows, keys = q_ref.shape[0], k_ref.shape[0]
    v_t = v_ref[...].T
    ones = jnp.ones((16, keys), v_t.dtype)
    for i in range(rows // block):
        n = (i + 1) * block if causal else keys
        span = pl.ds(i * block, block)
        halves = []
        for h in range(2):
            q = half_mask(q_ref[span, :], h)
            s = hide(dot(k_ref[0:n, :], q, NT), limit, causal, i * block)
            peak = jnp.max(s, axis=0, keepdims=True)
            e = jnp.exp2(s - peak).astype(jnp.bfloat16)
            v_aug = jnp.concatenate([v_t[h * 64:(h + 1) * 64, :n], ones[:, :n]], axis=0)
            mixed = dot(v_aug, e)
            total = mixed[64:65]
            halves.append(mixed[:64] / total)
            lse_ref[0, h:h + 1, span] = peak + jnp.log2(total)
        o_ref[span, :] = jnp.concatenate(halves, axis=0).T.astype(o_ref.dtype)

def attend_back_kernel(causal, block, limit_ref, q_ref, k_ref, v_ref, g_ref, o_ref, lse_ref, dq_ref, dk_ref, dv_ref, dk_acc, dv_acc):
    limit = None if causal else limit_ref[0]
    rows, keys = q_ref.shape[0], k_ref.shape[0]
    k_t = k_ref[...].T
    sel_row = lax.broadcasted_iota(jnp.int32, (16, 128), 0)
    sel_lane = lax.broadcasted_iota(jnp.int32, (16, 128), 1)
    pick = jnp.where(sel_row == lax.div(sel_lane, 64), 1.0, 0.0).astype(jnp.bfloat16)
    dk_acc[...] = jnp.zeros_like(dk_acc)
    dv_acc[...] = jnp.zeros_like(dv_acc)
    for i in range(rows // block):
        n = (i + 1) * block if causal else keys
        span = pl.ds(i * block, block)
        prod = g_ref[span, :].astype(jnp.float32) * o_ref[span, :].astype(jnp.float32)
        high = prod.astype(jnp.bfloat16)
        low = (prod - high.astype(jnp.float32)).astype(jnp.bfloat16)
        delta = dot(pick, high, NT) + dot(pick, low, NT)
        halves = []
        for h in range(2):
            q = half_mask(q_ref[span, :], h)
            g = half_mask(g_ref[span, :], h)
            s = hide(dot(k_ref[0:n, :], q, NT), limit, causal, i * block)
            p = jnp.exp2(s - lse_ref[0, h:h + 1, span])
            dp = dot(v_ref[0:n, :], g, NT)
            ds = (p * (dp - delta[h:h + 1])).astype(jnp.bfloat16)
            dv_acc[0:n, :] += dot(p.astype(jnp.bfloat16), g)
            dk_acc[0:n, :] += dot(ds, q)
            halves.append(dot(k_t[h * 64:(h + 1) * 64, :n], ds))
        dq_ref[span, :] = (jnp.concatenate(halves, axis=0).T * 0.125).astype(dq_ref.dtype)
    dk_ref[...] = (dk_acc[...] * (1.0 / LOG2E)).astype(dk_ref.dtype)
    dv_ref[...] = dv_acc[...].astype(dv_ref.dtype)

def gelu_parts(u):
    t = 1.0 / (1.0 + (0.3275911 * 0.7071067811865476) * jnp.abs(u))
    e = jnp.exp(-0.5 * (u * u))
    poly = t * (0.254829592 + t * (-0.284496736 + t * (1.421413741 + t * (-1.453152027 + t * 1.061405429))))
    tail = 0.5 * poly * e
    return jnp.where(u < 0, tail, 1.0 - tail), e * 0.3989422804014327


def ffn_kernel(dims, sent, h_ref, g_ref, x_ref, up_ref, down_ref, out_ref, dh_ref, ddown_ref, grad_ref, rest_ref,
               h_t, acc, act, du, made, own, rc, r2a, r2b, r3, r4, local_sem, send, recv):
    j = pl.program_id(0)
    steps = pl.num_programs(0)
    at = Place(dims)
    nz, ny, nx, nc = dims
    z, y, x, c = at.z, at.y, at.x, at.c
    oy, ox, oc = 1 - y, 1 - x, 1 - c
    rows, width = h_ref.shape
    chunk = up_ref.shape[1]
    half = chunk // 2
    block = rows // 2
    left, right = pl.ds(0, half), pl.ds(half, half)
    every = slice(None)

    def made_at(slot, core):
        return made.at[(slot, every, every, every, core)]

    def core_go(i):
        slot = lax.rem(i, 2)
        pltpu.make_async_copy(made_at(slot, c), own.at[i], local_sem.at[i]).start()
        push(made_at(slot, oc), rc.at[i], send.at[i, 0], recv.at[i, 0], at.dev(c=oc))

    def first_go(i):
        drain(own.at[i], local_sem.at[i])
        drain(rc.at[i], recv.at[i, 0])
        drain(rc.at[i], send.at[i, 0])

        @pl.loop(0, nz)
        def _(a):
            for b in range(ny):
                for d in range(nx):
                    add_to(own.at[i, a, b, d], rc.at[i, a, b, d])

        push(own.at[i, :, oy, :, :, left], r2a.at[i], send.at[i, 1], recv.at[i, 1], at.dev(y=oy))
        push(own.at[i, :, :, ox, :, right], r2b.at[i], send.at[i, 1], recv.at[i, 2], at.dev(x=ox))

    def second_go(i):
        drain(r2a.at[i], recv.at[i, 1])
        drain(r2b.at[i], recv.at[i, 2])

        @pl.loop(0, nz)
        def _(a):
            for b in range(2):
                add_to(own.at[i, a, y, b, :, left], r2a.at[i, a, b])
                add_to(own.at[i, a, b, x, :, right], r2b.at[i, a, b])

        push(own.at[i, :, y, ox, :, left], r3.at[i, :, :, left], send.at[i, 1], recv.at[i, 3], at.dev(x=ox))
        push(own.at[i, :, oy, x, :, right], r3.at[i, :, :, right], send.at[i, 1], recv.at[i, 4], at.dev(y=oy))

    def third_go(i):
        drain(r3.at[i, :, :, left], recv.at[i, 3])
        drain(r3.at[i, :, :, right], recv.at[i, 4])

        @pl.loop(0, nz)
        def _(a):
            add_to(own.at[i, a, y, x], r3.at[i, a])

        for k in range(1, nz):
            far = lax.rem(z + k, nz)
            push(own.at[i, far, y, x], r4.at[i, k - 1], send.at[i, 1], recv.at[i, 5], at.dev(z=far))

    def finish(i):
        drain(r4.at[i], recv.at[i, 5])
        total = own[i, z, y, x].astype(jnp.float32)
        for k in range(nz - 1):
            total = total + r4[i, k].astype(jnp.float32)
        grad_ref[i] = total
        for part in (r2a.at[i], r2b.at[i], r3.at[i], r4.at[i]):
            drain(part, send.at[i, 1])

    @pl.when(j == 0)
    def _():
        hello([at.dev(z=k) for k in at.z_others()] + [at.dev(y=oy), at.dev(x=ox), at.dev(c=oc)])
        acc[...] = x_ref[...]
        dh_ref[...] = jnp.zeros_like(dh_ref)

        @pl.loop(0, rows // block)
        def _(r):
            span = pl.ds(pl.multiple_of(r * block, block), block)
            h_t[:, span] = h_ref[span, :].T

    def after(late, then, first=0, end=sent):
        pl.when((j >= late + first) & (j < late + end))(lambda: then(j - late))

    after(1, first_go)
    after(2, third_go, 0, sent - 1)
    for r in range(rows // block):
        span = pl.ds(r * block, block)
        u = dot(h_ref[span, :], up_ref[...])
        g = dot(g_ref[span, :], down_ref[...], NT)
        big, small = gelu_parts(u)
        a = (u * big).astype(jnp.bfloat16)
        d = (g * (big + u * small)).astype(jnp.bfloat16)
        act[span, :] = a
        du[span, :] = d
        acc[span, :] += dot(a, down_ref[...])
        dh_ref[span, :] += dot(d, up_ref[...], NT)

    after(1, second_go)
    after(2, finish, 0, sent - 1)
    slot = lax.rem(j, 2)
    each = rows // (nz * ny * nx * nc)

    @pl.loop(0, nz)
    def _(a):
        n = ny * nx * nc * each
        part = dot(h_t[pl.ds(pl.multiple_of(a * n, n), n), :], du[...]).astype(made.dtype)
        made[slot, a] = part.reshape(ny, nx, nc, each, chunk)

    after(0, core_go)
    after(1, third_go, sent - 1)
    ddown_ref[...] = lax.dot_general(act[...], g_ref[...], TN, preferred_element_type=jnp.float32).astype(ddown_ref.dtype)
    after(1, finish, sent - 1)

    @pl.when(j >= sent)
    def _():
        pltpu.make_async_copy(made.at[slot], rest_ref.at[j - sent], local_sem.at[j]).start()

    @pl.when(j == steps - 1)
    def _():
        out_ref[...] = acc[...].astype(out_ref.dtype)
        for i in range(sent, 4):
            drain(rest_ref.at[i - sent], local_sem.at[i])


def ffn(dims, h, g, x, w_up, w_down, cid, sent=3, steps=4):
    nz, ny, nx, nc = dims
    rows, width = h.shape
    inner = w_up.shape[1]
    chunk = inner // steps
    each = width // (nz * ny * nx * nc)
    bf, f32 = jnp.bfloat16, jnp.float32
    fixed = lambda j: (0, 0)
    whole = pl.BlockSpec((rows, width), fixed)
    once = pl.BlockSpec((rows, width), fixed, pipeline_mode=pl.Buffered(1))
    tile = (each, chunk)
    out, dh, ddown, grad, rest = pl.pallas_call(
        functools.partial(ffn_kernel, dims, sent),
        grid=(steps,),
        out_shape=[
            jax.ShapeDtypeStruct((rows, width), bf),
            jax.ShapeDtypeStruct((rows, width), f32),
            jax.ShapeDtypeStruct((inner, width), bf),
            jax.ShapeDtypeStruct((sent, each, chunk), f32),
            jax.ShapeDtypeStruct((steps - sent, nz, ny, nx, nc, each, chunk), bf),
        ],
        in_specs=[once, once, once, pl.BlockSpec((width, chunk), lambda j: (0, j)), pl.BlockSpec((chunk, width), lambda j: (j, 0))],
        out_specs=[once, once, pl.BlockSpec((chunk, width), lambda j: (j, 0)),
                   pl.BlockSpec((sent, each, chunk), lambda j: (0, 0, 0)), pl.BlockSpec(memory_space=ANY)],
        scratch_shapes=[
            pltpu.VMEM((width, rows), bf), pltpu.VMEM((rows, width), f32), pltpu.VMEM((rows, chunk), bf), pltpu.VMEM((rows, chunk), bf),
            pltpu.VMEM((2, nz, ny, nx, nc) + tile, bf),
            pltpu.VMEM((sent, nz, ny, nx) + tile, bf), pltpu.VMEM((sent, nz, ny, nx) + tile, bf),
            pltpu.VMEM((sent, nz, nx, each, chunk // 2), bf), pltpu.VMEM((sent, nz, ny, each, chunk // 2), bf),
            pltpu.VMEM((sent, nz) + tile, bf), pltpu.VMEM((sent, nz - 1) + tile, bf),
            pltpu.SemaphoreType.DMA((steps,)), pltpu.SemaphoreType.DMA((sent, 2)), pltpu.SemaphoreType.DMA((sent, 6)),
        ],
        compiler_params=pltpu.CompilerParams(collective_id=cid, has_side_effects=True, vmem_limit_bytes=62 * 2**20, dimension_semantics=("arbitrary",)),
        name="feed_forward",
    )(h, g, x, w_up, w_down)
    grad = jnp.moveaxis(grad, 0, 1).reshape(each, sent * chunk)
    rest = jnp.moveaxis(rest, 0, 5).reshape(width, (steps - sent) * chunk)
    return out, dh, ddown, grad, rest
class Gather:
    def __init__(self, dims, units, ins, outs, send, recv):
        self.at, self.nz = Place(dims), dims[0]
        self.units, self.ins, self.outs, self.send, self.recv = units, ins, outs, send, recv

    def part(self, u, where, core=None):
        a, r0, nr, c0, ncol, _ = self.units[u]
        return self.outs[a].at[(*where, self.at.c if core is None else core, pl.ds(r0, nr), pl.ds(c0, ncol))]

    def held(self, u, k):
        where = [self.at.z, self.at.y, self.at.x]
        for axis in self.units[u][5][:k]:
            where[axis] = slice(None)
        return where

    def coming(self, u, k):
        where = self.held(u, k)
        axis = self.units[u][5][k]
        where[axis] = (slice(0, self.nz - 1), 1 - self.at.y, 1 - self.at.x)[axis]
        return where

    def to_core(self, u, where):
        block = self.part(u, where)
        push(block, block, self.send.at[u], self.recv.at[u, 3], self.at.dev(c=1 - self.at.c))

    def pass_on(self, u, k):
        axis = self.units[u][5][k]
        if axis == 0 and k == 0:
            self.to_core(u, self.held(u, 1))
        elif axis == 0:
            for z in self.at.z_others():
                where = self.held(u, k)
                where[0] = z
                self.to_core(u, where)
        else:
            self.to_core(u, self.coming(u, k))
            if k == 0:
                self.to_core(u, self.held(u, 0))

    def go(self, u, k):
        at = self.at
        if k > 0:
            drain(self.part(u, self.coming(u, k - 1)), self.recv.at[u, k - 1])
        if k < 3:
            a, r0, nr, c0, ncol, order = self.units[u]
            dst = self.part(u, self.held(u, k))
            src = self.ins[a].at[pl.ds(r0, nr), pl.ds(c0, ncol)] if k == 0 else dst
            targets = ([at.dev(z=z) for z in at.z_others()], [at.dev(y=1 - at.y)], [at.dev(x=1 - at.x)])[order[k]]
            for device in targets:
                push(src, dst, self.send.at[u], self.recv.at[u, k], device)
        if k > 0:
            self.pass_on(u, k - 1)

    def arrived(self, u):
        drain(self.part(u, [slice(None)] * 3, 1 - self.at.c), self.recv.at[u, 3])

    def sent(self, u):
        for k in range(3):
            where = self.held(u, k)
            if self.units[u][5][k] == 0:
                where[0] = slice(0, self.nz - 1)
            drain(self.part(u, where), self.send.at[u])
        drain(self.part(u, [slice(None)] * 3), self.send.at[u])


def norm_parts(values_in):
    center = values_in - jnp.mean(values_in, axis=-1, keepdims=True)
    return center * lax.rsqrt(jnp.mean(center * center, axis=-1, keepdims=True) + EPS)


FW_PATHS = ((2, 0, 1), (0, 2, 1), (0, 1, 2), (0, 2, 1), (0, 1, 2), (2, 0, 1), (0, 1, 2), (2, 0, 1), (2, 0, 1), (2, 1, 0), (0, 1, 2), (0, 2, 1), (0, 2, 1), (0, 1, 2), (0, 1, 2), (2, 1, 0), (0, 1, 2))
FW_UNITS = [(a, 0, 32, 0, 1024, FW_PATHS[a - 1]) for a in range(1, 9)]
FW_UNITS += [(9, 0, 32, 1024 * j, 1024, FW_PATHS[8 + j]) for j in range(4)]
FW_UNITS += [(10, 32 * j, 32, 0, 1024, FW_PATHS[12 + j]) for j in range(4)] + [(0, 0, 16, 0, 128, FW_PATHS[16])]
FW_ORDER = (
    (0, 0), (1, 0), (16, 0), (4, 0), (5, 0), (8, 0), (1, 1), (6, 0), (16, 1), (2, 0), (16, 2), (4, 1), (10, 0),
    (6, 1), (3, 0), (4, 2), (2, 1), (13, 0), (0, 1), (15, 0), (5, 1), (7, 0), (6, 2), (8, 1), (9, 0), (10, 1),
    (11, 0), (2, 2), (1, 2), (16, 3), (3, 1), (12, 0), (10, 2), (-2, 0), (13, 1), (14, 0), (4, 3), (15, 1), (7, 1),
    (4, 4), (1, 3), (0, 2), (13, 2), (1, 4), (15, 2), (6, 3), (9, 1), (5, 2), (6, 4), (0, 3), (2, 3), (9, 2), (0, 4),
    (8, 2), (2, 4), (-2, 1), (3, 2), (-2, 2), (11, 1), (-2, 3), (5, 3), (12, 1), (-2, 4), (5, 4), (10, 3), (-2, 5),
    (14, 1), (-1, 0), (-2, 6), (8, 3), (-2, 7), (-2, 8), (13, 3), (7, 2), (-2, 9), (11, 2), (3, 3), (-2, 10),
    (-2, 11), (3, 4), (12, 2), (14, 2), (-2, 12), (-2, 13), (7, 3), (-2, 14), (15, 3), (7, 4), (-2, 15), (-2, 16),
    (-2, 17), (-2, 18), (-2, 19), (-2, 20), (11, 3), (-2, 21), (-2, 22), (-2, 23), (-2, 24), (14, 3), (12, 3),
    (9, 3),
)


def forward_kernel(dims, n, *refs):
    shards, refs = refs[:n], refs[n:]
    block_in, out_grad, text_states, limits = refs[:4]
    full, refs = refs[4 : 4 + n], refs[4 + n :]
    g_out, x_out, q_out, k_out, v_out, cq_out, ck_out, cv_out, o_out, o2_out, h1_out, h2_out, h3_out, x1_out, x2_out, lse_out, lse2_out, vec = refs[:18]
    x_in, q, k, v, cq, ck, cv, o, o2, h1, h2, h3, x1, x2, lse, lse2, text, small = refs[18:36]
    w, near, own_g = refs[36:44], refs[44 : 44 + n], refs[44 + n]
    limit, local_sem, out_sem, send, recv, ex_send, ex_recv = refs[45 + n :]
    at = Place(dims)
    oy, ox, oc, me = 1 - at.y, 1 - at.x, 1 - at.c, at.seq
    hello([at.dev(z=p) for p in at.z_others()] + [at.dev(y=oy), at.dev(x=ox), at.dev(c=oc), at.dev(x=ox, c=oc)])
    net = Gather(dims, FW_UNITS, near, full, send, recv)
    rows, width = q.shape
    block = 256
    f32, bf = jnp.float32, jnp.bfloat16
    others = ((ox, at.c), (ox, oc), (at.x, oc))

    def exchange(src, dst, i, own):
        for px, pc in others:
            push(src.at[px * 2 + pc], dst.at[me], ex_send.at[i], ex_recv.at[i], at.dev(x=px, c=pc))
        pltpu.make_async_copy(own, dst.at[me], local_sem.at[n + i]).start()

    def exchanged(dst, i):
        drain(dst.at[0:3], ex_recv.at[i])
        drain(dst.at[0], local_sem.at[n + i])

    keep = []

    def put(src, dst):
        pltpu.make_async_copy(src, dst, out_sem.at[len(keep)]).start()
        keep.append(src)

    loads = 4 + n

    def load(a):
        net.arrived(a - 1)
        pltpu.make_async_copy(full[a], w[a - 1], local_sem.at[loads + a]).start()

    def loaded(a):
        drain(w[a - 1], local_sem.at[loads + a])

    def weight(a):
        return w[a - 1][...].reshape(width, width)

    def span_of(r):
        return pl.ds(pl.multiple_of(r * block, block), block)

    def first_norm():
        net.arrived(16)
        pltpu.make_async_copy(full[0], small, local_sem.at[n + 3]).start()
        drain(small, local_sem.at[n + 3])
        packed = small[...].reshape(-1, 16, 128).astype(f32)
        devices = packed.shape[0]
        piece = width // devices
        lane = lax.rem(lax.broadcasted_iota(jnp.int32, (128, width), 1), piece)
        spread = jnp.where(lane == lax.broadcasted_iota(jnp.int32, (128, width), 0), 1.0, 0.0).astype(bf)
        owner = lax.div(lax.broadcasted_iota(jnp.int32, (devices, width), 1), piece)
        mine = owner == lax.broadcasted_iota(jnp.int32, (devices, width), 0)
        vec[...] = jnp.zeros_like(vec)
        for i in range(6):
            vec[i : i + 1, :] = row_sum(jnp.where(mine, dot(packed[:, i, :].astype(bf), spread), 0.0))
        exchanged(x_in, 0)
        put(x_in, x_out)

        @pl.loop(0, 4)
        def _(r):
            x = x_in[r].astype(f32)
            x1[span_of(r), :] = x
            h1[span_of(r), :] = (norm_parts(x) * vec[0:1, :] + vec[1:2, :]).astype(bf)

        put(h1, h1_out)

    def project(a, dst, scale, kept):
        loaded(a)

        @pl.loop(0, rows // block)
        def _(r):
            made = dot(h1[span_of(r), :], weight(a))
            dst[span_of(r), :] = (made if scale is None else made * scale).astype(bf)

        put(dst, kept)

    def pair(causal, qs, ks, vs, os, ls, j):
        cols = pl.ds(pl.multiple_of(j * 128, 128), 128)
        attend_kernel(causal, 512, limit, qs.at[:, cols], ks.at[:, cols], vs.at[:, cols], os.at[:, cols], ls.at[pl.ds(j, 1)])

    self_attention = functools.partial(pair, True, q, k, v, o, lse)
    cross_attention = functools.partial(pair, False, cq, ck, cv, o2, lse2)
    count = width // 128

    def second_norm(i):
        if i == 0:
            put(o, o_out)
            put(lse, lse_out)
            loaded(4)
            loaded(5)

        @pl.loop(2 * i, 2 * i + 2)
        def _(r):
            x = x1[span_of(r), :] + dot(o[span_of(r), :], weight(4))
            x1[span_of(r), :] = x
            h = (norm_parts(x) * vec[2:3, :] + vec[3:4, :]).astype(bf)
            h2[span_of(r), :] = h
            cq[span_of(r), :] = (dot(h, weight(5)) * (LOG2E / 8)).astype(bf)

        if i == 1:
            put(x1, x1_out)
            put(h2, h2_out)
            put(cq, cq_out)

    def text_rows():
        loaded(6)
        loaded(7)
        ck[...] = dot(text[...], weight(6)).astype(bf)
        cv[...] = dot(text[...], weight(7)).astype(bf)
        put(ck, ck_out)
        put(cv, cv_out)

    def third_norm(i):
        if i == 0:
            put(o2, o2_out)
            put(lse2, lse2_out)
            loaded(8)

        @pl.loop(2 * i, 2 * i + 2)
        def _(r):
            x = x1[span_of(r), :] + dot(o2[span_of(r), :], weight(8))
            x2[span_of(r), :] = x
            h3[span_of(r), :] = (norm_parts(x) * vec[4:5, :] + vec[5:6, :]).astype(bf)

        if i == 1:
            put(x2, x2_out)
            put(h3, h3_out)

    pieces = [first_norm, lambda: project(1, q, LOG2E / 8, q_out), lambda: project(2, k, None, k_out), lambda: project(3, v, None, v_out)]
    pieces += [(self_attention, j) for j in range(count)] + [functools.partial(second_norm, i) for i in range(2)] + [text_rows]
    pieces += [(cross_attention, j) for j in range(count)] + [functools.partial(third_norm, i) for i in range(2)]

    for a in range(n):
        pltpu.make_async_copy(shards[a], near[a], local_sem.at[a]).start()
    exchange(block_in, x_in, 0, block_in.at[me])
    pltpu.make_async_copy(text_states.at[me], text, local_sem.at[n + 2]).start()
    pltpu.make_async_copy(out_grad.at[me], own_g, local_sem.at[n + 1]).start()
    for a in range(n):
        drain(near[a], local_sem.at[a])
    drain(own_g, local_sem.at[n + 1])
    for a in range(n):
        pltpu.make_async_copy(near[a], full[a].at[at.z, at.y, at.x, at.c], local_sem.at[a]).start()
    limit[0] = limits[me]
    begin = next(i for i, (_, step) in enumerate(FW_ORDER) if step > 0)

    def event(u, step):
        if u == -1:
            exchange(out_grad, g_out, 1, own_g)
        elif step == 4:
            load(u + 1)
        else:
            net.go(u, step)

    run_order(FW_ORDER[:begin], event, [])
    for a in range(n):
        drain(near[a], local_sem.at[a])
    drain(text, local_sem.at[n + 2])
    run_order(FW_ORDER[begin:], event, pieces)
    exchanged(g_out, 1)
    for u in range(8, 16):
        net.arrived(u)
    for u in range(len(FW_UNITS)):
        net.sent(u)
    drain(x_in.at[0:3], ex_send.at[0])
    drain(g_out.at[0:3], ex_send.at[1])
    for i, src in enumerate(keep):
        drain(src, out_sem.at[i])


def forward(dims, shards, block_in, out_grad, text_states, limits, cid):
    n = len(shards)
    bf, f32 = jnp.bfloat16, jnp.float32
    items, seg, width = block_in.shape
    rows, texts = items * seg, text_states.shape[1]
    wide, pairs = jax.ShapeDtypeStruct((rows, width), bf), width // 128
    short = jax.ShapeDtypeStruct((texts, width), bf)
    long = jax.ShapeDtypeStruct((rows, width), f32)
    sums = jax.ShapeDtypeStruct((pairs, 8, rows), f32)
    seg4 = jax.ShapeDtypeStruct(block_in.shape, bf)
    whole = [jax.ShapeDtypeStruct(tuple(dims) + s.shape, s.dtype) for s in shards]
    saved = [wide, wide, wide, wide, short, short, wide, wide, wide, wide, wide, long, long, sums, sums]
    out_shape = whole + [seg4, seg4] + saved + [jax.ShapeDtypeStruct((8, width), f32)]
    held = [pltpu.VMEM(s.shape, s.dtype) for s in [seg4] + saved + [short]] + [pltpu.VMEM(tuple(dims) + (16, 128), bf)]
    held += [pltpu.VMEM(s.shape, s.dtype) for s in whole[1:9]] + [pltpu.VMEM(s.shape, s.dtype) for s in shards]
    held += [pltpu.VMEM(block_in.shape[1:], bf)]
    units = len(FW_UNITS)
    any_spec = pl.BlockSpec(memory_space=ANY)
    outs = pl.pallas_call(
        functools.partial(forward_kernel, dims, n),
        out_shape=out_shape,
        in_specs=[any_spec] * (n + 3) + [pl.BlockSpec(memory_space=pltpu.SMEM)],
        out_specs=[any_spec] * (len(out_shape) - 1) + [pl.BlockSpec(memory_space=pltpu.VMEM)],
        scratch_shapes=held
        + [
            pltpu.SMEM((1,), jnp.int32),
            pltpu.SemaphoreType.DMA((2 * n + 8,)), pltpu.SemaphoreType.DMA((20,)),
            pltpu.SemaphoreType.DMA((units,)), pltpu.SemaphoreType.DMA((units, 4)),
            pltpu.SemaphoreType.DMA((2,)), pltpu.SemaphoreType.DMA((2,)),
        ],
        compiler_params=pltpu.CompilerParams(collective_id=cid, has_side_effects=True, vmem_limit_bytes=62 * 2**20),
        name="forward",
    )(*shards, block_in, out_grad, text_states, limits)
    full = [o.reshape((-1,) + o.shape[5:]) for o in outs[:n]]
    return full, outs[n:]
def run_order(order, event, pieces):
    i = 0
    while i < len(order):
        unit, step = order[i]
        i += 1
        if unit != -2:
            event(unit, step)
            continue
        piece = pieces[step]
        if callable(piece):
            piece()
            continue
        body, first = piece
        last, between = first, {first: []}
        while i < len(order):
            unit, step = order[i]
            if unit != -2:
                between[last].append((unit, step))
            else:
                piece = pieces[step]
                if callable(piece) or piece[0] is not body:
                    break
                last = piece[1]
                between[last] = []
            i += 1

        def one(j, body=body, between=between):
            body(j)
            for k, events in between.items():
                if events:
                    pl.when(j == k)(functools.partial(run_order, events, event, pieces))

        pl.loop(first, last + 1)(one)


class Scatter:
    def __init__(self, dims, send, recv, local):
        self.at, self.dims, self.send, self.recv, self.local, self.units = Place(dims), dims, send, recv, local, []

    def add(self, source, room, out, order, whole):
        self.units.append((source, room[0], room[1:], out, order, whole))

    def own(self, u, where):
        own, whole = self.units[u][1], self.units[u][5]
        return own.at[(*where, self.at.c)] if whole else own.at[tuple(where)]

    def left(self, u, k):
        where = [slice(None)] * 3
        for axis in self.units[u][4][:k]:
            where[axis] = (self.at.z, self.at.y, self.at.x)[axis]
        return where

    def add_in(self, u, k, bufs):
        where = self.left(u, k)
        open_axes = [axis for axis in range(3) if axis not in self.units[u][4][:k]]

        def one(index):
            spot = list(where)
            for axis, i in zip(open_axes, index):
                spot[axis] = i
            dst = self.own(u, spot)
            if len(bufs) == 1:
                dst[...] = dst[...] + bufs[0][tuple(index)]
            else:
                total = dst[...].astype(jnp.float32)
                for buf in bufs:
                    total = total + buf[tuple(index)].astype(jnp.float32)
                dst[...] = total.astype(dst.dtype)

        sizes = [self.dims[axis] for axis in open_axes]
        inner = list(itertools.product(*[range(n) for n in sizes[1:]]))

        @pl.loop(0, sizes[0])
        def _(i):
            for rest in inner:
                one((i, *rest))

    def bufs(self, u, k):
        buf = self.units[u][2][k]
        return [buf.at[i] for i in range(self.dims[0] - 1)] if self.units[u][4][k - 1] == 0 else [buf]

    def go(self, u, k):
        source, own, room, out, order, whole = self.units[u]
        at, every = self.at, slice(None)
        if k == 0:
            if not whole:
                pltpu.make_async_copy(source(every, every, every, at.c), own, self.local.at[u]).start()
            push(source(every, every, every, 1 - at.c), room[0], self.send.at[u], self.recv.at[u, 0], at.dev(c=1 - at.c))
            return
        drain(room[k - 1], self.recv.at[u, k - 1])
        if k == 4:
            total = self.own(u, (at.z, at.y, at.x))[...].astype(jnp.float32)
            for buf in self.bufs(u, 3):
                total = total + buf[...].astype(jnp.float32)
            out[...] = total
            for block in room:
                drain(block, self.send.at[u])
            return
        if k == 1:
            if not whole:
                drain(own, self.local.at[u])
            self.add_in(u, 0, [room[0]])
        else:
            self.add_in(u, k - 1, self.bufs(u, k - 1))
        where = self.left(u, k - 1)
        axis = order[k - 1]
        if axis == 0:
            for z in at.z_others():
                where[0] = z
                slot = lax.rem(z - at.z + self.dims[0], self.dims[0]) - 1
                push(self.own(u, where), room[k].at[slot], self.send.at[u], self.recv.at[u, k], at.dev(z=z))
        else:
            where[axis] = (None, 1 - at.y, 1 - at.x)[axis]
            device = at.dev(y=1 - at.y) if axis == 1 else at.dev(x=1 - at.x)
            push(self.own(u, where), room[k], self.send.at[u], self.recv.at[u, k], device)


def scatter_room(dims, tile, dtype, order, whole):
    nz, ny, nx, nc = dims
    rooms = [((nz, ny, nx, nc) if whole else (nz, ny, nx)) + tile, (nz, ny, nx) + tile]
    for k in range(3):
        lead = tuple(dims[axis] for axis in range(3) if axis not in order[: k + 1])
        rooms.append(((nz - 1,) if order[k] == 0 else ()) + lead + tile)
    return [pltpu.VMEM(shape, dtype) for shape in rooms]


def norm_back(x, dh, gain):
    center = x - jnp.mean(x, axis=-1, keepdims=True)
    r = lax.rsqrt(jnp.mean(center * center, axis=-1, keepdims=True) + EPS)
    n = center * r
    dn = dh * gain
    dx = r * (dn - jnp.mean(dn, axis=-1, keepdims=True) - n * jnp.mean(dn * n, axis=-1, keepdims=True))
    return dx, dh * n


def row_sum(rows):
    return jnp.sum(rows, axis=0, keepdims=True)


TN = (((0,), (0,)), ((), ()))


MIDDLE_PATHS = (
    (0, 2, 1), (1, 0, 2), (1, 0, 2), (1, 2, 0), (2, 1, 0), (2, 1, 0),
)
MIDDLE_ORDER = (
    (0, 0), (1, 0), (2, 0), (3, 0), (4, 0), (-2, 0), (0, 1), (1, 1), (-2, 1), (2, 1), (3, 1), (4, 1), (-2, 2),
    (5, 0), (-2, 3), (-2, 4), (5, 1), (-2, 5), (1, 2), (-2, 6), (-2, 7), (-2, 8), (-2, 9), (-2, 10), (-2, 11),
    (0, 2), (2, 2), (4, 2), (-2, 12), (-2, 13), (1, 3), (3, 2), (5, 2), (-2, 14), (4, 3), (0, 3), (1, 4), (-2, 15),
    (2, 3), (5, 3), (3, 3), (0, 4), (4, 4), (5, 4), (2, 4), (3, 4),
)
LAST_SPLIT = 640
LAST_PATHS = (
    (0, 2, 1), (1, 0, 2), (2, 0, 1), (2, 1, 0), (1, 2, 0), (2, 1, 0), (2, 1, 0), (0, 1, 2), (1, 0, 2), (1, 0, 2),
    (0, 1, 2),
)
LAST_ORDER = (
    (0, 0), (1, 0), (2, 0), (3, 0), (-2, 0), (0, 1), (-2, 1), (1, 1), (2, 1), (3, 1), (-2, 2), (-2, 3), (-2, 4),
    (-2, 5), (1, 2), (2, 2), (-2, 6), (4, 0), (5, 0), (6, 0), (0, 2), (-2, 7), (3, 2), (4, 1), (5, 1), (6, 1),
    (0, 3), (-2, 8), (1, 3), (-2, 9), (3, 3), (-2, 10), (7, 0), (8, 0), (9, 0), (5, 2), (2, 3), (-2, 11), (4, 2),
    (7, 1), (8, 1), (0, 4), (9, 1), (6, 2), (1, 4), (-2, 12), (3, 4), (5, 3), (2, 4), (-2, 13), (-2, 14), (8, 2),
    (-2, 15), (10, 0), (7, 2), (9, 2), (10, 1), (5, 4), (6, 3), (4, 3), (7, 3), (8, 3), (9, 3), (10, 2), (10, 3),
    (6, 4), (7, 4), (8, 4), (9, 4), (10, 4), (4, 4),
)


def middle_kernel(dims, *refs):
    (g_in, dh_in, x2_in, x1_in, vec, o2_in, cq_in, ck_in, cv_in, lse_in, h2_in, o_in, wco_in, wcq_in, wck_in, wcv_in, wo_in,
     text_in, limits, block_in, down_in, up_in) = refs[:22]
    block_out, text_out, dx_out, do_out, gcq_out, gck_out, gcv_out, go_out, sums, down_out, up_out, co_out = refs[22:34]
    (x2, dh3, dx, g, dy, do, o2, wco, cq, dcq, wcq, wck, wcv, ck, cv, dck, dcv, lse, text, tg, stage, dk_acc, dv_acc, limit,
     load_sem, out_sem, ex_send, ex_recv, send, recv, local, own_rows) = refs[34:66]
    rooms = refs[66:]
    at = Place(dims)
    nz = dims[0]
    oy, ox, oc, me = 1 - at.y, 1 - at.x, 1 - at.c, at.seq
    hello([at.dev(z=p) for p in at.z_others()] + [at.dev(y=oy), at.dev(x=ox), at.dev(c=oc), at.dev(x=ox, c=oc)])
    others = ((ox, at.c), (ox, oc), (at.x, oc))
    rows, width = g.shape
    block = 256
    f32, bf = jnp.float32, jnp.bfloat16
    every = slice(None)
    net = Scatter(dims, send, recv, local)
    quarter = width // 4
    room = [rooms[5 * j : 5 * j + 5] for j in range(6)]
    for j in range(4):
        cols = pl.ds(j * quarter, quarter)
        net.add(lambda *w, cols=cols: down_in.at[(*w, every, cols)], room[j], down_out.at[:, cols], MIDDLE_PATHS[j], False)
    net.add(lambda *w: up_in.at[w], room[4], up_out, MIDDLE_PATHS[4], False)
    net.add(lambda *w: room[5][0].at[w], room[5], co_out, MIDDLE_PATHS[5], True)

    def exchange(src, dst, i, own):
        for px, pc in others:
            push(src.at[px * 2 + pc], dst.at[me], ex_send.at[i], ex_recv.at[i], at.dev(x=px, c=pc))
        pltpu.make_async_copy(own, dst.at[me], local.at[6 + i]).start()

    started = []

    def load(src, dst):
        pltpu.make_async_copy(src, dst, load_sem.at[len(started)]).start()
        started.append(dst)
        return len(started) - 1

    def loaded(i):
        drain(started[i], load_sem.at[i])

    kept = []

    def put(src, dst):
        pltpu.make_async_copy(src, dst, out_sem.at[len(kept)]).start()
        kept.append(src)
        return len(kept) - 1

    def kept_done(i):
        drain(kept[i], out_sem.at[i])

    def span_of(r):
        return pl.ds(pl.multiple_of(r * block, block), block)

    def weight_grad(src, grad, made):
        @pl.loop(0, nz)
        def _(a):
            part = dot(src[:, pl.ds(pl.multiple_of(a * block, block), block)], grad[...], TN).astype(bf)
            made[a] = part.reshape(made.shape[1:])

    own_load = load(block_in.at[me], own_rows)
    first = [load(dh_in, dh3), load(x2_in, x2), load(g_in, g), load(wco_in, wco), load(o2_in, o2)]
    second = [load(cq_in, cq), load(ck_in, ck), load(cv_in, cv), load(lse_in, lse)]
    third = [load(text_in.at[me], text), load(wcq_in, wcq), load(wck_in, wck), load(wcv_in, wcv)]
    limit[0] = limits[me]
    run_order(MIDDLE_ORDER[:5], net.go, [])
    loaded(own_load)
    exchange(block_in, block_out, 0, own_rows)
    for i in first:
        loaded(i)
    sums[...] = jnp.zeros_like(sums)

    def last_norm(r):
        span = span_of(r)
        d = dh3[span, :]
        grad, gain_terms = norm_back(x2[span, :], d, vec[4:5, :])
        sums[4:5, :] += row_sum(gain_terms)
        sums[5:6, :] += row_sum(d)
        total = g[span, :].astype(f32) + grad
        dx[span, :] = total
        low = total.astype(bf)
        dy[span, :] = low
        do[span, :] = dot(low, wco[...], NT).astype(bf)

    def middle_norm(r):
        span = span_of(r)
        d = dot(dcq[span, :], wcq[...], NT)
        grad, gain_terms = norm_back(x2[span, :], d, vec[2:3, :])
        sums[2:3, :] += row_sum(gain_terms)
        sums[3:4, :] += row_sum(d)
        total = dx[span, :] + grad
        dx[span, :] = total
        low = total.astype(bf)
        dy[span, :] = low
        do[span, :] = dot(low, cq[...], NT).astype(bf)

    later = {}

    def after_last_norm():
        pl.loop(2, 4)(last_norm)
        later["x1"], later["o"], later["h2"] = load(x1_in, x2), load(o_in, g), load(h2_in, wco)

    def output_weight_grad():
        weight_grad(o2, dy, room[5][0])
        for i in second:
            loaded(i)

    def cross(j):
        cols = pl.ds(pl.multiple_of(j * 128, 128), 128)
        attend_back_kernel(
            False, 512, limit, cq.at[:, cols], ck.at[:, cols], cv.at[:, cols], do.at[:, cols], o2.at[:, cols], lse.at[pl.ds(j, 1)],
            dcq.at[:, cols], dck.at[:, cols], dcv.at[:, cols], dk_acc, dv_acc,
        )

    def query_weight_grad():
        later["wo"] = load(wo_in, cq)
        for i in third:
            loaded(i)
        loaded(later["h2"])
        weight_grad(wco, dcq, stage.at[0])
        later["cq"] = put(stage.at[0], gcq_out)
        loaded(later["x1"])
        loaded(later["wo"])

    def after_middle_norm():
        pl.loop(2, 4)(middle_norm)
        put(dx, dx_out)
        put(do, do_out)

    def self_weight_grad():
        loaded(later["o"])
        weight_grad(g, dy, stage.at[1])
        later["o"] = put(stage.at[1], go_out)

    def text_weight_grads():
        tg[...] = (dot(dck[...], wck[...], NT) + dot(dcv[...], wcv[...], NT)).reshape(tg.shape)
        exchange(tg, text_out, 1, tg.at[me])
        kept_done(later["cq"])
        weight_grad(text, dck, stage.at[0])
        put(stage.at[0], gck_out)
        kept_done(later["o"])
        weight_grad(text, dcv, stage.at[1])
        put(stage.at[1], gcv_out)

    pieces = [lambda: pl.loop(0, 2)(last_norm), after_last_norm, output_weight_grad]
    pieces += [(cross, j) for j in range(width // 128)]
    pieces += [query_weight_grad, lambda: pl.loop(0, 2)(middle_norm), after_middle_norm, self_weight_grad, text_weight_grads]
    run_order(MIDDLE_ORDER[5:], net.go, pieces)
    for i, dst in ((0, block_out), (1, text_out)):
        drain(dst.at[0:3], ex_recv.at[i])
        drain(dst.at[0:3], ex_send.at[i])
        drain(dst.at[0], local.at[6 + i])
    for i in range(len(kept)):
        if i not in (later["cq"], later["o"]):
            kept_done(i)


def middle(dims, args, cid):
    nz, ny, nx, nc = dims
    g, dh, x2, x1, vec, o2, cq, ck, cv, lse, h2, o, wco, wcq, wck, wcv, wo, text, limits, block_out, down, up = args
    rows, width = g.shape
    texts = text.shape[1]
    devices = nz * ny * nx * nc
    bf, f32 = jnp.bfloat16, jnp.float32
    each = width // devices
    long = down.shape[0] // devices
    down = down.reshape(nz, ny, nx, nc, long, width)
    up = up.reshape(nz, ny, nx, nc, each, up.shape[1])
    seg = block_out.shape
    held = jax.ShapeDtypeStruct((nz, ny, nx, nc, each, width), bf)
    wide, deep = jax.ShapeDtypeStruct((rows, width), bf), jax.ShapeDtypeStruct((rows, width), f32)
    out_shape = [
        jax.ShapeDtypeStruct(seg, bf), jax.ShapeDtypeStruct((seg[0], texts // seg[0], width), f32), deep, wide, held, held, held, held,
        jax.ShapeDtypeStruct((8, width), f32), jax.ShapeDtypeStruct((long, width), f32), jax.ShapeDtypeStruct((each, up.shape[5]), f32),
        jax.ShapeDtypeStruct((each, width), f32),
    ]
    any_spec, vm = pl.BlockSpec(memory_space=ANY), pl.BlockSpec(memory_space=pltpu.VMEM)
    big, square, short = pltpu.VMEM((rows, width), f32), pltpu.VMEM((rows, width), bf), pltpu.VMEM((texts, width), bf)
    dma = pltpu.SemaphoreType.DMA
    scratch = [big, big, big] + [square] * 10 + [short] * 4 + [pltpu.VMEM(lse.shape, f32), short]
    scratch += [pltpu.VMEM((seg[0], texts // seg[0], width), f32), pltpu.VMEM((2,) + held.shape, bf)]
    scratch += [pltpu.VMEM((texts, 128), f32)] * 2 + [pltpu.SMEM((1,), jnp.int32)]
    scratch += [dma((20,)), dma((12,)), dma((2,)), dma((2,)), dma((6,)), dma((6, 4)), dma((8,)), pltpu.VMEM(seg[1:], bf)]
    for j in range(4):
        scratch += scatter_room(dims, (long, width // 4), bf, MIDDLE_PATHS[j], False)
    scratch += scatter_room(dims, (each, up.shape[5]), bf, MIDDLE_PATHS[4], False)
    scratch += scatter_room(dims, (each, width), bf, MIDDLE_PATHS[5], True)
    specs = [any_spec] * 4 + [vm] + [any_spec] * 13 + [pl.BlockSpec(memory_space=pltpu.SMEM)] + [any_spec] * 3
    return pl.pallas_call(
        functools.partial(middle_kernel, dims),
        out_shape=out_shape,
        in_specs=specs,
        out_specs=[any_spec] * 8 + [vm] * 4,
        scratch_shapes=scratch,
        compiler_params=pltpu.CompilerParams(collective_id=cid, has_side_effects=True, vmem_limit_bytes=63 * 2**20),
        name="middle",
    )(g, dh, x2, x1, vec, o2, cq, ck, cv, lse, h2, o, wco, wcq, wck, wcv, wo, text, limits, block_out, down, up)


def last_kernel(dims, *refs):
    q_in, k_in, v_in, do_in, o_in, lse_in, h1_in, wq_in, wk_in, wv_in, x_in, dx_in, vec, gcq, gck, gcv, go, sums_in = refs[:18]
    grad_out, cq_out, ck_out, cv_out, o_out, q_out, k_out, v_out, small_out = refs[18:27]
    (q, k, v, do, o, lse, h_t, dq, dk, dv, dx, send_rows, small, dk_acc, dv_acc, sums,
     load_sem, ex_send, ex_recv, send, recv, local) = refs[27:49]
    rooms = refs[49:]
    at = Place(dims)
    nz, ny, nx, nc = dims
    oy, ox, oc, me = 1 - at.y, 1 - at.x, 1 - at.c, at.seq
    hello([at.dev(z=p) for p in at.z_others()] + [at.dev(y=oy), at.dev(x=ox), at.dev(c=oc), at.dev(x=ox, c=oc)])
    rows, width = q.shape
    block = 256
    f32, bf = jnp.float32, jnp.bfloat16
    every = slice(None)
    net = Scatter(dims, send, recv, local)
    room = [rooms[5 * j : 5 * j + 5] for j in range(10)] + [[small, *rooms[50:54]]]
    for j, (src, out) in enumerate(((gcq, cq_out), (gck, ck_out), (gcv, cv_out), (go, o_out))):
        net.add(lambda *w, src=src: src.at[w], room[j], out, LAST_PATHS[j], False)
    parts = ((0, LAST_SPLIT), (LAST_SPLIT, width - LAST_SPLIT))
    for j in range(6):
        out = (q_out, k_out, v_out)[j % 3].at[:, pl.ds(*parts[j // 3])]
        net.add(lambda *w, held=room[4 + j][0]: held.at[w], room[4 + j], out, LAST_PATHS[4 + j], True)
    net.add(lambda *w: small.at[w], room[10], small_out, LAST_PATHS[10], True)
    run_order(LAST_ORDER[:4], net.go, [])
    started = []

    def load(src, dst):
        pltpu.make_async_copy(src, dst, load_sem.at[len(started)]).start()
        started.append(dst)
        return len(started) - 1

    def loaded(i):
        drain(started[i], load_sem.at[i])

    first = [load(a, b) for a, b in ((q_in, q), (k_in, k), (v_in, v), (do_in, do), (o_in, o), (lse_in, lse), (h1_in, dq), (dx_in, dx))]

    def transpose():
        for i in first:
            loaded(i)

        @pl.loop(0, rows // block)
        def _(r):
            span = pl.ds(pl.multiple_of(r * block, block), block)
            h_t[:, span] = dq[span, :].T

    def pair(j):
        cols = pl.ds(pl.multiple_of(j * 128, 128), 128)
        attend_back_kernel(
            True, 256, None, q.at[:, cols], k.at[:, cols], v.at[:, cols], do.at[:, cols], o.at[:, cols], lse.at[pl.ds(j, 1)],
            dq.at[:, cols], dk.at[:, cols], dv.at[:, cols], dk_acc, dv_acc,
        )

    weights = []

    def weight_grads(part):
        if part == 1:
            weights.extend(load(a, b) for a, b in ((wq_in, q), (wk_in, k), (wv_in, v), (x_in, do)))
        for j, grad in enumerate((dq, dk, dv)):
            made = room[4 + 3 * part + j][0]

            @pl.loop(0, nz)
            def _(a, made=made, grad=grad):
                span = pl.ds(pl.multiple_of(a * block, block), block)
                product = dot(h_t[span, :], grad[:, pl.ds(*parts[part])]).astype(bf)
                made[a] = product.reshape(made.shape[1:])

        if part == 1:
            for i in weights:
                loaded(i)
            sums[...] = sums_in[...]

    def last_norm(r):
        span = pl.ds(pl.multiple_of(r * block, block), block)
        d = dot(dq[span, :], q[...], NT) + dot(dk[span, :], k[...], NT) + dot(dv[span, :], v[...], NT)
        grad, gain_terms = norm_back(do[span, :].astype(f32), d, vec[0:1, :])
        sums[0:1, :] += row_sum(gain_terms)
        sums[1:2, :] += row_sum(d)
        send_rows[r] = (dx[span, :] + grad).astype(bf)

    targets = ((ox, at.c), (ox, oc), (at.x, oc), (at.x, at.c))

    def send_norm(i):
        px, pc = targets[i]
        last_norm(px * 2 + pc)
        if i < 3:
            push(send_rows.at[px * 2 + pc], grad_out.at[me], ex_send, ex_recv, at.dev(x=px, c=pc))
        else:
            pltpu.make_async_copy(send_rows.at[me], grad_out.at[me], local.at[11]).start()

    def share_sums():
        devices = nz * ny * nx * nc
        piece = width // devices
        lanes = lax.broadcasted_iota(jnp.int32, (width, 128), 0)
        fold = jnp.where(lax.rem(lanes, piece) == lax.broadcasted_iota(jnp.int32, (width, 128), 1), 1.0, 0.0).astype(bf)
        mine = lax.div(lax.broadcasted_iota(jnp.int32, (devices, width), 1), piece) == lax.broadcasted_iota(jnp.int32, (devices, width), 0)
        shares = []
        for i in range(6):
            spread = jnp.where(mine, sums[i : i + 1, :], 0.0)
            total = jnp.zeros((devices, 128), f32)
            for _ in range(3):
                low = spread.astype(bf)
                spread = spread - low.astype(f32)
                total = total + dot(low, fold)
            shares.append(total[:, None, :])
        shares.append(jnp.zeros((devices, 2, 128), f32))
        small[...] = jnp.concatenate(shares, axis=1).reshape(small.shape)

    split = LAST_SPLIT // 128
    pieces = [transpose] + [(pair, j) for j in range(split)] + [lambda: weight_grads(0)]
    pieces += [(pair, j) for j in range(split, width // 128)] + [lambda: weight_grads(1)]
    pieces += [functools.partial(send_norm, i) for i in range(4)] + [share_sums]
    run_order(LAST_ORDER[4:], net.go, pieces)
    drain(grad_out.at[0:3], ex_recv)
    drain(grad_out.at[0:3], ex_send)
    drain(grad_out.at[0], local.at[11])


def last(dims, args, cid):
    nz, ny, nx, nc = dims
    q, k, v, do, o, lse, h1, wq, wk, wv, x, dx, vec, gcq, gck, gcv, go, sums = args
    rows, width = q.shape
    bf, f32 = jnp.bfloat16, jnp.float32
    each = width // (nz * ny * nx * nc)
    shard = jax.ShapeDtypeStruct((each, width), f32)
    out_shape = [jax.ShapeDtypeStruct((4, rows // 4, width), bf)] + [shard] * 7 + [jax.ShapeDtypeStruct((8, 128), f32)]
    any_spec, vm = pl.BlockSpec(memory_space=ANY), pl.BlockSpec(memory_space=pltpu.VMEM)
    square = pltpu.VMEM((rows, width), bf)
    dma = pltpu.SemaphoreType.DMA
    scratch = [square] * 5 + [pltpu.VMEM(lse.shape, f32)] + [square] * 4 + [pltpu.VMEM((rows, width), f32), pltpu.VMEM((4, rows // 4, width), bf)]
    scratch += [pltpu.VMEM((nz, ny, nx, nc, 8, 128), f32)] + [pltpu.VMEM((rows, 128), f32)] * 2 + [pltpu.VMEM((8, width), f32)]
    scratch += [dma((16,)), dma, dma, dma((11,)), dma((11, 4)), dma((12,))]
    for j in range(4):
        scratch += scatter_room(dims, (each, width), bf, LAST_PATHS[j], False)
    for j in range(6):
        scratch += scatter_room(dims, (each, LAST_SPLIT if j < 3 else width - LAST_SPLIT), bf, LAST_PATHS[4 + j], True)
    scratch += scatter_room(dims, (8, 128), f32, LAST_PATHS[10], True)[1:]
    return pl.pallas_call(
        functools.partial(last_kernel, dims),
        out_shape=out_shape,
        in_specs=[any_spec] * 12 + [vm] + [any_spec] * 4 + [vm],
        out_specs=[any_spec] + [vm] * 8,
        scratch_shapes=scratch,
        compiler_params=pltpu.CompilerParams(collective_id=cid, has_side_effects=True, vmem_limit_bytes=63 * 2**20),
        name="last",
    )(q, k, v, do, o, lse, h1, wq, wk, wv, x, dx, vec, gcq, gck, gcv, go, sums)

HEAD_DIM = 64


EPS = 1e-05


def norm_rows(values_in, gain, bias):
    center = values_in - jnp.mean(values_in, axis=-1, keepdims=True)
    spread = jnp.mean(center * center, axis=-1, keepdims=True)
    return center * lax.rsqrt(spread + EPS) * gain + bias


def contract_rows(left, right):
    return lax.dot_general(
        left, right, (((0,), (0,)), ((), ())), preferred_element_type=jnp.float32
    )


def times_transposed(left, right):
    return lax.dot_general(
        left, right, (((1,), (1,)), ((), ())), preferred_element_type=jnp.float32
    )


def product(left, right):
    return jnp.dot(left, right, preferred_element_type=jnp.float32)


def local_plain(
    block_in,
    text_states,
    caption_len,
    out_grad,
    first_gain,
    first_bias,
    query_weight,
    key_weight,
    value_weight,
    output_weight,
    second_gain,
    second_bias,
    cross_query,
    cross_key,
    cross_value,
    cross_output,
    third_gain,
    third_bias,
    up_weight,
    down_weight,
):
    gathered = (
        lax.all_gather(first_gain, ("dp", "seq"), axis=0, tiled=True),
        lax.all_gather(first_bias, ("dp", "seq"), axis=0, tiled=True),
        lax.all_gather(query_weight, ("dp", "seq"), axis=0, tiled=True),
        lax.all_gather(key_weight, ("dp", "seq"), axis=0, tiled=True),
        lax.all_gather(value_weight, ("dp", "seq"), axis=0, tiled=True),
        lax.all_gather(output_weight, ("dp", "seq"), axis=0, tiled=True),
        lax.all_gather(second_gain, ("dp", "seq"), axis=0, tiled=True),
        lax.all_gather(second_bias, ("dp", "seq"), axis=0, tiled=True),
        lax.all_gather(cross_query, ("dp", "seq"), axis=0, tiled=True),
        lax.all_gather(cross_key, ("dp", "seq"), axis=0, tiled=True),
        lax.all_gather(cross_value, ("dp", "seq"), axis=0, tiled=True),
        lax.all_gather(cross_output, ("dp", "seq"), axis=0, tiled=True),
        lax.all_gather(third_gain, ("dp", "seq"), axis=0, tiled=True),
        lax.all_gather(third_bias, ("dp", "seq"), axis=0, tiled=True),
        lax.all_gather(up_weight, ("dp", "seq"), axis=0, tiled=True),
        lax.all_gather(down_weight, ("dp", "seq"), axis=0, tiled=True),
    )
    (
        gain_one,
        bias_one,
        w_query,
        w_key,
        w_value,
        w_output,
        gain_two,
        bias_two,
        w_cquery,
        w_ckey,
        w_cvalue,
        w_coutput,
        gain_three,
        bias_three,
        w_up,
        w_down,
    ) = gathered
    item_count, seg_len, model_width = block_in.shape
    row_count = item_count * seg_len
    head_count = model_width // HEAD_DIM
    score_scale = HEAD_DIM ** (-0.5)
    text_count = text_states.shape[1]
    inputs_f = block_in.astype(jnp.float32).reshape(row_count, model_width)
    normed_one, pull_one = jax.vjp(
        norm_rows, inputs_f, gain_one.astype(jnp.float32), bias_one.astype(jnp.float32)
    )
    normed_one = normed_one.astype(jnp.bfloat16)
    query_rows = product(normed_one, w_query).astype(jnp.bfloat16)
    key_rows = product(normed_one, w_key).astype(jnp.bfloat16)
    value_rows = product(normed_one, w_value).astype(jnp.bfloat16)
    key_all, value_all = (
        lax.all_gather(
            key_rows.reshape(item_count, seg_len, model_width), "seq", axis=1, tiled=True
        ),
        lax.all_gather(
            value_rows.reshape(item_count, seg_len, model_width), "seq", axis=1, tiled=True
        ),
    )
    key_count = key_all.shape[1]
    first_pos = lax.axis_index("seq") * seg_len
    query_pos = first_pos + jnp.arange(seg_len, dtype=jnp.int32)
    causal = jnp.arange(key_count, dtype=jnp.int32)[None, :] <= query_pos[:, None]

    def self_scores(query_item, key_item):
        query_heads = query_item.reshape(seg_len, head_count, HEAD_DIM)
        key_heads = key_item.reshape(key_count, head_count, HEAD_DIM)
        scores = jnp.einsum(
            "qhd,khd->hqk", query_heads, key_heads, preferred_element_type=jnp.float32
        )
        return jnp.where(causal[None, :, :], scores * score_scale, -1e30)

    def self_forward(operands):
        query_item, key_item, value_item = operands
        scores = self_scores(query_item, key_item)
        row_peak = jnp.max(scores, axis=-1, keepdims=True)
        row_total = jnp.sum(jnp.exp(scores - row_peak), axis=-1, keepdims=True)
        log_total = row_peak + jnp.log(row_total)
        prob_bf = jnp.exp(scores - log_total).astype(jnp.bfloat16)
        value_heads = value_item.reshape(key_count, head_count, HEAD_DIM)
        mixed = jnp.einsum("hqk,khd->qhd", prob_bf, value_heads, preferred_element_type=jnp.float32)
        return (mixed.reshape(seg_len, model_width).astype(jnp.bfloat16), log_total)

    attended, log_totals = lax.map(
        self_forward, (query_rows.reshape(item_count, seg_len, model_width), key_all, value_all)
    )
    attended_rows = attended.reshape(row_count, model_width)
    after_self = inputs_f + product(attended_rows, w_output)
    normed_two, pull_two = jax.vjp(
        norm_rows, after_self, gain_two.astype(jnp.float32), bias_two.astype(jnp.float32)
    )
    normed_two = normed_two.astype(jnp.bfloat16)
    cross_rows = product(normed_two, w_cquery).astype(jnp.bfloat16)
    cross_heads = cross_rows.reshape(item_count, seg_len, head_count, HEAD_DIM)
    text_keys = jnp.einsum(
        "itc,cd->itd", text_states, w_ckey, preferred_element_type=jnp.float32
    ).astype(jnp.bfloat16)
    text_values = jnp.einsum(
        "itc,cd->itd", text_states, w_cvalue, preferred_element_type=jnp.float32
    ).astype(jnp.bfloat16)
    text_kheads = text_keys.reshape(item_count, text_count, head_count, HEAD_DIM)
    text_vheads = text_values.reshape(item_count, text_count, head_count, HEAD_DIM)
    text_mask = jnp.arange(text_count, dtype=jnp.int32)[None, :] < caption_len[:, None]
    cross_scores = jnp.einsum(
        "iqhd,ithd->ihqt", cross_heads, text_kheads, preferred_element_type=jnp.float32
    )
    cross_scores = jnp.where(text_mask[:, None, None, :], cross_scores * score_scale, -1e30)
    cross_peak = jnp.max(cross_scores, axis=-1, keepdims=True)
    cross_exp = jnp.exp(cross_scores - cross_peak)
    cross_prob = cross_exp / jnp.sum(cross_exp, axis=-1, keepdims=True)
    cross_prob_bf = cross_prob.astype(jnp.bfloat16)
    crossed = jnp.einsum(
        "ihqt,ithd->iqhd", cross_prob_bf, text_vheads, preferred_element_type=jnp.float32
    )
    crossed_rows = crossed.reshape(row_count, model_width).astype(jnp.bfloat16)
    after_cross = after_self + product(crossed_rows, w_coutput)
    normed_three, pull_three = jax.vjp(
        norm_rows, after_cross, gain_three.astype(jnp.float32), bias_three.astype(jnp.float32)
    )
    normed_three = normed_three.astype(jnp.bfloat16)
    hidden = product(normed_three, w_up)
    activated, pull_gelu = jax.vjp(lambda inner: jax.nn.gelu(inner, approximate=False), hidden)
    activated = activated.astype(jnp.bfloat16)
    layer_out = after_cross + product(activated, w_down)
    block_out = layer_out.astype(jnp.bfloat16).reshape(item_count, seg_len, model_width)
    back_weights = (
        lax.all_gather(first_gain, ("dp", "seq"), axis=0, tiled=True),
        lax.all_gather(first_bias, ("dp", "seq"), axis=0, tiled=True),
        lax.all_gather(query_weight, ("dp", "seq"), axis=0, tiled=True),
        lax.all_gather(key_weight, ("dp", "seq"), axis=0, tiled=True),
        lax.all_gather(value_weight, ("dp", "seq"), axis=0, tiled=True),
        lax.all_gather(output_weight, ("dp", "seq"), axis=0, tiled=True),
        lax.all_gather(second_gain, ("dp", "seq"), axis=0, tiled=True),
        lax.all_gather(second_bias, ("dp", "seq"), axis=0, tiled=True),
        lax.all_gather(cross_query, ("dp", "seq"), axis=0, tiled=True),
        lax.all_gather(cross_key, ("dp", "seq"), axis=0, tiled=True),
        lax.all_gather(cross_value, ("dp", "seq"), axis=0, tiled=True),
        lax.all_gather(cross_output, ("dp", "seq"), axis=0, tiled=True),
        lax.all_gather(third_gain, ("dp", "seq"), axis=0, tiled=True),
        lax.all_gather(third_bias, ("dp", "seq"), axis=0, tiled=True),
        lax.all_gather(up_weight, ("dp", "seq"), axis=0, tiled=True),
        lax.all_gather(down_weight, ("dp", "seq"), axis=0, tiled=True),
    )
    (
        unused_gain,
        unused_bias,
        w_query,
        w_key,
        w_value,
        w_output,
        unused_gtwo,
        unused_btwo,
        w_cquery,
        w_ckey,
        w_cvalue,
        w_coutput,
        unused_gthree,
        unused_bthree,
        w_up,
        w_down,
    ) = back_weights
    grad_rows = out_grad.reshape(row_count, model_width)
    down_part = contract_rows(activated, grad_rows)
    act_grad = times_transposed(grad_rows, w_down)
    hidden_grad = pull_gelu(act_grad)[0].astype(jnp.bfloat16)
    up_part = contract_rows(normed_three, hidden_grad)
    normed_three_grad = times_transposed(hidden_grad, w_up)
    resid_three, gain_three_part, bias_three_part = pull_three(normed_three_grad)
    cross_grad = grad_rows.astype(jnp.float32) + resid_three
    cross_out_bf = cross_grad.astype(jnp.bfloat16)
    coutput_part = contract_rows(crossed_rows, cross_out_bf)
    crossed_grad = times_transposed(cross_out_bf, w_coutput).astype(jnp.bfloat16)
    crossed_heads = crossed_grad.reshape(item_count, seg_len, head_count, HEAD_DIM)
    cross_dprob = jnp.einsum(
        "iqhd,ithd->ihqt", crossed_heads, text_vheads, preferred_element_type=jnp.float32
    )
    cross_dscore = cross_prob * (
        cross_dprob - jnp.sum(cross_dprob * cross_prob, axis=-1, keepdims=True)
    )
    cross_dscore = cross_dscore.astype(jnp.bfloat16)
    cquery_grad = (
        (
            jnp.einsum(
                "ihqt,ithd->iqhd", cross_dscore, text_kheads, preferred_element_type=jnp.float32
            )
            * score_scale
        )
        .astype(jnp.bfloat16)
        .reshape(row_count, model_width)
    )
    tkey_part = (
        jnp.einsum("ihqt,iqhd->ithd", cross_dscore, cross_heads, preferred_element_type=jnp.float32)
        * score_scale
    ).reshape(item_count, text_count, model_width)
    tvalue_part = jnp.einsum(
        "ihqt,iqhd->ithd", cross_prob_bf, crossed_heads, preferred_element_type=jnp.float32
    ).reshape(item_count, text_count, model_width)
    cquery_part = contract_rows(normed_two, cquery_grad)
    normed_two_grad = times_transposed(cquery_grad, w_cquery)
    resid_two, gain_two_part, bias_two_part = pull_two(normed_two_grad)
    self_grad = cross_grad + resid_two
    self_out_bf = self_grad.astype(jnp.bfloat16)
    output_part = contract_rows(attended_rows, self_out_bf)
    attended_grad = times_transposed(self_out_bf, w_output).astype(jnp.bfloat16)
    query_items = query_rows.reshape(item_count, seg_len, model_width)
    dout_items = attended_grad.reshape(item_count, seg_len, model_width)

    def self_backward(operands):
        query_item, key_item, value_item, dout_item, log_total = operands
        scores = self_scores(query_item, key_item)
        probs = jnp.exp(scores - log_total)
        prob_bf = probs.astype(jnp.bfloat16)
        query_heads = query_item.reshape(seg_len, head_count, HEAD_DIM)
        key_heads = key_item.reshape(key_count, head_count, HEAD_DIM)
        value_heads = value_item.reshape(key_count, head_count, HEAD_DIM)
        dout_heads = dout_item.reshape(seg_len, head_count, HEAD_DIM)
        dprob = jnp.einsum(
            "qhd,khd->hqk", dout_heads, value_heads, preferred_element_type=jnp.float32
        )
        dscore = (probs * (dprob - jnp.sum(dprob * probs, axis=-1, keepdims=True))).astype(
            jnp.bfloat16
        )
        dquery = (
            (
                jnp.einsum("hqk,khd->qhd", dscore, key_heads, preferred_element_type=jnp.float32)
                * score_scale
            )
            .astype(jnp.bfloat16)
            .reshape(seg_len, model_width)
        )
        dkey = (
            jnp.einsum("hqk,qhd->khd", dscore, query_heads, preferred_element_type=jnp.float32)
            * score_scale
        ).reshape(key_count, model_width)
        dvalue = jnp.einsum(
            "hqk,qhd->khd", prob_bf, dout_heads, preferred_element_type=jnp.float32
        ).reshape(key_count, model_width)
        return (dquery, dkey, dvalue)

    query_grad_items, key_part, value_part = lax.map(
        self_backward, (query_items, key_all, value_all, dout_items, log_totals)
    )
    key_own, value_own, tkey_own, tvalue_own = (
        lax.psum_scatter(
            key_part.astype(jnp.bfloat16), "seq", scatter_dimension=1, tiled=True
        ).astype(jnp.float32),
        lax.psum_scatter(
            value_part.astype(jnp.bfloat16), "seq", scatter_dimension=1, tiled=True
        ).astype(jnp.float32),
        lax.psum_scatter(
            tkey_part.astype(jnp.bfloat16), "seq", scatter_dimension=1, tiled=True
        ).astype(jnp.float32),
        lax.psum_scatter(
            tvalue_part.astype(jnp.bfloat16), "seq", scatter_dimension=1, tiled=True
        ).astype(jnp.float32),
    )
    key_grad_rows = key_own.astype(jnp.bfloat16).reshape(row_count, model_width)
    value_grad_rows = value_own.astype(jnp.bfloat16).reshape(row_count, model_width)
    query_grad_rows = query_grad_items.reshape(row_count, model_width)
    tkey_bf = tkey_own.astype(jnp.bfloat16)
    tvalue_bf = tvalue_own.astype(jnp.bfloat16)
    query_part = contract_rows(normed_one, query_grad_rows)
    key_wpart = contract_rows(normed_one, key_grad_rows)
    value_wpart = contract_rows(normed_one, value_grad_rows)
    normed_one_grad = (
        times_transposed(query_grad_rows, w_query)
        + times_transposed(key_grad_rows, w_key)
        + times_transposed(value_grad_rows, w_value)
    )
    resid_one, gain_one_part, bias_one_part = pull_one(normed_one_grad)
    input_grad = (self_grad + resid_one).reshape(item_count, seg_len, model_width)
    text_rows = tkey_own.shape[1]
    text_start = lax.axis_index("seq") * text_rows
    text_slice = lax.dynamic_slice_in_dim(text_states, text_start, text_rows, 1)
    ckey_part = jnp.einsum("itc,itd->cd", text_slice, tkey_bf, preferred_element_type=jnp.float32)
    cvalue_part = jnp.einsum(
        "itc,itd->cd", text_slice, tvalue_bf, preferred_element_type=jnp.float32
    )
    text_grad = jnp.einsum(
        "itd,cd->itc", tkey_bf, w_ckey, preferred_element_type=jnp.float32
    ) + jnp.einsum("itd,cd->itc", tvalue_bf, w_cvalue, preferred_element_type=jnp.float32)
    (
        first_gain_grad,
        first_bias_grad,
        query_grad,
        key_grad,
        value_grad,
        output_grad,
        second_gain_grad,
        second_bias_grad,
        cross_query_grad,
        cross_key_grad,
        cross_value_grad,
        cross_output_grad,
        third_gain_grad,
        third_bias_grad,
        up_grad,
        down_grad,
    ) = (
        lax.psum_scatter(gain_one_part, ("dp", "seq"), scatter_dimension=0, tiled=True),
        lax.psum_scatter(bias_one_part, ("dp", "seq"), scatter_dimension=0, tiled=True),
        lax.psum_scatter(query_part, ("dp", "seq"), scatter_dimension=0, tiled=True),
        lax.psum_scatter(key_wpart, ("dp", "seq"), scatter_dimension=0, tiled=True),
        lax.psum_scatter(value_wpart, ("dp", "seq"), scatter_dimension=0, tiled=True),
        lax.psum_scatter(output_part, ("dp", "seq"), scatter_dimension=0, tiled=True),
        lax.psum_scatter(gain_two_part, ("dp", "seq"), scatter_dimension=0, tiled=True),
        lax.psum_scatter(bias_two_part, ("dp", "seq"), scatter_dimension=0, tiled=True),
        lax.psum_scatter(cquery_part, ("dp", "seq"), scatter_dimension=0, tiled=True),
        lax.psum_scatter(ckey_part, ("dp", "seq"), scatter_dimension=0, tiled=True),
        lax.psum_scatter(cvalue_part, ("dp", "seq"), scatter_dimension=0, tiled=True),
        lax.psum_scatter(coutput_part, ("dp", "seq"), scatter_dimension=0, tiled=True),
        lax.psum_scatter(gain_three_part, ("dp", "seq"), scatter_dimension=0, tiled=True),
        lax.psum_scatter(bias_three_part, ("dp", "seq"), scatter_dimension=0, tiled=True),
        lax.psum_scatter(up_part, ("dp", "seq"), scatter_dimension=0, tiled=True),
        lax.psum_scatter(down_part, ("dp", "seq"), scatter_dimension=0, tiled=True),
    )
    return (
        block_out,
        input_grad,
        text_grad,
        first_gain_grad,
        first_bias_grad,
        query_grad,
        key_grad,
        value_grad,
        output_grad,
        second_gain_grad,
        second_bias_grad,
        cross_query_grad,
        cross_key_grad,
        cross_value_grad,
        cross_output_grad,
        third_gain_grad,
        third_bias_grad,
        up_grad,
        down_grad,
    )


def small_rows(vectors):
    packed = jnp.stack(vectors)
    return jnp.pad(packed, ((0, 16 - packed.shape[0]), (0, 128 - packed.shape[1])))


def local(seq_size, *args):
    block_in = args[0]
    if block_in.shape[0] != seq_size or seq_size != 4 or block_in.shape[1] * seq_size != 1024:
        return local_plain(*args)
    return local_items(seq_size, *args)


def local_items(
    seq_size,
    block_in,
    text_states,
    caption_len,
    out_grad,
    first_gain,
    first_bias,
    query_weight,
    key_weight,
    value_weight,
    output_weight,
    second_gain,
    second_bias,
    cross_query,
    cross_key,
    cross_value,
    cross_output,
    third_gain,
    third_bias,
    up_weight,
    down_weight,
):
    ny, nx, nc = 2, seq_size // 2, 2
    dp_size = 1024 // first_gain.shape[0] // seq_size
    dims = (dp_size // ny, ny, nx, nc)
    bf, f32 = jnp.bfloat16, jnp.float32
    seg, width = block_in.shape[1], block_in.shape[2]
    rows = seq_size * seg
    me = lax.axis_index("seq")
    small = small_rows([first_gain, first_bias, second_gain, second_bias, third_gain, third_bias])
    shards = [small, query_weight, key_weight, value_weight, output_weight, cross_query, cross_key, cross_value, cross_output, up_weight, down_weight]
    full, kept = forward(dims, shards, block_in, out_grad, text_states, caption_len, 1)
    small, w_query, w_key, w_value, w_output, w_cquery, w_ckey, w_cvalue, w_coutput, w_up, w_down = full
    grad_rows, inputs, q, k, v, cq, ck, cv, o, o2, normed_one, normed_two, normed_three, after_self, after_cross, lse, lse2, vectors = kept
    grad_rows = grad_rows.reshape(rows, width)
    block_out, dh3, down_part, up_grad_done, up_part = ffn(dims, normed_three, grad_rows, after_cross, w_up, w_down, 4)
    (
        block_out, text_grad, self_grad, do, g_cq, g_ck, g_cv, g_o, sums, down_grad, up_grad, coutput_grad,
    ) = middle(dims, (
        grad_rows, dh3, after_cross, after_self, vectors, o2, cq, ck, cv, lse2, normed_two, o, w_coutput, w_cquery, w_ckey, w_cvalue,
        w_output, text_states, caption_len, block_out.reshape(seq_size, seg, width), down_part, up_part,
    ), 2)
    up_grad = jnp.concatenate([up_grad_done, up_grad], axis=1)
    (
        input_grad, cquery_grad, ckey_grad, cvalue_grad, output_grad, query_grad, key_grad, value_grad, small_grad,
    ) = last(dims, (
        q, k, v, do, o, lse, normed_one, w_query, w_key, w_value, inputs.reshape(rows, width), self_grad, vectors,
        g_cq, g_ck, g_cv, g_o, sums,
    ), 3)
    input_grad = input_grad.astype(f32)
    vec = [small_grad[i, : first_gain.shape[0]] for i in range(6)]
    return (
        block_out, input_grad, text_grad,
        vec[0], vec[1], query_grad, key_grad, value_grad, output_grad,
        vec[2], vec[3], cquery_grad, ckey_grad, cvalue_grad, coutput_grad,
        vec[4], vec[5], up_grad, down_grad,
    )


def solution(mesh):
    return jax.shard_map(
        functools.partial(local, mesh.shape['seq']),
        mesh=mesh,
        in_specs=(
            P("dp", "seq", None),
            P("dp", None, None),
            P("dp"),
            P("dp", "seq", None),
            P(("dp", "seq")),
            P(("dp", "seq")),
            P(("dp", "seq"), None),
            P(("dp", "seq"), None),
            P(("dp", "seq"), None),
            P(("dp", "seq"), None),
            P(("dp", "seq")),
            P(("dp", "seq")),
            P(("dp", "seq"), None),
            P(("dp", "seq"), None),
            P(("dp", "seq"), None),
            P(("dp", "seq"), None),
            P(("dp", "seq")),
            P(("dp", "seq")),
            P(("dp", "seq"), None),
            P(("dp", "seq"), None),
        ),
        out_specs=(
            P("dp", "seq", None),
            P("dp", "seq", None),
            P("dp", "seq", None),
            P(("dp", "seq")),
            P(("dp", "seq")),
            P(("dp", "seq"), None),
            P(("dp", "seq"), None),
            P(("dp", "seq"), None),
            P(("dp", "seq"), None),
            P(("dp", "seq")),
            P(("dp", "seq")),
            P(("dp", "seq"), None),
            P(("dp", "seq"), None),
            P(("dp", "seq"), None),
            P(("dp", "seq"), None),
            P(("dp", "seq")),
            P(("dp", "seq")),
            P(("dp", "seq"), None),
            P(("dp", "seq"), None),
        ),
        check_vma=False,
    )
```

```python
import functools
import itertools

import jax
import jax.numpy as jnp
from jax import lax
from jax.experimental import pallas as pl
from jax.experimental.pallas import tpu as pltpu
from jax.sharding import PartitionSpec as P

MESH = pl.DeviceIdType.MESH
ANY = pl.ANY


class Place:
    def __init__(self, dims):
        self.nz, self.ny, self.nx, self.nc = dims
        dp, seq = lax.axis_index("dp"), lax.axis_index("seq")
        self.z, self.y = lax.div(dp, self.ny), lax.rem(dp, self.ny)
        self.x, self.c = lax.div(seq, self.nc), lax.rem(seq, self.nc)
        self.dp, self.seq = dp, seq

    def dev(self, z=None, y=None, x=None, c=None):
        z = self.z if z is None else z
        y = self.y if y is None else y
        x = self.x if x is None else x
        c = self.c if c is None else c
        return (z * self.ny + y, x * self.nc + c)

    def z_others(self):
        if self.nz != 4:
            return [lax.rem(self.z + k, self.nz) for k in range(1, self.nz)]
        near, far = 1 + lax.rem(self.z, 2), 3 - 3 * lax.div(self.z, 2)
        return [near, 6 - self.z - near - far, far]


def hello(peers):
    barrier = pltpu.get_barrier_semaphore()
    for peer in peers:
        pl.semaphore_signal(barrier, inc=1, device_id=peer, device_id_type=MESH)
    pl.semaphore_wait(barrier, len(peers))


def push(src, dst, send, recv, device):
    pltpu.make_async_remote_copy(
        src_ref=src, dst_ref=dst, send_sem=send, recv_sem=recv, device_id=device, device_id_type=MESH
    ).start()


def drain(ref, sem):
    pltpu.make_async_copy(ref, ref, sem).wait()


def add_to(dst, src):
    dst[...] = dst[...] + src[...]


LOG2E = 1.4426950408889634
NT = (((1,), (1,)), ((), ()))
NN = (((1,), (0,)), ((), ()))
def dot(a, b, dims=NN):
    return lax.dot_general(a, b, dims, preferred_element_type=jnp.float32)

def half_mask(x, h):
    lane = lax.broadcasted_iota(jnp.int32, x.shape, 1)
    keep = lane < 64 if h == 0 else lane >= 64
    return jnp.where(keep, x, jnp.zeros_like(x))

def hide(scores, limit, causal, start):
    rows, cols = scores.shape
    if causal:
        key = lax.broadcasted_iota(jnp.int32, (cols, cols), 0)
        query = lax.broadcasted_iota(jnp.int32, (cols, cols), 1)
        tail = jnp.where(key <= query, scores[rows - cols:], -1e30)
        return tail if rows == cols else jnp.concatenate([scores[:rows - cols], tail], axis=0)
    key = lax.broadcasted_iota(jnp.int32, (rows, cols), 0)
    return jnp.where(key < limit, scores, -1e30)

def attend_kernel(causal, block, limit_ref, q_ref, k_ref, v_ref, o_ref, lse_ref):
    limit = None if causal else limit_ref[0]
    rows, keys = q_ref.shape[0], k_ref.shape[0]
    v_t = v_ref[...].T
    ones = jnp.ones((16, keys), v_t.dtype)
    for i in range(rows // block):
        n = (i + 1) * block if causal else keys
        span = pl.ds(i * block, block)
        halves = []
        for h in range(2):
            q = half_mask(q_ref[span, :], h)
            s = hide(dot(k_ref[0:n, :], q, NT), limit, causal, i * block)
            peak = jnp.max(s, axis=0, keepdims=True)
            e = jnp.exp2(s - peak).astype(jnp.bfloat16)
            v_aug = jnp.concatenate([v_t[h * 64:(h + 1) * 64, :n], ones[:, :n]], axis=0)
            mixed = dot(v_aug, e)
            total = mixed[64:65]
            halves.append(mixed[:64] / total)
            lse_ref[0, h:h + 1, span] = peak + jnp.log2(total)
        o_ref[span, :] = jnp.concatenate(halves, axis=0).T.astype(o_ref.dtype)

def attend_back_kernel(causal, block, limit_ref, q_ref, k_ref, v_ref, g_ref, o_ref, lse_ref, dq_ref, dk_ref, dv_ref, dk_acc, dv_acc):
    limit = None if causal else limit_ref[0]
    rows, keys = q_ref.shape[0], k_ref.shape[0]
    k_t = k_ref[...].T
    sel_row = lax.broadcasted_iota(jnp.int32, (16, 128), 0)
    sel_lane = lax.broadcasted_iota(jnp.int32, (16, 128), 1)
    pick = jnp.where(sel_row == lax.div(sel_lane, 64), 1.0, 0.0).astype(jnp.bfloat16)
    dk_acc[...] = jnp.zeros_like(dk_acc)
    dv_acc[...] = jnp.zeros_like(dv_acc)
    for i in range(rows // block):
        n = (i + 1) * block if causal else keys
        span = pl.ds(i * block, block)
        prod = g_ref[span, :].astype(jnp.float32) * o_ref[span, :].astype(jnp.float32)
        high = prod.astype(jnp.bfloat16)
        low = (prod - high.astype(jnp.float32)).astype(jnp.bfloat16)
        delta = dot(pick, high, NT) + dot(pick, low, NT)
        halves = []
        for h in range(2):
            q = half_mask(q_ref[span, :], h)
            g = half_mask(g_ref[span, :], h)
            s = hide(dot(k_ref[0:n, :], q, NT), limit, causal, i * block)
            p = jnp.exp2(s - lse_ref[0, h:h + 1, span])
            dp = dot(v_ref[0:n, :], g, NT)
            ds = (p * (dp - delta[h:h + 1])).astype(jnp.bfloat16)
            dv_acc[0:n, :] += dot(p.astype(jnp.bfloat16), g)
            dk_acc[0:n, :] += dot(ds, q)
            halves.append(dot(k_t[h * 64:(h + 1) * 64, :n], ds))
        dq_ref[span, :] = (jnp.concatenate(halves, axis=0).T * 0.125).astype(dq_ref.dtype)
    dk_ref[...] = (dk_acc[...] * (1.0 / LOG2E)).astype(dk_ref.dtype)
    dv_ref[...] = dv_acc[...].astype(dv_ref.dtype)

def gelu_parts(u):
    t = 1.0 / (1.0 + (0.3275911 * 0.7071067811865476) * jnp.abs(u))
    e = jnp.exp(-0.5 * (u * u))
    poly = t * (0.254829592 + t * (-0.284496736 + t * (1.421413741 + t * (-1.453152027 + t * 1.061405429))))
    tail = 0.5 * poly * e
    return jnp.where(u < 0, tail, 1.0 - tail), e * 0.3989422804014327


def ffn_kernel(dims, sent, h_ref, g_ref, x_ref, up_in, down_ref, shard_ref, out_ref, dh_ref, ddown_ref, grad_ref, rest_ref,
               h_t, acc, act, du, made, own, rc, r2a, r2b, r3, r4, local_sem, send, recv,
               late, near, up_ref, late_send, late_recv):
    j = pl.program_id(0)
    steps = pl.num_programs(0)
    at = Place(dims)
    nz, ny, nx, nc = dims
    z, y, x, c = at.z, at.y, at.x, at.c
    oy, ox, oc = 1 - y, 1 - x, 1 - c
    rows, width = h_ref.shape
    chunk = up_in.shape[1]
    last = steps - 1
    net = Gather(dims, [(0, 0, near.shape[0], 0, chunk, (2, 1, 0))], [near], [late], late_send, late_recv)
    half = chunk // 2
    block = rows // 2
    left, right = pl.ds(0, half), pl.ds(half, half)
    every = slice(None)

    def made_at(slot, core):
        return made.at[(slot, every, every, every, core)]

    def core_go(i):
        slot = lax.rem(i, 2)
        pltpu.make_async_copy(made_at(slot, c), own.at[i], local_sem.at[i]).start()
        push(made_at(slot, oc), rc.at[i], send.at[i, 0], recv.at[i, 0], at.dev(c=oc))

    def first_go(i):
        drain(own.at[i], local_sem.at[i])
        drain(rc.at[i], recv.at[i, 0])
        drain(rc.at[i], send.at[i, 0])

        @pl.loop(0, nz)
        def _(a):
            for b in range(ny):
                for d in range(nx):
                    add_to(own.at[i, a, b, d], rc.at[i, a, b, d])

        push(own.at[i, :, oy, :, :, left], r2a.at[i], send.at[i, 1], recv.at[i, 1], at.dev(y=oy))
        push(own.at[i, :, :, ox, :, right], r2b.at[i], send.at[i, 1], recv.at[i, 2], at.dev(x=ox))

    def second_go(i):
        drain(r2a.at[i], recv.at[i, 1])
        drain(r2b.at[i], recv.at[i, 2])

        @pl.loop(0, nz)
        def _(a):
            for b in range(2):
                add_to(own.at[i, a, y, b, :, left], r2a.at[i, a, b])
                add_to(own.at[i, a, b, x, :, right], r2b.at[i, a, b])

        push(own.at[i, :, y, ox, :, left], r3.at[i, :, :, left], send.at[i, 1], recv.at[i, 3], at.dev(x=ox))
        push(own.at[i, :, oy, x, :, right], r3.at[i, :, :, right], send.at[i, 1], recv.at[i, 4], at.dev(y=oy))

    def third_go(i):
        drain(r3.at[i, :, :, left], recv.at[i, 3])
        drain(r3.at[i, :, :, right], recv.at[i, 4])

        @pl.loop(0, nz)
        def _(a):
            add_to(own.at[i, a, y, x], r3.at[i, a])

        for k in range(1, nz):
            far = lax.rem(z + k, nz)
            push(own.at[i, far, y, x], r4.at[i, k - 1], send.at[i, 1], recv.at[i, 5], at.dev(z=far))

    def finish(i):
        drain(r4.at[i], recv.at[i, 5])
        total = own[i, z, y, x].astype(jnp.float32)
        for k in range(nz - 1):
            total = total + r4[i, k].astype(jnp.float32)
        grad_ref[i] = total
        for part in (r2a.at[i], r2b.at[i], r3.at[i], r4.at[i]):
            drain(part, send.at[i, 1])

    @pl.when(j == 0)
    def _():
        hello([at.dev(z=k) for k in at.z_others()] + [at.dev(y=oy), at.dev(x=ox), at.dev(c=oc)])
        load = pltpu.make_async_copy(shard_ref.at[:, pl.ds(shard_ref.shape[1] - chunk, chunk)], near, local_sem.at[0])
        load.start()
        load.wait()
        late[z, y, x, c] = near[...]
        net.go(0, 0)
        acc[...] = x_ref[...]
        dh_ref[...] = jnp.zeros_like(dh_ref)

        @pl.loop(0, rows // block)
        def _(r):
            span = pl.ds(pl.multiple_of(r * block, block), block)
            h_t[:, span] = h_ref[span, :].T

    def after(late, then, first=0, end=sent):
        pl.when((j >= late + first) & (j < late + end))(lambda: then(j - late))

    @pl.when(j < last)
    def _():
        up_ref[...] = up_in[...]

    @pl.when(j == last)
    def _():
        net.arrived(0)
        up_ref[...] = late[...].reshape(up_ref.shape)

    after(1, first_go)
    after(2, third_go, 0, sent - 1)
    for r in range(rows // block):
        span = pl.ds(r * block, block)
        u = dot(h_ref[span, :], up_ref[...])
        g = dot(g_ref[span, :], down_ref[...], NT)
        big, small = gelu_parts(u)
        a = (u * big).astype(jnp.bfloat16)
        d = (g * (big + u * small)).astype(jnp.bfloat16)
        act[span, :] = a
        du[span, :] = d
        acc[span, :] += dot(a, down_ref[...])
        dh_ref[span, :] += dot(d, up_ref[...], NT)

    pl.when(j == 0)(lambda: net.go(0, 1))
    pl.when(j == 2)(lambda: net.go(0, 3))
    after(1, second_go)
    after(2, finish, 0, sent - 1)
    slot = lax.rem(j, 2)
    each = rows // (nz * ny * nx * nc)

    @pl.loop(0, nz)
    def _(a):
        n = ny * nx * nc * each
        part = dot(h_t[pl.ds(pl.multiple_of(a * n, n), n), :], du[...]).astype(made.dtype)
        made[slot, a] = part.reshape(ny, nx, nc, each, chunk)

    pl.when(j == 0)(lambda: net.go(0, 2))
    after(0, core_go)
    after(1, third_go, sent - 1)
    ddown_ref[...] = lax.dot_general(act[...], g_ref[...], TN, preferred_element_type=jnp.float32).astype(ddown_ref.dtype)
    after(1, finish, sent - 1)

    @pl.when(j >= sent)
    def _():
        pltpu.make_async_copy(made.at[slot], rest_ref.at[j - sent], local_sem.at[j]).start()

    @pl.when(j == steps - 1)
    def _():
        net.sent(0)
        out_ref[...] = acc[...].astype(out_ref.dtype)
        for i in range(sent, 4):
            drain(rest_ref.at[i - sent], local_sem.at[i])


def ffn(dims, h, g, x, w_up, w_down, up_shard, cid, sent=3, steps=4):
    nz, ny, nx, nc = dims
    rows, width = h.shape
    inner = w_up.shape[1]
    chunk = inner // steps
    each = width // (nz * ny * nx * nc)
    bf, f32 = jnp.bfloat16, jnp.float32
    fixed = lambda j: (0, 0)
    whole = pl.BlockSpec((rows, width), fixed)
    once = pl.BlockSpec((rows, width), fixed, pipeline_mode=pl.Buffered(1))
    tile = (each, chunk)
    out, dh, ddown, grad, rest = pl.pallas_call(
        functools.partial(ffn_kernel, dims, sent),
        grid=(steps,),
        out_shape=[
            jax.ShapeDtypeStruct((rows, width), bf),
            jax.ShapeDtypeStruct((rows, width), f32),
            jax.ShapeDtypeStruct((inner, width), bf),
            jax.ShapeDtypeStruct((sent, each, chunk), f32),
            jax.ShapeDtypeStruct((steps - sent, nz, ny, nx, nc, each, chunk), bf),
        ],
        in_specs=[once, once, once, pl.BlockSpec((width, chunk), lambda j: (0, jnp.minimum(j, steps - 2))),
                  pl.BlockSpec((chunk, width), lambda j: (j, 0)), pl.BlockSpec(memory_space=ANY)],
        out_specs=[once, once, pl.BlockSpec((chunk, width), lambda j: (j, 0)),
                   pl.BlockSpec((sent, each, chunk), lambda j: (0, 0, 0)), pl.BlockSpec(memory_space=ANY)],
        scratch_shapes=[
            pltpu.VMEM((width, rows), bf), pltpu.VMEM((rows, width), f32), pltpu.VMEM((rows, chunk), bf), pltpu.VMEM((rows, chunk), bf),
            pltpu.VMEM((2, nz, ny, nx, nc) + tile, bf),
            pltpu.VMEM((sent, nz, ny, nx) + tile, bf), pltpu.VMEM((sent, nz, ny, nx) + tile, bf),
            pltpu.VMEM((sent, nz, nx, each, chunk // 2), bf), pltpu.VMEM((sent, nz, ny, each, chunk // 2), bf),
            pltpu.VMEM((sent, nz) + tile, bf), pltpu.VMEM((sent, nz - 1) + tile, bf),
            pltpu.SemaphoreType.DMA((steps,)), pltpu.SemaphoreType.DMA((sent, 2)), pltpu.SemaphoreType.DMA((sent, 6)),
            pltpu.VMEM((nz, ny, nx, nc) + tile, bf), pltpu.VMEM(tile, bf), pltpu.VMEM((width, chunk), bf),
            pltpu.SemaphoreType.DMA((1,)), pltpu.SemaphoreType.DMA((1, 4)),
        ],
        compiler_params=pltpu.CompilerParams(collective_id=cid, has_side_effects=True, vmem_limit_bytes=62 * 2**20, dimension_semantics=("arbitrary",)),
        name="feed_forward",
    )(h, g, x, w_up, w_down, up_shard)
    grad = jnp.moveaxis(grad, 0, 1).reshape(each, sent * chunk)
    rest = jnp.moveaxis(rest, 0, 5).reshape(width, (steps - sent) * chunk)
    return out, dh, ddown, grad, rest
class Gather:
    def __init__(self, dims, units, ins, outs, send, recv):
        self.at, self.nz = Place(dims), dims[0]
        self.units, self.ins, self.outs, self.send, self.recv = units, ins, outs, send, recv

    def part(self, u, where, core=None):
        a, r0, nr, c0, ncol, _ = self.units[u]
        return self.outs[a].at[(*where, self.at.c if core is None else core, pl.ds(r0, nr), pl.ds(c0, ncol))]

    def held(self, u, k):
        where = [self.at.z, self.at.y, self.at.x]
        for axis in self.units[u][5][:k]:
            where[axis] = slice(None)
        return where

    def coming(self, u, k):
        where = self.held(u, k)
        axis = self.units[u][5][k]
        where[axis] = (slice(0, self.nz - 1), 1 - self.at.y, 1 - self.at.x)[axis]
        return where

    def to_core(self, u, where):
        block = self.part(u, where)
        push(block, block, self.send.at[u], self.recv.at[u, 3], self.at.dev(c=1 - self.at.c))

    def pass_on(self, u, k):
        axis = self.units[u][5][k]
        if axis == 0 and k == 0:
            self.to_core(u, self.held(u, 1))
        elif axis == 0:
            for z in self.at.z_others():
                where = self.held(u, k)
                where[0] = z
                self.to_core(u, where)
        else:
            self.to_core(u, self.coming(u, k))
            if k == 0:
                self.to_core(u, self.held(u, 0))

    def go(self, u, k):
        at = self.at
        if k > 0:
            drain(self.part(u, self.coming(u, k - 1)), self.recv.at[u, k - 1])
        if k < 3:
            a, r0, nr, c0, ncol, order = self.units[u]
            dst = self.part(u, self.held(u, k))
            src = self.ins[a].at[pl.ds(r0, nr), pl.ds(c0, ncol)] if k == 0 else dst
            targets = ([at.dev(z=z) for z in at.z_others()], [at.dev(y=1 - at.y)], [at.dev(x=1 - at.x)])[order[k]]
            for device in targets:
                push(src, dst, self.send.at[u], self.recv.at[u, k], device)
        if k > 0:
            self.pass_on(u, k - 1)

    def arrived(self, u):
        drain(self.part(u, [slice(None)] * 3, 1 - self.at.c), self.recv.at[u, 3])

    def sent(self, u):
        for k in range(3):
            where = self.held(u, k)
            if self.units[u][5][k] == 0:
                where[0] = slice(0, self.nz - 1)
            drain(self.part(u, where), self.send.at[u])
        drain(self.part(u, [slice(None)] * 3), self.send.at[u])


def norm_parts(values_in):
    center = values_in - jnp.mean(values_in, axis=-1, keepdims=True)
    return center * lax.rsqrt(jnp.mean(center * center, axis=-1, keepdims=True) + EPS)


FW_PATHS = ((0, 1, 2), (0, 1, 2), (0, 2, 1), (0, 1, 2), (2, 0, 1), (2, 0, 1), (2, 0, 1), (0, 1, 2), (2, 1, 0), (0, 2, 1), (2, 1, 0), (2, 1, 0), (0, 2, 1), (0, 1, 2), (0, 1, 2), (0, 2, 1), (0, 2, 1))
FW_UNITS = [(a, 0, 32, 0, 1024, FW_PATHS[a - 1]) for a in range(1, 9)]
FW_UNITS += [(9, 0, 32, 1024 * j, 1024, FW_PATHS[8 + j]) for j in range(4)]
FW_UNITS += [(10, 32 * j, 32, 0, 1024, FW_PATHS[12 + j]) for j in range(4)] + [(0, 0, 16, 0, 128, FW_PATHS[16])]
FW_ORDER = (
    (0, 0), (2, 0), (1, 0), (4, 0), (5, 0), (6, 0), (0, 1), (16, 0), (2, 1), (3, 0), (0, 2), (1, 1), (13, 0),
    (16, 1), (7, 0), (3, 1), (15, 0), (4, 1), (8, 0), (5, 1), (10, 0), (1, 2), (6, 1), (13, 1), (9, 0), (3, 2),
    (2, 2), (7, 1), (14, 0), (13, 2), (15, 1), (12, 0), (0, 3), (16, 2), (8, 1), (0, 4), (10, 1), (2, 3), (4, 2),
    (7, 2), (2, 4), (16, 3), (8, 2), (1, 3), (-2, 0), (10, 2), (1, 4), (5, 2), (-2, 1), (-2, 2), (3, 3), (-2, 3),
    (4, 3), (3, 4), (6, 2), (-2, 4), (4, 4), (-2, 5), (9, 1), (13, 3), (-2, 6), (5, 3), (14, 1), (-2, 7), (5, 4),
    (15, 2), (-2, 8), (12, 1), (-2, 9), (6, 3), (-2, 10), (7, 3), (6, 4), (-2, 11), (14, 2), (7, 4), (-2, 12),
    (9, 2), (-2, 13), (12, 2), (-1, 0), (15, 3), (8, 3), (-2, 14), (-2, 15), (-2, 16), (-2, 17), (14, 3), (-2, 18),
    (9, 3), (-2, 19), (-2, 20), (-2, 21), (-2, 22), (-2, 23), (-2, 24), (12, 3), (10, 3),
)


def forward_kernel(dims, n, *refs):
    shards, refs = refs[:n], refs[n:]
    block_in, out_grad, text_states, limits = refs[:4]
    full, refs = refs[4 : 4 + n], refs[4 + n :]
    g_out, x_out, q_out, k_out, v_out, cq_out, ck_out, cv_out, o_out, o2_out, h1_out, h2_out, h3_out, x1_out, x2_out, lse_out, lse2_out, vec = refs[:18]
    x_in, q, k, v, cq, ck, cv, o, o2, h1, h2, h3, x1, x2, lse, lse2, text, small = refs[18:36]
    w, near, own_g = refs[36:44], refs[44 : 44 + n], refs[44 + n]
    limit, local_sem, out_sem, send, recv, ex_send, ex_recv = refs[45 + n :]
    at = Place(dims)
    oy, ox, oc, me = 1 - at.y, 1 - at.x, 1 - at.c, at.seq
    hello([at.dev(z=p) for p in at.z_others()] + [at.dev(y=oy), at.dev(x=ox), at.dev(c=oc), at.dev(x=ox, c=oc)])
    net = Gather(dims, FW_UNITS, near, full, send, recv)
    rows, width = q.shape
    block = 256
    f32, bf = jnp.float32, jnp.bfloat16
    others = ((ox, at.c), (ox, oc), (at.x, oc))

    def exchange(src, dst, i, own):
        for px, pc in others:
            push(src.at[px * 2 + pc], dst.at[me], ex_send.at[i], ex_recv.at[i], at.dev(x=px, c=pc))
        pltpu.make_async_copy(own, dst.at[me], local_sem.at[n + i]).start()

    def exchanged(dst, i):
        drain(dst.at[0:3], ex_recv.at[i])
        drain(dst.at[0], local_sem.at[n + i])

    keep = []

    def put(src, dst):
        pltpu.make_async_copy(src, dst, out_sem.at[len(keep)]).start()
        keep.append(src)

    loads = 4 + n

    def load(a):
        net.arrived(a - 1)
        pltpu.make_async_copy(full[a], w[a - 1], local_sem.at[loads + a]).start()

    def loaded(a):
        drain(w[a - 1], local_sem.at[loads + a])

    def weight(a):
        return w[a - 1][...].reshape(width, width)

    def span_of(r):
        return pl.ds(pl.multiple_of(r * block, block), block)

    def first_norm():
        net.arrived(16)
        pltpu.make_async_copy(full[0], small, local_sem.at[n + 3]).start()
        drain(small, local_sem.at[n + 3])
        packed = small[...].reshape(-1, 16, 128).astype(f32)
        devices = packed.shape[0]
        piece = width // devices
        lane = lax.rem(lax.broadcasted_iota(jnp.int32, (128, width), 1), piece)
        spread = jnp.where(lane == lax.broadcasted_iota(jnp.int32, (128, width), 0), 1.0, 0.0).astype(bf)
        owner = lax.div(lax.broadcasted_iota(jnp.int32, (devices, width), 1), piece)
        mine = owner == lax.broadcasted_iota(jnp.int32, (devices, width), 0)
        vec[...] = jnp.zeros_like(vec)
        for i in range(6):
            vec[i : i + 1, :] = row_sum(jnp.where(mine, dot(packed[:, i, :].astype(bf), spread), 0.0))
        exchanged(x_in, 0)
        put(x_in, x_out)

        @pl.loop(0, 4)
        def _(r):
            x = x_in[r].astype(f32)
            x1[span_of(r), :] = x
            h1[span_of(r), :] = (norm_parts(x) * vec[0:1, :] + vec[1:2, :]).astype(bf)

        put(h1, h1_out)

    def project(a, dst, scale, kept):
        loaded(a)

        @pl.loop(0, rows // block)
        def _(r):
            made = dot(h1[span_of(r), :], weight(a))
            dst[span_of(r), :] = (made if scale is None else made * scale).astype(bf)

        put(dst, kept)

    def pair(causal, qs, ks, vs, os, ls, j):
        cols = pl.ds(pl.multiple_of(j * 128, 128), 128)
        attend_kernel(causal, 512, limit, qs.at[:, cols], ks.at[:, cols], vs.at[:, cols], os.at[:, cols], ls.at[pl.ds(j, 1)])

    self_attention = functools.partial(pair, True, q, k, v, o, lse)
    cross_attention = functools.partial(pair, False, cq, ck, cv, o2, lse2)
    count = width // 128

    def second_norm(i):
        if i == 0:
            put(o, o_out)
            put(lse, lse_out)
            loaded(4)
            loaded(5)

        @pl.loop(2 * i, 2 * i + 2)
        def _(r):
            x = x1[span_of(r), :] + dot(o[span_of(r), :], weight(4))
            x1[span_of(r), :] = x
            h = (norm_parts(x) * vec[2:3, :] + vec[3:4, :]).astype(bf)
            h2[span_of(r), :] = h
            cq[span_of(r), :] = (dot(h, weight(5)) * (LOG2E / 8)).astype(bf)

        if i == 1:
            put(x1, x1_out)
            put(h2, h2_out)
            put(cq, cq_out)

    def text_rows():
        loaded(6)
        loaded(7)
        ck[...] = dot(text[...], weight(6)).astype(bf)
        cv[...] = dot(text[...], weight(7)).astype(bf)
        put(ck, ck_out)
        put(cv, cv_out)

    def third_norm(i):
        if i == 0:
            put(o2, o2_out)
            put(lse2, lse2_out)
            loaded(8)

        @pl.loop(2 * i, 2 * i + 2)
        def _(r):
            x = x1[span_of(r), :] + dot(o2[span_of(r), :], weight(8))
            x2[span_of(r), :] = x
            h3[span_of(r), :] = (norm_parts(x) * vec[4:5, :] + vec[5:6, :]).astype(bf)

        if i == 1:
            put(x2, x2_out)
            put(h3, h3_out)

    pieces = [first_norm, lambda: project(1, q, LOG2E / 8, q_out), lambda: project(2, k, None, k_out), lambda: project(3, v, None, v_out)]
    pieces += [(self_attention, j) for j in range(count)] + [functools.partial(second_norm, i) for i in range(2)] + [text_rows]
    pieces += [(cross_attention, j) for j in range(count)] + [functools.partial(third_norm, i) for i in range(2)]

    for a in range(n):
        pltpu.make_async_copy(shards[a], near[a], local_sem.at[a]).start()
    exchange(block_in, x_in, 0, block_in.at[me])
    pltpu.make_async_copy(text_states.at[me], text, local_sem.at[n + 2]).start()
    pltpu.make_async_copy(out_grad.at[me], own_g, local_sem.at[n + 1]).start()
    for a in range(n):
        drain(near[a], local_sem.at[a])
    drain(own_g, local_sem.at[n + 1])
    for a in range(n):
        pltpu.make_async_copy(near[a], full[a].at[at.z, at.y, at.x, at.c], local_sem.at[a]).start()
    limit[0] = limits[me]
    begin = next(i for i, (_, step) in enumerate(FW_ORDER) if step > 0)

    def event(u, step):
        if u == -1:
            exchange(out_grad, g_out, 1, own_g)
        elif step == 4:
            load(u + 1)
        else:
            net.go(u, step)

    run_order(FW_ORDER[:begin], event, [])
    for a in range(n):
        drain(near[a], local_sem.at[a])
    drain(text, local_sem.at[n + 2])
    run_order(FW_ORDER[begin:], event, pieces)
    exchanged(g_out, 1)
    moved = sorted({u for u, _ in FW_ORDER if u >= 0})
    for u in moved:
        if 8 <= u < 16:
            net.arrived(u)
    for u in moved:
        net.sent(u)
    drain(x_in.at[0:3], ex_send.at[0])
    drain(g_out.at[0:3], ex_send.at[1])
    for i, src in enumerate(keep):
        drain(src, out_sem.at[i])


def forward(dims, shards, block_in, out_grad, text_states, limits, cid):
    n = len(shards)
    bf, f32 = jnp.bfloat16, jnp.float32
    items, seg, width = block_in.shape
    rows, texts = items * seg, text_states.shape[1]
    wide, pairs = jax.ShapeDtypeStruct((rows, width), bf), width // 128
    short = jax.ShapeDtypeStruct((texts, width), bf)
    long = jax.ShapeDtypeStruct((rows, width), f32)
    sums = jax.ShapeDtypeStruct((pairs, 8, rows), f32)
    seg4 = jax.ShapeDtypeStruct(block_in.shape, bf)
    whole = [jax.ShapeDtypeStruct(tuple(dims) + s.shape, s.dtype) for s in shards]
    saved = [wide, wide, wide, wide, short, short, wide, wide, wide, wide, wide, long, long, sums, sums]
    out_shape = whole + [seg4, seg4] + saved + [jax.ShapeDtypeStruct((8, width), f32)]
    held = [pltpu.VMEM(s.shape, s.dtype) for s in [seg4] + saved + [short]] + [pltpu.VMEM(tuple(dims) + (16, 128), bf)]
    held += [pltpu.VMEM(s.shape, s.dtype) for s in whole[1:9]] + [pltpu.VMEM(s.shape, s.dtype) for s in shards]
    held += [pltpu.VMEM(block_in.shape[1:], bf)]
    units = len(FW_UNITS)
    any_spec = pl.BlockSpec(memory_space=ANY)
    outs = pl.pallas_call(
        functools.partial(forward_kernel, dims, n),
        out_shape=out_shape,
        in_specs=[any_spec] * (n + 3) + [pl.BlockSpec(memory_space=pltpu.SMEM)],
        out_specs=[any_spec] * (len(out_shape) - 1) + [pl.BlockSpec(memory_space=pltpu.VMEM)],
        scratch_shapes=held
        + [
            pltpu.SMEM((1,), jnp.int32),
            pltpu.SemaphoreType.DMA((2 * n + 8,)), pltpu.SemaphoreType.DMA((20,)),
            pltpu.SemaphoreType.DMA((units,)), pltpu.SemaphoreType.DMA((units, 4)),
            pltpu.SemaphoreType.DMA((2,)), pltpu.SemaphoreType.DMA((2,)),
        ],
        compiler_params=pltpu.CompilerParams(collective_id=cid, has_side_effects=True, vmem_limit_bytes=62 * 2**20),
        name="forward",
    )(*shards, block_in, out_grad, text_states, limits)
    full = [o.reshape((-1,) + o.shape[5:]) for o in outs[:n]]
    return full, outs[n:]
def run_order(order, event, pieces):
    i = 0
    while i < len(order):
        unit, step = order[i]
        i += 1
        if unit != -2:
            event(unit, step)
            continue
        piece = pieces[step]
        if callable(piece):
            piece()
            continue
        body, first = piece
        last, between = first, {first: []}
        while i < len(order):
            unit, step = order[i]
            if unit != -2:
                between[last].append((unit, step))
            else:
                piece = pieces[step]
                if callable(piece) or piece[0] is not body:
                    break
                last = piece[1]
                between[last] = []
            i += 1

        def one(j, body=body, between=between):
            body(j)
            for k, events in between.items():
                if events:
                    pl.when(j == k)(functools.partial(run_order, events, event, pieces))

        pl.loop(first, last + 1)(one)


class Scatter:
    def __init__(self, dims, send, recv, local):
        self.at, self.dims, self.send, self.recv, self.local, self.units = Place(dims), dims, send, recv, local, []

    def add(self, source, room, out, order, whole):
        self.units.append((source, room[0], room[1:], out, order, whole))

    def own(self, u, where):
        own, whole = self.units[u][1], self.units[u][5]
        return own.at[(*where, self.at.c)] if whole else own.at[tuple(where)]

    def left(self, u, k):
        where = [slice(None)] * 3
        for axis in self.units[u][4][:k]:
            where[axis] = (self.at.z, self.at.y, self.at.x)[axis]
        return where

    def add_in(self, u, k, bufs):
        where = self.left(u, k)
        open_axes = [axis for axis in range(3) if axis not in self.units[u][4][:k]]

        def one(index):
            spot = list(where)
            for axis, i in zip(open_axes, index):
                spot[axis] = i
            dst = self.own(u, spot)
            if len(bufs) == 1:
                dst[...] = dst[...] + bufs[0][tuple(index)]
            else:
                total = dst[...].astype(jnp.float32)
                for buf in bufs:
                    total = total + buf[tuple(index)].astype(jnp.float32)
                dst[...] = total.astype(dst.dtype)

        sizes = [self.dims[axis] for axis in open_axes]
        inner = list(itertools.product(*[range(n) for n in sizes[1:]]))

        @pl.loop(0, sizes[0])
        def _(i):
            for rest in inner:
                one((i, *rest))

    def bufs(self, u, k):
        buf = self.units[u][2][k]
        return [buf.at[i] for i in range(self.dims[0] - 1)] if self.units[u][4][k - 1] == 0 else [buf]

    def go(self, u, k):
        source, own, room, out, order, whole = self.units[u]
        at, every = self.at, slice(None)
        if k == 0:
            if not whole:
                pltpu.make_async_copy(source(every, every, every, at.c), own, self.local.at[u]).start()
            push(source(every, every, every, 1 - at.c), room[0], self.send.at[u], self.recv.at[u, 0], at.dev(c=1 - at.c))
            return
        drain(room[k - 1], self.recv.at[u, k - 1])
        if k == 4:
            total = self.own(u, (at.z, at.y, at.x))[...].astype(jnp.float32)
            for buf in self.bufs(u, 3):
                total = total + buf[...].astype(jnp.float32)
            out[...] = total
            for block in room:
                drain(block, self.send.at[u])
            return
        if k == 1:
            if not whole:
                drain(own, self.local.at[u])
            self.add_in(u, 0, [room[0]])
        else:
            self.add_in(u, k - 1, self.bufs(u, k - 1))
        where = self.left(u, k - 1)
        axis = order[k - 1]
        if axis == 0:
            for z in at.z_others():
                where[0] = z
                slot = lax.rem(z - at.z + self.dims[0], self.dims[0]) - 1
                push(self.own(u, where), room[k].at[slot], self.send.at[u], self.recv.at[u, k], at.dev(z=z))
        else:
            where[axis] = (None, 1 - at.y, 1 - at.x)[axis]
            device = at.dev(y=1 - at.y) if axis == 1 else at.dev(x=1 - at.x)
            push(self.own(u, where), room[k], self.send.at[u], self.recv.at[u, k], device)


def scatter_room(dims, tile, dtype, order, whole):
    nz, ny, nx, nc = dims
    rooms = [((nz, ny, nx, nc) if whole else (nz, ny, nx)) + tile, (nz, ny, nx) + tile]
    for k in range(3):
        lead = tuple(dims[axis] for axis in range(3) if axis not in order[: k + 1])
        rooms.append(((nz - 1,) if order[k] == 0 else ()) + lead + tile)
    return [pltpu.VMEM(shape, dtype) for shape in rooms]


def norm_back(x, dh, gain):
    center = x - jnp.mean(x, axis=-1, keepdims=True)
    r = lax.rsqrt(jnp.mean(center * center, axis=-1, keepdims=True) + EPS)
    n = center * r
    dn = dh * gain
    dx = r * (dn - jnp.mean(dn, axis=-1, keepdims=True) - n * jnp.mean(dn * n, axis=-1, keepdims=True))
    return dx, dh * n


def row_sum(rows):
    return jnp.sum(rows, axis=0, keepdims=True)


TN = (((0,), (0,)), ((), ()))


MIDDLE_PATHS = (
    (0, 2, 1), (1, 0, 2), (1, 0, 2), (1, 2, 0), (2, 1, 0), (2, 1, 0),
)
MIDDLE_ORDER = (
    (0, 0), (1, 0), (2, 0), (3, 0), (4, 0), (-2, 0), (0, 1), (1, 1), (-2, 1), (2, 1), (3, 1), (4, 1), (-2, 2),
    (5, 0), (-2, 3), (-2, 4), (5, 1), (-2, 5), (1, 2), (-2, 6), (-2, 7), (-2, 8), (-2, 9), (-2, 10), (-2, 11),
    (0, 2), (2, 2), (4, 2), (-2, 12), (-2, 13), (1, 3), (3, 2), (5, 2), (-2, 14), (4, 3), (0, 3), (1, 4), (-2, 15),
    (2, 3), (5, 3), (3, 3), (0, 4), (4, 4), (5, 4), (2, 4), (3, 4),
)
LAST_SPLIT = 640
LAST_PATHS = (
    (0, 2, 1), (1, 0, 2), (2, 0, 1), (2, 1, 0), (1, 2, 0), (2, 1, 0), (2, 1, 0), (0, 1, 2), (1, 0, 2), (1, 0, 2),
    (0, 1, 2),
)
LAST_ORDER = (
    (0, 0), (1, 0), (2, 0), (3, 0), (-2, 0), (0, 1), (-2, 1), (1, 1), (2, 1), (3, 1), (-2, 2), (-2, 3), (-2, 4),
    (-2, 5), (1, 2), (2, 2), (-2, 6), (4, 0), (5, 0), (6, 0), (0, 2), (-2, 7), (3, 2), (4, 1), (5, 1), (6, 1),
    (0, 3), (-2, 8), (1, 3), (-2, 9), (3, 3), (-2, 10), (7, 0), (8, 0), (9, 0), (5, 2), (2, 3), (-2, 11), (4, 2),
    (7, 1), (8, 1), (0, 4), (9, 1), (6, 2), (1, 4), (-2, 12), (3, 4), (5, 3), (2, 4), (-2, 13), (-2, 14), (8, 2),
    (-2, 15), (10, 0), (7, 2), (9, 2), (10, 1), (5, 4), (6, 3), (4, 3), (7, 3), (8, 3), (9, 3), (10, 2), (10, 3),
    (6, 4), (7, 4), (8, 4), (9, 4), (10, 4), (4, 4),
)


def middle_kernel(dims, *refs):
    (g_in, dh_in, x2_in, x1_in, vec, o2_in, cq_in, ck_in, cv_in, lse_in, h2_in, o_in, wco_in, wcq_in, wck_in, wcv_in, wo_in,
     text_in, limits, block_in, down_in, up_in) = refs[:22]
    block_out, text_out, dx_out, do_out, gcq_out, gck_out, gcv_out, go_out, sums, down_out, up_out, co_out = refs[22:34]
    (x2, dh3, dx, g, dy, do, o2, wco, cq, dcq, wcq, wck, wcv, ck, cv, dck, dcv, lse, text, tg, stage, dk_acc, dv_acc, limit,
     load_sem, out_sem, ex_send, ex_recv, send, recv, local, own_rows) = refs[34:66]
    rooms = refs[66:]
    at = Place(dims)
    nz = dims[0]
    oy, ox, oc, me = 1 - at.y, 1 - at.x, 1 - at.c, at.seq
    hello([at.dev(z=p) for p in at.z_others()] + [at.dev(y=oy), at.dev(x=ox), at.dev(c=oc), at.dev(x=ox, c=oc)])
    others = ((ox, at.c), (ox, oc), (at.x, oc))
    rows, width = g.shape
    block = 256
    f32, bf = jnp.float32, jnp.bfloat16
    every = slice(None)
    net = Scatter(dims, send, recv, local)
    quarter = width // 4
    room = [rooms[5 * j : 5 * j + 5] for j in range(6)]
    for j in range(4):
        cols = pl.ds(j * quarter, quarter)
        net.add(lambda *w, cols=cols: down_in.at[(*w, every, cols)], room[j], down_out.at[:, cols], MIDDLE_PATHS[j], False)
    net.add(lambda *w: up_in.at[w], room[4], up_out, MIDDLE_PATHS[4], False)
    net.add(lambda *w: room[5][0].at[w], room[5], co_out, MIDDLE_PATHS[5], True)

    def exchange(src, dst, i, own):
        for px, pc in others:
            push(src.at[px * 2 + pc], dst.at[me], ex_send.at[i], ex_recv.at[i], at.dev(x=px, c=pc))
        pltpu.make_async_copy(own, dst.at[me], local.at[6 + i]).start()

    started = []

    def load(src, dst):
        pltpu.make_async_copy(src, dst, load_sem.at[len(started)]).start()
        started.append(dst)
        return len(started) - 1

    def loaded(i):
        drain(started[i], load_sem.at[i])

    kept = []

    def put(src, dst):
        pltpu.make_async_copy(src, dst, out_sem.at[len(kept)]).start()
        kept.append(src)
        return len(kept) - 1

    def kept_done(i):
        drain(kept[i], out_sem.at[i])

    def span_of(r):
        return pl.ds(pl.multiple_of(r * block, block), block)

    def weight_grad(src, grad, made):
        @pl.loop(0, nz)
        def _(a):
            part = dot(src[:, pl.ds(pl.multiple_of(a * block, block), block)], grad[...], TN).astype(bf)
            made[a] = part.reshape(made.shape[1:])

    own_load = load(block_in.at[me], own_rows)
    first = [load(dh_in, dh3), load(x2_in, x2), load(g_in, g), load(wco_in, wco), load(o2_in, o2)]
    second = [load(cq_in, cq), load(ck_in, ck), load(cv_in, cv), load(lse_in, lse)]
    third = [load(text_in.at[me], text), load(wcq_in, wcq), load(wck_in, wck), load(wcv_in, wcv)]
    limit[0] = limits[me]
    run_order(MIDDLE_ORDER[:5], net.go, [])
    loaded(own_load)
    exchange(block_in, block_out, 0, own_rows)
    for i in first[:-1]:
        loaded(i)
    sums[...] = jnp.zeros_like(sums)

    def last_norm(r):
        span = span_of(r)
        d = dh3[span, :]
        grad, gain_terms = norm_back(x2[span, :], d, vec[4:5, :])
        sums[4:5, :] += row_sum(gain_terms)
        sums[5:6, :] += row_sum(d)
        total = g[span, :].astype(f32) + grad
        dx[span, :] = total
        low = total.astype(bf)
        dy[span, :] = low
        do[span, :] = dot(low, wco[...], NT).astype(bf)

    def middle_norm(r):
        span = span_of(r)
        d = dot(dcq[span, :], wcq[...], NT)
        grad, gain_terms = norm_back(x2[span, :], d, vec[2:3, :])
        sums[2:3, :] += row_sum(gain_terms)
        sums[3:4, :] += row_sum(d)
        total = dx[span, :] + grad
        dx[span, :] = total
        low = total.astype(bf)
        dy[span, :] = low
        do[span, :] = dot(low, cq[...], NT).astype(bf)

    later = {}

    def after_last_norm():
        pl.loop(2, 4)(last_norm)
        later["x1"], later["o"], later["h2"] = load(x1_in, x2), load(o_in, g), load(h2_in, wco)

    def output_weight_grad():
        loaded(first[-1])
        weight_grad(o2, dy, room[5][0])
        for i in second:
            loaded(i)

    def cross(j):
        cols = pl.ds(pl.multiple_of(j * 128, 128), 128)
        attend_back_kernel(
            False, 512, limit, cq.at[:, cols], ck.at[:, cols], cv.at[:, cols], do.at[:, cols], o2.at[:, cols], lse.at[pl.ds(j, 1)],
            dcq.at[:, cols], dck.at[:, cols], dcv.at[:, cols], dk_acc, dv_acc,
        )

    def query_weight_grad():
        later["wo"] = load(wo_in, cq)
        for i in third:
            loaded(i)
        loaded(later["h2"])
        weight_grad(wco, dcq, stage.at[0])
        later["cq"] = put(stage.at[0], gcq_out)
        loaded(later["x1"])
        loaded(later["wo"])

    def after_middle_norm():
        pl.loop(2, 4)(middle_norm)
        put(dx, dx_out)
        put(do, do_out)

    def self_weight_grad():
        loaded(later["o"])
        weight_grad(g, dy, stage.at[1])
        later["o"] = put(stage.at[1], go_out)

    def text_weight_grads():
        tg[...] = (dot(dck[...], wck[...], NT) + dot(dcv[...], wcv[...], NT)).reshape(tg.shape)
        exchange(tg, text_out, 1, tg.at[me])
        kept_done(later["cq"])
        weight_grad(text, dck, stage.at[0])
        put(stage.at[0], gck_out)
        kept_done(later["o"])
        weight_grad(text, dcv, stage.at[1])
        put(stage.at[1], gcv_out)

    pieces = [lambda: pl.loop(0, 2)(last_norm), after_last_norm, output_weight_grad]
    pieces += [(cross, j) for j in range(width // 128)]
    pieces += [query_weight_grad, lambda: pl.loop(0, 2)(middle_norm), after_middle_norm, self_weight_grad, text_weight_grads]
    run_order(MIDDLE_ORDER[5:], net.go, pieces)
    for i, dst in ((0, block_out), (1, text_out)):
        drain(dst.at[0:3], ex_recv.at[i])
        drain(dst.at[0:3], ex_send.at[i])
        drain(dst.at[0], local.at[6 + i])
    for i in range(len(kept)):
        if i not in (later["cq"], later["o"]):
            kept_done(i)


def middle(dims, args, cid):
    nz, ny, nx, nc = dims
    g, dh, x2, x1, vec, o2, cq, ck, cv, lse, h2, o, wco, wcq, wck, wcv, wo, text, limits, block_out, down, up = args
    rows, width = g.shape
    texts = text.shape[1]
    devices = nz * ny * nx * nc
    bf, f32 = jnp.bfloat16, jnp.float32
    each = width // devices
    long = down.shape[0] // devices
    down = down.reshape(nz, ny, nx, nc, long, width)
    up = up.reshape(nz, ny, nx, nc, each, up.shape[1])
    seg = block_out.shape
    held = jax.ShapeDtypeStruct((nz, ny, nx, nc, each, width), bf)
    wide, deep = jax.ShapeDtypeStruct((rows, width), bf), jax.ShapeDtypeStruct((rows, width), f32)
    out_shape = [
        jax.ShapeDtypeStruct(seg, bf), jax.ShapeDtypeStruct((seg[0], texts // seg[0], width), f32), deep, wide, held, held, held, held,
        jax.ShapeDtypeStruct((8, width), f32), jax.ShapeDtypeStruct((long, width), f32), jax.ShapeDtypeStruct((each, up.shape[5]), f32),
        jax.ShapeDtypeStruct((each, width), f32),
    ]
    any_spec, vm = pl.BlockSpec(memory_space=ANY), pl.BlockSpec(memory_space=pltpu.VMEM)
    big, square, short = pltpu.VMEM((rows, width), f32), pltpu.VMEM((rows, width), bf), pltpu.VMEM((texts, width), bf)
    dma = pltpu.SemaphoreType.DMA
    scratch = [big, big, big] + [square] * 10 + [short] * 4 + [pltpu.VMEM(lse.shape, f32), short]
    scratch += [pltpu.VMEM((seg[0], texts // seg[0], width), f32), pltpu.VMEM((2,) + held.shape, bf)]
    scratch += [pltpu.VMEM((texts, 128), f32)] * 2 + [pltpu.SMEM((1,), jnp.int32)]
    scratch += [dma((20,)), dma((12,)), dma((2,)), dma((2,)), dma((6,)), dma((6, 4)), dma((8,)), pltpu.VMEM(seg[1:], bf)]
    for j in range(4):
        scratch += scatter_room(dims, (long, width // 4), bf, MIDDLE_PATHS[j], False)
    scratch += scatter_room(dims, (each, up.shape[5]), bf, MIDDLE_PATHS[4], False)
    scratch += scatter_room(dims, (each, width), bf, MIDDLE_PATHS[5], True)
    specs = [any_spec] * 4 + [vm] + [any_spec] * 13 + [pl.BlockSpec(memory_space=pltpu.SMEM)] + [any_spec] * 3
    return pl.pallas_call(
        functools.partial(middle_kernel, dims),
        out_shape=out_shape,
        in_specs=specs,
        out_specs=[any_spec] * 8 + [vm] * 4,
        scratch_shapes=scratch,
        compiler_params=pltpu.CompilerParams(collective_id=cid, has_side_effects=True, vmem_limit_bytes=63 * 2**20),
        name="middle",
    )(g, dh, x2, x1, vec, o2, cq, ck, cv, lse, h2, o, wco, wcq, wck, wcv, wo, text, limits, block_out, down, up)


def last_kernel(dims, *refs):
    q_in, k_in, v_in, do_in, o_in, lse_in, h1_in, wq_in, wk_in, wv_in, x_in, dx_in, vec, gcq, gck, gcv, go, sums_in = refs[:18]
    grad_out, cq_out, ck_out, cv_out, o_out, q_out, k_out, v_out, small_out = refs[18:27]
    (q, k, v, do, o, lse, h_t, dq, dk, dv, dx, send_rows, small, dk_acc, dv_acc, sums,
     load_sem, ex_send, ex_recv, send, recv, local) = refs[27:49]
    rooms = refs[49:]
    at = Place(dims)
    nz, ny, nx, nc = dims
    oy, ox, oc, me = 1 - at.y, 1 - at.x, 1 - at.c, at.seq
    hello([at.dev(z=p) for p in at.z_others()] + [at.dev(y=oy), at.dev(x=ox), at.dev(c=oc), at.dev(x=ox, c=oc)])
    rows, width = q.shape
    block = 256
    f32, bf = jnp.float32, jnp.bfloat16
    every = slice(None)
    net = Scatter(dims, send, recv, local)
    room = [rooms[5 * j : 5 * j + 5] for j in range(10)] + [[small, *rooms[50:54]]]
    for j, (src, out) in enumerate(((gcq, cq_out), (gck, ck_out), (gcv, cv_out), (go, o_out))):
        net.add(lambda *w, src=src: src.at[w], room[j], out, LAST_PATHS[j], False)
    parts = ((0, LAST_SPLIT), (LAST_SPLIT, width - LAST_SPLIT))
    for j in range(6):
        out = (q_out, k_out, v_out)[j % 3].at[:, pl.ds(*parts[j // 3])]
        net.add(lambda *w, held=room[4 + j][0]: held.at[w], room[4 + j], out, LAST_PATHS[4 + j], True)
    net.add(lambda *w: small.at[w], room[10], small_out, LAST_PATHS[10], True)
    run_order(LAST_ORDER[:4], net.go, [])
    started = []

    def load(src, dst):
        pltpu.make_async_copy(src, dst, load_sem.at[len(started)]).start()
        started.append(dst)
        return len(started) - 1

    def loaded(i):
        drain(started[i], load_sem.at[i])

    first = [load(a, b) for a, b in ((q_in, q), (k_in, k), (v_in, v), (do_in, do), (o_in, o), (lse_in, lse), (h1_in, send_rows), (dx_in, dx))]

    def begin():
        for i in first[:6]:
            loaded(i)

    def transpose():
        loaded(first[6])
        loaded(first[7])

        @pl.loop(0, rows // block)
        def _(r):
            h_t[:, pl.ds(pl.multiple_of(r * block, block), block)] = send_rows[r].T

    def pair(j):
        cols = pl.ds(pl.multiple_of(j * 128, 128), 128)
        attend_back_kernel(
            True, 256, None, q.at[:, cols], k.at[:, cols], v.at[:, cols], do.at[:, cols], o.at[:, cols], lse.at[pl.ds(j, 1)],
            dq.at[:, cols], dk.at[:, cols], dv.at[:, cols], dk_acc, dv_acc,
        )

    weights = []

    def weight_grads(part):
        if part == 0:
            transpose()
        if part == 1:
            weights.extend(load(a, b) for a, b in ((wq_in, q), (wk_in, k), (wv_in, v), (x_in, do)))
        for j, grad in enumerate((dq, dk, dv)):
            made = room[4 + 3 * part + j][0]

            @pl.loop(0, nz)
            def _(a, made=made, grad=grad):
                span = pl.ds(pl.multiple_of(a * block, block), block)
                product = dot(h_t[span, :], grad[:, pl.ds(*parts[part])]).astype(bf)
                made[a] = product.reshape(made.shape[1:])

        if part == 1:
            for i in weights:
                loaded(i)
            sums[...] = sums_in[...]

    def last_norm(r):
        span = pl.ds(pl.multiple_of(r * block, block), block)
        d = dot(dq[span, :], q[...], NT) + dot(dk[span, :], k[...], NT) + dot(dv[span, :], v[...], NT)
        grad, gain_terms = norm_back(do[span, :].astype(f32), d, vec[0:1, :])
        sums[0:1, :] += row_sum(gain_terms)
        sums[1:2, :] += row_sum(d)
        send_rows[r] = (dx[span, :] + grad).astype(bf)

    targets = ((ox, at.c), (ox, oc), (at.x, oc), (at.x, at.c))

    def send_norm(i):
        px, pc = targets[i]
        last_norm(px * 2 + pc)
        if i < 3:
            push(send_rows.at[px * 2 + pc], grad_out.at[me], ex_send, ex_recv, at.dev(x=px, c=pc))
        else:
            pltpu.make_async_copy(send_rows.at[me], grad_out.at[me], local.at[11]).start()

    def share_sums():
        devices = nz * ny * nx * nc
        piece = width // devices
        lanes = lax.broadcasted_iota(jnp.int32, (width, 128), 0)
        fold = jnp.where(lax.rem(lanes, piece) == lax.broadcasted_iota(jnp.int32, (width, 128), 1), 1.0, 0.0).astype(bf)
        mine = lax.div(lax.broadcasted_iota(jnp.int32, (devices, width), 1), piece) == lax.broadcasted_iota(jnp.int32, (devices, width), 0)
        shares = []
        for i in range(6):
            spread = jnp.where(mine, sums[i : i + 1, :], 0.0)
            total = jnp.zeros((devices, 128), f32)
            for _ in range(3):
                low = spread.astype(bf)
                spread = spread - low.astype(f32)
                total = total + dot(low, fold)
            shares.append(total[:, None, :])
        shares.append(jnp.zeros((devices, 2, 128), f32))
        small[...] = jnp.concatenate(shares, axis=1).reshape(small.shape)

    split = LAST_SPLIT // 128
    pieces = [begin] + [(pair, j) for j in range(split)] + [lambda: weight_grads(0)]
    pieces += [(pair, j) for j in range(split, width // 128)] + [lambda: weight_grads(1)]
    pieces += [functools.partial(send_norm, i) for i in range(4)] + [share_sums]
    run_order(LAST_ORDER[4:], net.go, pieces)
    drain(grad_out.at[0:3], ex_recv)
    drain(grad_out.at[0:3], ex_send)
    drain(grad_out.at[0], local.at[11])


def last(dims, args, cid):
    nz, ny, nx, nc = dims
    q, k, v, do, o, lse, h1, wq, wk, wv, x, dx, vec, gcq, gck, gcv, go, sums = args
    rows, width = q.shape
    bf, f32 = jnp.bfloat16, jnp.float32
    each = width // (nz * ny * nx * nc)
    shard = jax.ShapeDtypeStruct((each, width), f32)
    out_shape = [jax.ShapeDtypeStruct((4, rows // 4, width), bf)] + [shard] * 7 + [jax.ShapeDtypeStruct((8, 128), f32)]
    any_spec, vm = pl.BlockSpec(memory_space=ANY), pl.BlockSpec(memory_space=pltpu.VMEM)
    square = pltpu.VMEM((rows, width), bf)
    dma = pltpu.SemaphoreType.DMA
    scratch = [square] * 5 + [pltpu.VMEM(lse.shape, f32)] + [square] * 4 + [pltpu.VMEM((rows, width), f32), pltpu.VMEM((4, rows // 4, width), bf)]
    scratch += [pltpu.VMEM((nz, ny, nx, nc, 8, 128), f32)] + [pltpu.VMEM((rows, 128), f32)] * 2 + [pltpu.VMEM((8, width), f32)]
    scratch += [dma((16,)), dma, dma, dma((11,)), dma((11, 4)), dma((12,))]
    for j in range(4):
        scratch += scatter_room(dims, (each, width), bf, LAST_PATHS[j], False)
    for j in range(6):
        scratch += scatter_room(dims, (each, LAST_SPLIT if j < 3 else width - LAST_SPLIT), bf, LAST_PATHS[4 + j], True)
    scratch += scatter_room(dims, (8, 128), f32, LAST_PATHS[10], True)[1:]
    return pl.pallas_call(
        functools.partial(last_kernel, dims),
        out_shape=out_shape,
        in_specs=[any_spec] * 12 + [vm] + [any_spec] * 4 + [vm],
        out_specs=[any_spec] + [vm] * 8,
        scratch_shapes=scratch,
        compiler_params=pltpu.CompilerParams(collective_id=cid, has_side_effects=True, vmem_limit_bytes=63 * 2**20),
        name="last",
    )(q, k, v, do, o, lse, h1.reshape(4, rows // 4, width), wq, wk, wv, x, dx, vec, gcq, gck, gcv, go, sums)

HEAD_DIM = 64


EPS = 1e-05


def norm_rows(values_in, gain, bias):
    center = values_in - jnp.mean(values_in, axis=-1, keepdims=True)
    spread = jnp.mean(center * center, axis=-1, keepdims=True)
    return center * lax.rsqrt(spread + EPS) * gain + bias


def contract_rows(left, right):
    return lax.dot_general(
        left, right, (((0,), (0,)), ((), ())), preferred_element_type=jnp.float32
    )


def times_transposed(left, right):
    return lax.dot_general(
        left, right, (((1,), (1,)), ((), ())), preferred_element_type=jnp.float32
    )


def product(left, right):
    return jnp.dot(left, right, preferred_element_type=jnp.float32)


def local_plain(
    block_in,
    text_states,
    caption_len,
    out_grad,
    first_gain,
    first_bias,
    query_weight,
    key_weight,
    value_weight,
    output_weight,
    second_gain,
    second_bias,
    cross_query,
    cross_key,
    cross_value,
    cross_output,
    third_gain,
    third_bias,
    up_weight,
    down_weight,
):
    gathered = (
        lax.all_gather(first_gain, ("dp", "seq"), axis=0, tiled=True),
        lax.all_gather(first_bias, ("dp", "seq"), axis=0, tiled=True),
        lax.all_gather(query_weight, ("dp", "seq"), axis=0, tiled=True),
        lax.all_gather(key_weight, ("dp", "seq"), axis=0, tiled=True),
        lax.all_gather(value_weight, ("dp", "seq"), axis=0, tiled=True),
        lax.all_gather(output_weight, ("dp", "seq"), axis=0, tiled=True),
        lax.all_gather(second_gain, ("dp", "seq"), axis=0, tiled=True),
        lax.all_gather(second_bias, ("dp", "seq"), axis=0, tiled=True),
        lax.all_gather(cross_query, ("dp", "seq"), axis=0, tiled=True),
        lax.all_gather(cross_key, ("dp", "seq"), axis=0, tiled=True),
        lax.all_gather(cross_value, ("dp", "seq"), axis=0, tiled=True),
        lax.all_gather(cross_output, ("dp", "seq"), axis=0, tiled=True),
        lax.all_gather(third_gain, ("dp", "seq"), axis=0, tiled=True),
        lax.all_gather(third_bias, ("dp", "seq"), axis=0, tiled=True),
        lax.all_gather(up_weight, ("dp", "seq"), axis=0, tiled=True),
        lax.all_gather(down_weight, ("dp", "seq"), axis=0, tiled=True),
    )
    (
        gain_one,
        bias_one,
        w_query,
        w_key,
        w_value,
        w_output,
        gain_two,
        bias_two,
        w_cquery,
        w_ckey,
        w_cvalue,
        w_coutput,
        gain_three,
        bias_three,
        w_up,
        w_down,
    ) = gathered
    item_count, seg_len, model_width = block_in.shape
    row_count = item_count * seg_len
    head_count = model_width // HEAD_DIM
    score_scale = HEAD_DIM ** (-0.5)
    text_count = text_states.shape[1]
    inputs_f = block_in.astype(jnp.float32).reshape(row_count, model_width)
    normed_one, pull_one = jax.vjp(
        norm_rows, inputs_f, gain_one.astype(jnp.float32), bias_one.astype(jnp.float32)
    )
    normed_one = normed_one.astype(jnp.bfloat16)
    query_rows = product(normed_one, w_query).astype(jnp.bfloat16)
    key_rows = product(normed_one, w_key).astype(jnp.bfloat16)
    value_rows = product(normed_one, w_value).astype(jnp.bfloat16)
    key_all, value_all = (
        lax.all_gather(
            key_rows.reshape(item_count, seg_len, model_width), "seq", axis=1, tiled=True
        ),
        lax.all_gather(
            value_rows.reshape(item_count, seg_len, model_width), "seq", axis=1, tiled=True
        ),
    )
    key_count = key_all.shape[1]
    first_pos = lax.axis_index("seq") * seg_len
    query_pos = first_pos + jnp.arange(seg_len, dtype=jnp.int32)
    causal = jnp.arange(key_count, dtype=jnp.int32)[None, :] <= query_pos[:, None]

    def self_scores(query_item, key_item):
        query_heads = query_item.reshape(seg_len, head_count, HEAD_DIM)
        key_heads = key_item.reshape(key_count, head_count, HEAD_DIM)
        scores = jnp.einsum(
            "qhd,khd->hqk", query_heads, key_heads, preferred_element_type=jnp.float32
        )
        return jnp.where(causal[None, :, :], scores * score_scale, -1e30)

    def self_forward(operands):
        query_item, key_item, value_item = operands
        scores = self_scores(query_item, key_item)
        row_peak = jnp.max(scores, axis=-1, keepdims=True)
        row_total = jnp.sum(jnp.exp(scores - row_peak), axis=-1, keepdims=True)
        log_total = row_peak + jnp.log(row_total)
        prob_bf = jnp.exp(scores - log_total).astype(jnp.bfloat16)
        value_heads = value_item.reshape(key_count, head_count, HEAD_DIM)
        mixed = jnp.einsum("hqk,khd->qhd", prob_bf, value_heads, preferred_element_type=jnp.float32)
        return (mixed.reshape(seg_len, model_width).astype(jnp.bfloat16), log_total)

    attended, log_totals = lax.map(
        self_forward, (query_rows.reshape(item_count, seg_len, model_width), key_all, value_all)
    )
    attended_rows = attended.reshape(row_count, model_width)
    after_self = inputs_f + product(attended_rows, w_output)
    normed_two, pull_two = jax.vjp(
        norm_rows, after_self, gain_two.astype(jnp.float32), bias_two.astype(jnp.float32)
    )
    normed_two = normed_two.astype(jnp.bfloat16)
    cross_rows = product(normed_two, w_cquery).astype(jnp.bfloat16)
    cross_heads = cross_rows.reshape(item_count, seg_len, head_count, HEAD_DIM)
    text_keys = jnp.einsum(
        "itc,cd->itd", text_states, w_ckey, preferred_element_type=jnp.float32
    ).astype(jnp.bfloat16)
    text_values = jnp.einsum(
        "itc,cd->itd", text_states, w_cvalue, preferred_element_type=jnp.float32
    ).astype(jnp.bfloat16)
    text_kheads = text_keys.reshape(item_count, text_count, head_count, HEAD_DIM)
    text_vheads = text_values.reshape(item_count, text_count, head_count, HEAD_DIM)
    text_mask = jnp.arange(text_count, dtype=jnp.int32)[None, :] < caption_len[:, None]
    cross_scores = jnp.einsum(
        "iqhd,ithd->ihqt", cross_heads, text_kheads, preferred_element_type=jnp.float32
    )
    cross_scores = jnp.where(text_mask[:, None, None, :], cross_scores * score_scale, -1e30)
    cross_peak = jnp.max(cross_scores, axis=-1, keepdims=True)
    cross_exp = jnp.exp(cross_scores - cross_peak)
    cross_prob = cross_exp / jnp.sum(cross_exp, axis=-1, keepdims=True)
    cross_prob_bf = cross_prob.astype(jnp.bfloat16)
    crossed = jnp.einsum(
        "ihqt,ithd->iqhd", cross_prob_bf, text_vheads, preferred_element_type=jnp.float32
    )
    crossed_rows = crossed.reshape(row_count, model_width).astype(jnp.bfloat16)
    after_cross = after_self + product(crossed_rows, w_coutput)
    normed_three, pull_three = jax.vjp(
        norm_rows, after_cross, gain_three.astype(jnp.float32), bias_three.astype(jnp.float32)
    )
    normed_three = normed_three.astype(jnp.bfloat16)
    hidden = product(normed_three, w_up)
    activated, pull_gelu = jax.vjp(lambda inner: jax.nn.gelu(inner, approximate=False), hidden)
    activated = activated.astype(jnp.bfloat16)
    layer_out = after_cross + product(activated, w_down)
    block_out = layer_out.astype(jnp.bfloat16).reshape(item_count, seg_len, model_width)
    back_weights = (
        lax.all_gather(first_gain, ("dp", "seq"), axis=0, tiled=True),
        lax.all_gather(first_bias, ("dp", "seq"), axis=0, tiled=True),
        lax.all_gather(query_weight, ("dp", "seq"), axis=0, tiled=True),
        lax.all_gather(key_weight, ("dp", "seq"), axis=0, tiled=True),
        lax.all_gather(value_weight, ("dp", "seq"), axis=0, tiled=True),
        lax.all_gather(output_weight, ("dp", "seq"), axis=0, tiled=True),
        lax.all_gather(second_gain, ("dp", "seq"), axis=0, tiled=True),
        lax.all_gather(second_bias, ("dp", "seq"), axis=0, tiled=True),
        lax.all_gather(cross_query, ("dp", "seq"), axis=0, tiled=True),
        lax.all_gather(cross_key, ("dp", "seq"), axis=0, tiled=True),
        lax.all_gather(cross_value, ("dp", "seq"), axis=0, tiled=True),
        lax.all_gather(cross_output, ("dp", "seq"), axis=0, tiled=True),
        lax.all_gather(third_gain, ("dp", "seq"), axis=0, tiled=True),
        lax.all_gather(third_bias, ("dp", "seq"), axis=0, tiled=True),
        lax.all_gather(up_weight, ("dp", "seq"), axis=0, tiled=True),
        lax.all_gather(down_weight, ("dp", "seq"), axis=0, tiled=True),
    )
    (
        unused_gain,
        unused_bias,
        w_query,
        w_key,
        w_value,
        w_output,
        unused_gtwo,
        unused_btwo,
        w_cquery,
        w_ckey,
        w_cvalue,
        w_coutput,
        unused_gthree,
        unused_bthree,
        w_up,
        w_down,
    ) = back_weights
    grad_rows = out_grad.reshape(row_count, model_width)
    down_part = contract_rows(activated, grad_rows)
    act_grad = times_transposed(grad_rows, w_down)
    hidden_grad = pull_gelu(act_grad)[0].astype(jnp.bfloat16)
    up_part = contract_rows(normed_three, hidden_grad)
    normed_three_grad = times_transposed(hidden_grad, w_up)
    resid_three, gain_three_part, bias_three_part = pull_three(normed_three_grad)
    cross_grad = grad_rows.astype(jnp.float32) + resid_three
    cross_out_bf = cross_grad.astype(jnp.bfloat16)
    coutput_part = contract_rows(crossed_rows, cross_out_bf)
    crossed_grad = times_transposed(cross_out_bf, w_coutput).astype(jnp.bfloat16)
    crossed_heads = crossed_grad.reshape(item_count, seg_len, head_count, HEAD_DIM)
    cross_dprob = jnp.einsum(
        "iqhd,ithd->ihqt", crossed_heads, text_vheads, preferred_element_type=jnp.float32
    )
    cross_dscore = cross_prob * (
        cross_dprob - jnp.sum(cross_dprob * cross_prob, axis=-1, keepdims=True)
    )
    cross_dscore = cross_dscore.astype(jnp.bfloat16)
    cquery_grad = (
        (
            jnp.einsum(
                "ihqt,ithd->iqhd", cross_dscore, text_kheads, preferred_element_type=jnp.float32
            )
            * score_scale
        )
        .astype(jnp.bfloat16)
        .reshape(row_count, model_width)
    )
    tkey_part = (
        jnp.einsum("ihqt,iqhd->ithd", cross_dscore, cross_heads, preferred_element_type=jnp.float32)
        * score_scale
    ).reshape(item_count, text_count, model_width)
    tvalue_part = jnp.einsum(
        "ihqt,iqhd->ithd", cross_prob_bf, crossed_heads, preferred_element_type=jnp.float32
    ).reshape(item_count, text_count, model_width)
    cquery_part = contract_rows(normed_two, cquery_grad)
    normed_two_grad = times_transposed(cquery_grad, w_cquery)
    resid_two, gain_two_part, bias_two_part = pull_two(normed_two_grad)
    self_grad = cross_grad + resid_two
    self_out_bf = self_grad.astype(jnp.bfloat16)
    output_part = contract_rows(attended_rows, self_out_bf)
    attended_grad = times_transposed(self_out_bf, w_output).astype(jnp.bfloat16)
    query_items = query_rows.reshape(item_count, seg_len, model_width)
    dout_items = attended_grad.reshape(item_count, seg_len, model_width)

    def self_backward(operands):
        query_item, key_item, value_item, dout_item, log_total = operands
        scores = self_scores(query_item, key_item)
        probs = jnp.exp(scores - log_total)
        prob_bf = probs.astype(jnp.bfloat16)
        query_heads = query_item.reshape(seg_len, head_count, HEAD_DIM)
        key_heads = key_item.reshape(key_count, head_count, HEAD_DIM)
        value_heads = value_item.reshape(key_count, head_count, HEAD_DIM)
        dout_heads = dout_item.reshape(seg_len, head_count, HEAD_DIM)
        dprob = jnp.einsum(
            "qhd,khd->hqk", dout_heads, value_heads, preferred_element_type=jnp.float32
        )
        dscore = (probs * (dprob - jnp.sum(dprob * probs, axis=-1, keepdims=True))).astype(
            jnp.bfloat16
        )
        dquery = (
            (
                jnp.einsum("hqk,khd->qhd", dscore, key_heads, preferred_element_type=jnp.float32)
                * score_scale
            )
            .astype(jnp.bfloat16)
            .reshape(seg_len, model_width)
        )
        dkey = (
            jnp.einsum("hqk,qhd->khd", dscore, query_heads, preferred_element_type=jnp.float32)
            * score_scale
        ).reshape(key_count, model_width)
        dvalue = jnp.einsum(
            "hqk,qhd->khd", prob_bf, dout_heads, preferred_element_type=jnp.float32
        ).reshape(key_count, model_width)
        return (dquery, dkey, dvalue)

    query_grad_items, key_part, value_part = lax.map(
        self_backward, (query_items, key_all, value_all, dout_items, log_totals)
    )
    key_own, value_own, tkey_own, tvalue_own = (
        lax.psum_scatter(
            key_part.astype(jnp.bfloat16), "seq", scatter_dimension=1, tiled=True
        ).astype(jnp.float32),
        lax.psum_scatter(
            value_part.astype(jnp.bfloat16), "seq", scatter_dimension=1, tiled=True
        ).astype(jnp.float32),
        lax.psum_scatter(
            tkey_part.astype(jnp.bfloat16), "seq", scatter_dimension=1, tiled=True
        ).astype(jnp.float32),
        lax.psum_scatter(
            tvalue_part.astype(jnp.bfloat16), "seq", scatter_dimension=1, tiled=True
        ).astype(jnp.float32),
    )
    key_grad_rows = key_own.astype(jnp.bfloat16).reshape(row_count, model_width)
    value_grad_rows = value_own.astype(jnp.bfloat16).reshape(row_count, model_width)
    query_grad_rows = query_grad_items.reshape(row_count, model_width)
    tkey_bf = tkey_own.astype(jnp.bfloat16)
    tvalue_bf = tvalue_own.astype(jnp.bfloat16)
    query_part = contract_rows(normed_one, query_grad_rows)
    key_wpart = contract_rows(normed_one, key_grad_rows)
    value_wpart = contract_rows(normed_one, value_grad_rows)
    normed_one_grad = (
        times_transposed(query_grad_rows, w_query)
        + times_transposed(key_grad_rows, w_key)
        + times_transposed(value_grad_rows, w_value)
    )
    resid_one, gain_one_part, bias_one_part = pull_one(normed_one_grad)
    input_grad = (self_grad + resid_one).reshape(item_count, seg_len, model_width)
    text_rows = tkey_own.shape[1]
    text_start = lax.axis_index("seq") * text_rows
    text_slice = lax.dynamic_slice_in_dim(text_states, text_start, text_rows, 1)
    ckey_part = jnp.einsum("itc,itd->cd", text_slice, tkey_bf, preferred_element_type=jnp.float32)
    cvalue_part = jnp.einsum(
        "itc,itd->cd", text_slice, tvalue_bf, preferred_element_type=jnp.float32
    )
    text_grad = jnp.einsum(
        "itd,cd->itc", tkey_bf, w_ckey, preferred_element_type=jnp.float32
    ) + jnp.einsum("itd,cd->itc", tvalue_bf, w_cvalue, preferred_element_type=jnp.float32)
    (
        first_gain_grad,
        first_bias_grad,
        query_grad,
        key_grad,
        value_grad,
        output_grad,
        second_gain_grad,
        second_bias_grad,
        cross_query_grad,
        cross_key_grad,
        cross_value_grad,
        cross_output_grad,
        third_gain_grad,
        third_bias_grad,
        up_grad,
        down_grad,
    ) = (
        lax.psum_scatter(gain_one_part, ("dp", "seq"), scatter_dimension=0, tiled=True),
        lax.psum_scatter(bias_one_part, ("dp", "seq"), scatter_dimension=0, tiled=True),
        lax.psum_scatter(query_part, ("dp", "seq"), scatter_dimension=0, tiled=True),
        lax.psum_scatter(key_wpart, ("dp", "seq"), scatter_dimension=0, tiled=True),
        lax.psum_scatter(value_wpart, ("dp", "seq"), scatter_dimension=0, tiled=True),
        lax.psum_scatter(output_part, ("dp", "seq"), scatter_dimension=0, tiled=True),
        lax.psum_scatter(gain_two_part, ("dp", "seq"), scatter_dimension=0, tiled=True),
        lax.psum_scatter(bias_two_part, ("dp", "seq"), scatter_dimension=0, tiled=True),
        lax.psum_scatter(cquery_part, ("dp", "seq"), scatter_dimension=0, tiled=True),
        lax.psum_scatter(ckey_part, ("dp", "seq"), scatter_dimension=0, tiled=True),
        lax.psum_scatter(cvalue_part, ("dp", "seq"), scatter_dimension=0, tiled=True),
        lax.psum_scatter(coutput_part, ("dp", "seq"), scatter_dimension=0, tiled=True),
        lax.psum_scatter(gain_three_part, ("dp", "seq"), scatter_dimension=0, tiled=True),
        lax.psum_scatter(bias_three_part, ("dp", "seq"), scatter_dimension=0, tiled=True),
        lax.psum_scatter(up_part, ("dp", "seq"), scatter_dimension=0, tiled=True),
        lax.psum_scatter(down_part, ("dp", "seq"), scatter_dimension=0, tiled=True),
    )
    return (
        block_out,
        input_grad,
        text_grad,
        first_gain_grad,
        first_bias_grad,
        query_grad,
        key_grad,
        value_grad,
        output_grad,
        second_gain_grad,
        second_bias_grad,
        cross_query_grad,
        cross_key_grad,
        cross_value_grad,
        cross_output_grad,
        third_gain_grad,
        third_bias_grad,
        up_grad,
        down_grad,
    )


def small_rows(vectors):
    packed = jnp.stack(vectors)
    return jnp.pad(packed, ((0, 16 - packed.shape[0]), (0, 128 - packed.shape[1])))


def local(seq_size, *args):
    block_in = args[0]
    if block_in.shape[0] != seq_size or seq_size != 4 or block_in.shape[1] * seq_size != 1024:
        return local_plain(*args)
    return local_items(seq_size, *args)


def local_items(
    seq_size,
    block_in,
    text_states,
    caption_len,
    out_grad,
    first_gain,
    first_bias,
    query_weight,
    key_weight,
    value_weight,
    output_weight,
    second_gain,
    second_bias,
    cross_query,
    cross_key,
    cross_value,
    cross_output,
    third_gain,
    third_bias,
    up_weight,
    down_weight,
):
    ny, nx, nc = 2, seq_size // 2, 2
    dp_size = 1024 // first_gain.shape[0] // seq_size
    dims = (dp_size // ny, ny, nx, nc)
    bf, f32 = jnp.bfloat16, jnp.float32
    seg, width = block_in.shape[1], block_in.shape[2]
    rows = seq_size * seg
    me = lax.axis_index("seq")
    small = small_rows([first_gain, first_bias, second_gain, second_bias, third_gain, third_bias])
    shards = [small, query_weight, key_weight, value_weight, output_weight, cross_query, cross_key, cross_value, cross_output, up_weight, down_weight]
    full, kept = forward(dims, shards, block_in, out_grad, text_states, caption_len, 1)
    small, w_query, w_key, w_value, w_output, w_cquery, w_ckey, w_cvalue, w_coutput, w_up, w_down = full
    grad_rows, inputs, q, k, v, cq, ck, cv, o, o2, normed_one, normed_two, normed_three, after_self, after_cross, lse, lse2, vectors = kept
    grad_rows = grad_rows.reshape(rows, width)
    block_out, dh3, down_part, up_grad_done, up_part = ffn(dims, normed_three, grad_rows, after_cross, w_up, w_down, up_weight, 4)
    (
        block_out, text_grad, self_grad, do, g_cq, g_ck, g_cv, g_o, sums, down_grad, up_grad, coutput_grad,
    ) = middle(dims, (
        grad_rows, dh3, after_cross, after_self, vectors, o2, cq, ck, cv, lse2, normed_two, o, w_coutput, w_cquery, w_ckey, w_cvalue,
        w_output, text_states, caption_len, block_out.reshape(seq_size, seg, width), down_part, up_part,
    ), 2)
    up_grad = jnp.concatenate([up_grad_done, up_grad], axis=1)
    (
        input_grad, cquery_grad, ckey_grad, cvalue_grad, output_grad, query_grad, key_grad, value_grad, small_grad,
    ) = last(dims, (
        q, k, v, do, o, lse, normed_one, w_query, w_key, w_value, inputs.reshape(rows, width), self_grad, vectors,
        g_cq, g_ck, g_cv, g_o, sums,
    ), 3)
    input_grad = input_grad.astype(f32)
    vec = [small_grad[i, : first_gain.shape[0]] for i in range(6)]
    return (
        block_out, input_grad, text_grad,
        vec[0], vec[1], query_grad, key_grad, value_grad, output_grad,
        vec[2], vec[3], cquery_grad, ckey_grad, cvalue_grad, coutput_grad,
        vec[4], vec[5], up_grad, down_grad,
    )


def solution(mesh):
    return jax.shard_map(
        functools.partial(local, mesh.shape['seq']),
        mesh=mesh,
        in_specs=(
            P("dp", "seq", None),
            P("dp", None, None),
            P("dp"),
            P("dp", "seq", None),
            P(("dp", "seq")),
            P(("dp", "seq")),
            P(("dp", "seq"), None),
            P(("dp", "seq"), None),
            P(("dp", "seq"), None),
            P(("dp", "seq"), None),
            P(("dp", "seq")),
            P(("dp", "seq")),
            P(("dp", "seq"), None),
            P(("dp", "seq"), None),
            P(("dp", "seq"), None),
            P(("dp", "seq"), None),
            P(("dp", "seq")),
            P(("dp", "seq")),
            P(("dp", "seq"), None),
            P(("dp", "seq"), None),
        ),
        out_specs=(
            P("dp", "seq", None),
            P("dp", "seq", None),
            P("dp", "seq", None),
            P(("dp", "seq")),
            P(("dp", "seq")),
            P(("dp", "seq"), None),
            P(("dp", "seq"), None),
            P(("dp", "seq"), None),
            P(("dp", "seq"), None),
            P(("dp", "seq")),
            P(("dp", "seq")),
            P(("dp", "seq"), None),
            P(("dp", "seq"), None),
            P(("dp", "seq"), None),
            P(("dp", "seq"), None),
            P(("dp", "seq")),
            P(("dp", "seq")),
            P(("dp", "seq"), None),
            P(("dp", "seq"), None),
        ),
        check_vma=False,
    )
```

```python
import functools
import itertools

import jax
import jax.numpy as jnp
from jax import lax
from jax.experimental import pallas as pl
from jax.experimental.pallas import tpu as pltpu
from jax.sharding import PartitionSpec as P

MESH = pl.DeviceIdType.MESH
ANY = pl.ANY


class Place:
    def __init__(self, dims):
        self.nz, self.ny, self.nx, self.nc = dims
        dp, seq = lax.axis_index("dp"), lax.axis_index("seq")
        self.z, self.y = lax.div(dp, self.ny), lax.rem(dp, self.ny)
        self.x, self.c = lax.div(seq, self.nc), lax.rem(seq, self.nc)
        self.dp, self.seq = dp, seq

    def dev(self, z=None, y=None, x=None, c=None):
        z = self.z if z is None else z
        y = self.y if y is None else y
        x = self.x if x is None else x
        c = self.c if c is None else c
        return (z * self.ny + y, x * self.nc + c)

    def z_others(self):
        if self.nz != 4:
            return [lax.rem(self.z + k, self.nz) for k in range(1, self.nz)]
        near, far = 1 + lax.rem(self.z, 2), 3 - 3 * lax.div(self.z, 2)
        return [near, 6 - self.z - near - far, far]


def hello(peers):
    barrier = pltpu.get_barrier_semaphore()
    for peer in peers:
        pl.semaphore_signal(barrier, inc=1, device_id=peer, device_id_type=MESH)
    pl.semaphore_wait(barrier, len(peers))


def push(src, dst, send, recv, device):
    pltpu.make_async_remote_copy(
        src_ref=src, dst_ref=dst, send_sem=send, recv_sem=recv, device_id=device, device_id_type=MESH
    ).start()


def drain(ref, sem):
    pltpu.make_async_copy(ref, ref, sem).wait()


def add_to(dst, src):
    dst[...] = dst[...] + src[...]


LOG2E = 1.4426950408889634
NT = (((1,), (1,)), ((), ()))
NN = (((1,), (0,)), ((), ()))
def dot(a, b, dims=NN):
    return lax.dot_general(a, b, dims, preferred_element_type=jnp.float32)

def half_mask(x, h):
    lane = lax.broadcasted_iota(jnp.int32, x.shape, 1)
    keep = lane < 64 if h == 0 else lane >= 64
    return jnp.where(keep, x, jnp.zeros_like(x))

def hide(scores, limit, causal, start):
    rows, cols = scores.shape
    if causal:
        key = lax.broadcasted_iota(jnp.int32, (cols, cols), 0)
        query = lax.broadcasted_iota(jnp.int32, (cols, cols), 1)
        tail = jnp.where(key <= query, scores[rows - cols:], -1e30)
        return tail if rows == cols else jnp.concatenate([scores[:rows - cols], tail], axis=0)
    key = lax.broadcasted_iota(jnp.int32, (rows, cols), 0)
    return jnp.where(key < limit, scores, -1e30)

def attend_kernel(causal, block, limit_ref, q_ref, k_ref, v_ref, o_ref, lse_ref):
    limit = None if causal else limit_ref[0]
    rows, keys = q_ref.shape[0], k_ref.shape[0]
    v_t = v_ref[...].T
    ones = jnp.ones((16, keys), v_t.dtype)
    for i in range(rows // block):
        n = (i + 1) * block if causal else keys
        span = pl.ds(i * block, block)
        halves = []
        for h in range(2):
            q = half_mask(q_ref[span, :], h)
            s = hide(dot(k_ref[0:n, :], q, NT), limit, causal, i * block)
            peak = jnp.max(s, axis=0, keepdims=True)
            e = jnp.exp2(s - peak).astype(jnp.bfloat16)
            v_aug = jnp.concatenate([v_t[h * 64:(h + 1) * 64, :n], ones[:, :n]], axis=0)
            mixed = dot(v_aug, e)
            total = mixed[64:65]
            halves.append(mixed[:64] / total)
            lse_ref[0, h:h + 1, span] = peak + jnp.log2(total)
        o_ref[span, :] = jnp.concatenate(halves, axis=0).T.astype(o_ref.dtype)

def attend_back_kernel(causal, block, limit_ref, q_ref, k_ref, v_ref, g_ref, o_ref, lse_ref, dq_ref, dk_ref, dv_ref, dk_acc, dv_acc):
    limit = None if causal else limit_ref[0]
    rows, keys = q_ref.shape[0], k_ref.shape[0]
    k_t = k_ref[...].T
    sel_row = lax.broadcasted_iota(jnp.int32, (16, 128), 0)
    sel_lane = lax.broadcasted_iota(jnp.int32, (16, 128), 1)
    pick = jnp.where(sel_row == lax.div(sel_lane, 64), 1.0, 0.0).astype(jnp.bfloat16)
    dk_acc[...] = jnp.zeros_like(dk_acc)
    dv_acc[...] = jnp.zeros_like(dv_acc)
    for i in range(rows // block):
        n = (i + 1) * block if causal else keys
        span = pl.ds(i * block, block)
        prod = g_ref[span, :].astype(jnp.float32) * o_ref[span, :].astype(jnp.float32)
        high = prod.astype(jnp.bfloat16)
        low = (prod - high.astype(jnp.float32)).astype(jnp.bfloat16)
        delta = dot(pick, high, NT) + dot(pick, low, NT)
        halves = []
        for h in range(2):
            q = half_mask(q_ref[span, :], h)
            g = half_mask(g_ref[span, :], h)
            s = hide(dot(k_ref[0:n, :], q, NT), limit, causal, i * block)
            p = jnp.exp2(s - lse_ref[0, h:h + 1, span])
            dp = dot(v_ref[0:n, :], g, NT)
            ds = (p * (dp - delta[h:h + 1])).astype(jnp.bfloat16)
            dv_acc[0:n, :] += dot(p.astype(jnp.bfloat16), g)
            dk_acc[0:n, :] += dot(ds, q)
            halves.append(dot(k_t[h * 64:(h + 1) * 64, :n], ds))
        dq_ref[span, :] = (jnp.concatenate(halves, axis=0).T * 0.125).astype(dq_ref.dtype)
    dk_ref[...] = (dk_acc[...] * (1.0 / LOG2E)).astype(dk_ref.dtype)
    dv_ref[...] = dv_acc[...].astype(dv_ref.dtype)

def gelu_parts(u):
    t = 1.0 / (1.0 + (0.3275911 * 0.7071067811865476) * jnp.abs(u))
    e = jnp.exp(-0.5 * (u * u))
    poly = t * (0.254829592 + t * (-0.284496736 + t * (1.421413741 + t * (-1.453152027 + t * 1.061405429))))
    tail = 0.5 * poly * e
    return jnp.where(u < 0, tail, 1.0 - tail), e * 0.3989422804014327


def ffn_kernel(dims, sent, h_ref, g_ref, x_ref, up_in, down_ref, shard_ref, out_ref, dh_ref, ddown_ref, grad_ref, rest_ref,
               h_t, acc, act, du, made, own, rc, r2a, r2b, r3, r4, local_sem, send, recv,
               late, near, up_ref, late_send, late_recv):
    j = pl.program_id(0)
    steps = pl.num_programs(0)
    at = Place(dims)
    nz, ny, nx, nc = dims
    z, y, x, c = at.z, at.y, at.x, at.c
    oy, ox, oc = 1 - y, 1 - x, 1 - c
    rows, width = h_ref.shape
    chunk = up_in.shape[1]
    last = steps - 1
    net = Gather(dims, [(0, 0, near.shape[0], 0, chunk, (2, 1, 0))], [near], [late], late_send, late_recv)
    half = chunk // 2
    block = rows // 2
    left, right = pl.ds(0, half), pl.ds(half, half)
    every = slice(None)

    def made_at(slot, core):
        return made.at[(slot, every, every, every, core)]

    def core_go(i):
        slot = lax.rem(i, 2)
        pltpu.make_async_copy(made_at(slot, c), own.at[i], local_sem.at[i]).start()
        push(made_at(slot, oc), rc.at[i], send.at[i, 0], recv.at[i, 0], at.dev(c=oc))

    def first_go(i):
        drain(own.at[i], local_sem.at[i])
        drain(rc.at[i], recv.at[i, 0])
        drain(rc.at[i], send.at[i, 0])

        @pl.loop(0, nz)
        def _(a):
            for b in range(ny):
                for d in range(nx):
                    add_to(own.at[i, a, b, d], rc.at[i, a, b, d])

        push(own.at[i, :, oy, :, :, left], r2a.at[i], send.at[i, 1], recv.at[i, 1], at.dev(y=oy))
        push(own.at[i, :, :, ox, :, right], r2b.at[i], send.at[i, 1], recv.at[i, 2], at.dev(x=ox))

    def second_go(i):
        drain(r2a.at[i], recv.at[i, 1])
        drain(r2b.at[i], recv.at[i, 2])

        @pl.loop(0, nz)
        def _(a):
            for b in range(2):
                add_to(own.at[i, a, y, b, :, left], r2a.at[i, a, b])
                add_to(own.at[i, a, b, x, :, right], r2b.at[i, a, b])

        push(own.at[i, :, y, ox, :, left], r3.at[i, :, :, left], send.at[i, 1], recv.at[i, 3], at.dev(x=ox))
        push(own.at[i, :, oy, x, :, right], r3.at[i, :, :, right], send.at[i, 1], recv.at[i, 4], at.dev(y=oy))

    def third_go(i):
        drain(r3.at[i, :, :, left], recv.at[i, 3])
        drain(r3.at[i, :, :, right], recv.at[i, 4])

        @pl.loop(0, nz)
        def _(a):
            add_to(own.at[i, a, y, x], r3.at[i, a])

        for k in range(1, nz):
            far = lax.rem(z + k, nz)
            push(own.at[i, far, y, x], r4.at[i, k - 1], send.at[i, 1], recv.at[i, 5], at.dev(z=far))

    def finish(i):
        drain(r4.at[i], recv.at[i, 5])
        total = own[i, z, y, x].astype(jnp.float32)
        for k in range(nz - 1):
            total = total + r4[i, k].astype(jnp.float32)
        grad_ref[i] = total
        for part in (r2a.at[i], r2b.at[i], r3.at[i], r4.at[i]):
            drain(part, send.at[i, 1])

    @pl.when(j == 0)
    def _():
        hello([at.dev(z=k) for k in at.z_others()] + [at.dev(y=oy), at.dev(x=ox), at.dev(c=oc)])
        load = pltpu.make_async_copy(shard_ref.at[:, pl.ds(shard_ref.shape[1] - chunk, chunk)], near, local_sem.at[0])
        load.start()
        load.wait()
        late[z, y, x, c] = near[...]
        net.go(0, 0)
        acc[...] = x_ref[...]
        dh_ref[...] = jnp.zeros_like(dh_ref)

        @pl.loop(0, rows // block)
        def _(r):
            span = pl.ds(pl.multiple_of(r * block, block), block)
            h_t[:, span] = h_ref[span, :].T

    def after(late, then, first=0, end=sent):
        pl.when((j >= late + first) & (j < late + end))(lambda: then(j - late))

    @pl.when(j < last)
    def _():
        up_ref[...] = up_in[...]

    @pl.when(j == last)
    def _():
        net.arrived(0)
        up_ref[...] = late[...].reshape(up_ref.shape)

    after(1, first_go)
    after(2, third_go, 0, sent - 1)
    for r in range(rows // block):
        span = pl.ds(r * block, block)
        u = dot(h_ref[span, :], up_ref[...])
        g = dot(g_ref[span, :], down_ref[...], NT)
        big, small = gelu_parts(u)
        a = (u * big).astype(jnp.bfloat16)
        d = (g * (big + u * small)).astype(jnp.bfloat16)
        act[span, :] = a
        du[span, :] = d
        acc[span, :] += dot(a, down_ref[...])
        dh_ref[span, :] += dot(d, up_ref[...], NT)

    pl.when(j == 0)(lambda: net.go(0, 1))
    pl.when(j == 2)(lambda: net.go(0, 3))
    after(1, second_go)
    after(2, finish, 0, sent - 1)
    slot = lax.rem(j, 2)
    each = rows // (nz * ny * nx * nc)

    @pl.loop(0, nz)
    def _(a):
        n = ny * nx * nc * each
        part = dot(h_t[pl.ds(pl.multiple_of(a * n, n), n), :], du[...]).astype(made.dtype)
        made[slot, a] = part.reshape(ny, nx, nc, each, chunk)

    pl.when(j == 0)(lambda: net.go(0, 2))
    after(0, core_go)
    after(1, third_go, sent - 1)
    ddown_ref[...] = lax.dot_general(act[...], g_ref[...], TN, preferred_element_type=jnp.float32).astype(ddown_ref.dtype)
    after(1, finish, sent - 1)

    @pl.when(j >= sent)
    def _():
        pltpu.make_async_copy(made.at[slot], rest_ref.at[j - sent], local_sem.at[j]).start()

    @pl.when(j == steps - 1)
    def _():
        net.sent(0)
        out_ref[...] = acc[...].astype(out_ref.dtype)
        for i in range(sent, 4):
            drain(rest_ref.at[i - sent], local_sem.at[i])


def ffn(dims, h, g, x, w_up, w_down, up_shard, cid, sent=3, steps=4):
    nz, ny, nx, nc = dims
    rows, width = h.shape
    inner = w_up.shape[1]
    chunk = inner // steps
    each = width // (nz * ny * nx * nc)
    bf, f32 = jnp.bfloat16, jnp.float32
    fixed = lambda j: (0, 0)
    whole = pl.BlockSpec((rows, width), fixed)
    once = pl.BlockSpec((rows, width), fixed, pipeline_mode=pl.Buffered(1))
    tile = (each, chunk)
    out, dh, ddown, grad, rest = pl.pallas_call(
        functools.partial(ffn_kernel, dims, sent),
        grid=(steps,),
        out_shape=[
            jax.ShapeDtypeStruct((rows, width), bf),
            jax.ShapeDtypeStruct((rows, width), f32),
            jax.ShapeDtypeStruct((inner, width), bf),
            jax.ShapeDtypeStruct((sent, each, chunk), f32),
            jax.ShapeDtypeStruct((steps - sent, nz, ny, nx, nc, each, chunk), bf),
        ],
        in_specs=[once, once, once, pl.BlockSpec((width, chunk), lambda j: (0, jnp.minimum(j, steps - 2))),
                  pl.BlockSpec((chunk, width), lambda j: (j, 0)), pl.BlockSpec(memory_space=ANY)],
        out_specs=[once, once, pl.BlockSpec((chunk, width), lambda j: (j, 0)),
                   pl.BlockSpec((sent, each, chunk), lambda j: (0, 0, 0)), pl.BlockSpec(memory_space=ANY)],
        scratch_shapes=[
            pltpu.VMEM((width, rows), bf), pltpu.VMEM((rows, width), f32), pltpu.VMEM((rows, chunk), bf), pltpu.VMEM((rows, chunk), bf),
            pltpu.VMEM((2, nz, ny, nx, nc) + tile, bf),
            pltpu.VMEM((sent, nz, ny, nx) + tile, bf), pltpu.VMEM((sent, nz, ny, nx) + tile, bf),
            pltpu.VMEM((sent, nz, nx, each, chunk // 2), bf), pltpu.VMEM((sent, nz, ny, each, chunk // 2), bf),
            pltpu.VMEM((sent, nz) + tile, bf), pltpu.VMEM((sent, nz - 1) + tile, bf),
            pltpu.SemaphoreType.DMA((steps,)), pltpu.SemaphoreType.DMA((sent, 2)), pltpu.SemaphoreType.DMA((sent, 6)),
            pltpu.VMEM((nz, ny, nx, nc) + tile, bf), pltpu.VMEM(tile, bf), pltpu.VMEM((width, chunk), bf),
            pltpu.SemaphoreType.DMA((1,)), pltpu.SemaphoreType.DMA((1, 4)),
        ],
        compiler_params=pltpu.CompilerParams(collective_id=cid, has_side_effects=True, vmem_limit_bytes=62 * 2**20, dimension_semantics=("arbitrary",)),
        name="feed_forward",
    )(h, g, x, w_up, w_down, up_shard)
    grad = jnp.moveaxis(grad, 0, 1).reshape(each, sent * chunk)
    rest = jnp.moveaxis(rest, 0, 5).reshape(width, (steps - sent) * chunk)
    return out, dh, ddown, grad, rest
class Gather:
    def __init__(self, dims, units, ins, outs, send, recv):
        self.at, self.nz = Place(dims), dims[0]
        self.units, self.ins, self.outs, self.send, self.recv = units, ins, outs, send, recv

    def part(self, u, where, core=None):
        a, r0, nr, c0, ncol, _ = self.units[u]
        return self.outs[a].at[(*where, self.at.c if core is None else core, pl.ds(r0, nr), pl.ds(c0, ncol))]

    def held(self, u, k):
        where = [self.at.z, self.at.y, self.at.x]
        for axis in self.units[u][5][:k]:
            where[axis] = slice(None)
        return where

    def coming(self, u, k):
        where = self.held(u, k)
        axis = self.units[u][5][k]
        where[axis] = (slice(0, self.nz - 1), 1 - self.at.y, 1 - self.at.x)[axis]
        return where

    def to_core(self, u, where):
        block = self.part(u, where)
        push(block, block, self.send.at[u], self.recv.at[u, 3], self.at.dev(c=1 - self.at.c))

    def pass_on(self, u, k):
        axis = self.units[u][5][k]
        if axis == 0 and k == 0:
            self.to_core(u, self.held(u, 1))
        elif axis == 0:
            for z in self.at.z_others():
                where = self.held(u, k)
                where[0] = z
                self.to_core(u, where)
        else:
            self.to_core(u, self.coming(u, k))
            if k == 0:
                self.to_core(u, self.held(u, 0))

    def go(self, u, k):
        at = self.at
        if k > 0:
            drain(self.part(u, self.coming(u, k - 1)), self.recv.at[u, k - 1])
        if k < 3:
            a, r0, nr, c0, ncol, order = self.units[u]
            dst = self.part(u, self.held(u, k))
            src = self.ins[a].at[pl.ds(r0, nr), pl.ds(c0, ncol)] if k == 0 else dst
            targets = ([at.dev(z=z) for z in at.z_others()], [at.dev(y=1 - at.y)], [at.dev(x=1 - at.x)])[order[k]]
            for device in targets:
                push(src, dst, self.send.at[u], self.recv.at[u, k], device)
        if k > 0:
            self.pass_on(u, k - 1)

    def arrived(self, u):
        drain(self.part(u, [slice(None)] * 3, 1 - self.at.c), self.recv.at[u, 3])

    def sent(self, u):
        for k in range(3):
            where = self.held(u, k)
            if self.units[u][5][k] == 0:
                where[0] = slice(0, self.nz - 1)
            drain(self.part(u, where), self.send.at[u])
        drain(self.part(u, [slice(None)] * 3), self.send.at[u])


def norm_parts(values_in):
    center = values_in - jnp.mean(values_in, axis=-1, keepdims=True)
    return center * lax.rsqrt(jnp.mean(center * center, axis=-1, keepdims=True) + EPS)


FW_PATHS = ((0, 2, 1), (0, 1, 2), (0, 1, 2), (0, 1, 2), (2, 0, 1), (2, 0, 1), (2, 0, 1), (0, 1, 2), (0, 1, 2), (2, 0, 1), (0, 1, 2), (1, 2, 0), (2, 0, 1), (2, 0, 1), (2, 1, 0), (0, 1, 2), (0, 1, 2))
FW_UNITS = [(a, 0, 32, 0, 1024, FW_PATHS[a - 1]) for a in range(1, 9)]
FW_UNITS += [(9, 0, 32, 1024 * j, 1024, FW_PATHS[8 + j]) for j in range(4)]
FW_UNITS += [(10, 32 * j, 32, 0, 1024, FW_PATHS[12 + j]) for j in range(4)] + [(0, 0, 16, 0, 128, FW_PATHS[16])]
FW_ORDER = (
    (5, 0), (1, 0), (16, 0), (0, 0), (4, 0), (6, 0), (1, 1), (2, 0), (16, 1), (3, 0), (0, 1), (10, 0), (1, 2),
    (16, 2), (2, 1), (15, 0), (3, 1), (7, 0), (5, 1), (12, 0), (4, 1), (13, 0), (2, 2), (6, 1), (9, 0), (10, 1),
    (8, 0), (3, 2), (0, 2), (15, 1), (10, 2), (7, 1), (1, 3), (16, 3), (12, 1), (1, 4), (14, 0), (13, 1), (0, 3),
    (-2, 0), (5, 2), (0, 4), (15, 2), (-2, 1), (2, 3), (-2, 2), (9, 1), (2, 4), (7, 2), (4, 2), (-2, 3), (-2, 4),
    (3, 3), (5, 3), (-2, 5), (3, 4), (6, 2), (5, 4), (-2, 6), (-2, 7), (8, 1), (-2, 8), (10, 3), (4, 3), (14, 1),
    (-2, 9), (4, 4), (-2, 10), (12, 2), (-2, 11), (6, 3), (15, 3), (-2, 12), (6, 4), (8, 2), (13, 2), (14, 2),
    (-2, 13), (7, 3), (-2, 14), (-2, 15), (7, 4), (-2, 16), (9, 2), (-1, 0), (12, 3), (-2, 17), (-2, 18), (-2, 19),
    (8, 3), (-2, 20), (-2, 21), (-2, 22), (-2, 23), (13, 3), (-2, 24), (14, 3), (9, 3),
)


def forward_kernel(dims, n, *refs):
    shards, refs = refs[:n], refs[n:]
    block_in, out_grad, text_states, limits = refs[:4]
    full, refs = refs[4 : 4 + n], refs[4 + n :]
    g_out, x_out, q_out, k_out, v_out, cq_out, ck_out, cv_out, o_out, o2_out, h1_out, h2_out, h3_out, x1_out, x2_out, lse_out, lse2_out, vec = refs[:18]
    x_in, q, k, v, cq, ck, cv, o, o2, h1, h2, h3, x1, x2, lse, lse2, text, small = refs[18:36]
    w, near, own_g = refs[36:44], refs[44 : 44 + n], refs[44 + n]
    limit, local_sem, out_sem, send, recv, ex_send, ex_recv = refs[45 + n :]
    at = Place(dims)
    oy, ox, oc, me = 1 - at.y, 1 - at.x, 1 - at.c, at.seq
    hello([at.dev(z=p) for p in at.z_others()] + [at.dev(y=oy), at.dev(x=ox), at.dev(c=oc), at.dev(x=ox, c=oc)])
    net = Gather(dims, FW_UNITS, near, full, send, recv)
    rows, width = q.shape
    block = 256
    f32, bf = jnp.float32, jnp.bfloat16
    others = ((ox, at.c), (ox, oc), (at.x, oc))

    def exchange(src, dst, i, own):
        for px, pc in others:
            push(src.at[px * 2 + pc], dst.at[me], ex_send.at[i], ex_recv.at[i], at.dev(x=px, c=pc))
        pltpu.make_async_copy(own, dst.at[me], local_sem.at[n + i]).start()

    def exchanged(dst, i):
        drain(dst.at[0:3], ex_recv.at[i])
        drain(dst.at[0], local_sem.at[n + i])

    keep = []

    def put(src, dst):
        pltpu.make_async_copy(src, dst, out_sem.at[len(keep)]).start()
        keep.append(src)

    loads = 4 + n

    def load(a):
        net.arrived(a - 1)
        pltpu.make_async_copy(full[a], w[a - 1], local_sem.at[loads + a]).start()

    def loaded(a):
        drain(w[a - 1], local_sem.at[loads + a])

    def weight(a):
        return w[a - 1][...].reshape(width, width)

    def span_of(r):
        return pl.ds(pl.multiple_of(r * block, block), block)

    def first_norm():
        net.arrived(16)
        pltpu.make_async_copy(full[0], small, local_sem.at[n + 3]).start()
        drain(small, local_sem.at[n + 3])
        packed = small[...].reshape(-1, 16, 128).astype(f32)
        devices = packed.shape[0]
        piece = width // devices
        lane = lax.rem(lax.broadcasted_iota(jnp.int32, (128, width), 1), piece)
        spread = jnp.where(lane == lax.broadcasted_iota(jnp.int32, (128, width), 0), 1.0, 0.0).astype(bf)
        owner = lax.div(lax.broadcasted_iota(jnp.int32, (devices, width), 1), piece)
        mine = owner == lax.broadcasted_iota(jnp.int32, (devices, width), 0)
        vec[...] = jnp.zeros_like(vec)
        for i in range(6):
            vec[i : i + 1, :] = row_sum(jnp.where(mine, dot(packed[:, i, :].astype(bf), spread), 0.0))
        exchanged(x_in, 0)
        put(x_in, x_out)

        @pl.loop(0, 4)
        def _(r):
            x = x_in[r].astype(f32)
            x1[span_of(r), :] = x
            h1[span_of(r), :] = (norm_parts(x) * vec[0:1, :] + vec[1:2, :]).astype(bf)

        put(h1, h1_out)

    def project(a, dst, scale, kept):
        loaded(a)

        @pl.loop(0, rows // block)
        def _(r):
            made = dot(h1[span_of(r), :], weight(a))
            dst[span_of(r), :] = (made if scale is None else made * scale).astype(bf)

        put(dst, kept)

    def pair(causal, qs, ks, vs, os, ls, j):
        cols = pl.ds(pl.multiple_of(j * 128, 128), 128)
        attend_kernel(causal, 512, limit, qs.at[:, cols], ks.at[:, cols], vs.at[:, cols], os.at[:, cols], ls.at[pl.ds(j, 1)])

    self_attention = functools.partial(pair, True, q, k, v, o, lse)
    cross_attention = functools.partial(pair, False, cq, ck, cv, o2, lse2)
    count = width // 128

    def second_norm(i):
        if i == 0:
            put(o, o_out)
            put(lse, lse_out)
            loaded(4)
            loaded(5)

        @pl.loop(2 * i, 2 * i + 2)
        def _(r):
            x = x1[span_of(r), :] + dot(o[span_of(r), :], weight(4))
            x1[span_of(r), :] = x
            h = (norm_parts(x) * vec[2:3, :] + vec[3:4, :]).astype(bf)
            h2[span_of(r), :] = h
            cq[span_of(r), :] = (dot(h, weight(5)) * (LOG2E / 8)).astype(bf)

        if i == 1:
            put(x1, x1_out)
            put(h2, h2_out)
            put(cq, cq_out)

    def text_rows():
        loaded(6)
        loaded(7)
        ck[...] = dot(text[...], weight(6)).astype(bf)
        cv[...] = dot(text[...], weight(7)).astype(bf)
        put(ck, ck_out)
        put(cv, cv_out)

    def third_norm(i):
        if i == 0:
            put(o2, o2_out)
            put(lse2, lse2_out)
            loaded(8)

        @pl.loop(2 * i, 2 * i + 2)
        def _(r):
            x = x1[span_of(r), :] + dot(o2[span_of(r), :], weight(8))
            x2[span_of(r), :] = x
            h3[span_of(r), :] = (norm_parts(x) * vec[4:5, :] + vec[5:6, :]).astype(bf)

        if i == 1:
            put(x2, x2_out)
            put(h3, h3_out)

    pieces = [first_norm, lambda: project(1, q, LOG2E / 8, q_out), lambda: project(2, k, None, k_out), lambda: project(3, v, None, v_out)]
    pieces += [(self_attention, j) for j in range(count)] + [functools.partial(second_norm, i) for i in range(2)] + [text_rows]
    pieces += [(cross_attention, j) for j in range(count)] + [functools.partial(third_norm, i) for i in range(2)]

    for a in range(n):
        pltpu.make_async_copy(shards[a], near[a], local_sem.at[a]).start()
    exchange(block_in, x_in, 0, block_in.at[me])
    pltpu.make_async_copy(text_states.at[me], text, local_sem.at[n + 2]).start()
    pltpu.make_async_copy(out_grad.at[me], own_g, local_sem.at[n + 1]).start()
    for a in range(n):
        drain(near[a], local_sem.at[a])
    drain(own_g, local_sem.at[n + 1])
    for a in range(n):
        pltpu.make_async_copy(near[a], full[a].at[at.z, at.y, at.x, at.c], local_sem.at[a]).start()
    limit[0] = limits[me]
    begin = next(i for i, (_, step) in enumerate(FW_ORDER) if step > 0)

    def event(u, step):
        if u == -1:
            exchange(out_grad, g_out, 1, own_g)
        elif step == 4:
            load(u + 1)
        else:
            net.go(u, step)

    run_order(FW_ORDER[:begin], event, [])
    for a in range(n):
        drain(near[a], local_sem.at[a])
    drain(text, local_sem.at[n + 2])
    run_order(FW_ORDER[begin:], event, pieces)
    exchanged(g_out, 1)
    moved = sorted({u for u, _ in FW_ORDER if u >= 0})
    for u in moved:
        if 8 <= u < 16:
            net.arrived(u)
    for u in moved:
        net.sent(u)
    drain(x_in.at[0:3], ex_send.at[0])
    drain(g_out.at[0:3], ex_send.at[1])
    for i, src in enumerate(keep):
        drain(src, out_sem.at[i])


def forward(dims, shards, block_in, out_grad, text_states, limits, cid):
    n = len(shards)
    bf, f32 = jnp.bfloat16, jnp.float32
    items, seg, width = block_in.shape
    rows, texts = items * seg, text_states.shape[1]
    wide, pairs = jax.ShapeDtypeStruct((rows, width), bf), width // 128
    short = jax.ShapeDtypeStruct((texts, width), bf)
    long = jax.ShapeDtypeStruct((rows, width), f32)
    sums = jax.ShapeDtypeStruct((pairs, 8, rows), f32)
    seg4 = jax.ShapeDtypeStruct(block_in.shape, bf)
    whole = [jax.ShapeDtypeStruct(tuple(dims) + s.shape, s.dtype) for s in shards]
    saved = [wide, wide, wide, wide, short, short, wide, wide, wide, wide, wide, long, long, sums, sums]
    out_shape = whole + [seg4, seg4] + saved + [jax.ShapeDtypeStruct((8, width), f32)]
    held = [pltpu.VMEM(s.shape, s.dtype) for s in [seg4] + saved + [short]] + [pltpu.VMEM(tuple(dims) + (16, 128), bf)]
    held += [pltpu.VMEM(s.shape, s.dtype) for s in whole[1:9]] + [pltpu.VMEM(s.shape, s.dtype) for s in shards]
    held += [pltpu.VMEM(block_in.shape[1:], bf)]
    units = len(FW_UNITS)
    any_spec = pl.BlockSpec(memory_space=ANY)
    outs = pl.pallas_call(
        functools.partial(forward_kernel, dims, n),
        out_shape=out_shape,
        in_specs=[any_spec] * (n + 3) + [pl.BlockSpec(memory_space=pltpu.SMEM)],
        out_specs=[any_spec] * (len(out_shape) - 1) + [pl.BlockSpec(memory_space=pltpu.VMEM)],
        scratch_shapes=held
        + [
            pltpu.SMEM((1,), jnp.int32),
            pltpu.SemaphoreType.DMA((2 * n + 8,)), pltpu.SemaphoreType.DMA((20,)),
            pltpu.SemaphoreType.DMA((units,)), pltpu.SemaphoreType.DMA((units, 4)),
            pltpu.SemaphoreType.DMA((2,)), pltpu.SemaphoreType.DMA((2,)),
        ],
        compiler_params=pltpu.CompilerParams(collective_id=cid, has_side_effects=True, vmem_limit_bytes=62 * 2**20),
        name="forward",
    )(*shards, block_in, out_grad, text_states, limits)
    full = [o.reshape((-1,) + o.shape[5:]) for o in outs[:n]]
    return full, outs[n:]
def run_order(order, event, pieces):
    i = 0
    while i < len(order):
        unit, step = order[i]
        i += 1
        if unit != -2:
            event(unit, step)
            continue
        piece = pieces[step]
        if callable(piece):
            piece()
            continue
        body, first = piece
        last, between = first, {first: []}
        while i < len(order):
            unit, step = order[i]
            if unit != -2:
                between[last].append((unit, step))
            else:
                piece = pieces[step]
                if callable(piece) or piece[0] is not body:
                    break
                last = piece[1]
                between[last] = []
            i += 1

        def one(j, body=body, between=between):
            body(j)
            for k, events in between.items():
                if events:
                    pl.when(j == k)(functools.partial(run_order, events, event, pieces))

        pl.loop(first, last + 1)(one)


class Scatter:
    def __init__(self, dims, send, recv, local):
        self.at, self.dims, self.send, self.recv, self.local, self.units = Place(dims), dims, send, recv, local, []

    def add(self, source, room, out, order, whole):
        self.units.append((source, room[0], room[1:], out, order, whole))

    def own(self, u, where):
        own, whole = self.units[u][1], self.units[u][5]
        return own.at[(*where, self.at.c)] if whole else own.at[tuple(where)]

    def left(self, u, k):
        where = [slice(None)] * 3
        for axis in self.units[u][4][:k]:
            where[axis] = (self.at.z, self.at.y, self.at.x)[axis]
        return where

    def add_in(self, u, k, bufs):
        where = self.left(u, k)
        open_axes = [axis for axis in range(3) if axis not in self.units[u][4][:k]]

        def one(index):
            spot = list(where)
            for axis, i in zip(open_axes, index):
                spot[axis] = i
            dst = self.own(u, spot)
            if len(bufs) == 1:
                dst[...] = dst[...] + bufs[0][tuple(index)]
            else:
                total = dst[...].astype(jnp.float32)
                for buf in bufs:
                    total = total + buf[tuple(index)].astype(jnp.float32)
                dst[...] = total.astype(dst.dtype)

        sizes = [self.dims[axis] for axis in open_axes]
        inner = list(itertools.product(*[range(n) for n in sizes[1:]]))

        @pl.loop(0, sizes[0])
        def _(i):
            for rest in inner:
                one((i, *rest))

    def bufs(self, u, k):
        buf = self.units[u][2][k]
        return [buf.at[i] for i in range(self.dims[0] - 1)] if self.units[u][4][k - 1] == 0 else [buf]

    def go(self, u, k):
        source, own, room, out, order, whole = self.units[u]
        at, every = self.at, slice(None)
        if k == 0:
            if not whole:
                pltpu.make_async_copy(source(every, every, every, at.c), own, self.local.at[u]).start()
            push(source(every, every, every, 1 - at.c), room[0], self.send.at[u], self.recv.at[u, 0], at.dev(c=1 - at.c))
            return
        drain(room[k - 1], self.recv.at[u, k - 1])
        if k == 4:
            total = self.own(u, (at.z, at.y, at.x))[...].astype(jnp.float32)
            for buf in self.bufs(u, 3):
                total = total + buf[...].astype(jnp.float32)
            out[...] = total
            for block in room:
                drain(block, self.send.at[u])
            return
        if k == 1:
            if not whole:
                drain(own, self.local.at[u])
            self.add_in(u, 0, [room[0]])
        else:
            self.add_in(u, k - 1, self.bufs(u, k - 1))
        where = self.left(u, k - 1)
        axis = order[k - 1]
        if axis == 0:
            for z in at.z_others():
                where[0] = z
                slot = lax.rem(z - at.z + self.dims[0], self.dims[0]) - 1
                push(self.own(u, where), room[k].at[slot], self.send.at[u], self.recv.at[u, k], at.dev(z=z))
        else:
            where[axis] = (None, 1 - at.y, 1 - at.x)[axis]
            device = at.dev(y=1 - at.y) if axis == 1 else at.dev(x=1 - at.x)
            push(self.own(u, where), room[k], self.send.at[u], self.recv.at[u, k], device)


def scatter_room(dims, tile, dtype, order, whole):
    nz, ny, nx, nc = dims
    rooms = [((nz, ny, nx, nc) if whole else (nz, ny, nx)) + tile, (nz, ny, nx) + tile]
    for k in range(3):
        lead = tuple(dims[axis] for axis in range(3) if axis not in order[: k + 1])
        rooms.append(((nz - 1,) if order[k] == 0 else ()) + lead + tile)
    return [pltpu.VMEM(shape, dtype) for shape in rooms]


def norm_back(x, dh, gain):
    center = x - jnp.mean(x, axis=-1, keepdims=True)
    r = lax.rsqrt(jnp.mean(center * center, axis=-1, keepdims=True) + EPS)
    n = center * r
    dn = dh * gain
    dx = r * (dn - jnp.mean(dn, axis=-1, keepdims=True) - n * jnp.mean(dn * n, axis=-1, keepdims=True))
    return dx, dh * n


def row_sum(rows):
    return jnp.sum(rows, axis=0, keepdims=True)


TN = (((0,), (0,)), ((), ()))


MIDDLE_PATHS = (
    (1, 0, 2), (0, 1, 2), (1, 0, 2), (1, 2, 0), (2, 1, 0), (2, 1, 0),
)
MIDDLE_ORDER = (
    (0, 0), (1, 0), (2, 0), (3, 0), (4, 0), (-2, 0), (0, 1), (1, 1), (-2, 1), (2, 1), (3, 1), (-2, 2), (5, 0),
    (4, 1), (-2, 3), (-2, 4), (5, 1), (0, 2), (-2, 5), (-2, 6), (-2, 7), (-2, 8), (-2, 9), (-2, 10), (2, 2), (1, 2),
    (-2, 11), (-2, 12), (4, 2), (-2, 13), (3, 2), (0, 3), (1, 3), (-2, 14), (5, 2), (4, 3), (-2, 15), (2, 3), (3, 3),
    (0, 4), (1, 4), (5, 3), (4, 4), (2, 4), (3, 4), (5, 4),
)
LAST_SPLIT = 640
LAST_PATHS = (
    (2, 0, 1), (0, 1, 2), (1, 2, 0), (2, 1, 0), (1, 0, 2), (2, 1, 0), (2, 1, 0), (1, 0, 2), (1, 0, 2), (1, 0, 2),
    (0, 1, 2),
)
LAST_ORDER = (
    (0, 0), (1, 0), (2, 0), (3, 0), (-2, 0), (0, 1), (-2, 1), (1, 1), (2, 1), (-2, 2), (3, 1), (-2, 3), (0, 2),
    (-2, 4), (-2, 5), (2, 2), (-2, 6), (4, 0), (5, 0), (6, 0), (3, 2), (1, 2), (-2, 7), (2, 3), (4, 1), (5, 1),
    (6, 1), (-2, 8), (3, 3), (0, 3), (-2, 9), (1, 3), (-2, 10), (7, 0), (8, 0), (9, 0), (5, 2), (2, 4), (4, 2),
    (0, 4), (-2, 11), (7, 1), (8, 1), (3, 4), (9, 1), (6, 2), (1, 4), (-2, 12), (5, 3), (-2, 13), (4, 3), (7, 2),
    (-2, 14), (-2, 15), (10, 0), (5, 4), (8, 2), (10, 1), (7, 3), (9, 2), (6, 3), (8, 3), (10, 2), (10, 3), (9, 3),
    (4, 4), (7, 4), (8, 4), (10, 4), (6, 4), (9, 4),
)


def middle_kernel(dims, *refs):
    (g_in, dh_in, x2_in, x1_in, vec, o2_in, cq_in, ck_in, cv_in, lse_in, h2_in, o_in, wco_in, wcq_in, wck_in, wcv_in, wo_in,
     text_in, limits, block_in, down_in, up_in) = refs[:22]
    block_out, text_out, dx_out, do_out, gcq_out, gck_out, gcv_out, go_out, sums, down_out, up_out, co_out = refs[22:34]
    (x2, dh3, dx, g, dy, do, o2, wco, cq, dcq, wcq, wck, wcv, ck, cv, dck, dcv, lse, text, tg, stage, dk_acc, dv_acc, limit,
     load_sem, out_sem, ex_send, ex_recv, send, recv, local, own_rows) = refs[34:66]
    rooms = refs[66:]
    at = Place(dims)
    nz = dims[0]
    oy, ox, oc, me = 1 - at.y, 1 - at.x, 1 - at.c, at.seq
    hello([at.dev(z=p) for p in at.z_others()] + [at.dev(y=oy), at.dev(x=ox), at.dev(c=oc), at.dev(x=ox, c=oc)])
    others = ((ox, at.c), (ox, oc), (at.x, oc))
    rows, width = g.shape
    block = 256
    f32, bf = jnp.float32, jnp.bfloat16
    every = slice(None)
    net = Scatter(dims, send, recv, local)
    quarter = width // 4
    room = [rooms[5 * j : 5 * j + 5] for j in range(6)]
    for j in range(4):
        cols = pl.ds(j * quarter, quarter)
        net.add(lambda *w, cols=cols: down_in.at[(*w, every, cols)], room[j], down_out.at[:, cols], MIDDLE_PATHS[j], False)
    net.add(lambda *w: up_in.at[w], room[4], up_out, MIDDLE_PATHS[4], False)
    net.add(lambda *w: room[5][0].at[w], room[5], co_out, MIDDLE_PATHS[5], True)

    def exchange(src, dst, i, own):
        for px, pc in others:
            push(src.at[px * 2 + pc], dst.at[me], ex_send.at[i], ex_recv.at[i], at.dev(x=px, c=pc))
        pltpu.make_async_copy(own, dst.at[me], local.at[6 + i]).start()

    started = []

    def load(src, dst):
        pltpu.make_async_copy(src, dst, load_sem.at[len(started)]).start()
        started.append(dst)
        return len(started) - 1

    def loaded(i):
        drain(started[i], load_sem.at[i])

    kept = []

    def put(src, dst):
        pltpu.make_async_copy(src, dst, out_sem.at[len(kept)]).start()
        kept.append(src)
        return len(kept) - 1

    def kept_done(i):
        drain(kept[i], out_sem.at[i])

    def span_of(r):
        return pl.ds(pl.multiple_of(r * block, block), block)

    def weight_grad(src, grad, made):
        @pl.loop(0, nz)
        def _(a):
            part = dot(src[:, pl.ds(pl.multiple_of(a * block, block), block)], grad[...], TN).astype(bf)
            made[a] = part.reshape(made.shape[1:])

    own_load = load(block_in.at[me], own_rows)
    first = [load(dh_in, dh3), load(x2_in, x2), load(g_in, g), load(wco_in, wco), load(o2_in, o2)]
    second = [load(cq_in, cq), load(ck_in, ck), load(cv_in, cv), load(lse_in, lse)]
    third = [load(text_in.at[me], text), load(wcq_in, wcq), load(wck_in, wck), load(wcv_in, wcv)]
    limit[0] = limits[me]
    run_order(MIDDLE_ORDER[:5], net.go, [])
    loaded(own_load)
    exchange(block_in, block_out, 0, own_rows)
    for i in first[:-1]:
        loaded(i)
    sums[...] = jnp.zeros_like(sums)

    def last_norm(r):
        span = span_of(r)
        d = dh3[span, :]
        grad, gain_terms = norm_back(x2[span, :], d, vec[4:5, :])
        sums[4:5, :] += row_sum(gain_terms)
        sums[5:6, :] += row_sum(d)
        total = g[span, :].astype(f32) + grad
        dx[span, :] = total
        low = total.astype(bf)
        dy[span, :] = low
        do[span, :] = dot(low, wco[...], NT).astype(bf)

    def middle_norm(r):
        span = span_of(r)
        d = dot(dcq[span, :], wcq[...], NT)
        grad, gain_terms = norm_back(x2[span, :], d, vec[2:3, :])
        sums[2:3, :] += row_sum(gain_terms)
        sums[3:4, :] += row_sum(d)
        total = dx[span, :] + grad
        dx[span, :] = total
        low = total.astype(bf)
        dy[span, :] = low
        do[span, :] = dot(low, cq[...], NT).astype(bf)

    later = {}

    def after_last_norm():
        pl.loop(2, 4)(last_norm)
        later["x1"], later["o"], later["h2"] = load(x1_in, x2), load(o_in, g), load(h2_in, wco)

    def output_weight_grad():
        loaded(first[-1])
        weight_grad(o2, dy, room[5][0])
        for i in second:
            loaded(i)

    def cross(j):
        cols = pl.ds(pl.multiple_of(j * 128, 128), 128)
        attend_back_kernel(
            False, 512, limit, cq.at[:, cols], ck.at[:, cols], cv.at[:, cols], do.at[:, cols], o2.at[:, cols], lse.at[pl.ds(j, 1)],
            dcq.at[:, cols], dck.at[:, cols], dcv.at[:, cols], dk_acc, dv_acc,
        )

    def query_weight_grad():
        later["wo"] = load(wo_in, cq)
        for i in third:
            loaded(i)
        loaded(later["h2"])
        weight_grad(wco, dcq, stage.at[0])
        later["cq"] = put(stage.at[0], gcq_out)
        loaded(later["x1"])
        loaded(later["wo"])

    def after_middle_norm():
        pl.loop(2, 4)(middle_norm)
        put(dx, dx_out)
        put(do, do_out)

    def self_weight_grad():
        loaded(later["o"])
        weight_grad(g, dy, stage.at[1])
        later["o"] = put(stage.at[1], go_out)

    def text_weight_grads():
        tg[...] = (dot(dck[...], wck[...], NT) + dot(dcv[...], wcv[...], NT)).reshape(tg.shape)
        exchange(tg, text_out, 1, tg.at[me])
        kept_done(later["cq"])
        weight_grad(text, dck, stage.at[0])
        put(stage.at[0], gck_out)
        kept_done(later["o"])
        weight_grad(text, dcv, stage.at[1])
        put(stage.at[1], gcv_out)

    pieces = [lambda: pl.loop(0, 2)(last_norm), after_last_norm, output_weight_grad]
    pieces += [(cross, j) for j in range(width // 128)]
    pieces += [query_weight_grad, lambda: pl.loop(0, 2)(middle_norm), after_middle_norm, self_weight_grad, text_weight_grads]
    run_order(MIDDLE_ORDER[5:], net.go, pieces)
    for i, dst in ((0, block_out), (1, text_out)):
        drain(dst.at[0:3], ex_recv.at[i])
        drain(dst.at[0:3], ex_send.at[i])
        drain(dst.at[0], local.at[6 + i])
    for i in range(len(kept)):
        if i not in (later["cq"], later["o"]):
            kept_done(i)


def middle(dims, args, cid):
    nz, ny, nx, nc = dims
    g, dh, x2, x1, vec, o2, cq, ck, cv, lse, h2, o, wco, wcq, wck, wcv, wo, text, limits, block_out, down, up = args
    rows, width = g.shape
    texts = text.shape[1]
    devices = nz * ny * nx * nc
    bf, f32 = jnp.bfloat16, jnp.float32
    each = width // devices
    long = down.shape[0] // devices
    down = down.reshape(nz, ny, nx, nc, long, width)
    up = up.reshape(nz, ny, nx, nc, each, up.shape[1])
    seg = block_out.shape
    held = jax.ShapeDtypeStruct((nz, ny, nx, nc, each, width), bf)
    wide, deep = jax.ShapeDtypeStruct((rows, width), bf), jax.ShapeDtypeStruct((rows, width), f32)
    out_shape = [
        jax.ShapeDtypeStruct(seg, bf), jax.ShapeDtypeStruct((seg[0], texts // seg[0], width), f32), deep, wide, held, held, held, held,
        jax.ShapeDtypeStruct((8, width), f32), jax.ShapeDtypeStruct((long, width), f32), jax.ShapeDtypeStruct((each, up.shape[5]), f32),
        jax.ShapeDtypeStruct((each, width), f32),
    ]
    any_spec, vm = pl.BlockSpec(memory_space=ANY), pl.BlockSpec(memory_space=pltpu.VMEM)
    big, square, short = pltpu.VMEM((rows, width), f32), pltpu.VMEM((rows, width), bf), pltpu.VMEM((texts, width), bf)
    dma = pltpu.SemaphoreType.DMA
    scratch = [big, big, big] + [square] * 10 + [short] * 4 + [pltpu.VMEM(lse.shape, f32), short]
    scratch += [pltpu.VMEM((seg[0], texts // seg[0], width), f32), pltpu.VMEM((2,) + held.shape, bf)]
    scratch += [pltpu.VMEM((texts, 128), f32)] * 2 + [pltpu.SMEM((1,), jnp.int32)]
    scratch += [dma((20,)), dma((12,)), dma((2,)), dma((2,)), dma((6,)), dma((6, 4)), dma((8,)), pltpu.VMEM(seg[1:], bf)]
    for j in range(4):
        scratch += scatter_room(dims, (long, width // 4), bf, MIDDLE_PATHS[j], False)
    scratch += scatter_room(dims, (each, up.shape[5]), bf, MIDDLE_PATHS[4], False)
    scratch += scatter_room(dims, (each, width), bf, MIDDLE_PATHS[5], True)
    specs = [any_spec] * 4 + [vm] + [any_spec] * 13 + [pl.BlockSpec(memory_space=pltpu.SMEM)] + [any_spec] * 3
    return pl.pallas_call(
        functools.partial(middle_kernel, dims),
        out_shape=out_shape,
        in_specs=specs,
        out_specs=[any_spec] * 8 + [vm] * 4,
        scratch_shapes=scratch,
        compiler_params=pltpu.CompilerParams(collective_id=cid, has_side_effects=True, vmem_limit_bytes=63 * 2**20),
        name="middle",
    )(g, dh, x2, x1, vec, o2, cq, ck, cv, lse, h2, o, wco, wcq, wck, wcv, wo, text, limits, block_out, down, up)


def last_kernel(dims, *refs):
    q_in, k_in, v_in, do_in, o_in, lse_in, h1_in, wq_in, wk_in, wv_in, x_in, dx_in, vec, gcq, gck, gcv, go, sums_in = refs[:18]
    grad_out, cq_out, ck_out, cv_out, o_out, q_out, k_out, v_out, small_out = refs[18:27]
    (q, k, v, do, o, lse, h_t, dq, dk, dv, dx, send_rows, small, dk_acc, dv_acc, sums,
     load_sem, ex_send, ex_recv, send, recv, local) = refs[27:49]
    rooms = refs[49:]
    at = Place(dims)
    nz, ny, nx, nc = dims
    oy, ox, oc, me = 1 - at.y, 1 - at.x, 1 - at.c, at.seq
    hello([at.dev(z=p) for p in at.z_others()] + [at.dev(y=oy), at.dev(x=ox), at.dev(c=oc), at.dev(x=ox, c=oc)])
    rows, width = q.shape
    block = 256
    f32, bf = jnp.float32, jnp.bfloat16
    every = slice(None)
    net = Scatter(dims, send, recv, local)
    room = [rooms[5 * j : 5 * j + 5] for j in range(10)] + [[small, *rooms[50:54]]]
    for j, (src, out) in enumerate(((gcq, cq_out), (gck, ck_out), (gcv, cv_out), (go, o_out))):
        net.add(lambda *w, src=src: src.at[w], room[j], out, LAST_PATHS[j], False)
    parts = ((0, LAST_SPLIT), (LAST_SPLIT, width - LAST_SPLIT))
    for j in range(6):
        out = (q_out, k_out, v_out)[j % 3].at[:, pl.ds(*parts[j // 3])]
        net.add(lambda *w, held=room[4 + j][0]: held.at[w], room[4 + j], out, LAST_PATHS[4 + j], True)
    net.add(lambda *w: small.at[w], room[10], small_out, LAST_PATHS[10], True)
    run_order(LAST_ORDER[:4], net.go, [])
    started = []

    def load(src, dst):
        pltpu.make_async_copy(src, dst, load_sem.at[len(started)]).start()
        started.append(dst)
        return len(started) - 1

    def loaded(i):
        drain(started[i], load_sem.at[i])

    first = [load(a, b) for a, b in ((q_in, q), (k_in, k), (v_in, v), (do_in, do), (o_in, o), (lse_in, lse), (h1_in, send_rows), (dx_in, dx))]

    def begin():
        for i in first[:6]:
            loaded(i)

    def transpose():
        loaded(first[6])
        loaded(first[7])

        @pl.loop(0, rows // block)
        def _(r):
            h_t[:, pl.ds(pl.multiple_of(r * block, block), block)] = send_rows[r].T

    def pair(j):
        cols = pl.ds(pl.multiple_of(j * 128, 128), 128)
        attend_back_kernel(
            True, 256, None, q.at[:, cols], k.at[:, cols], v.at[:, cols], do.at[:, cols], o.at[:, cols], lse.at[pl.ds(j, 1)],
            dq.at[:, cols], dk.at[:, cols], dv.at[:, cols], dk_acc, dv_acc,
        )

    weights = []

    def weight_grads(part):
        if part == 0:
            transpose()
        if part == 1:
            weights.extend(load(a, b) for a, b in ((wq_in, q), (wk_in, k), (wv_in, v), (x_in, do)))
        for j, grad in enumerate((dq, dk, dv)):
            made = room[4 + 3 * part + j][0]

            @pl.loop(0, nz)
            def _(a, made=made, grad=grad):
                span = pl.ds(pl.multiple_of(a * block, block), block)
                product = dot(h_t[span, :], grad[:, pl.ds(*parts[part])]).astype(bf)
                made[a] = product.reshape(made.shape[1:])

        if part == 1:
            for i in weights:
                loaded(i)
            sums[...] = sums_in[...]

    def last_norm(r):
        span = pl.ds(pl.multiple_of(r * block, block), block)
        d = dot(dq[span, :], q[...], NT) + dot(dk[span, :], k[...], NT) + dot(dv[span, :], v[...], NT)
        grad, gain_terms = norm_back(do[span, :].astype(f32), d, vec[0:1, :])
        sums[0:1, :] += row_sum(gain_terms)
        sums[1:2, :] += row_sum(d)
        send_rows[r] = (dx[span, :] + grad).astype(bf)

    targets = ((ox, at.c), (ox, oc), (at.x, oc), (at.x, at.c))

    def send_norm(i):
        px, pc = targets[i]
        last_norm(px * 2 + pc)
        if i < 3:
            push(send_rows.at[px * 2 + pc], grad_out.at[me], ex_send, ex_recv, at.dev(x=px, c=pc))
        else:
            pltpu.make_async_copy(send_rows.at[me], grad_out.at[me], local.at[11]).start()

    def share_sums():
        devices = nz * ny * nx * nc
        piece = width // devices
        lanes = lax.broadcasted_iota(jnp.int32, (width, 128), 0)
        fold = jnp.where(lax.rem(lanes, piece) == lax.broadcasted_iota(jnp.int32, (width, 128), 1), 1.0, 0.0).astype(bf)
        mine = lax.div(lax.broadcasted_iota(jnp.int32, (devices, width), 1), piece) == lax.broadcasted_iota(jnp.int32, (devices, width), 0)
        shares = []
        for i in range(6):
            spread = jnp.where(mine, sums[i : i + 1, :], 0.0)
            total = jnp.zeros((devices, 128), f32)
            for _ in range(3):
                low = spread.astype(bf)
                spread = spread - low.astype(f32)
                total = total + dot(low, fold)
            shares.append(total[:, None, :])
        shares.append(jnp.zeros((devices, 2, 128), f32))
        small[...] = jnp.concatenate(shares, axis=1).reshape(small.shape)

    split = LAST_SPLIT // 128
    pieces = [begin] + [(pair, j) for j in range(split)] + [lambda: weight_grads(0)]
    pieces += [(pair, j) for j in range(split, width // 128)] + [lambda: weight_grads(1)]
    pieces += [functools.partial(send_norm, i) for i in range(4)] + [share_sums]
    run_order(LAST_ORDER[4:], net.go, pieces)
    drain(grad_out.at[0:3], ex_recv)
    drain(grad_out.at[0:3], ex_send)
    drain(grad_out.at[0], local.at[11])


def last(dims, args, cid):
    nz, ny, nx, nc = dims
    q, k, v, do, o, lse, h1, wq, wk, wv, x, dx, vec, gcq, gck, gcv, go, sums = args
    rows, width = q.shape
    bf, f32 = jnp.bfloat16, jnp.float32
    each = width // (nz * ny * nx * nc)
    shard = jax.ShapeDtypeStruct((each, width), f32)
    out_shape = [jax.ShapeDtypeStruct((4, rows // 4, width), bf)] + [shard] * 7 + [jax.ShapeDtypeStruct((8, 128), f32)]
    any_spec, vm = pl.BlockSpec(memory_space=ANY), pl.BlockSpec(memory_space=pltpu.VMEM)
    square = pltpu.VMEM((rows, width), bf)
    dma = pltpu.SemaphoreType.DMA
    scratch = [square] * 5 + [pltpu.VMEM(lse.shape, f32)] + [square] * 4 + [pltpu.VMEM((rows, width), f32), pltpu.VMEM((4, rows // 4, width), bf)]
    scratch += [pltpu.VMEM((nz, ny, nx, nc, 8, 128), f32)] + [pltpu.VMEM((rows, 128), f32)] * 2 + [pltpu.VMEM((8, width), f32)]
    scratch += [dma((16,)), dma, dma, dma((11,)), dma((11, 4)), dma((12,))]
    for j in range(4):
        scratch += scatter_room(dims, (each, width), bf, LAST_PATHS[j], False)
    for j in range(6):
        scratch += scatter_room(dims, (each, LAST_SPLIT if j < 3 else width - LAST_SPLIT), bf, LAST_PATHS[4 + j], True)
    scratch += scatter_room(dims, (8, 128), f32, LAST_PATHS[10], True)[1:]
    return pl.pallas_call(
        functools.partial(last_kernel, dims),
        out_shape=out_shape,
        in_specs=[any_spec] * 12 + [vm] + [any_spec] * 4 + [vm],
        out_specs=[any_spec] + [vm] * 8,
        scratch_shapes=scratch,
        compiler_params=pltpu.CompilerParams(collective_id=cid, has_side_effects=True, vmem_limit_bytes=63 * 2**20),
        name="last",
    )(q, k, v, do, o, lse, h1.reshape(4, rows // 4, width), wq, wk, wv, x, dx, vec, gcq, gck, gcv, go, sums)

HEAD_DIM = 64


EPS = 1e-05


def norm_rows(values_in, gain, bias):
    center = values_in - jnp.mean(values_in, axis=-1, keepdims=True)
    spread = jnp.mean(center * center, axis=-1, keepdims=True)
    return center * lax.rsqrt(spread + EPS) * gain + bias


def contract_rows(left, right):
    return lax.dot_general(
        left, right, (((0,), (0,)), ((), ())), preferred_element_type=jnp.float32
    )


def times_transposed(left, right):
    return lax.dot_general(
        left, right, (((1,), (1,)), ((), ())), preferred_element_type=jnp.float32
    )


def product(left, right):
    return jnp.dot(left, right, preferred_element_type=jnp.float32)


def local_plain(
    block_in,
    text_states,
    caption_len,
    out_grad,
    first_gain,
    first_bias,
    query_weight,
    key_weight,
    value_weight,
    output_weight,
    second_gain,
    second_bias,
    cross_query,
    cross_key,
    cross_value,
    cross_output,
    third_gain,
    third_bias,
    up_weight,
    down_weight,
):
    gathered = (
        lax.all_gather(first_gain, ("dp", "seq"), axis=0, tiled=True),
        lax.all_gather(first_bias, ("dp", "seq"), axis=0, tiled=True),
        lax.all_gather(query_weight, ("dp", "seq"), axis=0, tiled=True),
        lax.all_gather(key_weight, ("dp", "seq"), axis=0, tiled=True),
        lax.all_gather(value_weight, ("dp", "seq"), axis=0, tiled=True),
        lax.all_gather(output_weight, ("dp", "seq"), axis=0, tiled=True),
        lax.all_gather(second_gain, ("dp", "seq"), axis=0, tiled=True),
        lax.all_gather(second_bias, ("dp", "seq"), axis=0, tiled=True),
        lax.all_gather(cross_query, ("dp", "seq"), axis=0, tiled=True),
        lax.all_gather(cross_key, ("dp", "seq"), axis=0, tiled=True),
        lax.all_gather(cross_value, ("dp", "seq"), axis=0, tiled=True),
        lax.all_gather(cross_output, ("dp", "seq"), axis=0, tiled=True),
        lax.all_gather(third_gain, ("dp", "seq"), axis=0, tiled=True),
        lax.all_gather(third_bias, ("dp", "seq"), axis=0, tiled=True),
        lax.all_gather(up_weight, ("dp", "seq"), axis=0, tiled=True),
        lax.all_gather(down_weight, ("dp", "seq"), axis=0, tiled=True),
    )
    (
        gain_one,
        bias_one,
        w_query,
        w_key,
        w_value,
        w_output,
        gain_two,
        bias_two,
        w_cquery,
        w_ckey,
        w_cvalue,
        w_coutput,
        gain_three,
        bias_three,
        w_up,
        w_down,
    ) = gathered
    item_count, seg_len, model_width = block_in.shape
    row_count = item_count * seg_len
    head_count = model_width // HEAD_DIM
    score_scale = HEAD_DIM ** (-0.5)
    text_count = text_states.shape[1]
    inputs_f = block_in.astype(jnp.float32).reshape(row_count, model_width)
    normed_one, pull_one = jax.vjp(
        norm_rows, inputs_f, gain_one.astype(jnp.float32), bias_one.astype(jnp.float32)
    )
    normed_one = normed_one.astype(jnp.bfloat16)
    query_rows = product(normed_one, w_query).astype(jnp.bfloat16)
    key_rows = product(normed_one, w_key).astype(jnp.bfloat16)
    value_rows = product(normed_one, w_value).astype(jnp.bfloat16)
    key_all, value_all = (
        lax.all_gather(
            key_rows.reshape(item_count, seg_len, model_width), "seq", axis=1, tiled=True
        ),
        lax.all_gather(
            value_rows.reshape(item_count, seg_len, model_width), "seq", axis=1, tiled=True
        ),
    )
    key_count = key_all.shape[1]
    first_pos = lax.axis_index("seq") * seg_len
    query_pos = first_pos + jnp.arange(seg_len, dtype=jnp.int32)
    causal = jnp.arange(key_count, dtype=jnp.int32)[None, :] <= query_pos[:, None]

    def self_scores(query_item, key_item):
        query_heads = query_item.reshape(seg_len, head_count, HEAD_DIM)
        key_heads = key_item.reshape(key_count, head_count, HEAD_DIM)
        scores = jnp.einsum(
            "qhd,khd->hqk", query_heads, key_heads, preferred_element_type=jnp.float32
        )
        return jnp.where(causal[None, :, :], scores * score_scale, -1e30)

    def self_forward(operands):
        query_item, key_item, value_item = operands
        scores = self_scores(query_item, key_item)
        row_peak = jnp.max(scores, axis=-1, keepdims=True)
        row_total = jnp.sum(jnp.exp(scores - row_peak), axis=-1, keepdims=True)
        log_total = row_peak + jnp.log(row_total)
        prob_bf = jnp.exp(scores - log_total).astype(jnp.bfloat16)
        value_heads = value_item.reshape(key_count, head_count, HEAD_DIM)
        mixed = jnp.einsum("hqk,khd->qhd", prob_bf, value_heads, preferred_element_type=jnp.float32)
        return (mixed.reshape(seg_len, model_width).astype(jnp.bfloat16), log_total)

    attended, log_totals = lax.map(
        self_forward, (query_rows.reshape(item_count, seg_len, model_width), key_all, value_all)
    )
    attended_rows = attended.reshape(row_count, model_width)
    after_self = inputs_f + product(attended_rows, w_output)
    normed_two, pull_two = jax.vjp(
        norm_rows, after_self, gain_two.astype(jnp.float32), bias_two.astype(jnp.float32)
    )
    normed_two = normed_two.astype(jnp.bfloat16)
    cross_rows = product(normed_two, w_cquery).astype(jnp.bfloat16)
    cross_heads = cross_rows.reshape(item_count, seg_len, head_count, HEAD_DIM)
    text_keys = jnp.einsum(
        "itc,cd->itd", text_states, w_ckey, preferred_element_type=jnp.float32
    ).astype(jnp.bfloat16)
    text_values = jnp.einsum(
        "itc,cd->itd", text_states, w_cvalue, preferred_element_type=jnp.float32
    ).astype(jnp.bfloat16)
    text_kheads = text_keys.reshape(item_count, text_count, head_count, HEAD_DIM)
    text_vheads = text_values.reshape(item_count, text_count, head_count, HEAD_DIM)
    text_mask = jnp.arange(text_count, dtype=jnp.int32)[None, :] < caption_len[:, None]
    cross_scores = jnp.einsum(
        "iqhd,ithd->ihqt", cross_heads, text_kheads, preferred_element_type=jnp.float32
    )
    cross_scores = jnp.where(text_mask[:, None, None, :], cross_scores * score_scale, -1e30)
    cross_peak = jnp.max(cross_scores, axis=-1, keepdims=True)
    cross_exp = jnp.exp(cross_scores - cross_peak)
    cross_prob = cross_exp / jnp.sum(cross_exp, axis=-1, keepdims=True)
    cross_prob_bf = cross_prob.astype(jnp.bfloat16)
    crossed = jnp.einsum(
        "ihqt,ithd->iqhd", cross_prob_bf, text_vheads, preferred_element_type=jnp.float32
    )
    crossed_rows = crossed.reshape(row_count, model_width).astype(jnp.bfloat16)
    after_cross = after_self + product(crossed_rows, w_coutput)
    normed_three, pull_three = jax.vjp(
        norm_rows, after_cross, gain_three.astype(jnp.float32), bias_three.astype(jnp.float32)
    )
    normed_three = normed_three.astype(jnp.bfloat16)
    hidden = product(normed_three, w_up)
    activated, pull_gelu = jax.vjp(lambda inner: jax.nn.gelu(inner, approximate=False), hidden)
    activated = activated.astype(jnp.bfloat16)
    layer_out = after_cross + product(activated, w_down)
    block_out = layer_out.astype(jnp.bfloat16).reshape(item_count, seg_len, model_width)
    back_weights = (
        lax.all_gather(first_gain, ("dp", "seq"), axis=0, tiled=True),
        lax.all_gather(first_bias, ("dp", "seq"), axis=0, tiled=True),
        lax.all_gather(query_weight, ("dp", "seq"), axis=0, tiled=True),
        lax.all_gather(key_weight, ("dp", "seq"), axis=0, tiled=True),
        lax.all_gather(value_weight, ("dp", "seq"), axis=0, tiled=True),
        lax.all_gather(output_weight, ("dp", "seq"), axis=0, tiled=True),
        lax.all_gather(second_gain, ("dp", "seq"), axis=0, tiled=True),
        lax.all_gather(second_bias, ("dp", "seq"), axis=0, tiled=True),
        lax.all_gather(cross_query, ("dp", "seq"), axis=0, tiled=True),
        lax.all_gather(cross_key, ("dp", "seq"), axis=0, tiled=True),
        lax.all_gather(cross_value, ("dp", "seq"), axis=0, tiled=True),
        lax.all_gather(cross_output, ("dp", "seq"), axis=0, tiled=True),
        lax.all_gather(third_gain, ("dp", "seq"), axis=0, tiled=True),
        lax.all_gather(third_bias, ("dp", "seq"), axis=0, tiled=True),
        lax.all_gather(up_weight, ("dp", "seq"), axis=0, tiled=True),
        lax.all_gather(down_weight, ("dp", "seq"), axis=0, tiled=True),
    )
    (
        unused_gain,
        unused_bias,
        w_query,
        w_key,
        w_value,
        w_output,
        unused_gtwo,
        unused_btwo,
        w_cquery,
        w_ckey,
        w_cvalue,
        w_coutput,
        unused_gthree,
        unused_bthree,
        w_up,
        w_down,
    ) = back_weights
    grad_rows = out_grad.reshape(row_count, model_width)
    down_part = contract_rows(activated, grad_rows)
    act_grad = times_transposed(grad_rows, w_down)
    hidden_grad = pull_gelu(act_grad)[0].astype(jnp.bfloat16)
    up_part = contract_rows(normed_three, hidden_grad)
    normed_three_grad = times_transposed(hidden_grad, w_up)
    resid_three, gain_three_part, bias_three_part = pull_three(normed_three_grad)
    cross_grad = grad_rows.astype(jnp.float32) + resid_three
    cross_out_bf = cross_grad.astype(jnp.bfloat16)
    coutput_part = contract_rows(crossed_rows, cross_out_bf)
    crossed_grad = times_transposed(cross_out_bf, w_coutput).astype(jnp.bfloat16)
    crossed_heads = crossed_grad.reshape(item_count, seg_len, head_count, HEAD_DIM)
    cross_dprob = jnp.einsum(
        "iqhd,ithd->ihqt", crossed_heads, text_vheads, preferred_element_type=jnp.float32
    )
    cross_dscore = cross_prob * (
        cross_dprob - jnp.sum(cross_dprob * cross_prob, axis=-1, keepdims=True)
    )
    cross_dscore = cross_dscore.astype(jnp.bfloat16)
    cquery_grad = (
        (
            jnp.einsum(
                "ihqt,ithd->iqhd", cross_dscore, text_kheads, preferred_element_type=jnp.float32
            )
            * score_scale
        )
        .astype(jnp.bfloat16)
        .reshape(row_count, model_width)
    )
    tkey_part = (
        jnp.einsum("ihqt,iqhd->ithd", cross_dscore, cross_heads, preferred_element_type=jnp.float32)
        * score_scale
    ).reshape(item_count, text_count, model_width)
    tvalue_part = jnp.einsum(
        "ihqt,iqhd->ithd", cross_prob_bf, crossed_heads, preferred_element_type=jnp.float32
    ).reshape(item_count, text_count, model_width)
    cquery_part = contract_rows(normed_two, cquery_grad)
    normed_two_grad = times_transposed(cquery_grad, w_cquery)
    resid_two, gain_two_part, bias_two_part = pull_two(normed_two_grad)
    self_grad = cross_grad + resid_two
    self_out_bf = self_grad.astype(jnp.bfloat16)
    output_part = contract_rows(attended_rows, self_out_bf)
    attended_grad = times_transposed(self_out_bf, w_output).astype(jnp.bfloat16)
    query_items = query_rows.reshape(item_count, seg_len, model_width)
    dout_items = attended_grad.reshape(item_count, seg_len, model_width)

    def self_backward(operands):
        query_item, key_item, value_item, dout_item, log_total = operands
        scores = self_scores(query_item, key_item)
        probs = jnp.exp(scores - log_total)
        prob_bf = probs.astype(jnp.bfloat16)
        query_heads = query_item.reshape(seg_len, head_count, HEAD_DIM)
        key_heads = key_item.reshape(key_count, head_count, HEAD_DIM)
        value_heads = value_item.reshape(key_count, head_count, HEAD_DIM)
        dout_heads = dout_item.reshape(seg_len, head_count, HEAD_DIM)
        dprob = jnp.einsum(
            "qhd,khd->hqk", dout_heads, value_heads, preferred_element_type=jnp.float32
        )
        dscore = (probs * (dprob - jnp.sum(dprob * probs, axis=-1, keepdims=True))).astype(
            jnp.bfloat16
        )
        dquery = (
            (
                jnp.einsum("hqk,khd->qhd", dscore, key_heads, preferred_element_type=jnp.float32)
                * score_scale
            )
            .astype(jnp.bfloat16)
            .reshape(seg_len, model_width)
        )
        dkey = (
            jnp.einsum("hqk,qhd->khd", dscore, query_heads, preferred_element_type=jnp.float32)
            * score_scale
        ).reshape(key_count, model_width)
        dvalue = jnp.einsum(
            "hqk,qhd->khd", prob_bf, dout_heads, preferred_element_type=jnp.float32
        ).reshape(key_count, model_width)
        return (dquery, dkey, dvalue)

    query_grad_items, key_part, value_part = lax.map(
        self_backward, (query_items, key_all, value_all, dout_items, log_totals)
    )
    key_own, value_own, tkey_own, tvalue_own = (
        lax.psum_scatter(
            key_part.astype(jnp.bfloat16), "seq", scatter_dimension=1, tiled=True
        ).astype(jnp.float32),
        lax.psum_scatter(
            value_part.astype(jnp.bfloat16), "seq", scatter_dimension=1, tiled=True
        ).astype(jnp.float32),
        lax.psum_scatter(
            tkey_part.astype(jnp.bfloat16), "seq", scatter_dimension=1, tiled=True
        ).astype(jnp.float32),
        lax.psum_scatter(
            tvalue_part.astype(jnp.bfloat16), "seq", scatter_dimension=1, tiled=True
        ).astype(jnp.float32),
    )
    key_grad_rows = key_own.astype(jnp.bfloat16).reshape(row_count, model_width)
    value_grad_rows = value_own.astype(jnp.bfloat16).reshape(row_count, model_width)
    query_grad_rows = query_grad_items.reshape(row_count, model_width)
    tkey_bf = tkey_own.astype(jnp.bfloat16)
    tvalue_bf = tvalue_own.astype(jnp.bfloat16)
    query_part = contract_rows(normed_one, query_grad_rows)
    key_wpart = contract_rows(normed_one, key_grad_rows)
    value_wpart = contract_rows(normed_one, value_grad_rows)
    normed_one_grad = (
        times_transposed(query_grad_rows, w_query)
        + times_transposed(key_grad_rows, w_key)
        + times_transposed(value_grad_rows, w_value)
    )
    resid_one, gain_one_part, bias_one_part = pull_one(normed_one_grad)
    input_grad = (self_grad + resid_one).reshape(item_count, seg_len, model_width)
    text_rows = tkey_own.shape[1]
    text_start = lax.axis_index("seq") * text_rows
    text_slice = lax.dynamic_slice_in_dim(text_states, text_start, text_rows, 1)
    ckey_part = jnp.einsum("itc,itd->cd", text_slice, tkey_bf, preferred_element_type=jnp.float32)
    cvalue_part = jnp.einsum(
        "itc,itd->cd", text_slice, tvalue_bf, preferred_element_type=jnp.float32
    )
    text_grad = jnp.einsum(
        "itd,cd->itc", tkey_bf, w_ckey, preferred_element_type=jnp.float32
    ) + jnp.einsum("itd,cd->itc", tvalue_bf, w_cvalue, preferred_element_type=jnp.float32)
    (
        first_gain_grad,
        first_bias_grad,
        query_grad,
        key_grad,
        value_grad,
        output_grad,
        second_gain_grad,
        second_bias_grad,
        cross_query_grad,
        cross_key_grad,
        cross_value_grad,
        cross_output_grad,
        third_gain_grad,
        third_bias_grad,
        up_grad,
        down_grad,
    ) = (
        lax.psum_scatter(gain_one_part, ("dp", "seq"), scatter_dimension=0, tiled=True),
        lax.psum_scatter(bias_one_part, ("dp", "seq"), scatter_dimension=0, tiled=True),
        lax.psum_scatter(query_part, ("dp", "seq"), scatter_dimension=0, tiled=True),
        lax.psum_scatter(key_wpart, ("dp", "seq"), scatter_dimension=0, tiled=True),
        lax.psum_scatter(value_wpart, ("dp", "seq"), scatter_dimension=0, tiled=True),
        lax.psum_scatter(output_part, ("dp", "seq"), scatter_dimension=0, tiled=True),
        lax.psum_scatter(gain_two_part, ("dp", "seq"), scatter_dimension=0, tiled=True),
        lax.psum_scatter(bias_two_part, ("dp", "seq"), scatter_dimension=0, tiled=True),
        lax.psum_scatter(cquery_part, ("dp", "seq"), scatter_dimension=0, tiled=True),
        lax.psum_scatter(ckey_part, ("dp", "seq"), scatter_dimension=0, tiled=True),
        lax.psum_scatter(cvalue_part, ("dp", "seq"), scatter_dimension=0, tiled=True),
        lax.psum_scatter(coutput_part, ("dp", "seq"), scatter_dimension=0, tiled=True),
        lax.psum_scatter(gain_three_part, ("dp", "seq"), scatter_dimension=0, tiled=True),
        lax.psum_scatter(bias_three_part, ("dp", "seq"), scatter_dimension=0, tiled=True),
        lax.psum_scatter(up_part, ("dp", "seq"), scatter_dimension=0, tiled=True),
        lax.psum_scatter(down_part, ("dp", "seq"), scatter_dimension=0, tiled=True),
    )
    return (
        block_out,
        input_grad,
        text_grad,
        first_gain_grad,
        first_bias_grad,
        query_grad,
        key_grad,
        value_grad,
        output_grad,
        second_gain_grad,
        second_bias_grad,
        cross_query_grad,
        cross_key_grad,
        cross_value_grad,
        cross_output_grad,
        third_gain_grad,
        third_bias_grad,
        up_grad,
        down_grad,
    )


def small_rows(vectors):
    packed = jnp.stack(vectors)
    return jnp.pad(packed, ((0, 16 - packed.shape[0]), (0, 128 - packed.shape[1])))


def local(seq_size, *args):
    block_in = args[0]
    if block_in.shape[0] != seq_size or seq_size != 4 or block_in.shape[1] * seq_size != 1024:
        return local_plain(*args)
    return local_items(seq_size, *args)


def local_items(
    seq_size,
    block_in,
    text_states,
    caption_len,
    out_grad,
    first_gain,
    first_bias,
    query_weight,
    key_weight,
    value_weight,
    output_weight,
    second_gain,
    second_bias,
    cross_query,
    cross_key,
    cross_value,
    cross_output,
    third_gain,
    third_bias,
    up_weight,
    down_weight,
):
    ny, nx, nc = 2, seq_size // 2, 2
    dp_size = 1024 // first_gain.shape[0] // seq_size
    dims = (dp_size // ny, ny, nx, nc)
    bf, f32 = jnp.bfloat16, jnp.float32
    seg, width = block_in.shape[1], block_in.shape[2]
    rows = seq_size * seg
    me = lax.axis_index("seq")
    small = small_rows([first_gain, first_bias, second_gain, second_bias, third_gain, third_bias])
    shards = [small, query_weight, key_weight, value_weight, output_weight, cross_query, cross_key, cross_value, cross_output, up_weight, down_weight]
    full, kept = forward(dims, shards, block_in, out_grad, text_states, caption_len, 1)
    small, w_query, w_key, w_value, w_output, w_cquery, w_ckey, w_cvalue, w_coutput, w_up, w_down = full
    grad_rows, inputs, q, k, v, cq, ck, cv, o, o2, normed_one, normed_two, normed_three, after_self, after_cross, lse, lse2, vectors = kept
    grad_rows = grad_rows.reshape(rows, width)
    block_out, dh3, down_part, up_grad_done, up_part = ffn(dims, normed_three, grad_rows, after_cross, w_up, w_down, up_weight, 4)
    (
        block_out, text_grad, self_grad, do, g_cq, g_ck, g_cv, g_o, sums, down_grad, up_grad, coutput_grad,
    ) = middle(dims, (
        grad_rows, dh3, after_cross, after_self, vectors, o2, cq, ck, cv, lse2, normed_two, o, w_coutput, w_cquery, w_ckey, w_cvalue,
        w_output, text_states, caption_len, block_out.reshape(seq_size, seg, width), down_part, up_part,
    ), 2)
    up_grad = jnp.concatenate([up_grad_done, up_grad], axis=1)
    (
        input_grad, cquery_grad, ckey_grad, cvalue_grad, output_grad, query_grad, key_grad, value_grad, small_grad,
    ) = last(dims, (
        q, k, v, do, o, lse, normed_one, w_query, w_key, w_value, inputs.reshape(rows, width), self_grad, vectors,
        g_cq, g_ck, g_cv, g_o, sums,
    ), 3)
    input_grad = input_grad.astype(f32)
    vec = [small_grad[i, : first_gain.shape[0]] for i in range(6)]
    return (
        block_out, input_grad, text_grad,
        vec[0], vec[1], query_grad, key_grad, value_grad, output_grad,
        vec[2], vec[3], cquery_grad, ckey_grad, cvalue_grad, coutput_grad,
        vec[4], vec[5], up_grad, down_grad,
    )


def solution(mesh):
    return jax.shard_map(
        functools.partial(local, mesh.shape['seq']),
        mesh=mesh,
        in_specs=(
            P("dp", "seq", None),
            P("dp", None, None),
            P("dp"),
            P("dp", "seq", None),
            P(("dp", "seq")),
            P(("dp", "seq")),
            P(("dp", "seq"), None),
            P(("dp", "seq"), None),
            P(("dp", "seq"), None),
            P(("dp", "seq"), None),
            P(("dp", "seq")),
            P(("dp", "seq")),
            P(("dp", "seq"), None),
            P(("dp", "seq"), None),
            P(("dp", "seq"), None),
            P(("dp", "seq"), None),
            P(("dp", "seq")),
            P(("dp", "seq")),
            P(("dp", "seq"), None),
            P(("dp", "seq"), None),
        ),
        out_specs=(
            P("dp", "seq", None),
            P("dp", "seq", None),
            P("dp", "seq", None),
            P(("dp", "seq")),
            P(("dp", "seq")),
            P(("dp", "seq"), None),
            P(("dp", "seq"), None),
            P(("dp", "seq"), None),
            P(("dp", "seq"), None),
            P(("dp", "seq")),
            P(("dp", "seq")),
            P(("dp", "seq"), None),
            P(("dp", "seq"), None),
            P(("dp", "seq"), None),
            P(("dp", "seq"), None),
            P(("dp", "seq")),
            P(("dp", "seq")),
            P(("dp", "seq"), None),
            P(("dp", "seq"), None),
        ),
        check_vma=False,
    )
```

```python
import functools
import itertools

import jax
import jax.numpy as jnp
from jax import lax
from jax.experimental import pallas as pl
from jax.experimental.pallas import tpu as pltpu
from jax.sharding import PartitionSpec as P

MESH = pl.DeviceIdType.MESH
ANY = pl.ANY


class Place:
    def __init__(self, dims):
        self.nz, self.ny, self.nx, self.nc = dims
        dp, seq = lax.axis_index("dp"), lax.axis_index("seq")
        self.z, self.y = lax.div(dp, self.ny), lax.rem(dp, self.ny)
        self.x, self.c = lax.div(seq, self.nc), lax.rem(seq, self.nc)
        self.dp, self.seq = dp, seq

    def dev(self, z=None, y=None, x=None, c=None):
        z = self.z if z is None else z
        y = self.y if y is None else y
        x = self.x if x is None else x
        c = self.c if c is None else c
        return (z * self.ny + y, x * self.nc + c)

    def z_others(self):
        if self.nz != 4:
            return [lax.rem(self.z + k, self.nz) for k in range(1, self.nz)]
        near, far = 1 + lax.rem(self.z, 2), 3 - 3 * lax.div(self.z, 2)
        return [near, 6 - self.z - near - far, far]


def hello(peers):
    barrier = pltpu.get_barrier_semaphore()
    for peer in peers:
        pl.semaphore_signal(barrier, inc=1, device_id=peer, device_id_type=MESH)
    pl.semaphore_wait(barrier, len(peers))


def push(src, dst, send, recv, device):
    pltpu.make_async_remote_copy(
        src_ref=src, dst_ref=dst, send_sem=send, recv_sem=recv, device_id=device, device_id_type=MESH
    ).start()


def drain(ref, sem):
    pltpu.make_async_copy(ref, ref, sem).wait()


def add_to(dst, src):
    dst[...] = dst[...] + src[...]


LOG2E = 1.4426950408889634
NT = (((1,), (1,)), ((), ()))
NN = (((1,), (0,)), ((), ()))
def dot(a, b, dims=NN):
    return lax.dot_general(a, b, dims, preferred_element_type=jnp.float32)

def half_mask(x, h):
    lane = lax.broadcasted_iota(jnp.int32, x.shape, 1)
    keep = lane < 64 if h == 0 else lane >= 64
    return jnp.where(keep, x, jnp.zeros_like(x))

def hide(scores, limit, causal, start):
    rows, cols = scores.shape
    if causal:
        key = lax.broadcasted_iota(jnp.int32, (cols, cols), 0)
        query = lax.broadcasted_iota(jnp.int32, (cols, cols), 1)
        tail = jnp.where(key <= query, scores[rows - cols:], -1e30)
        return tail if rows == cols else jnp.concatenate([scores[:rows - cols], tail], axis=0)
    key = lax.broadcasted_iota(jnp.int32, (rows, cols), 0)
    return jnp.where(key < limit, scores, -1e30)

def attend_kernel(causal, block, limit_ref, q_ref, k_ref, v_ref, o_ref, lse_ref):
    limit = None if causal else limit_ref[0]
    rows, keys = q_ref.shape[0], k_ref.shape[0]
    v_t = v_ref[...].T
    ones = jnp.ones((16, keys), v_t.dtype)
    for i in range(rows // block):
        n = (i + 1) * block if causal else keys
        span = pl.ds(i * block, block)
        halves = []
        for h in range(2):
            q = half_mask(q_ref[span, :], h)
            s = hide(dot(k_ref[0:n, :], q, NT), limit, causal, i * block)
            peak = jnp.max(s, axis=0, keepdims=True)
            e = jnp.exp2(s - peak).astype(jnp.bfloat16)
            v_aug = jnp.concatenate([v_t[h * 64:(h + 1) * 64, :n], ones[:, :n]], axis=0)
            mixed = dot(v_aug, e)
            total = mixed[64:65]
            halves.append(mixed[:64] / total)
            lse_ref[0, h:h + 1, span] = peak + jnp.log2(total)
        o_ref[span, :] = jnp.concatenate(halves, axis=0).T.astype(o_ref.dtype)

def attend_back_kernel(causal, block, limit_ref, q_ref, k_ref, v_ref, g_ref, o_ref, lse_ref, dq_ref, dk_ref, dv_ref, dk_acc, dv_acc):
    limit = None if causal else limit_ref[0]
    rows, keys = q_ref.shape[0], k_ref.shape[0]
    k_t = k_ref[...].T
    sel_row = lax.broadcasted_iota(jnp.int32, (16, 128), 0)
    sel_lane = lax.broadcasted_iota(jnp.int32, (16, 128), 1)
    pick = jnp.where(sel_row == lax.div(sel_lane, 64), 1.0, 0.0).astype(jnp.bfloat16)
    dk_acc[...] = jnp.zeros_like(dk_acc)
    dv_acc[...] = jnp.zeros_like(dv_acc)
    for i in range(rows // block):
        n = (i + 1) * block if causal else keys
        span = pl.ds(i * block, block)
        prod = g_ref[span, :].astype(jnp.float32) * o_ref[span, :].astype(jnp.float32)
        high = prod.astype(jnp.bfloat16)
        low = (prod - high.astype(jnp.float32)).astype(jnp.bfloat16)
        delta = dot(pick, high, NT) + dot(pick, low, NT)
        halves = []
        for h in range(2):
            q = half_mask(q_ref[span, :], h)
            g = half_mask(g_ref[span, :], h)
            s = hide(dot(k_ref[0:n, :], q, NT), limit, causal, i * block)
            p = jnp.exp2(s - lse_ref[0, h:h + 1, span])
            dp = dot(v_ref[0:n, :], g, NT)
            ds = (p * (dp - delta[h:h + 1])).astype(jnp.bfloat16)
            dv_acc[0:n, :] += dot(p.astype(jnp.bfloat16), g)
            dk_acc[0:n, :] += dot(ds, q)
            halves.append(dot(k_t[h * 64:(h + 1) * 64, :n], ds))
        dq_ref[span, :] = (jnp.concatenate(halves, axis=0).T * 0.125).astype(dq_ref.dtype)
    dk_ref[...] = (dk_acc[...] * (1.0 / LOG2E)).astype(dk_ref.dtype)
    dv_ref[...] = dv_acc[...].astype(dv_ref.dtype)

def gelu_parts(u):
    t = 1.0 / (1.0 + (0.3275911 * 0.7071067811865476) * jnp.abs(u))
    e = jnp.exp(-0.5 * (u * u))
    poly = t * (0.254829592 + t * (-0.284496736 + t * (1.421413741 + t * (-1.453152027 + t * 1.061405429))))
    tail = 0.5 * poly * e
    return jnp.where(u < 0, tail, 1.0 - tail), e * 0.3989422804014327


def ffn_kernel(dims, sent, h_ref, g_ref, x_ref, up_in, down_ref, shard_ref, out_ref, dh_ref, ddown_ref, grad_ref, rest_ref,
               h_t, acc, act, du, made, own, rc, r2a, r2b, r3, r4, local_sem, send, recv,
               late, near, up_ref, late_send, late_recv):
    j = pl.program_id(0)
    steps = pl.num_programs(0)
    at = Place(dims)
    nz, ny, nx, nc = dims
    z, y, x, c = at.z, at.y, at.x, at.c
    oy, ox, oc = 1 - y, 1 - x, 1 - c
    rows, width = h_ref.shape
    chunk = up_in.shape[1]
    last = steps - 1
    net = Gather(dims, [(0, 0, near.shape[0], 0, chunk, (2, 1, 0))], [near], [late], late_send, late_recv)
    half = chunk // 2
    block = rows // 2
    left, right = pl.ds(0, half), pl.ds(half, half)
    every = slice(None)

    def made_at(slot, core):
        return made.at[(slot, every, every, every, core)]

    def core_go(i):
        slot = lax.rem(i, 2)
        pltpu.make_async_copy(made_at(slot, c), own.at[i], local_sem.at[i]).start()
        push(made_at(slot, oc), rc.at[i], send.at[i, 0], recv.at[i, 0], at.dev(c=oc))

    def first_go(i):
        drain(own.at[i], local_sem.at[i])
        drain(rc.at[i], recv.at[i, 0])
        drain(rc.at[i], send.at[i, 0])

        @pl.loop(0, nz)
        def _(a):
            for b in range(ny):
                for d in range(nx):
                    add_to(own.at[i, a, b, d], rc.at[i, a, b, d])

        push(own.at[i, :, oy, :, :, left], r2a.at[i], send.at[i, 1], recv.at[i, 1], at.dev(y=oy))
        push(own.at[i, :, :, ox, :, right], r2b.at[i], send.at[i, 1], recv.at[i, 2], at.dev(x=ox))

    def second_go(i):
        drain(r2a.at[i], recv.at[i, 1])
        drain(r2b.at[i], recv.at[i, 2])

        @pl.loop(0, nz)
        def _(a):
            for b in range(2):
                add_to(own.at[i, a, y, b, :, left], r2a.at[i, a, b])
                add_to(own.at[i, a, b, x, :, right], r2b.at[i, a, b])

        push(own.at[i, :, y, ox, :, left], r3.at[i, :, :, left], send.at[i, 1], recv.at[i, 3], at.dev(x=ox))
        push(own.at[i, :, oy, x, :, right], r3.at[i, :, :, right], send.at[i, 1], recv.at[i, 4], at.dev(y=oy))

    def third_go(i):
        drain(r3.at[i, :, :, left], recv.at[i, 3])
        drain(r3.at[i, :, :, right], recv.at[i, 4])

        @pl.loop(0, nz)
        def _(a):
            add_to(own.at[i, a, y, x], r3.at[i, a])

        for k in range(1, nz):
            far = lax.rem(z + k, nz)
            push(own.at[i, far, y, x], r4.at[i, k - 1], send.at[i, 1], recv.at[i, 5], at.dev(z=far))

    def finish(i):
        drain(r4.at[i], recv.at[i, 5])
        total = own[i, z, y, x].astype(jnp.float32)
        for k in range(nz - 1):
            total = total + r4[i, k].astype(jnp.float32)
        grad_ref[i] = total
        for part in (r2a.at[i], r2b.at[i], r3.at[i], r4.at[i]):
            drain(part, send.at[i, 1])

    @pl.when(j == 0)
    def _():
        hello([at.dev(z=k) for k in at.z_others()] + [at.dev(y=oy), at.dev(x=ox), at.dev(c=oc)])
        load = pltpu.make_async_copy(shard_ref.at[:, pl.ds(shard_ref.shape[1] - chunk, chunk)], near, local_sem.at[0])
        load.start()
        load.wait()
        late[z, y, x, c] = near[...]
        net.go(0, 0)
        acc[...] = x_ref[...]
        dh_ref[...] = jnp.zeros_like(dh_ref)

        @pl.loop(0, rows // block)
        def _(r):
            span = pl.ds(pl.multiple_of(r * block, block), block)
            h_t[:, span] = h_ref[span, :].T

    def after(late, then, first=0, end=sent):
        pl.when((j >= late + first) & (j < late + end))(lambda: then(j - late))

    @pl.when(j < last)
    def _():
        up_ref[...] = up_in[...]

    @pl.when(j == last)
    def _():
        net.arrived(0)
        up_ref[...] = late[...].reshape(up_ref.shape)

    after(1, first_go)
    after(2, third_go, 0, sent - 1)
    for r in range(rows // block):
        span = pl.ds(r * block, block)
        u = dot(h_ref[span, :], up_ref[...])
        g = dot(g_ref[span, :], down_ref[...], NT)
        big, small = gelu_parts(u)
        a = (u * big).astype(jnp.bfloat16)
        d = (g * (big + u * small)).astype(jnp.bfloat16)
        act[span, :] = a
        du[span, :] = d
        acc[span, :] += dot(a, down_ref[...])
        dh_ref[span, :] += dot(d, up_ref[...], NT)

    pl.when(j == 0)(lambda: net.go(0, 1))
    pl.when(j == 2)(lambda: net.go(0, 3))
    after(1, second_go)
    after(2, finish, 0, sent - 1)
    slot = lax.rem(j, 2)
    each = rows // (nz * ny * nx * nc)

    @pl.loop(0, nz)
    def _(a):
        n = ny * nx * nc * each
        part = dot(h_t[pl.ds(pl.multiple_of(a * n, n), n), :], du[...]).astype(made.dtype)
        made[slot, a] = part.reshape(ny, nx, nc, each, chunk)

    pl.when(j == 0)(lambda: net.go(0, 2))
    after(0, core_go)
    after(1, third_go, sent - 1)
    ddown_ref[...] = lax.dot_general(act[...], g_ref[...], TN, preferred_element_type=jnp.float32).astype(ddown_ref.dtype)
    after(1, finish, sent - 1)

    @pl.when(j >= sent)
    def _():
        pltpu.make_async_copy(made.at[slot], rest_ref.at[j - sent], local_sem.at[j]).start()

    @pl.when(j == steps - 1)
    def _():
        net.sent(0)
        out_ref[...] = acc[...].astype(out_ref.dtype)
        for i in range(sent, 4):
            drain(rest_ref.at[i - sent], local_sem.at[i])


def ffn(dims, h, g, x, w_up, w_down, up_shard, cid, sent=3, steps=4):
    nz, ny, nx, nc = dims
    rows, width = h.shape
    inner = w_up.shape[1]
    chunk = inner // steps
    each = width // (nz * ny * nx * nc)
    bf, f32 = jnp.bfloat16, jnp.float32
    fixed = lambda j: (0, 0)
    whole = pl.BlockSpec((rows, width), fixed)
    once = pl.BlockSpec((rows, width), fixed, pipeline_mode=pl.Buffered(1))
    tile = (each, chunk)
    out, dh, ddown, grad, rest = pl.pallas_call(
        functools.partial(ffn_kernel, dims, sent),
        grid=(steps,),
        out_shape=[
            jax.ShapeDtypeStruct((rows, width), bf),
            jax.ShapeDtypeStruct((rows, width), f32),
            jax.ShapeDtypeStruct((inner, width), bf),
            jax.ShapeDtypeStruct((sent, each, chunk), f32),
            jax.ShapeDtypeStruct((steps - sent, nz, ny, nx, nc, each, chunk), bf),
        ],
        in_specs=[once, once, once, pl.BlockSpec((width, chunk), lambda j: (0, jnp.minimum(j, steps - 2))),
                  pl.BlockSpec((chunk, width), lambda j: (j, 0)), pl.BlockSpec(memory_space=ANY)],
        out_specs=[once, once, pl.BlockSpec((chunk, width), lambda j: (j, 0)),
                   pl.BlockSpec((sent, each, chunk), lambda j: (0, 0, 0)), pl.BlockSpec(memory_space=ANY)],
        scratch_shapes=[
            pltpu.VMEM((width, rows), bf), pltpu.VMEM((rows, width), f32), pltpu.VMEM((rows, chunk), bf), pltpu.VMEM((rows, chunk), bf),
            pltpu.VMEM((2, nz, ny, nx, nc) + tile, bf),
            pltpu.VMEM((sent, nz, ny, nx) + tile, bf), pltpu.VMEM((sent, nz, ny, nx) + tile, bf),
            pltpu.VMEM((sent, nz, nx, each, chunk // 2), bf), pltpu.VMEM((sent, nz, ny, each, chunk // 2), bf),
            pltpu.VMEM((sent, nz) + tile, bf), pltpu.VMEM((sent, nz - 1) + tile, bf),
            pltpu.SemaphoreType.DMA((steps,)), pltpu.SemaphoreType.DMA((sent, 2)), pltpu.SemaphoreType.DMA((sent, 6)),
            pltpu.VMEM((nz, ny, nx, nc) + tile, bf), pltpu.VMEM(tile, bf), pltpu.VMEM((width, chunk), bf),
            pltpu.SemaphoreType.DMA((1,)), pltpu.SemaphoreType.DMA((1, 4)),
        ],
        compiler_params=pltpu.CompilerParams(collective_id=cid, has_side_effects=True, vmem_limit_bytes=62 * 2**20, dimension_semantics=("arbitrary",)),
        name="feed_forward",
    )(h, g, x, w_up, w_down, up_shard)
    grad = jnp.moveaxis(grad, 0, 1).reshape(each, sent * chunk)
    rest = jnp.moveaxis(rest, 0, 5).reshape(width, (steps - sent) * chunk)
    return out, dh, ddown, grad, rest
class Gather:
    def __init__(self, dims, units, ins, outs, send, recv):
        self.at, self.nz = Place(dims), dims[0]
        self.units, self.ins, self.outs, self.send, self.recv = units, ins, outs, send, recv

    def part(self, u, where, core=None):
        a, r0, nr, c0, ncol, _ = self.units[u]
        return self.outs[a].at[(*where, self.at.c if core is None else core, pl.ds(r0, nr), pl.ds(c0, ncol))]

    def held(self, u, k):
        where = [self.at.z, self.at.y, self.at.x]
        for axis in self.units[u][5][:k]:
            where[axis] = slice(None)
        return where

    def coming(self, u, k):
        where = self.held(u, k)
        axis = self.units[u][5][k]
        where[axis] = (slice(0, self.nz - 1), 1 - self.at.y, 1 - self.at.x)[axis]
        return where

    def to_core(self, u, where):
        block = self.part(u, where)
        push(block, block, self.send.at[u], self.recv.at[u, 3], self.at.dev(c=1 - self.at.c))

    def pass_on(self, u, k):
        axis = self.units[u][5][k]
        if axis == 0 and k == 0:
            self.to_core(u, self.held(u, 1))
        elif axis == 0:
            for z in self.at.z_others():
                where = self.held(u, k)
                where[0] = z
                self.to_core(u, where)
        else:
            self.to_core(u, self.coming(u, k))
            if k == 0:
                self.to_core(u, self.held(u, 0))

    def go(self, u, k):
        at = self.at
        if k > 0:
            drain(self.part(u, self.coming(u, k - 1)), self.recv.at[u, k - 1])
        if k < 3:
            a, r0, nr, c0, ncol, order = self.units[u]
            dst = self.part(u, self.held(u, k))
            src = self.ins[a].at[pl.ds(r0, nr), pl.ds(c0, ncol)] if k == 0 else dst
            targets = ([at.dev(z=z) for z in at.z_others()], [at.dev(y=1 - at.y)], [at.dev(x=1 - at.x)])[order[k]]
            for device in targets:
                push(src, dst, self.send.at[u], self.recv.at[u, k], device)
        if k > 0:
            self.pass_on(u, k - 1)

    def arrived(self, u):
        drain(self.part(u, [slice(None)] * 3, 1 - self.at.c), self.recv.at[u, 3])

    def sent(self, u):
        for k in range(3):
            where = self.held(u, k)
            if self.units[u][5][k] == 0:
                where[0] = slice(0, self.nz - 1)
            drain(self.part(u, where), self.send.at[u])
        drain(self.part(u, [slice(None)] * 3), self.send.at[u])


def norm_parts(values_in):
    center = values_in - jnp.mean(values_in, axis=-1, keepdims=True)
    return center * lax.rsqrt(jnp.mean(center * center, axis=-1, keepdims=True) + EPS)


FW_PATHS = ((0, 2, 1), (0, 1, 2), (0, 1, 2), (0, 1, 2), (2, 0, 1), (2, 0, 1), (2, 0, 1), (0, 1, 2), (0, 1, 2), (2, 0, 1), (0, 1, 2), (1, 2, 0), (2, 0, 1), (2, 0, 1), (2, 1, 0), (0, 1, 2), (0, 1, 2))
FW_UNITS = [(a, 0, 32, 0, 1024, FW_PATHS[a - 1]) for a in range(1, 9)]
FW_UNITS += [(9, 0, 32, 1024 * j, 1024, FW_PATHS[8 + j]) for j in range(4)]
FW_UNITS += [(10, 32 * j, 32, 0, 1024, FW_PATHS[12 + j]) for j in range(4)] + [(0, 0, 16, 0, 128, FW_PATHS[16])]
FW_ORDER = (
    (5, 0), (1, 0), (16, 0), (0, 0), (4, 0), (6, 0), (1, 1), (2, 0), (16, 1), (3, 0), (0, 1), (10, 0), (1, 2),
    (16, 2), (2, 1), (15, 0), (3, 1), (7, 0), (5, 1), (12, 0), (4, 1), (13, 0), (2, 2), (6, 1), (9, 0), (10, 1),
    (8, 0), (3, 2), (0, 2), (15, 1), (10, 2), (7, 1), (1, 3), (16, 3), (12, 1), (1, 4), (14, 0), (13, 1), (0, 3),
    (-2, 0), (5, 2), (0, 4), (15, 2), (-2, 1), (2, 3), (-2, 2), (9, 1), (2, 4), (7, 2), (4, 2), (-2, 3), (-2, 4),
    (3, 3), (5, 3), (-2, 5), (3, 4), (6, 2), (5, 4), (-2, 6), (-2, 7), (8, 1), (-2, 8), (10, 3), (4, 3), (14, 1),
    (-2, 9), (4, 4), (-2, 10), (12, 2), (-2, 11), (6, 3), (15, 3), (-2, 12), (6, 4), (8, 2), (13, 2), (14, 2),
    (-2, 13), (7, 3), (-2, 14), (-2, 15), (7, 4), (-2, 16), (9, 2), (-1, 0), (12, 3), (-2, 17), (-2, 18), (-2, 19),
    (8, 3), (-2, 20), (-2, 21), (-2, 22), (-2, 23), (13, 3), (-2, 24), (14, 3), (9, 3),
)


def forward_kernel(dims, n, *refs):
    shards, refs = refs[:n], refs[n:]
    block_in, out_grad, text_states, limits = refs[:4]
    full, refs = refs[4 : 4 + n], refs[4 + n :]
    g_out, x_out, q_out, k_out, v_out, cq_out, ck_out, cv_out, o_out, o2_out, h1_out, h2_out, h3_out, x1_out, x2_out, lse_out, lse2_out, vec = refs[:18]
    x_in, q, k, v, cq, ck, cv, o, o2, h1, h2, h3, x1, x2, lse, lse2, text, small = refs[18:36]
    w, near, own_g = refs[36:44], refs[44 : 44 + n], refs[44 + n]
    limit, local_sem, out_sem, send, recv, ex_send, ex_recv = refs[45 + n :]
    at = Place(dims)
    oy, ox, oc, me = 1 - at.y, 1 - at.x, 1 - at.c, at.seq
    hello([at.dev(z=p) for p in at.z_others()] + [at.dev(y=oy), at.dev(x=ox), at.dev(c=oc), at.dev(x=ox, c=oc)])
    net = Gather(dims, FW_UNITS, near, full, send, recv)
    rows, width = q.shape
    block = 256
    f32, bf = jnp.float32, jnp.bfloat16
    others = ((ox, at.c), (ox, oc), (at.x, oc))

    def exchange(src, dst, i, own):
        for px, pc in others:
            push(src.at[px * 2 + pc], dst.at[me], ex_send.at[i], ex_recv.at[i], at.dev(x=px, c=pc))
        pltpu.make_async_copy(own, dst.at[me], local_sem.at[n + i]).start()

    def exchanged(dst, i):
        drain(dst.at[0:3], ex_recv.at[i])
        drain(dst.at[0], local_sem.at[n + i])

    keep = []

    def put(src, dst):
        pltpu.make_async_copy(src, dst, out_sem.at[len(keep)]).start()
        keep.append(src)

    loads = 4 + n

    def load(a):
        net.arrived(a - 1)
        pltpu.make_async_copy(full[a], w[a - 1], local_sem.at[loads + a]).start()

    def loaded(a):
        drain(w[a - 1], local_sem.at[loads + a])

    def weight(a):
        return w[a - 1][...].reshape(width, width)

    def span_of(r):
        return pl.ds(pl.multiple_of(r * block, block), block)

    def first_norm():
        net.arrived(16)
        pltpu.make_async_copy(full[0], small, local_sem.at[n + 3]).start()
        drain(small, local_sem.at[n + 3])
        packed = small[...].reshape(-1, 16, 128).astype(f32)
        devices = packed.shape[0]
        piece = width // devices
        lane = lax.rem(lax.broadcasted_iota(jnp.int32, (128, width), 1), piece)
        spread = jnp.where(lane == lax.broadcasted_iota(jnp.int32, (128, width), 0), 1.0, 0.0).astype(bf)
        owner = lax.div(lax.broadcasted_iota(jnp.int32, (devices, width), 1), piece)
        mine = owner == lax.broadcasted_iota(jnp.int32, (devices, width), 0)
        vec[...] = jnp.zeros_like(vec)
        for i in range(6):
            vec[i : i + 1, :] = row_sum(jnp.where(mine, dot(packed[:, i, :].astype(bf), spread), 0.0))
        exchanged(x_in, 0)
        put(x_in, x_out)

        @pl.loop(0, 4)
        def _(r):
            x = x_in[r].astype(f32)
            x1[span_of(r), :] = x
            h1[span_of(r), :] = (norm_parts(x) * vec[0:1, :] + vec[1:2, :]).astype(bf)

        put(h1, h1_out)

    def project(a, dst, scale, kept):
        loaded(a)

        @pl.loop(0, rows // block)
        def _(r):
            made = dot(h1[span_of(r), :], weight(a))
            dst[span_of(r), :] = (made if scale is None else made * scale).astype(bf)

        put(dst, kept)

    def pair(causal, qs, ks, vs, os, ls, j):
        cols = pl.ds(pl.multiple_of(j * 128, 128), 128)
        attend_kernel(causal, 512, limit, qs.at[:, cols], ks.at[:, cols], vs.at[:, cols], os.at[:, cols], ls.at[pl.ds(j, 1)])

    self_attention = functools.partial(pair, True, q, k, v, o, lse)
    cross_attention = functools.partial(pair, False, cq, ck, cv, o2, lse2)
    count = width // 128

    def second_norm(i):
        if i == 0:
            put(o, o_out)
            put(lse, lse_out)
            loaded(4)
            loaded(5)

        @pl.loop(2 * i, 2 * i + 2)
        def _(r):
            x = x1[span_of(r), :] + dot(o[span_of(r), :], weight(4))
            x1[span_of(r), :] = x
            h = (norm_parts(x) * vec[2:3, :] + vec[3:4, :]).astype(bf)
            h2[span_of(r), :] = h
            cq[span_of(r), :] = (dot(h, weight(5)) * (LOG2E / 8)).astype(bf)

        if i == 1:
            put(x1, x1_out)
            put(h2, h2_out)
            put(cq, cq_out)

    def text_rows():
        loaded(6)
        loaded(7)
        ck[...] = dot(text[...], weight(6)).astype(bf)
        cv[...] = dot(text[...], weight(7)).astype(bf)
        put(ck, ck_out)
        put(cv, cv_out)

    def third_norm(i):
        if i == 0:
            put(o2, o2_out)
            put(lse2, lse2_out)
            loaded(8)

        @pl.loop(2 * i, 2 * i + 2)
        def _(r):
            x = x1[span_of(r), :] + dot(o2[span_of(r), :], weight(8))
            x2[span_of(r), :] = x
            h3[span_of(r), :] = (norm_parts(x) * vec[4:5, :] + vec[5:6, :]).astype(bf)

        if i == 1:
            put(x2, x2_out)
            put(h3, h3_out)

    pieces = [first_norm, lambda: project(1, q, LOG2E / 8, q_out), lambda: project(2, k, None, k_out), lambda: project(3, v, None, v_out)]
    pieces += [(self_attention, j) for j in range(count)] + [functools.partial(second_norm, i) for i in range(2)] + [text_rows]
    pieces += [(cross_attention, j) for j in range(count)] + [functools.partial(third_norm, i) for i in range(2)]

    for a in range(n):
        pltpu.make_async_copy(shards[a], near[a], local_sem.at[a]).start()
    exchange(block_in, x_in, 0, block_in.at[me])
    pltpu.make_async_copy(text_states.at[me], text, local_sem.at[n + 2]).start()
    pltpu.make_async_copy(out_grad.at[me], own_g, local_sem.at[n + 1]).start()
    for a in range(n):
        drain(near[a], local_sem.at[a])
    drain(own_g, local_sem.at[n + 1])
    for a in range(n):
        pltpu.make_async_copy(near[a], full[a].at[at.z, at.y, at.x, at.c], local_sem.at[a]).start()
    limit[0] = limits[me]
    begin = next(i for i, (_, step) in enumerate(FW_ORDER) if step > 0)

    def event(u, step):
        if u == -1:
            exchange(out_grad, g_out, 1, own_g)
        elif step == 4:
            load(u + 1)
        else:
            net.go(u, step)

    run_order(FW_ORDER[:begin], event, [])
    for a in range(n):
        drain(near[a], local_sem.at[a])
    drain(text, local_sem.at[n + 2])
    run_order(FW_ORDER[begin:], event, pieces)
    exchanged(g_out, 1)
    moved = sorted({u for u, _ in FW_ORDER if u >= 0})
    for u in moved:
        if 8 <= u < 16:
            net.arrived(u)
    for u in moved:
        net.sent(u)
    drain(x_in.at[0:3], ex_send.at[0])
    drain(g_out.at[0:3], ex_send.at[1])
    for i, src in enumerate(keep):
        drain(src, out_sem.at[i])


def forward(dims, shards, block_in, out_grad, text_states, limits, cid):
    n = len(shards)
    bf, f32 = jnp.bfloat16, jnp.float32
    items, seg, width = block_in.shape
    rows, texts = items * seg, text_states.shape[1]
    wide, pairs = jax.ShapeDtypeStruct((rows, width), bf), width // 128
    short = jax.ShapeDtypeStruct((texts, width), bf)
    long = jax.ShapeDtypeStruct((rows, width), f32)
    sums = jax.ShapeDtypeStruct((pairs, 8, rows), f32)
    seg4 = jax.ShapeDtypeStruct(block_in.shape, bf)
    whole = [jax.ShapeDtypeStruct(tuple(dims) + s.shape, s.dtype) for s in shards]
    saved = [wide, wide, wide, wide, short, short, wide, wide, wide, wide, wide, long, long, sums, sums]
    out_shape = whole + [seg4, seg4] + saved + [jax.ShapeDtypeStruct((8, width), f32)]
    held = [pltpu.VMEM(s.shape, s.dtype) for s in [seg4] + saved + [short]] + [pltpu.VMEM(tuple(dims) + (16, 128), bf)]
    held += [pltpu.VMEM(s.shape, s.dtype) for s in whole[1:9]] + [pltpu.VMEM(s.shape, s.dtype) for s in shards]
    held += [pltpu.VMEM(block_in.shape[1:], bf)]
    units = len(FW_UNITS)
    any_spec = pl.BlockSpec(memory_space=ANY)
    outs = pl.pallas_call(
        functools.partial(forward_kernel, dims, n),
        out_shape=out_shape,
        in_specs=[any_spec] * (n + 3) + [pl.BlockSpec(memory_space=pltpu.SMEM)],
        out_specs=[any_spec] * (len(out_shape) - 1) + [pl.BlockSpec(memory_space=pltpu.VMEM)],
        scratch_shapes=held
        + [
            pltpu.SMEM((1,), jnp.int32),
            pltpu.SemaphoreType.DMA((2 * n + 8,)), pltpu.SemaphoreType.DMA((20,)),
            pltpu.SemaphoreType.DMA((units,)), pltpu.SemaphoreType.DMA((units, 4)),
            pltpu.SemaphoreType.DMA((2,)), pltpu.SemaphoreType.DMA((2,)),
        ],
        compiler_params=pltpu.CompilerParams(collective_id=cid, has_side_effects=True, vmem_limit_bytes=62 * 2**20),
        name="forward",
    )(*shards, block_in, out_grad, text_states, limits)
    full = [o.reshape((-1,) + o.shape[5:]) for o in outs[:n]]
    return full, outs[n:]
def run_order(order, event, pieces):
    i = 0
    while i < len(order):
        unit, step = order[i]
        i += 1
        if unit != -2:
            event(unit, step)
            continue
        piece = pieces[step]
        if callable(piece):
            piece()
            continue
        body, first = piece
        last, between = first, {first: []}
        while i < len(order):
            unit, step = order[i]
            if unit != -2:
                between[last].append((unit, step))
            else:
                piece = pieces[step]
                if callable(piece) or piece[0] is not body:
                    break
                last = piece[1]
                between[last] = []
            i += 1

        def one(j, body=body, between=between):
            body(j)
            for k, events in between.items():
                if events:
                    pl.when(j == k)(functools.partial(run_order, events, event, pieces))

        pl.loop(first, last + 1)(one)


class Scatter:
    def __init__(self, dims, send, recv, local):
        self.at, self.dims, self.send, self.recv, self.local, self.units = Place(dims), dims, send, recv, local, []

    def add(self, source, room, out, order, whole):
        self.units.append((source, room[0], room[1:], out, order, whole))

    def own(self, u, where):
        own, whole = self.units[u][1], self.units[u][5]
        return own.at[(*where, self.at.c)] if whole else own.at[tuple(where)]

    def left(self, u, k):
        where = [slice(None)] * 3
        for axis in self.units[u][4][:k]:
            where[axis] = (self.at.z, self.at.y, self.at.x)[axis]
        return where

    def add_in(self, u, k, bufs):
        where = self.left(u, k)
        open_axes = [axis for axis in range(3) if axis not in self.units[u][4][:k]]

        def one(index):
            spot = list(where)
            for axis, i in zip(open_axes, index):
                spot[axis] = i
            dst = self.own(u, spot)
            if len(bufs) == 1:
                dst[...] = dst[...] + bufs[0][tuple(index)]
            else:
                total = dst[...].astype(jnp.float32)
                for buf in bufs:
                    total = total + buf[tuple(index)].astype(jnp.float32)
                dst[...] = total.astype(dst.dtype)

        sizes = [self.dims[axis] for axis in open_axes]
        inner = list(itertools.product(*[range(n) for n in sizes[1:]]))

        @pl.loop(0, sizes[0])
        def _(i):
            for rest in inner:
                one((i, *rest))

    def bufs(self, u, k):
        buf = self.units[u][2][k]
        return [buf.at[i] for i in range(self.dims[0] - 1)] if self.units[u][4][k - 1] == 0 else [buf]

    def go(self, u, k):
        source, own, room, out, order, whole = self.units[u]
        at, every = self.at, slice(None)
        if k == 0:
            if not whole:
                pltpu.make_async_copy(source(every, every, every, at.c), own, self.local.at[u]).start()
            push(source(every, every, every, 1 - at.c), room[0], self.send.at[u], self.recv.at[u, 0], at.dev(c=1 - at.c))
            return
        drain(room[k - 1], self.recv.at[u, k - 1])
        if k == 4:
            total = self.own(u, (at.z, at.y, at.x))[...].astype(jnp.float32)
            for buf in self.bufs(u, 3):
                total = total + buf[...].astype(jnp.float32)
            out[...] = total
            for block in room:
                drain(block, self.send.at[u])
            return
        if k == 1:
            if not whole:
                drain(own, self.local.at[u])
            self.add_in(u, 0, [room[0]])
        else:
            self.add_in(u, k - 1, self.bufs(u, k - 1))
        where = self.left(u, k - 1)
        axis = order[k - 1]
        if axis == 0:
            for z in at.z_others():
                where[0] = z
                slot = lax.rem(z - at.z + self.dims[0], self.dims[0]) - 1
                push(self.own(u, where), room[k].at[slot], self.send.at[u], self.recv.at[u, k], at.dev(z=z))
        else:
            where[axis] = (None, 1 - at.y, 1 - at.x)[axis]
            device = at.dev(y=1 - at.y) if axis == 1 else at.dev(x=1 - at.x)
            push(self.own(u, where), room[k], self.send.at[u], self.recv.at[u, k], device)


def scatter_room(dims, tile, dtype, order, whole):
    nz, ny, nx, nc = dims
    rooms = [((nz, ny, nx, nc) if whole else (nz, ny, nx)) + tile, (nz, ny, nx) + tile]
    for k in range(3):
        lead = tuple(dims[axis] for axis in range(3) if axis not in order[: k + 1])
        rooms.append(((nz - 1,) if order[k] == 0 else ()) + lead + tile)
    return [pltpu.VMEM(shape, dtype) for shape in rooms]


def norm_back(x, dh, gain):
    center = x - jnp.mean(x, axis=-1, keepdims=True)
    r = lax.rsqrt(jnp.mean(center * center, axis=-1, keepdims=True) + EPS)
    n = center * r
    dn = dh * gain
    dx = r * (dn - jnp.mean(dn, axis=-1, keepdims=True) - n * jnp.mean(dn * n, axis=-1, keepdims=True))
    return dx, dh * n


def row_sum(rows):
    return jnp.sum(rows, axis=0, keepdims=True)


TN = (((0,), (0,)), ((), ()))


MIDDLE_PATHS = (
    (1, 0, 2), (0, 1, 2), (1, 0, 2), (1, 2, 0), (2, 1, 0), (2, 1, 0),
)
MIDDLE_ORDER = (
    (0, 0), (1, 0), (2, 0), (3, 0), (4, 0), (-2, 0), (0, 1), (1, 1), (-2, 1), (2, 1), (3, 1), (-2, 2), (5, 0),
    (4, 1), (-2, 3), (-2, 4), (5, 1), (0, 2), (-2, 5), (-2, 6), (-2, 7), (-2, 8), (-2, 9), (-2, 10), (2, 2), (1, 2),
    (-2, 11), (-2, 12), (4, 2), (-2, 13), (3, 2), (0, 3), (1, 3), (-2, 14), (5, 2), (4, 3), (-2, 15), (2, 3), (3, 3),
    (0, 4), (1, 4), (5, 3), (4, 4), (2, 4), (3, 4), (5, 4),
)
LAST_SPLIT = 640
LAST_PATHS = (
    (2, 0, 1), (0, 1, 2), (1, 2, 0), (2, 1, 0), (1, 0, 2), (2, 1, 0), (2, 1, 0), (1, 0, 2), (1, 0, 2), (1, 0, 2),
    (0, 1, 2),
)
LAST_ORDER = (
    (0, 0), (1, 0), (2, 0), (3, 0), (-2, 0), (0, 1), (-2, 1), (1, 1), (2, 1), (-2, 2), (3, 1), (-2, 3), (0, 2),
    (-2, 4), (-2, 5), (2, 2), (-2, 6), (4, 0), (5, 0), (6, 0), (3, 2), (1, 2), (-2, 7), (2, 3), (4, 1), (5, 1),
    (6, 1), (-2, 8), (3, 3), (0, 3), (-2, 9), (1, 3), (-2, 10), (7, 0), (8, 0), (9, 0), (5, 2), (2, 4), (4, 2),
    (0, 4), (-2, 11), (7, 1), (8, 1), (3, 4), (9, 1), (6, 2), (1, 4), (-2, 12), (5, 3), (-2, 13), (4, 3), (7, 2),
    (-2, 14), (-2, 15), (10, 0), (5, 4), (8, 2), (10, 1), (7, 3), (9, 2), (6, 3), (8, 3), (10, 2), (10, 3), (9, 3),
    (4, 4), (7, 4), (8, 4), (10, 4), (6, 4), (9, 4),
)


def middle_kernel(dims, *refs):
    (g_in, dh_in, x2_in, x1_in, vec, o2_in, cq_in, ck_in, cv_in, lse_in, h2_in, o_in, wco_in, wcq_in, wck_in, wcv_in, wo_in,
     text_in, limits, block_in, down_in, up_in) = refs[:22]
    block_out, text_out, dx_out, do_out, gcq_out, gck_out, gcv_out, go_out, sums, down_out, up_out, co_out = refs[22:34]
    (x2, dh3, dx, g, dy, do, o2, wco, cq, dcq, wcq, wck, wcv, ck, cv, dck, dcv, lse, text, tg, stage, dk_acc, dv_acc, limit,
     load_sem, out_sem, ex_send, ex_recv, send, recv, local, own_rows) = refs[34:66]
    rooms = refs[66:]
    at = Place(dims)
    nz = dims[0]
    oy, ox, oc, me = 1 - at.y, 1 - at.x, 1 - at.c, at.seq
    hello([at.dev(z=p) for p in at.z_others()] + [at.dev(y=oy), at.dev(x=ox), at.dev(c=oc), at.dev(x=ox, c=oc)])
    others = ((ox, at.c), (ox, oc), (at.x, oc))
    rows, width = g.shape
    block = 256
    f32, bf = jnp.float32, jnp.bfloat16
    every = slice(None)
    net = Scatter(dims, send, recv, local)
    quarter = width // 4
    room = [rooms[5 * j : 5 * j + 5] for j in range(6)]
    for j in range(4):
        cols = pl.ds(j * quarter, quarter)
        net.add(lambda *w, cols=cols: down_in.at[(*w, every, cols)], room[j], down_out.at[:, cols], MIDDLE_PATHS[j], False)
    net.add(lambda *w: up_in.at[w], room[4], up_out, MIDDLE_PATHS[4], False)
    net.add(lambda *w: room[5][0].at[w], room[5], co_out, MIDDLE_PATHS[5], True)

    def exchange(src, dst, i, own):
        for px, pc in others:
            push(src.at[px * 2 + pc], dst.at[me], ex_send.at[i], ex_recv.at[i], at.dev(x=px, c=pc))
        pltpu.make_async_copy(own, dst.at[me], local.at[6 + i]).start()

    started = []

    def load(src, dst):
        pltpu.make_async_copy(src, dst, load_sem.at[len(started)]).start()
        started.append(dst)
        return len(started) - 1

    def loaded(i):
        drain(started[i], load_sem.at[i])

    kept = []

    def put(src, dst):
        pltpu.make_async_copy(src, dst, out_sem.at[len(kept)]).start()
        kept.append(src)
        return len(kept) - 1

    def kept_done(i):
        drain(kept[i], out_sem.at[i])

    def span_of(r):
        return pl.ds(pl.multiple_of(r * block, block), block)

    def weight_grad(src, grad, made):
        @pl.loop(0, nz)
        def _(a):
            part = dot(src[:, pl.ds(pl.multiple_of(a * block, block), block)], grad[...], TN).astype(bf)
            made[a] = part.reshape(made.shape[1:])

    own_load = load(block_in.at[me], own_rows)
    first = [load(dh_in, dh3), load(x2_in, x2), load(g_in, g), load(wco_in, wco), load(o2_in, o2)]
    second = [load(cq_in, cq), load(ck_in, ck), load(cv_in, cv), load(lse_in, lse)]
    third = [load(text_in.at[me], text), load(wcq_in, wcq), load(wck_in, wck), load(wcv_in, wcv)]
    limit[0] = limits[me]
    run_order(MIDDLE_ORDER[:5], net.go, [])
    loaded(own_load)
    exchange(block_in, block_out, 0, own_rows)
    for i in first[:-1]:
        loaded(i)
    sums[...] = jnp.zeros_like(sums)

    def last_norm(r):
        span = span_of(r)
        d = dh3[span, :]
        grad, gain_terms = norm_back(x2[span, :], d, vec[4:5, :])
        sums[4:5, :] += row_sum(gain_terms)
        sums[5:6, :] += row_sum(d)
        total = g[span, :].astype(f32) + grad
        dx[span, :] = total
        low = total.astype(bf)
        dy[span, :] = low
        do[span, :] = dot(low, wco[...], NT).astype(bf)

    def middle_norm(r):
        span = span_of(r)
        d = dot(dcq[span, :], wcq[...], NT)
        grad, gain_terms = norm_back(x2[span, :], d, vec[2:3, :])
        sums[2:3, :] += row_sum(gain_terms)
        sums[3:4, :] += row_sum(d)
        total = dx[span, :] + grad
        dx[span, :] = total
        low = total.astype(bf)
        dy[span, :] = low
        do[span, :] = dot(low, cq[...], NT).astype(bf)

    later = {}

    def after_last_norm():
        pl.loop(2, 4)(last_norm)
        later["x1"], later["o"], later["h2"] = load(x1_in, x2), load(o_in, g), load(h2_in, wco)

    def output_weight_grad():
        loaded(first[-1])
        weight_grad(o2, dy, room[5][0])
        for i in second:
            loaded(i)

    def cross(j):
        cols = pl.ds(pl.multiple_of(j * 128, 128), 128)
        attend_back_kernel(
            False, 512, limit, cq.at[:, cols], ck.at[:, cols], cv.at[:, cols], do.at[:, cols], o2.at[:, cols], lse.at[pl.ds(j, 1)],
            dcq.at[:, cols], dck.at[:, cols], dcv.at[:, cols], dk_acc, dv_acc,
        )

    def query_weight_grad():
        later["wo"] = load(wo_in, cq)
        for i in third:
            loaded(i)
        loaded(later["h2"])
        weight_grad(wco, dcq, stage.at[0])
        later["cq"] = put(stage.at[0], gcq_out)
        tg[...] = (dot(dck[...], wck[...], NT) + dot(dcv[...], wcv[...], NT)).reshape(tg.shape)
        exchange(tg, text_out, 1, tg.at[me])
        loaded(later["x1"])
        loaded(later["wo"])

    def after_middle_norm():
        pl.loop(2, 4)(middle_norm)
        put(dx, dx_out)
        put(do, do_out)

    def self_weight_grad():
        loaded(later["o"])
        weight_grad(g, dy, stage.at[1])
        later["o"] = put(stage.at[1], go_out)

    def text_weight_grads():
        kept_done(later["cq"])
        weight_grad(text, dck, stage.at[0])
        put(stage.at[0], gck_out)
        kept_done(later["o"])
        weight_grad(text, dcv, stage.at[1])
        put(stage.at[1], gcv_out)

    pieces = [lambda: pl.loop(0, 2)(last_norm), after_last_norm, output_weight_grad]
    pieces += [(cross, j) for j in range(width // 128)]
    pieces += [query_weight_grad, lambda: pl.loop(0, 2)(middle_norm), after_middle_norm, self_weight_grad, text_weight_grads]
    run_order(MIDDLE_ORDER[5:], net.go, pieces)
    for i, dst in ((0, block_out), (1, text_out)):
        drain(dst.at[0:3], ex_recv.at[i])
        drain(dst.at[0:3], ex_send.at[i])
        drain(dst.at[0], local.at[6 + i])
    for i in range(len(kept)):
        if i not in (later["cq"], later["o"]):
            kept_done(i)


def middle(dims, args, cid):
    nz, ny, nx, nc = dims
    g, dh, x2, x1, vec, o2, cq, ck, cv, lse, h2, o, wco, wcq, wck, wcv, wo, text, limits, block_out, down, up = args
    rows, width = g.shape
    texts = text.shape[1]
    devices = nz * ny * nx * nc
    bf, f32 = jnp.bfloat16, jnp.float32
    each = width // devices
    long = down.shape[0] // devices
    down = down.reshape(nz, ny, nx, nc, long, width)
    up = up.reshape(nz, ny, nx, nc, each, up.shape[1])
    seg = block_out.shape
    held = jax.ShapeDtypeStruct((nz, ny, nx, nc, each, width), bf)
    wide, deep = jax.ShapeDtypeStruct((rows, width), bf), jax.ShapeDtypeStruct((rows, width), f32)
    out_shape = [
        jax.ShapeDtypeStruct(seg, bf), jax.ShapeDtypeStruct((seg[0], texts // seg[0], width), f32), deep, wide, held, held, held, held,
        jax.ShapeDtypeStruct((8, width), f32), jax.ShapeDtypeStruct((long, width), f32), jax.ShapeDtypeStruct((each, up.shape[5]), f32),
        jax.ShapeDtypeStruct((each, width), f32),
    ]
    any_spec, vm = pl.BlockSpec(memory_space=ANY), pl.BlockSpec(memory_space=pltpu.VMEM)
    big, square, short = pltpu.VMEM((rows, width), f32), pltpu.VMEM((rows, width), bf), pltpu.VMEM((texts, width), bf)
    dma = pltpu.SemaphoreType.DMA
    scratch = [big, big, big] + [square] * 10 + [short] * 4 + [pltpu.VMEM(lse.shape, f32), short]
    scratch += [pltpu.VMEM((seg[0], texts // seg[0], width), f32), pltpu.VMEM((2,) + held.shape, bf)]
    scratch += [pltpu.VMEM((texts, 128), f32)] * 2 + [pltpu.SMEM((1,), jnp.int32)]
    scratch += [dma((20,)), dma((12,)), dma((2,)), dma((2,)), dma((6,)), dma((6, 4)), dma((8,)), pltpu.VMEM(seg[1:], bf)]
    for j in range(4):
        scratch += scatter_room(dims, (long, width // 4), bf, MIDDLE_PATHS[j], False)
    scratch += scatter_room(dims, (each, up.shape[5]), bf, MIDDLE_PATHS[4], False)
    scratch += scatter_room(dims, (each, width), bf, MIDDLE_PATHS[5], True)
    specs = [any_spec] * 4 + [vm] + [any_spec] * 13 + [pl.BlockSpec(memory_space=pltpu.SMEM)] + [any_spec] * 3
    return pl.pallas_call(
        functools.partial(middle_kernel, dims),
        out_shape=out_shape,
        in_specs=specs,
        out_specs=[any_spec] * 8 + [vm] * 4,
        scratch_shapes=scratch,
        compiler_params=pltpu.CompilerParams(collective_id=cid, has_side_effects=True, vmem_limit_bytes=63 * 2**20),
        name="middle",
    )(g, dh, x2, x1, vec, o2, cq, ck, cv, lse, h2, o, wco, wcq, wck, wcv, wo, text, limits, block_out, down, up)


def last_kernel(dims, *refs):
    q_in, k_in, v_in, do_in, o_in, lse_in, h1_in, wq_in, wk_in, wv_in, x_in, dx_in, vec, gcq, gck, gcv, go, sums_in = refs[:18]
    grad_out, cq_out, ck_out, cv_out, o_out, q_out, k_out, v_out, small_out = refs[18:27]
    (q, k, v, do, o, lse, h_t, dq, dk, dv, dx, send_rows, small, dk_acc, dv_acc, sums,
     load_sem, ex_send, ex_recv, send, recv, local) = refs[27:49]
    rooms = refs[49:]
    at = Place(dims)
    nz, ny, nx, nc = dims
    oy, ox, oc, me = 1 - at.y, 1 - at.x, 1 - at.c, at.seq
    hello([at.dev(z=p) for p in at.z_others()] + [at.dev(y=oy), at.dev(x=ox), at.dev(c=oc), at.dev(x=ox, c=oc)])
    rows, width = q.shape
    block = 256
    f32, bf = jnp.float32, jnp.bfloat16
    every = slice(None)
    net = Scatter(dims, send, recv, local)
    room = [rooms[5 * j : 5 * j + 5] for j in range(10)] + [[small, *rooms[50:54]]]
    for j, (src, out) in enumerate(((gcq, cq_out), (gck, ck_out), (gcv, cv_out), (go, o_out))):
        net.add(lambda *w, src=src: src.at[w], room[j], out, LAST_PATHS[j], False)
    parts = ((0, LAST_SPLIT), (LAST_SPLIT, width - LAST_SPLIT))
    for j in range(6):
        out = (q_out, k_out, v_out)[j % 3].at[:, pl.ds(*parts[j // 3])]
        net.add(lambda *w, held=room[4 + j][0]: held.at[w], room[4 + j], out, LAST_PATHS[4 + j], True)
    net.add(lambda *w: small.at[w], room[10], small_out, LAST_PATHS[10], True)
    run_order(LAST_ORDER[:4], net.go, [])
    started = []

    def load(src, dst):
        pltpu.make_async_copy(src, dst, load_sem.at[len(started)]).start()
        started.append(dst)
        return len(started) - 1

    def loaded(i):
        drain(started[i], load_sem.at[i])

    first = [load(a, b) for a, b in ((q_in, q), (k_in, k), (v_in, v), (do_in, do), (o_in, o), (lse_in, lse), (h1_in, send_rows), (dx_in, dx))]

    def begin():
        for i in first[:6]:
            loaded(i)

    def transpose():
        loaded(first[6])
        loaded(first[7])

        @pl.loop(0, rows // block)
        def _(r):
            h_t[:, pl.ds(pl.multiple_of(r * block, block), block)] = send_rows[r].T

    def pair(j):
        cols = pl.ds(pl.multiple_of(j * 128, 128), 128)
        attend_back_kernel(
            True, 256, None, q.at[:, cols], k.at[:, cols], v.at[:, cols], do.at[:, cols], o.at[:, cols], lse.at[pl.ds(j, 1)],
            dq.at[:, cols], dk.at[:, cols], dv.at[:, cols], dk_acc, dv_acc,
        )

    weights = []

    def weight_grads(part):
        if part == 0:
            transpose()
        if part == 1:
            weights.extend(load(a, b) for a, b in ((wq_in, q), (wk_in, k), (wv_in, v), (x_in, do)))
        for j, grad in enumerate((dq, dk, dv)):
            made = room[4 + 3 * part + j][0]

            @pl.loop(0, nz)
            def _(a, made=made, grad=grad):
                span = pl.ds(pl.multiple_of(a * block, block), block)
                product = dot(h_t[span, :], grad[:, pl.ds(*parts[part])]).astype(bf)
                made[a] = product.reshape(made.shape[1:])

        if part == 1:
            for i in weights:
                loaded(i)
            sums[...] = sums_in[...]

    def last_norm(r):
        span = pl.ds(pl.multiple_of(r * block, block), block)
        d = dot(dq[span, :], q[...], NT) + dot(dk[span, :], k[...], NT) + dot(dv[span, :], v[...], NT)
        grad, gain_terms = norm_back(do[span, :].astype(f32), d, vec[0:1, :])
        sums[0:1, :] += row_sum(gain_terms)
        sums[1:2, :] += row_sum(d)
        send_rows[r] = (dx[span, :] + grad).astype(bf)

    targets = ((ox, at.c), (ox, oc), (at.x, oc), (at.x, at.c))

    def send_norm(i):
        px, pc = targets[i]
        last_norm(px * 2 + pc)
        if i < 3:
            push(send_rows.at[px * 2 + pc], grad_out.at[me], ex_send, ex_recv, at.dev(x=px, c=pc))
        else:
            pltpu.make_async_copy(send_rows.at[me], grad_out.at[me], local.at[11]).start()

    def share_sums():
        devices = nz * ny * nx * nc
        piece = width // devices
        lanes = lax.broadcasted_iota(jnp.int32, (width, 128), 0)
        fold = jnp.where(lax.rem(lanes, piece) == lax.broadcasted_iota(jnp.int32, (width, 128), 1), 1.0, 0.0).astype(bf)
        mine = lax.div(lax.broadcasted_iota(jnp.int32, (devices, width), 1), piece) == lax.broadcasted_iota(jnp.int32, (devices, width), 0)
        shares = []
        for i in range(6):
            spread = jnp.where(mine, sums[i : i + 1, :], 0.0)
            total = jnp.zeros((devices, 128), f32)
            for _ in range(3):
                low = spread.astype(bf)
                spread = spread - low.astype(f32)
                total = total + dot(low, fold)
            shares.append(total[:, None, :])
        shares.append(jnp.zeros((devices, 2, 128), f32))
        small[...] = jnp.concatenate(shares, axis=1).reshape(small.shape)

    split = LAST_SPLIT // 128
    pieces = [begin] + [(pair, j) for j in range(split)] + [lambda: weight_grads(0)]
    pieces += [(pair, j) for j in range(split, width // 128)] + [lambda: weight_grads(1)]
    pieces += [functools.partial(send_norm, i) for i in range(4)] + [share_sums]
    run_order(LAST_ORDER[4:], net.go, pieces)
    drain(grad_out.at[0:3], ex_recv)
    drain(grad_out.at[0:3], ex_send)
    drain(grad_out.at[0], local.at[11])


def last(dims, args, cid):
    nz, ny, nx, nc = dims
    q, k, v, do, o, lse, h1, wq, wk, wv, x, dx, vec, gcq, gck, gcv, go, sums = args
    rows, width = q.shape
    bf, f32 = jnp.bfloat16, jnp.float32
    each = width // (nz * ny * nx * nc)
    shard = jax.ShapeDtypeStruct((each, width), f32)
    out_shape = [jax.ShapeDtypeStruct((4, rows // 4, width), bf)] + [shard] * 7 + [jax.ShapeDtypeStruct((8, 128), f32)]
    any_spec, vm = pl.BlockSpec(memory_space=ANY), pl.BlockSpec(memory_space=pltpu.VMEM)
    square = pltpu.VMEM((rows, width), bf)
    dma = pltpu.SemaphoreType.DMA
    scratch = [square] * 5 + [pltpu.VMEM(lse.shape, f32)] + [square] * 4 + [pltpu.VMEM((rows, width), f32), pltpu.VMEM((4, rows // 4, width), bf)]
    scratch += [pltpu.VMEM((nz, ny, nx, nc, 8, 128), f32)] + [pltpu.VMEM((rows, 128), f32)] * 2 + [pltpu.VMEM((8, width), f32)]
    scratch += [dma((16,)), dma, dma, dma((11,)), dma((11, 4)), dma((12,))]
    for j in range(4):
        scratch += scatter_room(dims, (each, width), bf, LAST_PATHS[j], False)
    for j in range(6):
        scratch += scatter_room(dims, (each, LAST_SPLIT if j < 3 else width - LAST_SPLIT), bf, LAST_PATHS[4 + j], True)
    scratch += scatter_room(dims, (8, 128), f32, LAST_PATHS[10], True)[1:]
    return pl.pallas_call(
        functools.partial(last_kernel, dims),
        out_shape=out_shape,
        in_specs=[any_spec] * 12 + [vm] + [any_spec] * 4 + [vm],
        out_specs=[any_spec] + [vm] * 8,
        scratch_shapes=scratch,
        compiler_params=pltpu.CompilerParams(collective_id=cid, has_side_effects=True, vmem_limit_bytes=63 * 2**20),
        name="last",
    )(q, k, v, do, o, lse, h1.reshape(4, rows // 4, width), wq, wk, wv, x, dx, vec, gcq, gck, gcv, go, sums)

HEAD_DIM = 64


EPS = 1e-05


def norm_rows(values_in, gain, bias):
    center = values_in - jnp.mean(values_in, axis=-1, keepdims=True)
    spread = jnp.mean(center * center, axis=-1, keepdims=True)
    return center * lax.rsqrt(spread + EPS) * gain + bias


def contract_rows(left, right):
    return lax.dot_general(
        left, right, (((0,), (0,)), ((), ())), preferred_element_type=jnp.float32
    )


def times_transposed(left, right):
    return lax.dot_general(
        left, right, (((1,), (1,)), ((), ())), preferred_element_type=jnp.float32
    )


def product(left, right):
    return jnp.dot(left, right, preferred_element_type=jnp.float32)


def local_plain(
    block_in,
    text_states,
    caption_len,
    out_grad,
    first_gain,
    first_bias,
    query_weight,
    key_weight,
    value_weight,
    output_weight,
    second_gain,
    second_bias,
    cross_query,
    cross_key,
    cross_value,
    cross_output,
    third_gain,
    third_bias,
    up_weight,
    down_weight,
):
    gathered = (
        lax.all_gather(first_gain, ("dp", "seq"), axis=0, tiled=True),
        lax.all_gather(first_bias, ("dp", "seq"), axis=0, tiled=True),
        lax.all_gather(query_weight, ("dp", "seq"), axis=0, tiled=True),
        lax.all_gather(key_weight, ("dp", "seq"), axis=0, tiled=True),
        lax.all_gather(value_weight, ("dp", "seq"), axis=0, tiled=True),
        lax.all_gather(output_weight, ("dp", "seq"), axis=0, tiled=True),
        lax.all_gather(second_gain, ("dp", "seq"), axis=0, tiled=True),
        lax.all_gather(second_bias, ("dp", "seq"), axis=0, tiled=True),
        lax.all_gather(cross_query, ("dp", "seq"), axis=0, tiled=True),
        lax.all_gather(cross_key, ("dp", "seq"), axis=0, tiled=True),
        lax.all_gather(cross_value, ("dp", "seq"), axis=0, tiled=True),
        lax.all_gather(cross_output, ("dp", "seq"), axis=0, tiled=True),
        lax.all_gather(third_gain, ("dp", "seq"), axis=0, tiled=True),
        lax.all_gather(third_bias, ("dp", "seq"), axis=0, tiled=True),
        lax.all_gather(up_weight, ("dp", "seq"), axis=0, tiled=True),
        lax.all_gather(down_weight, ("dp", "seq"), axis=0, tiled=True),
    )
    (
        gain_one,
        bias_one,
        w_query,
        w_key,
        w_value,
        w_output,
        gain_two,
        bias_two,
        w_cquery,
        w_ckey,
        w_cvalue,
        w_coutput,
        gain_three,
        bias_three,
        w_up,
        w_down,
    ) = gathered
    item_count, seg_len, model_width = block_in.shape
    row_count = item_count * seg_len
    head_count = model_width // HEAD_DIM
    score_scale = HEAD_DIM ** (-0.5)
    text_count = text_states.shape[1]
    inputs_f = block_in.astype(jnp.float32).reshape(row_count, model_width)
    normed_one, pull_one = jax.vjp(
        norm_rows, inputs_f, gain_one.astype(jnp.float32), bias_one.astype(jnp.float32)
    )
    normed_one = normed_one.astype(jnp.bfloat16)
    query_rows = product(normed_one, w_query).astype(jnp.bfloat16)
    key_rows = product(normed_one, w_key).astype(jnp.bfloat16)
    value_rows = product(normed_one, w_value).astype(jnp.bfloat16)
    key_all, value_all = (
        lax.all_gather(
            key_rows.reshape(item_count, seg_len, model_width), "seq", axis=1, tiled=True
        ),
        lax.all_gather(
            value_rows.reshape(item_count, seg_len, model_width), "seq", axis=1, tiled=True
        ),
    )
    key_count = key_all.shape[1]
    first_pos = lax.axis_index("seq") * seg_len
    query_pos = first_pos + jnp.arange(seg_len, dtype=jnp.int32)
    causal = jnp.arange(key_count, dtype=jnp.int32)[None, :] <= query_pos[:, None]

    def self_scores(query_item, key_item):
        query_heads = query_item.reshape(seg_len, head_count, HEAD_DIM)
        key_heads = key_item.reshape(key_count, head_count, HEAD_DIM)
        scores = jnp.einsum(
            "qhd,khd->hqk", query_heads, key_heads, preferred_element_type=jnp.float32
        )
        return jnp.where(causal[None, :, :], scores * score_scale, -1e30)

    def self_forward(operands):
        query_item, key_item, value_item = operands
        scores = self_scores(query_item, key_item)
        row_peak = jnp.max(scores, axis=-1, keepdims=True)
        row_total = jnp.sum(jnp.exp(scores - row_peak), axis=-1, keepdims=True)
        log_total = row_peak + jnp.log(row_total)
        prob_bf = jnp.exp(scores - log_total).astype(jnp.bfloat16)
        value_heads = value_item.reshape(key_count, head_count, HEAD_DIM)
        mixed = jnp.einsum("hqk,khd->qhd", prob_bf, value_heads, preferred_element_type=jnp.float32)
        return (mixed.reshape(seg_len, model_width).astype(jnp.bfloat16), log_total)

    attended, log_totals = lax.map(
        self_forward, (query_rows.reshape(item_count, seg_len, model_width), key_all, value_all)
    )
    attended_rows = attended.reshape(row_count, model_width)
    after_self = inputs_f + product(attended_rows, w_output)
    normed_two, pull_two = jax.vjp(
        norm_rows, after_self, gain_two.astype(jnp.float32), bias_two.astype(jnp.float32)
    )
    normed_two = normed_two.astype(jnp.bfloat16)
    cross_rows = product(normed_two, w_cquery).astype(jnp.bfloat16)
    cross_heads = cross_rows.reshape(item_count, seg_len, head_count, HEAD_DIM)
    text_keys = jnp.einsum(
        "itc,cd->itd", text_states, w_ckey, preferred_element_type=jnp.float32
    ).astype(jnp.bfloat16)
    text_values = jnp.einsum(
        "itc,cd->itd", text_states, w_cvalue, preferred_element_type=jnp.float32
    ).astype(jnp.bfloat16)
    text_kheads = text_keys.reshape(item_count, text_count, head_count, HEAD_DIM)
    text_vheads = text_values.reshape(item_count, text_count, head_count, HEAD_DIM)
    text_mask = jnp.arange(text_count, dtype=jnp.int32)[None, :] < caption_len[:, None]
    cross_scores = jnp.einsum(
        "iqhd,ithd->ihqt", cross_heads, text_kheads, preferred_element_type=jnp.float32
    )
    cross_scores = jnp.where(text_mask[:, None, None, :], cross_scores * score_scale, -1e30)
    cross_peak = jnp.max(cross_scores, axis=-1, keepdims=True)
    cross_exp = jnp.exp(cross_scores - cross_peak)
    cross_prob = cross_exp / jnp.sum(cross_exp, axis=-1, keepdims=True)
    cross_prob_bf = cross_prob.astype(jnp.bfloat16)
    crossed = jnp.einsum(
        "ihqt,ithd->iqhd", cross_prob_bf, text_vheads, preferred_element_type=jnp.float32
    )
    crossed_rows = crossed.reshape(row_count, model_width).astype(jnp.bfloat16)
    after_cross = after_self + product(crossed_rows, w_coutput)
    normed_three, pull_three = jax.vjp(
        norm_rows, after_cross, gain_three.astype(jnp.float32), bias_three.astype(jnp.float32)
    )
    normed_three = normed_three.astype(jnp.bfloat16)
    hidden = product(normed_three, w_up)
    activated, pull_gelu = jax.vjp(lambda inner: jax.nn.gelu(inner, approximate=False), hidden)
    activated = activated.astype(jnp.bfloat16)
    layer_out = after_cross + product(activated, w_down)
    block_out = layer_out.astype(jnp.bfloat16).reshape(item_count, seg_len, model_width)
    back_weights = (
        lax.all_gather(first_gain, ("dp", "seq"), axis=0, tiled=True),
        lax.all_gather(first_bias, ("dp", "seq"), axis=0, tiled=True),
        lax.all_gather(query_weight, ("dp", "seq"), axis=0, tiled=True),
        lax.all_gather(key_weight, ("dp", "seq"), axis=0, tiled=True),
        lax.all_gather(value_weight, ("dp", "seq"), axis=0, tiled=True),
        lax.all_gather(output_weight, ("dp", "seq"), axis=0, tiled=True),
        lax.all_gather(second_gain, ("dp", "seq"), axis=0, tiled=True),
        lax.all_gather(second_bias, ("dp", "seq"), axis=0, tiled=True),
        lax.all_gather(cross_query, ("dp", "seq"), axis=0, tiled=True),
        lax.all_gather(cross_key, ("dp", "seq"), axis=0, tiled=True),
        lax.all_gather(cross_value, ("dp", "seq"), axis=0, tiled=True),
        lax.all_gather(cross_output, ("dp", "seq"), axis=0, tiled=True),
        lax.all_gather(third_gain, ("dp", "seq"), axis=0, tiled=True),
        lax.all_gather(third_bias, ("dp", "seq"), axis=0, tiled=True),
        lax.all_gather(up_weight, ("dp", "seq"), axis=0, tiled=True),
        lax.all_gather(down_weight, ("dp", "seq"), axis=0, tiled=True),
    )
    (
        unused_gain,
        unused_bias,
        w_query,
        w_key,
        w_value,
        w_output,
        unused_gtwo,
        unused_btwo,
        w_cquery,
        w_ckey,
        w_cvalue,
        w_coutput,
        unused_gthree,
        unused_bthree,
        w_up,
        w_down,
    ) = back_weights
    grad_rows = out_grad.reshape(row_count, model_width)
    down_part = contract_rows(activated, grad_rows)
    act_grad = times_transposed(grad_rows, w_down)
    hidden_grad = pull_gelu(act_grad)[0].astype(jnp.bfloat16)
    up_part = contract_rows(normed_three, hidden_grad)
    normed_three_grad = times_transposed(hidden_grad, w_up)
    resid_three, gain_three_part, bias_three_part = pull_three(normed_three_grad)
    cross_grad = grad_rows.astype(jnp.float32) + resid_three
    cross_out_bf = cross_grad.astype(jnp.bfloat16)
    coutput_part = contract_rows(crossed_rows, cross_out_bf)
    crossed_grad = times_transposed(cross_out_bf, w_coutput).astype(jnp.bfloat16)
    crossed_heads = crossed_grad.reshape(item_count, seg_len, head_count, HEAD_DIM)
    cross_dprob = jnp.einsum(
        "iqhd,ithd->ihqt", crossed_heads, text_vheads, preferred_element_type=jnp.float32
    )
    cross_dscore = cross_prob * (
        cross_dprob - jnp.sum(cross_dprob * cross_prob, axis=-1, keepdims=True)
    )
    cross_dscore = cross_dscore.astype(jnp.bfloat16)
    cquery_grad = (
        (
            jnp.einsum(
                "ihqt,ithd->iqhd", cross_dscore, text_kheads, preferred_element_type=jnp.float32
            )
            * score_scale
        )
        .astype(jnp.bfloat16)
        .reshape(row_count, model_width)
    )
    tkey_part = (
        jnp.einsum("ihqt,iqhd->ithd", cross_dscore, cross_heads, preferred_element_type=jnp.float32)
        * score_scale
    ).reshape(item_count, text_count, model_width)
    tvalue_part = jnp.einsum(
        "ihqt,iqhd->ithd", cross_prob_bf, crossed_heads, preferred_element_type=jnp.float32
    ).reshape(item_count, text_count, model_width)
    cquery_part = contract_rows(normed_two, cquery_grad)
    normed_two_grad = times_transposed(cquery_grad, w_cquery)
    resid_two, gain_two_part, bias_two_part = pull_two(normed_two_grad)
    self_grad = cross_grad + resid_two
    self_out_bf = self_grad.astype(jnp.bfloat16)
    output_part = contract_rows(attended_rows, self_out_bf)
    attended_grad = times_transposed(self_out_bf, w_output).astype(jnp.bfloat16)
    query_items = query_rows.reshape(item_count, seg_len, model_width)
    dout_items = attended_grad.reshape(item_count, seg_len, model_width)

    def self_backward(operands):
        query_item, key_item, value_item, dout_item, log_total = operands
        scores = self_scores(query_item, key_item)
        probs = jnp.exp(scores - log_total)
        prob_bf = probs.astype(jnp.bfloat16)
        query_heads = query_item.reshape(seg_len, head_count, HEAD_DIM)
        key_heads = key_item.reshape(key_count, head_count, HEAD_DIM)
        value_heads = value_item.reshape(key_count, head_count, HEAD_DIM)
        dout_heads = dout_item.reshape(seg_len, head_count, HEAD_DIM)
        dprob = jnp.einsum(
            "qhd,khd->hqk", dout_heads, value_heads, preferred_element_type=jnp.float32
        )
        dscore = (probs * (dprob - jnp.sum(dprob * probs, axis=-1, keepdims=True))).astype(
            jnp.bfloat16
        )
        dquery = (
            (
                jnp.einsum("hqk,khd->qhd", dscore, key_heads, preferred_element_type=jnp.float32)
                * score_scale
            )
            .astype(jnp.bfloat16)
            .reshape(seg_len, model_width)
        )
        dkey = (
            jnp.einsum("hqk,qhd->khd", dscore, query_heads, preferred_element_type=jnp.float32)
            * score_scale
        ).reshape(key_count, model_width)
        dvalue = jnp.einsum(
            "hqk,qhd->khd", prob_bf, dout_heads, preferred_element_type=jnp.float32
        ).reshape(key_count, model_width)
        return (dquery, dkey, dvalue)

    query_grad_items, key_part, value_part = lax.map(
        self_backward, (query_items, key_all, value_all, dout_items, log_totals)
    )
    key_own, value_own, tkey_own, tvalue_own = (
        lax.psum_scatter(
            key_part.astype(jnp.bfloat16), "seq", scatter_dimension=1, tiled=True
        ).astype(jnp.float32),
        lax.psum_scatter(
            value_part.astype(jnp.bfloat16), "seq", scatter_dimension=1, tiled=True
        ).astype(jnp.float32),
        lax.psum_scatter(
            tkey_part.astype(jnp.bfloat16), "seq", scatter_dimension=1, tiled=True
        ).astype(jnp.float32),
        lax.psum_scatter(
            tvalue_part.astype(jnp.bfloat16), "seq", scatter_dimension=1, tiled=True
        ).astype(jnp.float32),
    )
    key_grad_rows = key_own.astype(jnp.bfloat16).reshape(row_count, model_width)
    value_grad_rows = value_own.astype(jnp.bfloat16).reshape(row_count, model_width)
    query_grad_rows = query_grad_items.reshape(row_count, model_width)
    tkey_bf = tkey_own.astype(jnp.bfloat16)
    tvalue_bf = tvalue_own.astype(jnp.bfloat16)
    query_part = contract_rows(normed_one, query_grad_rows)
    key_wpart = contract_rows(normed_one, key_grad_rows)
    value_wpart = contract_rows(normed_one, value_grad_rows)
    normed_one_grad = (
        times_transposed(query_grad_rows, w_query)
        + times_transposed(key_grad_rows, w_key)
        + times_transposed(value_grad_rows, w_value)
    )
    resid_one, gain_one_part, bias_one_part = pull_one(normed_one_grad)
    input_grad = (self_grad + resid_one).reshape(item_count, seg_len, model_width)
    text_rows = tkey_own.shape[1]
    text_start = lax.axis_index("seq") * text_rows
    text_slice = lax.dynamic_slice_in_dim(text_states, text_start, text_rows, 1)
    ckey_part = jnp.einsum("itc,itd->cd", text_slice, tkey_bf, preferred_element_type=jnp.float32)
    cvalue_part = jnp.einsum(
        "itc,itd->cd", text_slice, tvalue_bf, preferred_element_type=jnp.float32
    )
    text_grad = jnp.einsum(
        "itd,cd->itc", tkey_bf, w_ckey, preferred_element_type=jnp.float32
    ) + jnp.einsum("itd,cd->itc", tvalue_bf, w_cvalue, preferred_element_type=jnp.float32)
    (
        first_gain_grad,
        first_bias_grad,
        query_grad,
        key_grad,
        value_grad,
        output_grad,
        second_gain_grad,
        second_bias_grad,
        cross_query_grad,
        cross_key_grad,
        cross_value_grad,
        cross_output_grad,
        third_gain_grad,
        third_bias_grad,
        up_grad,
        down_grad,
    ) = (
        lax.psum_scatter(gain_one_part, ("dp", "seq"), scatter_dimension=0, tiled=True),
        lax.psum_scatter(bias_one_part, ("dp", "seq"), scatter_dimension=0, tiled=True),
        lax.psum_scatter(query_part, ("dp", "seq"), scatter_dimension=0, tiled=True),
        lax.psum_scatter(key_wpart, ("dp", "seq"), scatter_dimension=0, tiled=True),
        lax.psum_scatter(value_wpart, ("dp", "seq"), scatter_dimension=0, tiled=True),
        lax.psum_scatter(output_part, ("dp", "seq"), scatter_dimension=0, tiled=True),
        lax.psum_scatter(gain_two_part, ("dp", "seq"), scatter_dimension=0, tiled=True),
        lax.psum_scatter(bias_two_part, ("dp", "seq"), scatter_dimension=0, tiled=True),
        lax.psum_scatter(cquery_part, ("dp", "seq"), scatter_dimension=0, tiled=True),
        lax.psum_scatter(ckey_part, ("dp", "seq"), scatter_dimension=0, tiled=True),
        lax.psum_scatter(cvalue_part, ("dp", "seq"), scatter_dimension=0, tiled=True),
        lax.psum_scatter(coutput_part, ("dp", "seq"), scatter_dimension=0, tiled=True),
        lax.psum_scatter(gain_three_part, ("dp", "seq"), scatter_dimension=0, tiled=True),
        lax.psum_scatter(bias_three_part, ("dp", "seq"), scatter_dimension=0, tiled=True),
        lax.psum_scatter(up_part, ("dp", "seq"), scatter_dimension=0, tiled=True),
        lax.psum_scatter(down_part, ("dp", "seq"), scatter_dimension=0, tiled=True),
    )
    return (
        block_out,
        input_grad,
        text_grad,
        first_gain_grad,
        first_bias_grad,
        query_grad,
        key_grad,
        value_grad,
        output_grad,
        second_gain_grad,
        second_bias_grad,
        cross_query_grad,
        cross_key_grad,
        cross_value_grad,
        cross_output_grad,
        third_gain_grad,
        third_bias_grad,
        up_grad,
        down_grad,
    )


def widen_kernel(src, dst):
    dst[...] = src[...].astype(jnp.float32)


def widen(values):
    rows, width = values.shape
    block = pl.BlockSpec((rows // 4, width), lambda i: (i, 0))
    return pl.pallas_call(
        widen_kernel,
        grid=(4,),
        out_shape=jax.ShapeDtypeStruct((rows, width), jnp.float32),
        in_specs=[block],
        out_specs=block,
        compiler_params=pltpu.CompilerParams(vmem_limit_bytes=16 * 2**20),
        name="widen",
    )(values)


def small_rows(vectors):
    packed = jnp.stack(vectors)
    return jnp.pad(packed, ((0, 16 - packed.shape[0]), (0, 128 - packed.shape[1])))


def local(seq_size, *args):
    block_in = args[0]
    if block_in.shape[0] != seq_size or seq_size != 4 or block_in.shape[1] * seq_size != 1024:
        return local_plain(*args)
    return local_items(seq_size, *args)


def local_items(
    seq_size,
    block_in,
    text_states,
    caption_len,
    out_grad,
    first_gain,
    first_bias,
    query_weight,
    key_weight,
    value_weight,
    output_weight,
    second_gain,
    second_bias,
    cross_query,
    cross_key,
    cross_value,
    cross_output,
    third_gain,
    third_bias,
    up_weight,
    down_weight,
):
    ny, nx, nc = 2, seq_size // 2, 2
    dp_size = 1024 // first_gain.shape[0] // seq_size
    dims = (dp_size // ny, ny, nx, nc)
    bf, f32 = jnp.bfloat16, jnp.float32
    seg, width = block_in.shape[1], block_in.shape[2]
    rows = seq_size * seg
    me = lax.axis_index("seq")
    small = small_rows([first_gain, first_bias, second_gain, second_bias, third_gain, third_bias])
    shards = [small, query_weight, key_weight, value_weight, output_weight, cross_query, cross_key, cross_value, cross_output, up_weight, down_weight]
    full, kept = forward(dims, shards, block_in, out_grad, text_states, caption_len, 1)
    small, w_query, w_key, w_value, w_output, w_cquery, w_ckey, w_cvalue, w_coutput, w_up, w_down = full
    grad_rows, inputs, q, k, v, cq, ck, cv, o, o2, normed_one, normed_two, normed_three, after_self, after_cross, lse, lse2, vectors = kept
    grad_rows = grad_rows.reshape(rows, width)
    block_out, dh3, down_part, up_grad_done, up_part = ffn(dims, normed_three, grad_rows, after_cross, w_up, w_down, up_weight, 4)
    (
        block_out, text_grad, self_grad, do, g_cq, g_ck, g_cv, g_o, sums, down_grad, up_grad, coutput_grad,
    ) = middle(dims, (
        grad_rows, dh3, after_cross, after_self, vectors, o2, cq, ck, cv, lse2, normed_two, o, w_coutput, w_cquery, w_ckey, w_cvalue,
        w_output, text_states, caption_len, block_out.reshape(seq_size, seg, width), down_part, up_part,
    ), 2)
    up_grad = jnp.concatenate([up_grad_done, up_grad], axis=1)
    (
        input_grad, cquery_grad, ckey_grad, cvalue_grad, output_grad, query_grad, key_grad, value_grad, small_grad,
    ) = last(dims, (
        q, k, v, do, o, lse, normed_one, w_query, w_key, w_value, inputs.reshape(rows, width), self_grad, vectors,
        g_cq, g_ck, g_cv, g_o, sums,
    ), 3)
    input_grad = widen(input_grad.reshape(rows, width)).reshape(block_in.shape)
    vec = [small_grad[i, : first_gain.shape[0]] for i in range(6)]
    return (
        block_out, input_grad, text_grad,
        vec[0], vec[1], query_grad, key_grad, value_grad, output_grad,
        vec[2], vec[3], cquery_grad, ckey_grad, cvalue_grad, coutput_grad,
        vec[4], vec[5], up_grad, down_grad,
    )


def solution(mesh):
    return jax.shard_map(
        functools.partial(local, mesh.shape['seq']),
        mesh=mesh,
        in_specs=(
            P("dp", "seq", None),
            P("dp", None, None),
            P("dp"),
            P("dp", "seq", None),
            P(("dp", "seq")),
            P(("dp", "seq")),
            P(("dp", "seq"), None),
            P(("dp", "seq"), None),
            P(("dp", "seq"), None),
            P(("dp", "seq"), None),
            P(("dp", "seq")),
            P(("dp", "seq")),
            P(("dp", "seq"), None),
            P(("dp", "seq"), None),
            P(("dp", "seq"), None),
            P(("dp", "seq"), None),
            P(("dp", "seq")),
            P(("dp", "seq")),
            P(("dp", "seq"), None),
            P(("dp", "seq"), None),
        ),
        out_specs=(
            P("dp", "seq", None),
            P("dp", "seq", None),
            P("dp", "seq", None),
            P(("dp", "seq")),
            P(("dp", "seq")),
            P(("dp", "seq"), None),
            P(("dp", "seq"), None),
            P(("dp", "seq"), None),
            P(("dp", "seq"), None),
            P(("dp", "seq")),
            P(("dp", "seq")),
            P(("dp", "seq"), None),
            P(("dp", "seq"), None),
            P(("dp", "seq"), None),
            P(("dp", "seq"), None),
            P(("dp", "seq")),
            P(("dp", "seq")),
            P(("dp", "seq"), None),
            P(("dp", "seq"), None),
        ),
        check_vma=False,
    )
```
